32 devices in a mesh: seq: 16 (over z, y, core), rows: 2 (over x).
Axes of the slice: x: 2, y: 2, z: 4, core: 2. Of those that a mesh axis runs over, the one named last changes fastest.
Arguments:
- inputs: bfloat16 [4, 2048, 1024], P('rows', 'seq'), may hold values from -6 to 6
- memory: bfloat16 [4, 512, 1024], P('rows', 'seq'), may hold values from -6 to 6
- out_grad: bfloat16 [4, 2048, 1024], P('rows', 'seq'), may hold values from -6 to 6
- token_docs: int32 [4, 2048], P('rows', 'seq'), may hold values from 0 to 3, as said below
- memory_docs: int32 [4, 512], P('rows', 'seq'), may hold values from 0 to 3, as said below
- self_project: bfloat16 [1024, 3072], P(('seq', 'rows')), may hold values from -0.1875 to 0.1875
- self_output: bfloat16 [1024, 1024], P(('seq', 'rows')), may hold values from -6 to 6
- cross_query: bfloat16 [1024, 1024], P(('seq', 'rows')), may hold values from -0.1875 to 0.1875
- cross_memory: bfloat16 [1024, 2048], P(('seq', 'rows')), may hold values from -0.1875 to 0.1875
- cross_output: bfloat16 [1024, 1024], P(('seq', 'rows')), may hold values from -6 to 6
- inner_weight: bfloat16 [1024, 4096], P(('seq', 'rows')), may hold values from -0.1875 to 0.1875
- outer_weight: bfloat16 [4096, 1024], P(('seq', 'rows')), may hold values from -0.09375 to 0.09375
- adapter_down: bfloat16 [1024, 512], P(('seq', 'rows')), may hold values from -0.1875 to 0.1875
- adapter_up: bfloat16 [512, 1024], P(('seq', 'rows')), may hold values from -0.25 to 0.25
- norm_gains: bfloat16 [3, 1024], P(None, ('seq', 'rows')), may hold values from 0.5 to 1.5
- prefixes: bfloat16 [4, 30, 1024], P(None, None, ('seq', 'rows')), may hold values from -6 to 6
Outputs:
- layer_out: bfloat16 [4, 2048, 1024], P('rows', 'seq')
- input_grad: float32 [4, 2048, 1024], P('rows', 'seq')
- memory_grad: float32 [4, 512, 1024], P('rows', 'seq')
- prefix_grad: float32 [4, 30, 1024], P(None, None, ('seq', 'rows'))
- down_grad: float32 [1024, 512], P(('seq', 'rows'))
- up_grad: float32 [512, 1024], P(('seq', 'rows'))
The draws below stay inside these ranges and needn't reach their ends.
Inputs may be any that keep to these rules, and one draw needn't show every extreme that they name: `token_docs`: document numbers never fall along a row; decoder and memory tokens with equal numbers belong to one document; in each row one document runs from the first 128 tokens to the last 128. `memory_docs`: document numbers never fall along a row; in each row the document that spans the decoder row runs from the first 32 memory tokens to the last 32.
All inputs are finite; a program needn't handle non-finite values.
Results may differ from the reference program's by a relative error of at most 0.028.
Values may be sent and summed in bfloat16 or wider, within the bound.
A program may use at most 320 MiB of HBM per device.

```python
import math
import jax
import jax.numpy as jnp
from jax import lax

D = 1024
HEADS = 16
HEAD_DIM = 64
FF = 4096
ADAPTER = 512
PREFIX = 30
S_DEV = 128
M_DEV = 32
LENGTH = 2048
MEMORY = 512
ROWS = 4


def lead_count(key):
    return jax.random.randint(jax.random.fold_in(key, 7), (ROWS, 1, 1), 1, 3)


def doc_numbers(key, length, edge, lead):
    early = jax.random.randint(jax.random.fold_in(key, 1), (ROWS, 3, 1), 1, edge)
    late = length - jax.random.randint(jax.random.fold_in(key, 2), (ROWS, 3, 1), 1, edge)
    slot = jnp.arange(3, dtype=jnp.int32).reshape(1, 3, 1)
    bounds = jnp.where(slot < lead, early, late)
    places = jnp.arange(length, dtype=jnp.int32).reshape(1, 1, length)
    return jnp.sum((places >= bounds).astype(jnp.int32), axis=1)


def draw_token_docs(key, part):
    lead = lead_count(key)
    key = jax.random.fold_in(key, 11)
    return doc_numbers(key, LENGTH, S_DEV, lead)


def draw_memory_docs(key, part):
    lead = lead_count(key)
    key = jax.random.fold_in(key, 13)
    return doc_numbers(key, MEMORY, M_DEV, lead)


def level_of(key, dims, pieces, least, top_value):
    loudness, own = 1.0, jax.random.fold_in(key, 6)
    for axis_at, parts in pieces:
        draws = jnp.exp(jax.random.uniform(jax.random.fold_in(own, axis_at), (parts,), jnp.float32, least / len(pieces), top_value / len(pieces)))
        loudness = loudness * jnp.repeat(draws, dims[axis_at] // parts).reshape([-1 if axis == axis_at else 1 for axis in range(len(dims))])
    return loudness


def gaussian(rng, shape, scale, limit, cuts=(), kind=jnp.bfloat16):
    values = scale * jax.random.normal(rng, shape, jnp.float32)
    if cuts:
        values = values * level_of(rng, shape, cuts, -0.22, 0.18)
    return jnp.clip(values, -limit, limit).astype(kind)


def setup_inputs(seed: int = 0) -> dict:
    key_list = jax.random.split(jax.random.key(seed), 17)
    inputs = gaussian(key_list[0], (ROWS, LENGTH, D), 1.0, 6.0, ((0, 2), (1, 16)))
    memory = gaussian(key_list[1], (ROWS, MEMORY, D), 1.0, 6.0, ((0, 2), (1, 16)))
    out_grad = gaussian(key_list[2], (ROWS, LENGTH, D), 1.0, 6.0, ((0, 2), (1, 16)))
    token_docs = draw_token_docs(jax.random.fold_in(key_list[16], 71), 0)
    memory_docs = draw_memory_docs(jax.random.fold_in(key_list[16], 71), 0)
    self_project = gaussian(key_list[5], (D, 3 * D), D ** -0.5, 0.1875, ((0, 32),))
    self_output = gaussian(key_list[6], (D, D), 1 ** -0.5, 6.0, ((0, 32),))
    cross_query = gaussian(key_list[7], (D, D), D ** -0.5, 0.1875, ((0, 32),))
    cross_memory = gaussian(key_list[8], (D, 2 * D), D ** -0.5, 0.1875, ((0, 32),))
    cross_output = gaussian(key_list[9], (D, D), 1 ** -0.5, 6.0, ((0, 32),))
    inner_weight = gaussian(key_list[10], (D, FF), D ** -0.5, 0.1875, ((0, 32),))
    outer_weight = gaussian(key_list[11], (FF, D), FF ** -0.5, 0.09375, ((0, 32),))
    adapter_down = gaussian(key_list[12], (D, ADAPTER), D ** -0.5, 0.1875, ((0, 32),))
    adapter_up = gaussian(key_list[13], (ADAPTER, D), ADAPTER ** -0.5, 0.25, ((0, 32),))
    norm_gains = jnp.clip(1.0 + 0.1 * jax.random.normal(key_list[14], (3, D), jnp.float32), 0.5, 1.5).astype(jnp.bfloat16)
    prefixes = gaussian(key_list[15], (4, PREFIX, D), 1.0, 6.0, ((2, 32),))
    return dict(inputs=inputs, memory=memory, out_grad=out_grad, token_docs=token_docs, memory_docs=memory_docs, self_project=self_project, self_output=self_output, cross_query=cross_query, cross_memory=cross_memory, cross_output=cross_output, inner_weight=inner_weight, outer_weight=outer_weight, adapter_down=adapter_down, adapter_up=adapter_up, norm_gains=norm_gains, prefixes=prefixes)


@jax.custom_vjp
def low(v):
    return lax.optimization_barrier(v.astype(jnp.bfloat16)).astype(jnp.float32)

@jax.custom_vjp
def low_back(v):
    return v

def low_keep(v):
    return (low(v), None)

def low_pass(kept, grad):
    return (grad,)

def back_keep(v):
    return (v, None)

def back_low(kept, grad):
    return (low(grad),)
low.defvjp(low_keep, low_pass)
low_back.defvjp(back_keep, back_low)
highest = lax.Precision.HIGHEST

def both_ways(values):
    return low_back(low(values))

def norm_rows(resid, gain):
    middle = lax.optimization_barrier(jnp.mean(resid, axis=-1, keepdims=True))
    centred = resid - middle
    spread = lax.optimization_barrier(jnp.mean(centred * centred, axis=-1, keepdims=True))
    return centred * lax.rsqrt(spread + 1e-05) * gain

def heads_of(matrix):
    return matrix.reshape(matrix.shape[0], HEADS, HEAD_DIM)

def attention(queries, keys, values, pref_keys, pref_values, query_docs, key_docs, causal):
    query_len = queries.shape[0]
    block_len = math.gcd(query_len, 512)
    key_heads = heads_of(keys)
    value_heads = heads_of(values)
    prefix_keys = heads_of(pref_keys)
    prefix_values = heads_of(pref_values)
    key_pos = jnp.arange(keys.shape[0], dtype=jnp.int32)

    def query_block(block_inputs):
        query_rows, docs_rows, pos_rows = block_inputs
        query_heads = query_rows.reshape(block_len, HEADS, HEAD_DIM)
        allowed = docs_rows[:, None] == key_docs[None, :]
        if causal:
            allowed = allowed & (key_pos[None, :] <= pos_rows[:, None])
        scores = jnp.einsum('qhd,khd->hqk', query_heads, key_heads, precision=highest) * 0.125
        scores = low_back(jnp.where(allowed[None], scores, -1000000000.0))
        prefix_scores = low_back(jnp.einsum('qhd,phd->hqp', query_heads, prefix_keys, precision=highest) * 0.125)
        weights = jnp.exp(scores)
        prefix_weights = jnp.exp(prefix_scores)
        totals = lax.optimization_barrier(jnp.sum(weights, axis=-1)) + lax.optimization_barrier(jnp.sum(prefix_weights, axis=-1))
        summed = low_back(jnp.einsum('hqk,khd->qhd', low(weights), value_heads, precision=highest) + jnp.einsum('hqp,phd->qhd', low(prefix_weights), prefix_values, precision=highest))
        return (summed / totals.T[:, :, None]).reshape(block_len, D)
    positions = jnp.arange(query_len, dtype=jnp.int32)
    blocks = lax.map(jax.checkpoint(query_block), (queries.reshape(-1, block_len, D), query_docs.reshape(-1, block_len), positions.reshape(-1, block_len)))
    return blocks.reshape(query_len, D)

def layer(tokens, memory_rows, prefixes, adapter_down, adapter_up, token_docs, memory_docs, frozen):
    self_project, self_output, cross_query, cross_memory, cross_output, inner_weight, outer_weight, norm_gains = frozen
    projected = jnp.dot(tokens, self_project, precision=highest)
    queries = both_ways(projected[:, :D])
    keys = both_ways(projected[:, D:2 * D])
    values = both_ways(projected[:, 2 * D:])
    attended = low(attention(queries, keys, values, prefixes[0], prefixes[1], token_docs, token_docs, True))
    first_out = low_back(jnp.dot(attended, self_output, precision=highest))
    first_norm = norm_rows(tokens + first_out, norm_gains[0])
    first_low = low(first_norm)
    cross_queries = both_ways(jnp.dot(first_low, cross_query, precision=highest))
    memory_pairs = both_ways(jnp.dot(memory_rows, cross_memory, precision=highest))
    crossed = low(attention(cross_queries, memory_pairs[:, :D], memory_pairs[:, D:], prefixes[2], prefixes[3], token_docs, memory_docs, False))
    second_out = low_back(jnp.dot(crossed, cross_output, precision=highest))
    second_norm = norm_rows(first_norm + second_out, norm_gains[1])
    second_low = low(second_norm)
    hidden_pre = low_back(jnp.dot(second_low, inner_weight, precision=highest))
    hidden_act = low(jax.nn.gelu(hidden_pre, approximate=False))
    feed_out = low_back(jnp.dot(hidden_act, outer_weight, precision=highest))
    adapter_pre = low_back(jnp.dot(second_low, adapter_down, precision=highest))
    adapter_act = low(jax.nn.gelu(adapter_pre, approximate=False))
    adapter_out = low_back(jnp.dot(adapter_act, adapter_up, precision=highest))
    return norm_rows(second_norm + feed_out + 4.0 * adapter_out, norm_gains[2])

def reference(inputs, memory, out_grad, token_docs, memory_docs, self_project, self_output, cross_query, cross_memory, cross_output, inner_weight, outer_weight, adapter_down, adapter_up, norm_gains, prefixes):
    frozen = tuple((weight.astype(jnp.float32) for weight in (self_project, self_output, cross_query, cross_memory, cross_output, inner_weight, outer_weight, norm_gains)))
    prefix_all = prefixes.astype(jnp.float32)
    down_all = adapter_down.astype(jnp.float32)
    up_all = adapter_up.astype(jnp.float32)

    def one_row(running, row_items):
        tokens, memory_rows, cotangent, docs_row, memory_docs_row = row_items

        def forward(tokens_in, memory_in, prefix_in, down_in, up_in):
            return layer(tokens_in, memory_in, prefix_in, down_in, up_in, docs_row, memory_docs_row, frozen)
        layer_out, pullback = jax.vjp(forward, tokens.astype(jnp.float32), memory_rows.astype(jnp.float32), prefix_all, down_all, up_all)
        row_grads = pullback(cotangent.astype(jnp.float32))
        running = (running[0] + row_grads[2], running[1] + row_grads[3], running[2] + row_grads[4])
        return (running, (layer_out.astype(jnp.bfloat16), row_grads[0], row_grads[1]))
    zero_grads = (jnp.zeros((4, PREFIX, D), jnp.float32), jnp.zeros((D, ADAPTER), jnp.float32), jnp.zeros((ADAPTER, D), jnp.float32))
    totals, per_row = lax.scan(one_row, zero_grads, (inputs, memory, out_grad, token_docs, memory_docs))
    return (per_row[0], per_row[1], per_row[2], totals[0], totals[1], totals[2])
```

```python
import math

import jax
import jax.numpy as jnp
from jax import lax
from jax.experimental import pallas as pl
from jax.experimental.pallas import tpu as pltpu
from jax.sharding import PartitionSpec as P

D = 1024
HEADS = 16
HEAD_DIM = 64
ADAPTER = 512
PREFIX = 30
S_DEV = 128
M_DEV = 32


score_scale = 0.125
masked_score = -1000000000.0


def heads_of(matrix):
    return matrix.reshape(matrix.shape[0], HEADS, HEAD_DIM)


def dot_right(left, right):
    return lax.dot_general(
        left, right, (((1,), (1,)), ((), ())), preferred_element_type=jnp.float32
    )


def dot_left(left, right):
    return lax.dot_general(
        left, right, (((0,), (0,)), ((), ())), preferred_element_type=jnp.float32
    )


def norm_rows(resid, gain):
    middle = jnp.mean(resid, axis=-1, keepdims=True)
    centred = resid - middle
    spread = jnp.mean(centred * centred, axis=-1, keepdims=True)
    return centred * lax.rsqrt(spread + 1e-05) * gain


def norm_back(resid, gain, upstream):
    unused, pullback = jax.vjp(lambda values: norm_rows(values, gain), resid)
    return pullback(upstream)[0]


def gelu_back(pre_act, upstream):
    unused, pullback = jax.vjp(lambda values: jax.nn.gelu(values, approximate=False), pre_act)
    return pullback(upstream)[0]


def allowed_keys(query_docs, key_docs, query_pos, key_pos, causal):
    allowed = query_docs[:, None] == key_docs[None, :]
    if causal:
        allowed = allowed & (key_pos[None, :] <= query_pos[:, None])
    return allowed


def prefix_terms(queries, prefix_keys, prefix_values):
    scores = (
        jnp.einsum(
            "qhd,phd->hqp", queries, heads_of(prefix_keys), preferred_element_type=jnp.float32
        )
        * score_scale
    )
    weights = jnp.exp(scores)
    summed = jnp.einsum(
        "hqp,phd->qhd",
        weights.astype(jnp.bfloat16),
        heads_of(prefix_values),
        preferred_element_type=jnp.float32,
    )
    return (jnp.sum(weights, axis=-1), summed)


def fold_keys(running, arrived, queries, query_docs, key_docs, query_first, causal):
    key_count = arrived.shape[0]
    block_len = math.gcd(key_count, 512)
    query_count = queries.shape[0]
    query_pos = query_first + jnp.arange(query_count, dtype=jnp.int32)
    key_width = arrived.shape[1] // 2

    def fold_one_block(current, element):
        key_block, block_index = element
        key_first = block_index * block_len

        def compute(present):
            block_docs = lax.dynamic_slice_in_dim(key_docs, key_first, block_len, 0)
            allowed = allowed_keys(
                query_docs,
                block_docs,
                query_pos,
                key_first + jnp.arange(block_len, dtype=jnp.int32),
                causal,
            )
            scores = (
                jnp.einsum(
                    "qhd,khd->hqk",
                    queries,
                    heads_of(key_block[:, :key_width]),
                    preferred_element_type=jnp.float32,
                )
                * score_scale
            )
            weights = jnp.exp(jnp.where(allowed[None], scores, masked_score))
            summed = jnp.einsum(
                "hqk,khd->qhd",
                weights.astype(jnp.bfloat16),
                heads_of(key_block[:, key_width:]),
                preferred_element_type=jnp.float32,
            )
            return (present[0] + jnp.sum(weights, axis=-1), present[1] + summed)

        if causal:
            return (
                lax.cond(
                    key_first <= query_first + query_count - 1, compute, lambda held: held, current
                ),
                None,
            )
        return (compute(current), None)

    running, unused = lax.scan(
        fold_one_block,
        running,
        (
            arrived.reshape(key_count // block_len, block_len, arrived.shape[1]),
            jnp.arange(key_count // block_len, dtype=jnp.int32),
        ),
    )
    return running


def attend_back(
    queries,
    gathered,
    prefix_keys,
    prefix_values,
    grad_out,
    attended,
    totals,
    query_docs,
    key_docs,
    query_first,
    causal,
):
    query_count = queries.shape[0]
    key_count = gathered.shape[0]
    key_width = gathered.shape[1] // 2
    block_len = math.gcd(key_count, 512)
    query_pos = query_first + jnp.arange(query_count, dtype=jnp.int32)
    grad_heads = heads_of(grad_out)
    grad_summed = (grad_heads / totals.T[:, :, None]).astype(jnp.bfloat16)
    row_dot = jnp.sum(grad_heads * heads_of(attended), axis=-1).T / totals
    prefix_key_heads = heads_of(prefix_keys)
    prefix_value_heads = heads_of(prefix_values)
    prefix_weights = jnp.exp(
        jnp.einsum("qhd,phd->hqp", queries, prefix_key_heads, preferred_element_type=jnp.float32)
        * score_scale
    )
    prefix_dots = jnp.einsum(
        "qhd,phd->hqp", grad_summed, prefix_value_heads, preferred_element_type=jnp.float32
    )
    prefix_slopes = (prefix_weights * (prefix_dots - row_dot[:, :, None])).astype(jnp.bfloat16)
    query_grad = jnp.einsum(
        "hqp,phd->qhd", prefix_slopes, prefix_key_heads, preferred_element_type=jnp.float32
    )
    key_grad_prefix = (
        jnp.einsum("hqp,qhd->phd", prefix_slopes, queries, preferred_element_type=jnp.float32)
        * score_scale
    ).reshape(-1, D)
    value_grad_prefix = jnp.einsum(
        "hqp,qhd->phd",
        prefix_weights.astype(jnp.bfloat16),
        grad_summed,
        preferred_element_type=jnp.float32,
    ).reshape(-1, D)

    def attend_one_block(current, element):
        key_block, block_index = element
        key_first = block_index * block_len

        def compute(present):
            block_docs = lax.dynamic_slice_in_dim(key_docs, key_first, block_len, 0)
            allowed = allowed_keys(
                query_docs,
                block_docs,
                query_pos,
                key_first + jnp.arange(block_len, dtype=jnp.int32),
                causal,
            )
            key_heads = heads_of(key_block[:, :key_width])
            value_heads = heads_of(key_block[:, key_width:])
            scores = (
                jnp.einsum("qhd,khd->hqk", queries, key_heads, preferred_element_type=jnp.float32)
                * score_scale
            )
            weights = jnp.exp(jnp.where(allowed[None], scores, masked_score))
            dots = jnp.einsum(
                "qhd,khd->hqk", grad_summed, value_heads, preferred_element_type=jnp.float32
            )
            slopes = (weights * (dots - row_dot[:, :, None])).astype(jnp.bfloat16)
            present = present + jnp.einsum(
                "hqk,khd->qhd", slopes, key_heads, preferred_element_type=jnp.float32
            )
            key_grad = (
                jnp.einsum("hqk,qhd->khd", slopes, queries, preferred_element_type=jnp.float32)
                * score_scale
            )
            value_grad = jnp.einsum(
                "hqk,qhd->khd",
                weights.astype(jnp.bfloat16),
                grad_summed,
                preferred_element_type=jnp.float32,
            )
            return (
                present,
                jnp.concatenate(
                    [key_grad.reshape(block_len, D), value_grad.reshape(block_len, D)], axis=1
                ),
            )

        if causal:
            return lax.cond(
                key_first <= query_first + query_count - 1,
                compute,
                lambda held: (held, jnp.zeros((block_len, 2 * D), jnp.float32)),
                current,
            )
        return compute(current)

    query_grad, key_terms = lax.scan(
        attend_one_block,
        query_grad,
        (
            gathered.reshape(key_count // block_len, block_len, gathered.shape[1]),
            jnp.arange(key_count // block_len, dtype=jnp.int32),
        ),
    )
    query_low = (query_grad * score_scale).astype(jnp.bfloat16).reshape(query_count, D)
    key_terms = key_terms.reshape(key_count, 2 * D)
    return (query_low, key_terms, key_grad_prefix, value_grad_prefix, grad_summed, row_dot)


def fetch_all(
    self_project,
    self_output,
    cross_query,
    cross_memory,
    cross_output,
    inner_weight,
    outer_weight,
    adapter_down,
    adapter_up,
    norm_gains,
    prefixes,
):
    return (
        lax.all_gather(self_project, ("seq", "rows"), axis=0, tiled=True),
        lax.all_gather(self_output, ("seq", "rows"), axis=0, tiled=True),
        lax.all_gather(cross_query, ("seq", "rows"), axis=0, tiled=True),
        lax.all_gather(cross_memory, ("seq", "rows"), axis=0, tiled=True),
        lax.all_gather(cross_output, ("seq", "rows"), axis=0, tiled=True),
        lax.all_gather(inner_weight, ("seq", "rows"), axis=0, tiled=True),
        lax.all_gather(outer_weight, ("seq", "rows"), axis=0, tiled=True),
        lax.all_gather(adapter_down, ("seq", "rows"), axis=0, tiled=True),
        lax.all_gather(adapter_up, ("seq", "rows"), axis=0, tiled=True),
        lax.all_gather(norm_gains, ("seq", "rows"), axis=1, tiled=True),
        lax.all_gather(prefixes, ("seq", "rows"), axis=2, tiled=True),
    )


def fetch_again(
    self_project,
    self_output,
    cross_query,
    cross_memory,
    cross_output,
    inner_weight,
    outer_weight,
    adapter_down,
    adapter_up,
    norm_gains,
    prefixes,
):
    return (
        lax.all_gather(self_project, ("seq", "rows"), axis=0, tiled=True),
        lax.all_gather(self_output, ("seq", "rows"), axis=0, tiled=True),
        lax.all_gather(cross_query, ("seq", "rows"), axis=0, tiled=True),
        lax.all_gather(cross_memory, ("seq", "rows"), axis=0, tiled=True),
        lax.all_gather(cross_output, ("seq", "rows"), axis=0, tiled=True),
        lax.all_gather(inner_weight, ("seq", "rows"), axis=0, tiled=True),
        lax.all_gather(outer_weight, ("seq", "rows"), axis=0, tiled=True),
        lax.all_gather(adapter_down, ("seq", "rows"), axis=0, tiled=True),
        lax.all_gather(adapter_up, ("seq", "rows"), axis=0, tiled=True),
        lax.all_gather(norm_gains, ("seq", "rows"), axis=1, tiled=True),
        lax.all_gather(prefixes, ("seq", "rows"), axis=2, tiled=True),
    )


def forward_row(tokens, memory_rows, query_docs, token_docs, memory_docs, query_first, weights):
    (
        self_project,
        self_output,
        cross_query,
        cross_memory,
        cross_output,
        inner_weight,
        outer_weight,
        adapter_down,
        adapter_up,
        norm_gains,
        prefixes,
    ) = weights
    gains = norm_gains.astype(jnp.float32)
    projected = jnp.dot(tokens, self_project, preferred_element_type=jnp.float32).astype(
        jnp.bfloat16
    )
    queries = heads_of(projected[:, :D])
    local_pairs = projected[:, D:]
    start_self = prefix_terms(queries, prefixes[0], prefixes[1])
    totals, summed = fold_keys(
        start_self,
        lax.all_gather(local_pairs, "seq", axis=0, tiled=True),
        queries,
        query_docs,
        token_docs,
        query_first,
        True,
    )
    attended = (summed / totals.T[:, :, None]).reshape(-1, D)
    first_resid = tokens.astype(jnp.float32) + jnp.dot(
        attended.astype(jnp.bfloat16), self_output, preferred_element_type=jnp.float32
    )
    first_norm = norm_rows(first_resid, gains[0])
    first_low = first_norm.astype(jnp.bfloat16)
    cross_queries = heads_of(
        jnp.dot(first_low, cross_query, preferred_element_type=jnp.float32).astype(jnp.bfloat16)
    )
    memory_pairs = jnp.dot(memory_rows, cross_memory, preferred_element_type=jnp.float32).astype(
        jnp.bfloat16
    )
    start_cross = prefix_terms(cross_queries, prefixes[2], prefixes[3])
    cross_totals, cross_summed = fold_keys(
        start_cross,
        lax.all_gather(memory_pairs, "seq", axis=0, tiled=True),
        cross_queries,
        query_docs,
        memory_docs,
        query_first,
        False,
    )
    crossed = (cross_summed / cross_totals.T[:, :, None]).reshape(-1, D)
    second_resid = first_norm + jnp.dot(
        crossed.astype(jnp.bfloat16), cross_output, preferred_element_type=jnp.float32
    )
    second_norm = norm_rows(second_resid, gains[1])
    second_low = second_norm.astype(jnp.bfloat16)
    hidden_pre = jnp.dot(second_low, inner_weight, preferred_element_type=jnp.float32)
    hidden_act = jax.nn.gelu(hidden_pre, approximate=False).astype(jnp.bfloat16)
    adapter_pre = jnp.dot(second_low, adapter_down, preferred_element_type=jnp.float32)
    adapter_act = jax.nn.gelu(adapter_pre, approximate=False).astype(jnp.bfloat16)
    third_resid = (
        second_norm
        + jnp.dot(hidden_act, outer_weight, preferred_element_type=jnp.float32)
        + 4.0 * jnp.dot(adapter_act, adapter_up, preferred_element_type=jnp.float32)
    )
    layer_out = norm_rows(third_resid, gains[2]).astype(jnp.bfloat16)
    saved = (
        queries,
        local_pairs,
        totals,
        attended,
        first_resid,
        cross_queries,
        memory_pairs,
        cross_totals,
        crossed,
        second_resid,
        second_low,
        hidden_pre,
        adapter_pre,
        adapter_act,
        third_resid,
    )
    return (layer_out, saved)


def backward_row(cotangent, saved, weights, query_docs, token_docs, memory_docs, query_first):
    (
        self_project,
        self_output,
        cross_query,
        cross_memory,
        cross_output,
        inner_weight,
        outer_weight,
        adapter_down,
        adapter_up,
        norm_gains,
        prefixes,
    ) = weights
    (
        queries,
        local_pairs,
        totals,
        attended,
        first_resid,
        cross_queries,
        memory_pairs,
        cross_totals,
        crossed,
        second_resid,
        second_low,
        hidden_pre,
        adapter_pre,
        adapter_act,
        third_resid,
    ) = saved
    gains = norm_gains.astype(jnp.float32)
    third_grad = norm_back(third_resid, gains[2], cotangent.astype(jnp.float32))
    feed_low = third_grad.astype(jnp.bfloat16)
    adapter_low = (4.0 * third_grad).astype(jnp.bfloat16)
    hidden_grad = gelu_back(hidden_pre, dot_right(feed_low, outer_weight)).astype(jnp.bfloat16)
    up_grad = dot_left(adapter_act, adapter_low)
    adapter_grad = gelu_back(adapter_pre, dot_right(adapter_low, adapter_up)).astype(jnp.bfloat16)
    down_grad = dot_left(second_low, adapter_grad)
    second_grad = (
        third_grad + dot_right(hidden_grad, inner_weight) + dot_right(adapter_grad, adapter_down)
    )
    second_resid_grad = norm_back(second_resid, gains[1], second_grad)
    self_all, memory_all = (
        lax.all_gather(local_pairs, "seq", axis=0, tiled=True),
        lax.all_gather(memory_pairs, "seq", axis=0, tiled=True),
    )
    cross_out_grad = dot_right(second_resid_grad.astype(jnp.bfloat16), cross_output)
    (
        cross_query_low,
        memory_terms,
        cross_key_prefix,
        cross_value_prefix,
        cross_summed_grad,
        cross_dot,
    ) = attend_back(
        cross_queries,
        memory_all,
        prefixes[2],
        prefixes[3],
        cross_out_grad,
        crossed,
        cross_totals,
        query_docs,
        memory_docs,
        query_first,
        False,
    )
    first_grad = second_resid_grad + dot_right(cross_query_low, cross_query)
    first_resid_grad = norm_back(first_resid, gains[0], first_grad)
    self_out_grad = dot_right(first_resid_grad.astype(jnp.bfloat16), self_output)
    query_low, self_terms, self_key_prefix, self_value_prefix, self_summed_grad, self_dot = (
        attend_back(
            queries,
            self_all,
            prefixes[0],
            prefixes[1],
            self_out_grad,
            attended,
            totals,
            query_docs,
            token_docs,
            query_first,
            True,
        )
    )
    self_sums, memory_sums = (
        lax.psum_scatter(
            self_terms.astype(jnp.bfloat16), "seq", scatter_dimension=0, tiled=True
        ).astype(jnp.float32),
        lax.psum_scatter(
            memory_terms.astype(jnp.bfloat16), "seq", scatter_dimension=0, tiled=True
        ).astype(jnp.float32),
    )
    project_grad = jnp.concatenate([query_low, self_sums.astype(jnp.bfloat16)], axis=1)
    input_grad = first_resid_grad + dot_right(project_grad, self_project)
    memory_grad = dot_right(memory_sums.astype(jnp.bfloat16), cross_memory)
    prefix_grad = jnp.stack(
        [self_key_prefix, self_value_prefix, cross_key_prefix, cross_value_prefix]
    )
    return (input_grad, memory_grad, (down_grad, up_grad, prefix_grad))


def per_device(
    inputs,
    memory,
    out_grad,
    token_docs,
    memory_docs,
    self_project,
    self_output,
    cross_query,
    cross_memory,
    cross_output,
    inner_weight,
    outer_weight,
    adapter_down,
    adapter_up,
    norm_gains,
    prefixes,
):
    docs_full, memory_full = (
        lax.all_gather(token_docs, "seq", axis=1, tiled=True),
        lax.all_gather(memory_docs, "seq", axis=1, tiled=True),
    )
    query_first = lax.axis_index("seq") * inputs.shape[1]
    outputs = []
    input_grads = []
    memory_grads = []
    adjusted_grads = None
    for row_index in range(inputs.shape[0]):
        weights = fetch_all(
            self_project,
            self_output,
            cross_query,
            cross_memory,
            cross_output,
            inner_weight,
            outer_weight,
            adapter_down,
            adapter_up,
            norm_gains,
            prefixes,
        )
        layer_out, saved = forward_row(
            inputs[row_index],
            memory[row_index],
            token_docs[row_index],
            docs_full[row_index],
            memory_full[row_index],
            query_first,
            weights,
        )
        weights_back = fetch_again(
            self_project,
            self_output,
            cross_query,
            cross_memory,
            cross_output,
            inner_weight,
            outer_weight,
            adapter_down,
            adapter_up,
            norm_gains,
            prefixes,
        )
        input_grad, memory_grad, row_grads = backward_row(
            out_grad[row_index],
            saved,
            weights_back,
            token_docs[row_index],
            docs_full[row_index],
            memory_full[row_index],
            query_first,
        )
        shares = (
            lax.psum_scatter(row_grads[0], ("seq", "rows"), scatter_dimension=0, tiled=True),
            lax.psum_scatter(row_grads[1], ("seq", "rows"), scatter_dimension=0, tiled=True),
            lax.psum_scatter(row_grads[2], ("seq", "rows"), scatter_dimension=2, tiled=True),
        )
        if adjusted_grads is None:
            adjusted_grads = shares
        else:
            adjusted_grads = tuple(
                (former + latter for former, latter in zip(adjusted_grads, shares))
            )
        outputs.append(layer_out)
        input_grads.append(input_grad)
        memory_grads.append(memory_grad)
    return (
        jnp.stack(outputs),
        jnp.stack(input_grads),
        jnp.stack(memory_grads),
        adjusted_grads[2],
        adjusted_grads[0],
        adjusted_grads[1],
    )


MESH_ID = pl.DeviceIdType.MESH
F32 = jnp.float32
BF16 = jnp.bfloat16
VMEM_BYTES = 60 * 1024 * 1024
PAIRS = HEADS // 2
LANES = 2 * HEAD_DIM
Q_AT, K_AT, V_AT, SELF_OUT_AT, CROSS_Q_AT, MEM_K_AT, MEM_V_AT, CROSS_OUT_AT, SMALL_AT = range(0, 288, 32)
SMALL_ROWS = 16
FIRST_ROWS = SMALL_AT + SMALL_ROWS
FEED_ROWS = 288


def whole(space=pltpu.VMEM):
    return pl.BlockSpec(memory_space=space)


def params(collective_id=None):
    if collective_id is None:
        return pltpu.CompilerParams(vmem_limit_bytes=VMEM_BYTES)
    return pltpu.CompilerParams(
        vmem_limit_bytes=VMEM_BYTES, collective_id=collective_id, has_side_effects=True
    )


def remote(src, dst, send_sem, recv_sem, device):
    return pltpu.make_async_remote_copy(
        src_ref=src, dst_ref=dst, send_sem=send_sem, recv_sem=recv_sem,
        device_id=device, device_id_type=MESH_ID,
    )


def greet(peers):
    barrier = pltpu.get_barrier_semaphore()
    for peer in peers:
        pl.semaphore_signal(barrier, inc=1, device_id=peer, device_id_type=MESH_ID)
    pl.semaphore_wait(barrier, len(peers))


def dot_nn(left, right):
    return lax.dot_general(left, right, (((1,), (0,)), ((), ())), preferred_element_type=F32)


def gather_kernel(
    project, self_out, cross_q, cross_mem, cross_out, small, memory,
    full, memory_full, local_sem, *sems,
):
    seq, x = lax.axis_index("seq"), lax.axis_index("rows")
    z, y, core = seq // 4, (seq // 2) % 2, seq % 2

    def device(z, y, core, x):
        return ((z * 2 + y) * 2 + core, x)

    along_z = [device((z + step) % 4, y, core, x) for step in (1, 2, 3)]
    along_x, along_y = device(z, y, core, 1 - x), device(z, 1 - y, core, x)
    other_core = device(z, y, 1 - core, x)
    greet(along_z + [along_x, along_y, other_core])
    send0, recv0, send1, recv1, send2, recv2, send3, recv3 = sems

    pieces = [
        (project.at[:, pl.ds(0, 1024)], Q_AT, 32),
        (project.at[:, pl.ds(1024, 1024)], K_AT, 32),
        (project.at[:, pl.ds(2048, 1024)], V_AT, 32),
        (small, SMALL_AT, SMALL_ROWS),
        (self_out, SELF_OUT_AT, 32),
        (cross_q, CROSS_Q_AT, 32),
        (cross_mem.at[:, pl.ds(0, 1024)], MEM_K_AT, 32),
        (cross_mem.at[:, pl.ds(1024, 1024)], MEM_V_AT, 32),
        (cross_out, CROSS_OUT_AT, 32),
    ]
    stages = []
    for k, (source, first, count) in enumerate(pieces):
        rows = pl.ds(first, count)
        mine = full.at[z, y, core, x, rows]
        near, far = pl.ds(0, 2), pl.ds(2, 2)
        near1, far1 = full.at[near, y, core, x, rows], full.at[far, y, core, x, rows]
        near2, far2 = full.at[near, y, core, :, rows], full.at[far, :, core, x, rows]
        half = full.at[:, :, core, :, rows]
        stages.append((
            pltpu.make_async_copy(source, mine, local_sem.at[k]),
            [remote(source, mine, send0.at[k, d], recv0.at[k, d], along_z[d]) for d in range(3)],
            [remote(near1, near1, send1.at[k, 0], recv1.at[k, 0], along_x),
             remote(far1, far1, send1.at[k, 1], recv1.at[k, 1], along_y)],
            [remote(near2, near2, send2.at[k, 0], recv2.at[k, 0], along_y),
             remote(far2, far2, send2.at[k, 1], recv2.at[k, 1], along_x)],
            [remote(half, half, send3.at[k, 0], recv3.at[k, 0], other_core)],
        ))
    k = len(pieces)
    mine = memory_full.at[z, y, core]
    column = memory_full.at[:, y, core]
    half = memory_full.at[:, :, core]
    stages.append((
        pltpu.make_async_copy(memory, mine, local_sem.at[k]),
        [remote(memory, mine, send0.at[k, d], recv0.at[k, d], along_z[d]) for d in range(3)],
        [remote(column, column, send1.at[k, 1], recv1.at[k, 1], along_y)],
        [],
        [remote(half, half, send3.at[k, 0], recv3.at[k, 0], other_core)],
    ))
    order = list(range(4)) + [k] + list(range(4, k))
    stages = [stages[at] for at in order]
    for local, *_ in stages:
        local.start()
    total = len(stages)
    for tick in range(total + 4):
        for level in range(5):
            k = tick - level
            if not 0 <= k < total:
                continue
            if level == 1:
                stages[k][0].wait()
            if level > 0:
                for copy in stages[k][level]:
                    copy.wait_recv()
            if level < 4:
                for copy in stages[k][level + 1]:
                    copy.start()
    for _, *levels in stages:
        for level in levels:
            for copy in level:
                copy.wait_send()


def gather_first(project, self_out, cross_q, cross_mem, cross_out, small, memory):
    count = 10
    sems = []
    for width in (3, 2, 2, 1):
        sems += [pltpu.SemaphoreType.DMA((count, width))] * 2
    full, memory_full = pl.pallas_call(
        gather_kernel,
        out_shape=(
            jax.ShapeDtypeStruct((4, 2, 2, 2, FIRST_ROWS, D), BF16),
            jax.ShapeDtypeStruct((4, 2, 2) + memory.shape, BF16),
        ),
        in_specs=[whole(pl.ANY)] * 7,
        out_specs=(whole(pl.ANY), whole(pl.ANY)),
        scratch_shapes=[pltpu.SemaphoreType.DMA((count,))] + sems,
        compiler_params=params(0),
        name="gather_first",
    )(project, self_out, cross_q, cross_mem, cross_out, small, memory)
    return full.reshape(32, FIRST_ROWS, D), memory_full.reshape((16,) + memory.shape)


def project_kernel(tokens, full, arrived, weights, staged, weight_sem, local_sem, send_sem, recv_sem):
    seq, x = lax.axis_index("seq"), lax.axis_index("rows")
    fetches = [
        pltpu.make_async_copy(full.at[:, pl.ds(32 * part, 32)], weights.at[part], weight_sem.at[part])
        for part in range(3)
    ]
    for fetch in fetches:
        fetch.start()
    greet([((seq + step) % 16, x) for step in range(1, 16)])
    rows = tokens[...].reshape(2 * S_DEV, D)
    for part in range(3):
        fetches[part].wait()
        result = dot_nn(rows, weights[part].reshape(D, D)).astype(BF16)
        for row in range(2):
            for pair in range(PAIRS):
                staged[pair, row, part] = result[
                    row * S_DEV:(row + 1) * S_DEV, pair * LANES:(pair + 1) * LANES
                ]
    copies = []
    for step in range(1, 16):
        to = (seq + step) % 16
        copies.append(remote(
            staged.at[to // 2, to % 2], arrived.at[seq], send_sem.at[step], recv_sem.at[step], (to, x)
        ))
    own = pltpu.make_async_copy(staged.at[seq // 2, seq % 2], arrived.at[seq], local_sem)
    own.start()
    for copy in copies:
        copy.start()
    own.wait()
    for copy in copies:
        copy.wait()


def project_exchange(tokens, full):
    return pl.pallas_call(
        project_kernel,
        out_shape=jax.ShapeDtypeStruct((16, 3, S_DEV, LANES), BF16),
        in_specs=[whole(), whole(pl.ANY)],
        out_specs=whole(pl.ANY),
        scratch_shapes=[
            pltpu.VMEM((3, 32, 32, D), BF16),
            pltpu.VMEM((PAIRS, 2, 3, S_DEV, LANES), BF16),
            pltpu.SemaphoreType.DMA((3,)),
            pltpu.SemaphoreType.DMA,
            pltpu.SemaphoreType.DMA((16,)),
            pltpu.SemaphoreType.DMA((16,)),
        ],
        compiler_params=params(1),
        name="project_exchange",
    )(tokens, full)


def head_masks():
    lane = lax.broadcasted_iota(jnp.int32, (1, LANES), 1)
    first = (lane < HEAD_DIM).astype(F32).astype(BF16)
    return first, (1.0 - first.astype(F32)).astype(BF16)


def stack_heads(block):
    first, second = head_masks()
    return jnp.concatenate([block * first, block * second], axis=0)


def merge_heads(stacked):
    half = stacked.shape[0] // 2
    lane = lax.broadcasted_iota(jnp.int32, (half, LANES), 1)
    return jnp.where(lane < HEAD_DIM, stacked[:half], stacked[half:])


def rows_in_lanes(values):
    lane = lax.broadcasted_iota(jnp.int32, (8, LANES), 1)
    row = lax.broadcasted_iota(jnp.int32, (8, LANES), 0)
    picks = (lane // HEAD_DIM == row).astype(F32)
    return lax.dot_general(
        picks, values, (((1,), (1,)), ((), ())),
        precision=lax.Precision.HIGHEST, preferred_element_type=F32,
    )


def self_forward_kernel(
    arrived, docs_row, docs_column, prefix_keys, prefix_values,
    gathered, attended, inverse, staged, sums, parts, local_sem, send_sem, recv_sem,
):
    seq, x = lax.axis_index("seq"), lax.axis_index("rows")
    block = 2 * S_DEV
    greet([((seq + step) % 16, x) for step in range(1, 16)])
    pair, row = seq // 2, seq % 2
    columns = pl.ds(pl.multiple_of(pair * LANES, LANES), LANES)
    mine = gathered.at[row, :, columns]
    away = (
        lax.broadcasted_iota(jnp.int32, (block, block), 1)
        - lax.broadcasted_iota(jnp.int32, (block, block), 0)
    )
    prefix_lane = lax.broadcasted_iota(jnp.int32, (2 * block, 32), 1)

    def one_block(step, carry):
        at = (step + seq // 2) % 8
        queries = stack_heads(arrived[pl.ds(2 * at, 2), 0].reshape(block, LANES))
        query_docs = docs_column[pl.ds(at * block, block)]
        scores = dot_right(queries, prefix_keys[...]) * score_scale
        weights = jnp.where(prefix_lane < PREFIX, jnp.exp(scores), 0.0)
        sums[...] = jnp.concatenate([weights, jnp.zeros((2 * block, LANES - 32), F32)], axis=1)
        parts[...] = dot_nn(weights.astype(BF16), prefix_values[...])

        def one_tile(key_at, carry):
            keys = arrived[pl.ds(2 * key_at, 2), 1].reshape(block, LANES)
            values = arrived[pl.ds(2 * key_at, 2), 2].reshape(block, LANES)
            key_docs = docs_row[:, pl.ds(pl.multiple_of(key_at * block, block), block)]
            same = jnp.concatenate([query_docs, query_docs], axis=1) == key_docs
            allowed = same & (away <= (at - key_at) * block)
            scores = dot_right(queries, keys) * score_scale
            weights = jnp.where(allowed[None], jnp.exp(scores).reshape(2, block, block), 0.0)
            weights = weights.reshape(2 * block, block)
            sums[...] += weights[:, :LANES] + weights[:, LANES:]
            parts[...] += dot_nn(weights.astype(BF16), values)
            return carry

        lax.fori_loop(0, at + 1, one_tile, 0)
        totals = 1.0 / jnp.sum(sums[...], axis=1, keepdims=True)
        result = merge_heads(parts[...] * totals)
        here = pl.ds(at * block, block)
        attended[here] = result
        inverse[here] = merge_heads(jnp.broadcast_to(totals, (2 * block, LANES)))
        staged[pl.ds(2 * at, 2)] = result.astype(BF16).reshape(2, S_DEV, LANES)
        for half in range(2):
            to = 2 * at + half

            @pl.when(to != seq)
            def _():
                remote(staged.at[to], mine, send_sem.at[to], recv_sem.at[seq], (to, x)).start()

            @pl.when(to == seq)
            def _():
                pltpu.make_async_copy(staged.at[to], mine, local_sem).start()

        return carry

    lax.fori_loop(0, 8, one_block, 0)
    pltpu.make_async_copy(staged.at[seq], mine, local_sem).wait()
    for step in range(1, 16):
        other = (seq + step) % 16
        remote(staged.at[other], mine, send_sem.at[other], recv_sem.at[other], (other, x)).wait()


def self_forward(arrived, docs_row, docs_column, prefix_keys, prefix_values):
    length = 16 * S_DEV
    return pl.pallas_call(
        self_forward_kernel,
        out_shape=(
            jax.ShapeDtypeStruct((2, S_DEV, D), BF16),
            jax.ShapeDtypeStruct((length, LANES), F32),
            jax.ShapeDtypeStruct((length, LANES), F32),
        ),
        in_specs=[whole()] * 5,
        out_specs=(whole(), whole(), whole()),
        scratch_shapes=[
            pltpu.VMEM((16, S_DEV, LANES), BF16),
            pltpu.VMEM((4 * S_DEV, LANES), F32),
            pltpu.VMEM((4 * S_DEV, LANES), F32),
            pltpu.SemaphoreType.DMA,
            pltpu.SemaphoreType.DMA((16,)),
            pltpu.SemaphoreType.DMA((16,)),
        ],
        compiler_params=params(2),
        name="self_forward",
    )(arrived, docs_row, docs_column, prefix_keys, prefix_values)


def self_backward_kernel(
    arrived, grad_out, attended, inverse, docs_row, docs_column, prefix_keys, prefix_values,
    gathered, prefix_grads,
    grads, grad_low, delta, query_grads, key_grads, value_grads, staged,
    local_sem, in_send, in_recv, out_send, out_recv, query_send, query_recv,
):
    seq, x = lax.axis_index("seq"), lax.axis_index("rows")
    block = 2 * S_DEV
    pair, row = seq // 2, seq % 2
    greet([((seq + step) % 16, x) for step in range(1, 16)])

    def heads_for(to):
        return grad_out.at[to % 2, :, pl.ds(pl.multiple_of((to // 2) * LANES, LANES), LANES)]

    own = pltpu.make_async_copy(heads_for(seq), grads.at[seq], local_sem.at[0])
    own.start()
    arrivals = []
    for step in range(1, 16):
        to = (seq + step) % 16
        arrivals.append(remote(heads_for(to), grads.at[seq], in_send.at[step], in_recv.at[step], (to, x)))
        arrivals[-1].start()
    own.wait()
    for copy in arrivals:
        copy.wait()

    pad_row = lax.broadcasted_iota(jnp.int32, (64, block), 0) % 32
    prefix_key_stack = stack_heads(prefix_keys[...])
    prefix_value_stack = stack_heads(prefix_values[...])

    def head_rows(at, count):
        there = delta[:, pl.ds(pl.multiple_of(at * block, block), block)]
        return jnp.concatenate(
            [jnp.broadcast_to(there[0:1], (count, block)), jnp.broadcast_to(there[1:2], (count, block))],
            axis=0,
        )

    prefix_grads[...] = jnp.zeros(prefix_grads.shape, F32)

    def prepare(at, carry):
        here = pl.ds(at * block, block)
        grad = grads[pl.ds(2 * at, 2)].reshape(block, LANES).astype(F32) * inverse[here]
        low = grad.astype(BF16)
        grad_low[here] = low
        delta[:, pl.ds(pl.multiple_of(at * block, block), block)] = rows_in_lanes(grad * attended[here])
        queries = arrived[pl.ds(2 * at, 2), 0].reshape(block, LANES)
        weights = jnp.exp(dot_right(prefix_key_stack, queries) * score_scale)
        weights = jnp.where(pad_row < PREFIX, weights, 0.0)
        slopes = (weights * (dot_right(prefix_value_stack, low) - head_rows(at, 32))).astype(BF16)
        prefix_grads[0] += merge_heads(dot_nn(slopes, queries)) * score_scale
        prefix_grads[1] += merge_heads(dot_nn(weights.astype(BF16), low))
        query_grads[here] = dot_left(slopes, prefix_key_stack)
        return carry

    lax.fori_loop(0, 8, prepare, 0)
    away = (
        lax.broadcasted_iota(jnp.int32, (block, block), 0)
        - lax.broadcasted_iota(jnp.int32, (block, block), 1)
    )

    def send_block(part, count, at, send, recv):
        for half in range(2):
            to = 2 * at + half
            source = staged.at[to, pl.ds(part, count)]
            mine = gathered.at[pair, row, pl.ds(part, count)]

            @pl.when(to != seq)
            def _():
                remote(source, mine, send.at[to], recv.at[seq], (to, x)).start()

            @pl.when(to == seq)
            def _():
                pltpu.make_async_copy(source, mine, local_sem.at[1 + part]).start()

    def one_block(step, carry):
        key_at = (step + seq // 2) % 8
        keys = stack_heads(arrived[pl.ds(2 * key_at, 2), 1].reshape(block, LANES))
        values = stack_heads(arrived[pl.ds(2 * key_at, 2), 2].reshape(block, LANES))
        key_docs = docs_column[pl.ds(key_at * block, block)]
        key_docs = jnp.concatenate([key_docs, key_docs], axis=1)
        key_grads[...] = jnp.zeros(key_grads.shape, F32)
        value_grads[...] = jnp.zeros(value_grads.shape, F32)

        def one_tile(at, carry):
            here = pl.ds(at * block, block)
            queries = arrived[pl.ds(2 * at, 2), 0].reshape(block, LANES)
            low = grad_low[here]
            query_docs = docs_row[:, pl.ds(pl.multiple_of(at * block, block), block)]
            allowed = (key_docs == query_docs) & (away <= (at - key_at) * block)
            weights = jnp.exp(dot_right(keys, queries) * score_scale).reshape(2, block, block)
            weights = jnp.where(allowed[None], weights, 0.0).reshape(2 * block, block)
            slopes = (weights * (dot_right(values, low) - head_rows(at, block))).astype(BF16)
            key_grads[...] += dot_nn(slopes, queries)
            value_grads[...] += dot_nn(weights.astype(BF16), low)
            query_grads[here] += dot_left(slopes, keys)
            return carry

        lax.fori_loop(key_at, 8, one_tile, 0)
        there = pl.ds(2 * key_at, 2)
        staged[there, 1] = (merge_heads(key_grads[...]) * score_scale).astype(BF16).reshape(2, S_DEV, LANES)
        staged[there, 2] = merge_heads(value_grads[...]).astype(BF16).reshape(2, S_DEV, LANES)
        send_block(1, 2, key_at, out_send, out_recv)
        return carry

    lax.fori_loop(0, 8, one_block, 0)

    def last_block(step, carry):
        at = (step + seq // 2) % 8
        result = (query_grads[pl.ds(at * block, block)] * score_scale).astype(BF16)
        staged[pl.ds(2 * at, 2), 0] = result.reshape(2, S_DEV, LANES)
        send_block(0, 1, at, query_send, query_recv)
        return carry

    lax.fori_loop(0, 8, last_block, 0)
    pltpu.make_async_copy(staged.at[seq, pl.ds(1, 2)], gathered.at[pair, row, pl.ds(1, 2)], local_sem.at[2]).wait()
    pltpu.make_async_copy(staged.at[seq, pl.ds(0, 1)], gathered.at[pair, row, pl.ds(0, 1)], local_sem.at[1]).wait()
    for step in range(1, 16):
        other = (seq + step) % 16
        mine = gathered.at[other // 2, other % 2]
        remote(
            staged.at[other, pl.ds(1, 2)], mine.at[pl.ds(1, 2)], out_send.at[other], out_recv.at[other], (other, x)
        ).wait()
        remote(
            staged.at[other, pl.ds(0, 1)], mine.at[pl.ds(0, 1)], query_send.at[other], query_recv.at[other], (other, x)
        ).wait()


def self_backward(arrived, grad_out, attended, inverse, docs_row, docs_column, prefix_keys, prefix_values):
    length = 16 * S_DEV
    dma = pltpu.SemaphoreType.DMA
    return pl.pallas_call(
        self_backward_kernel,
        out_shape=(
            jax.ShapeDtypeStruct((PAIRS, 2, 3, S_DEV, LANES), BF16),
            jax.ShapeDtypeStruct((2, 32, LANES), F32),
        ),
        in_specs=[whole()] * 8,
        out_specs=(whole(), whole()),
        scratch_shapes=[
            pltpu.VMEM((16, S_DEV, LANES), BF16),
            pltpu.VMEM((length, LANES), BF16),
            pltpu.VMEM((8, length), F32),
            pltpu.VMEM((length, LANES), F32),
            pltpu.VMEM((4 * S_DEV, LANES), F32),
            pltpu.VMEM((4 * S_DEV, LANES), F32),
            pltpu.VMEM((16, 3, S_DEV, LANES), BF16),
            dma((3,)), dma((16,)), dma((16,)), dma((16,)), dma((16,)), dma((16,)), dma((16,)),
        ],
        compiler_params=params(3),
        name="self_backward",
    )(arrived, grad_out, attended, inverse, docs_row, docs_column, prefix_keys, prefix_values)


def cross_forward_kernel(
    queries, keys, values, query_docs, key_docs, prefix_keys, prefix_values, crossed, inverse
):
    stacked = stack_heads(queries[0])
    count = 2 * S_DEV
    prefix_lane = lax.broadcasted_iota(jnp.int32, (count, 32), 1)
    scores = dot_right(stacked, prefix_keys[...]) * score_scale
    prefix_weights = jnp.where(prefix_lane < PREFIX, jnp.exp(scores), 0.0)
    memory_len = keys.shape[0] * keys.shape[2]
    scores = dot_right(stacked, keys[...].reshape(memory_len, LANES)) * score_scale
    allowed = query_docs[0] == key_docs[0]
    weights = jnp.where(allowed[None], jnp.exp(scores).reshape(2, S_DEV, memory_len), 0.0)
    weights = weights.reshape(count, memory_len)
    totals = jnp.sum(weights, axis=1, keepdims=True) + jnp.sum(prefix_weights, axis=1, keepdims=True)
    totals = 1.0 / totals
    summed = dot_nn(weights.astype(BF16), values[...].reshape(memory_len, LANES))
    summed += dot_nn(prefix_weights.astype(BF16), prefix_values[...])
    crossed[0] = merge_heads(summed * totals)
    inverse[0] = merge_heads(jnp.broadcast_to(totals, (count, LANES)))


def cross_forward(queries, memory_pairs, query_docs, key_docs, prefix_keys, prefix_values):
    memory_len = 16 * M_DEV
    head_block = pl.BlockSpec((1, S_DEV, LANES), lambda row, pair: (row, 0, pair))
    keys = pl.BlockSpec((16, 1, M_DEV, LANES), lambda row, pair: (0, row, 0, pair))
    values = pl.BlockSpec((16, 1, M_DEV, LANES), lambda row, pair: (0, row, 0, PAIRS + pair))
    prefix = pl.BlockSpec((32, LANES), lambda row, pair: (0, pair))
    return pl.pallas_call(
        cross_forward_kernel,
        grid=(2, PAIRS),
        out_shape=(jax.ShapeDtypeStruct((2, S_DEV, D), F32),) * 2,
        in_specs=[
            head_block, keys, values,
            pl.BlockSpec((1, S_DEV, memory_len), lambda row, pair: (row, 0, 0)),
            pl.BlockSpec((1, 1, memory_len), lambda row, pair: (row, 0, 0)),
            prefix, prefix,
        ],
        out_specs=(head_block, head_block),
        compiler_params=params(),
        name="cross_forward",
    )(queries, memory_pairs, memory_pairs, query_docs, key_docs, prefix_keys, prefix_values)


def cross_backward_kernel(
    queries, keys, values, query_docs, key_docs, prefix_keys, prefix_values, grad_out, crossed, inverse,
    query_grad, key_grad, value_grad, prefix_grads,
):
    row = pl.program_id(1)
    memory_len = keys.shape[0] * keys.shape[2]
    heads = queries[0]
    grad = grad_out[0] * inverse[0]
    low = grad.astype(BF16)
    delta = rows_in_lanes(grad * crossed[0])

    def head_rows(count):
        return jnp.concatenate(
            [jnp.broadcast_to(delta[0:1], (count, S_DEV)), jnp.broadcast_to(delta[1:2], (count, S_DEV))],
            axis=0,
        )

    pad_row = lax.broadcasted_iota(jnp.int32, (64, S_DEV), 0) % 32
    prefix_key_stack = stack_heads(prefix_keys[...])
    weights = jnp.exp(dot_right(prefix_key_stack, heads) * score_scale)
    weights = jnp.where(pad_row < PREFIX, weights, 0.0)
    slopes = (weights * (dot_right(stack_heads(prefix_values[...]), low) - head_rows(32))).astype(BF16)
    from_prefix = dot_left(slopes, prefix_key_stack)
    prefix_key_grad = merge_heads(dot_nn(slopes, heads)) * score_scale
    prefix_value_grad = merge_heads(dot_nn(weights.astype(BF16), low))

    @pl.when(row == 0)
    def _():
        prefix_grads[0] = prefix_key_grad
        prefix_grads[1] = prefix_value_grad

    @pl.when(row > 0)
    def _():
        prefix_grads[0] += prefix_key_grad
        prefix_grads[1] += prefix_value_grad

    key_stack = stack_heads(keys[...].reshape(memory_len, LANES))
    value_stack = stack_heads(values[...].reshape(memory_len, LANES))
    allowed = key_docs[0] == query_docs[0]
    weights = jnp.exp(dot_right(key_stack, heads) * score_scale).reshape(2, memory_len, S_DEV)
    weights = jnp.where(allowed[None], weights, 0.0).reshape(2 * memory_len, S_DEV)
    slopes = (weights * (dot_right(value_stack, low) - head_rows(memory_len))).astype(BF16)
    key_grad[...] = (merge_heads(dot_nn(slopes, heads)) * score_scale).astype(BF16).reshape(key_grad.shape)
    value_grad[...] = merge_heads(dot_nn(weights.astype(BF16), low)).astype(BF16).reshape(value_grad.shape)
    query_grad[0] = ((from_prefix + dot_left(slopes, key_stack)) * score_scale).astype(BF16)


def cross_backward(queries, memory_pairs, query_docs, key_docs, prefix_keys, prefix_values, grad_out, crossed, inverse):
    memory_len = 16 * M_DEV
    head_block = pl.BlockSpec((1, S_DEV, LANES), lambda pair, row: (row, 0, pair))
    keys = pl.BlockSpec((16, 1, M_DEV, LANES), lambda pair, row: (0, row, 0, pair))
    values = pl.BlockSpec((16, 1, M_DEV, LANES), lambda pair, row: (0, row, 0, PAIRS + pair))
    prefix = pl.BlockSpec((32, LANES), lambda pair, row: (0, pair))
    terms = jax.ShapeDtypeStruct((16, 2, M_DEV, D), BF16)
    return pl.pallas_call(
        cross_backward_kernel,
        grid=(PAIRS, 2),
        out_shape=(
            jax.ShapeDtypeStruct((2, S_DEV, D), BF16), terms, terms,
            jax.ShapeDtypeStruct((2, 32, D), F32),
        ),
        in_specs=[
            head_block, keys, values,
            pl.BlockSpec((1, 1, S_DEV), lambda pair, row: (row, 0, 0)),
            pl.BlockSpec((1, memory_len, LANES), lambda pair, row: (row, 0, 0)),
            prefix, prefix, head_block, head_block, head_block,
        ],
        out_specs=(
            head_block, keys, keys, pl.BlockSpec((2, 32, LANES), lambda pair, row: (0, 0, pair)),
        ),
        compiler_params=params(),
        name="cross_backward",
    )(queries, memory_pairs, memory_pairs, query_docs, key_docs, prefix_keys, prefix_values, grad_out, crossed, inverse)


def gelu_parts(pre):
    upper = 0.5 * (1.0 + lax.erf(pre * (0.5 ** 0.5)))
    return upper


def gelu_slope(pre):
    return gelu_parts(pre) + pre * jnp.exp(-0.5 * pre * pre) * (1.0 / math.sqrt(2.0 * math.pi))


def norm_back_rows(resid, gain, upstream):
    middle = jnp.mean(resid, axis=-1, keepdims=True)
    centred = resid - middle
    scale = lax.rsqrt(jnp.mean(centred * centred, axis=-1, keepdims=True) + 1e-05)
    unit = centred * scale
    pulled = upstream * gain
    return scale * (
        pulled - jnp.mean(pulled, axis=-1, keepdims=True) - unit * jnp.mean(pulled * unit, axis=-1, keepdims=True)
    )


def feed_kernel(
    normed, cotangent, gain, inner, outer, mixed,
    layer_out, second_grad, small_grads,
    low, pre, adapter_pre, total, feed_low,
):
    step = pl.program_id(0)
    down = mixed[:, :, :ADAPTER].reshape(D, ADAPTER)
    up_left = mixed[:, :16, ADAPTER:].reshape(ADAPTER, ADAPTER)
    up_right = mixed[:, 16:, ADAPTER:].reshape(ADAPTER, ADAPTER)
    half = ADAPTER

    @pl.when(step == 0)
    def _():
        low[...] = normed[...].astype(BF16)
        adapter_pre[...] = dot_nn(low[...], down)
        act = adapter_pre[...]
        act = (act * gelu_parts(act)).astype(BF16)
        total[:, :half] = normed[:, :half] + 4.0 * dot_nn(act, up_left)
        total[:, half:] = normed[:, half:] + 4.0 * dot_nn(act, up_right)

    @pl.when(step < 4)
    def _():
        hidden = dot_nn(low[...], inner[...].reshape(D, D))
        pre[jnp.minimum(step, 3)] = hidden
        act = (hidden * gelu_parts(hidden)).astype(BF16)
        total[...] += dot_nn(act, outer[...].reshape(D, D))

    @pl.when(step == 3)
    def _():
        resid = total[...]
        layer_out[...] = norm_rows(resid, gain[...]).astype(BF16)
        third_grad = norm_back_rows(resid, gain[...], cotangent[...].astype(F32))
        feed_low[...] = third_grad.astype(BF16)
        adapter_low = (4.0 * third_grad).astype(BF16)
        act = adapter_pre[...]
        upper = gelu_parts(act)
        slope = gelu_slope(act)
        act = (act * upper).astype(BF16)
        grad = dot_right(adapter_low[:, :half], up_left) + dot_right(adapter_low[:, half:], up_right)
        grad = (slope * grad).astype(BF16)
        second_grad[...] = third_grad + dot_right(grad, down)
        small_grads[:, :, :half] = dot_left(low[...], grad).astype(BF16).reshape(32, 32, half)
        small_grads[:, :16, half:] = dot_left(act, adapter_low[:, :half]).astype(BF16).reshape(32, 16, half)
        small_grads[:, 16:, half:] = dot_left(act, adapter_low[:, half:]).astype(BF16).reshape(32, 16, half)

    @pl.when(step >= 4)
    def _():
        hidden = pre[jnp.clip(7 - step, 0, 3)]
        grad = dot_right(feed_low[...], outer[...].reshape(D, D))
        grad = (gelu_slope(hidden) * grad).astype(BF16)
        second_grad[...] += dot_right(grad, inner[...].reshape(D, D))


def feed_forward_backward(normed, cotangent, gain, weights):
    tokens = normed.shape[0]
    at = lambda step: jnp.minimum(step, 7 - step)
    still = lambda step: (0, 0)
    rows = pl.BlockSpec((tokens, D), still)
    return pl.pallas_call(
        feed_kernel,
        grid=(8,),
        out_shape=(
            jax.ShapeDtypeStruct((tokens, D), BF16),
            jax.ShapeDtypeStruct((tokens, D), F32),
            jax.ShapeDtypeStruct((32, 32, D), BF16),
        ),
        in_specs=[
            rows, rows, pl.BlockSpec((1, D), still),
            pl.BlockSpec((32, 32, D), lambda step: (0, at(step), 0)),
            pl.BlockSpec((8, 128, D), lambda step: (at(step), 1, 0)),
            pl.BlockSpec((32, 32, D), lambda step: (0, 8, 0)),
        ],
        out_specs=(rows, rows, pl.BlockSpec((32, 32, D), lambda step: (0, 0, 0))),
        scratch_shapes=[
            pltpu.VMEM((tokens, D), BF16),
            pltpu.VMEM((4, tokens, D), F32),
            pltpu.VMEM((tokens, ADAPTER), F32),
            pltpu.VMEM((tokens, D), F32),
            pltpu.VMEM((tokens, D), BF16),
        ],
        compiler_params=params(),
        name="feed",
    )(normed, cotangent, gain, weights, weights, weights)


def fast_device(
    inputs, memory, out_grad, token_docs, memory_docs, self_project, self_output, cross_query,
    cross_memory, cross_output, inner_weight, outer_weight, adapter_down, adapter_up, norm_gains, prefixes,
):
    seq, x = lax.axis_index("seq"), lax.axis_index("rows")
    tokens = 2 * S_DEV
    mixed = jnp.concatenate(
        [adapter_down, jnp.concatenate([adapter_up[:, :ADAPTER], adapter_up[:, ADAPTER:]], axis=0)], axis=1
    )
    feed_flat = jnp.concatenate(
        [inner_weight[:, part * D:(part + 1) * D] for part in range(4)] + [outer_weight, mixed], axis=0
    )
    feed_weights = lax.all_gather(feed_flat, ("seq", "rows"), axis=0, tiled=True).reshape(32, FEED_ROWS, D)

    small = jnp.concatenate([
        norm_gains.reshape(-1), prefixes.reshape(-1),
        token_docs.astype(BF16).reshape(-1), memory_docs.astype(BF16).reshape(-1),
    ])
    small = jnp.pad(small, (0, SMALL_ROWS * D - small.shape[0])).reshape(SMALL_ROWS, D)
    full, memory_all = gather_first(
        self_project, self_output, cross_query, cross_memory, cross_output, small, memory
    )

    def weight(first):
        return full[:, first:first + 32].reshape(D, D)

    flat = full[:, SMALL_AT:SMALL_AT + 5].reshape(32, 5 * D)
    gains = flat[:, :96].reshape(32, 3, 32).transpose(1, 0, 2).reshape(3, D).astype(F32)
    prefix_parts = flat[:, 96:3936].reshape(32, 4, PREFIX, 32)
    cross_prefixes = prefix_parts[:, 2:].transpose(1, 2, 0, 3).reshape(2, PREFIX, D)
    cross_prefixes = jnp.pad(cross_prefixes, ((0, 0), (0, 2), (0, 0)))
    pair_prefixes = lax.dynamic_slice_in_dim(prefix_parts[:, :2], 4 * (seq // 2), 4, 0)
    pair_prefixes = pair_prefixes.transpose(1, 2, 0, 3).reshape(2, PREFIX, LANES)
    pair_prefixes = jnp.pad(pair_prefixes, ((0, 0), (0, 2), (0, 0)))
    row_docs = lax.dynamic_index_in_dim(flat[:, 3936:4256].reshape(16, 2, 320), x, 1, False).astype(F32)
    own_docs = lax.dynamic_index_in_dim(row_docs[:, :256].reshape(16, 2, S_DEV), seq % 2, 1, False)
    docs_row = own_docs.reshape(1, 16 * S_DEV)
    docs_column = jnp.broadcast_to(docs_row.reshape(-1, 1), (16 * S_DEV, LANES))
    memory_row = row_docs[:, 256:].reshape(16, 2, M_DEV).transpose(1, 0, 2).reshape(2, 1, 16 * M_DEV)
    memory_column = jnp.broadcast_to(memory_row.reshape(2, -1, 1), (2, 16 * M_DEV, LANES))
    query_row = token_docs.astype(F32).reshape(2, 1, S_DEV)
    query_column = jnp.broadcast_to(query_row.reshape(2, S_DEV, 1), (2, S_DEV, 16 * M_DEV))

    arrived = project_exchange(inputs, full)
    attended, pair_attended, pair_inverse = self_forward(
        arrived, docs_row, docs_column, pair_prefixes[0], pair_prefixes[1]
    )
    memory_pairs = jnp.concatenate(
        [jnp.dot(memory_all.reshape(-1, D), weight(at), preferred_element_type=F32) for at in (MEM_K_AT, MEM_V_AT)],
        axis=1,
    ).astype(BF16).reshape(16, 2, M_DEV, 2 * D)

    first_resid = inputs.reshape(tokens, D).astype(F32) + jnp.dot(
        attended.reshape(tokens, D), weight(SELF_OUT_AT), preferred_element_type=F32
    )
    first_norm = norm_rows(first_resid, gains[0])
    cross_queries = jnp.dot(
        first_norm.astype(BF16), weight(CROSS_Q_AT), preferred_element_type=F32
    ).astype(BF16).reshape(2, S_DEV, D)
    crossed, cross_inverse = cross_forward(
        cross_queries, memory_pairs, query_column, memory_row, cross_prefixes[0], cross_prefixes[1]
    )
    second_resid = first_norm + jnp.dot(
        crossed.reshape(tokens, D).astype(BF16), weight(CROSS_OUT_AT), preferred_element_type=F32
    )
    second_norm = norm_rows(second_resid, gains[1])

    layer_out, second_grad, small_grads = feed_forward_backward(
        second_norm, out_grad.reshape(tokens, D), gains[2:3], feed_weights
    )
    small_sums = lax.psum_scatter(small_grads.reshape(1024, D), "seq", scatter_dimension=0, tiled=True)

    second_resid_grad = norm_back_rows(second_resid, gains[1], second_grad)
    cross_out_grad = dot_right(second_resid_grad.astype(BF16), weight(CROSS_OUT_AT))
    cross_query_grad, key_terms, value_terms, cross_prefix_grads = cross_backward(
        cross_queries, memory_pairs, query_row, memory_column, cross_prefixes[0], cross_prefixes[1],
        cross_out_grad.reshape(2, S_DEV, D), crossed, cross_inverse,
    )
    memory_terms = dot_right(key_terms.reshape(-1, D), weight(MEM_K_AT)) + dot_right(
        value_terms.reshape(-1, D), weight(MEM_V_AT)
    )
    prefix_flat = cross_prefix_grads[:, :PREFIX].reshape(2 * PREFIX, 16, 64).transpose(1, 0, 2).reshape(16, -1)
    prefix_flat = jnp.pad(prefix_flat, ((0, 0), (0, 8 * D - prefix_flat.shape[1]))).reshape(16, 8, D)
    memory_terms = jnp.concatenate(
        [memory_terms.astype(BF16).reshape(16, 64, D), prefix_flat.astype(BF16)], axis=1
    )
    memory_sums = lax.psum_scatter(memory_terms, "seq", scatter_dimension=0, tiled=False)

    first_grad = second_resid_grad + dot_right(cross_query_grad.reshape(tokens, D), weight(CROSS_Q_AT))
    first_resid_grad = norm_back_rows(first_resid, gains[0], first_grad)
    self_out_grad = dot_right(first_resid_grad.astype(BF16), weight(SELF_OUT_AT))
    project_grads, self_prefix_grads = self_backward(
        arrived, self_out_grad.astype(BF16).reshape(2, S_DEV, D), pair_attended, pair_inverse,
        docs_row, docs_column, pair_prefixes[0], pair_prefixes[1],
    )
    project_grads = project_grads.transpose(2, 1, 3, 0, 4).reshape(3, tokens, D)
    input_grad = first_resid_grad
    for part in range(3):
        input_grad = input_grad + dot_right(project_grads[part], weight(32 * part))

    def swapped(values):
        return lax.ppermute(values, "rows", [(0, 1), (1, 0)])

    halves = small_sums.astype(F32).reshape(2, 32, D)
    give = lax.dynamic_index_in_dim(halves, 1 - x, 0, False)
    keep = lax.dynamic_index_in_dim(halves, x, 0, False)
    prefix_half = memory_sums[64:].astype(F32).reshape(-1)[:60 * 64].reshape(60, 2, 32)
    cross_give = lax.dynamic_index_in_dim(prefix_half, 1 - x, 1, False)
    cross_keep = lax.dynamic_index_in_dim(prefix_half, x, 1, False)
    pair_sum = self_prefix_grads + lax.ppermute(
        self_prefix_grads, "seq", [(at, at ^ 1) for at in range(16)]
    )
    pair_sum = pair_sum[:, :PREFIX].reshape(60, 2, 2, 32)
    pair_sum = lax.dynamic_index_in_dim(pair_sum, seq % 2, 1, False)
    self_give = lax.dynamic_index_in_dim(pair_sum, 1 - x, 1, False)
    self_keep = lax.dynamic_index_in_dim(pair_sum, x, 1, False)
    keep = keep + swapped(give)
    prefix_grad = jnp.concatenate([self_keep, cross_keep], axis=0) + swapped(
        jnp.concatenate([self_give, cross_give], axis=0)
    )
    return (
        layer_out.reshape(2, S_DEV, D),
        input_grad.reshape(2, S_DEV, D),
        memory_sums[:64].astype(F32).reshape(2, M_DEV, D),
        prefix_grad.reshape(4, PREFIX, 32),
        keep[:, :ADAPTER],
        jnp.concatenate([keep[:16, ADAPTER:], keep[16:, ADAPTER:]], axis=1),
    )


def solution(mesh):
    placed = (
        P("rows", "seq", None),
        P("rows", "seq", None),
        P("rows", "seq", None),
        P("rows", "seq"),
        P("rows", "seq"),
        P(("seq", "rows"), None),
        P(("seq", "rows"), None),
        P(("seq", "rows"), None),
        P(("seq", "rows"), None),
        P(("seq", "rows"), None),
        P(("seq", "rows"), None),
        P(("seq", "rows"), None),
        P(("seq", "rows"), None),
        P(("seq", "rows"), None),
        P(None, ("seq", "rows")),
        P(None, None, ("seq", "rows")),
    )
    small_slice = mesh.shape["seq"] == 16 and mesh.shape["rows"] == 2
    return jax.shard_map(
        fast_device if small_slice else per_device,
        mesh=mesh,
        in_specs=placed,
        out_specs=(
            P("rows", "seq", None),
            P("rows", "seq", None),
            P("rows", "seq", None),
            P(None, None, ("seq", "rows")),
            P(("seq", "rows"), None),
            P(("seq", "rows"), None),
        ),
        check_vma=False,
    )
```

```python
import math

import jax
import jax.numpy as jnp
from jax import lax
from jax.experimental import pallas as pl
from jax.experimental.pallas import tpu as pltpu
from jax.sharding import PartitionSpec as P

D = 1024
HEADS = 16
HEAD_DIM = 64
ADAPTER = 512
PREFIX = 30
S_DEV = 128
M_DEV = 32


score_scale = 0.125
masked_score = -1000000000.0


def heads_of(matrix):
    return matrix.reshape(matrix.shape[0], HEADS, HEAD_DIM)


def dot_right(left, right):
    return lax.dot_general(
        left, right, (((1,), (1,)), ((), ())), preferred_element_type=jnp.float32
    )


def dot_left(left, right):
    return lax.dot_general(
        left, right, (((0,), (0,)), ((), ())), preferred_element_type=jnp.float32
    )


def norm_rows(resid, gain):
    middle = jnp.mean(resid, axis=-1, keepdims=True)
    centred = resid - middle
    spread = jnp.mean(centred * centred, axis=-1, keepdims=True)
    return centred * lax.rsqrt(spread + 1e-05) * gain


def norm_back(resid, gain, upstream):
    unused, pullback = jax.vjp(lambda values: norm_rows(values, gain), resid)
    return pullback(upstream)[0]


def gelu_back(pre_act, upstream):
    unused, pullback = jax.vjp(lambda values: jax.nn.gelu(values, approximate=False), pre_act)
    return pullback(upstream)[0]


def allowed_keys(query_docs, key_docs, query_pos, key_pos, causal):
    allowed = query_docs[:, None] == key_docs[None, :]
    if causal:
        allowed = allowed & (key_pos[None, :] <= query_pos[:, None])
    return allowed


def prefix_terms(queries, prefix_keys, prefix_values):
    scores = (
        jnp.einsum(
            "qhd,phd->hqp", queries, heads_of(prefix_keys), preferred_element_type=jnp.float32
        )
        * score_scale
    )
    weights = jnp.exp(scores)
    summed = jnp.einsum(
        "hqp,phd->qhd",
        weights.astype(jnp.bfloat16),
        heads_of(prefix_values),
        preferred_element_type=jnp.float32,
    )
    return (jnp.sum(weights, axis=-1), summed)


def fold_keys(running, arrived, queries, query_docs, key_docs, query_first, causal):
    key_count = arrived.shape[0]
    block_len = math.gcd(key_count, 512)
    query_count = queries.shape[0]
    query_pos = query_first + jnp.arange(query_count, dtype=jnp.int32)
    key_width = arrived.shape[1] // 2

    def fold_one_block(current, element):
        key_block, block_index = element
        key_first = block_index * block_len

        def compute(present):
            block_docs = lax.dynamic_slice_in_dim(key_docs, key_first, block_len, 0)
            allowed = allowed_keys(
                query_docs,
                block_docs,
                query_pos,
                key_first + jnp.arange(block_len, dtype=jnp.int32),
                causal,
            )
            scores = (
                jnp.einsum(
                    "qhd,khd->hqk",
                    queries,
                    heads_of(key_block[:, :key_width]),
                    preferred_element_type=jnp.float32,
                )
                * score_scale
            )
            weights = jnp.exp(jnp.where(allowed[None], scores, masked_score))
            summed = jnp.einsum(
                "hqk,khd->qhd",
                weights.astype(jnp.bfloat16),
                heads_of(key_block[:, key_width:]),
                preferred_element_type=jnp.float32,
            )
            return (present[0] + jnp.sum(weights, axis=-1), present[1] + summed)

        if causal:
            return (
                lax.cond(
                    key_first <= query_first + query_count - 1, compute, lambda held: held, current
                ),
                None,
            )
        return (compute(current), None)

    running, unused = lax.scan(
        fold_one_block,
        running,
        (
            arrived.reshape(key_count // block_len, block_len, arrived.shape[1]),
            jnp.arange(key_count // block_len, dtype=jnp.int32),
        ),
    )
    return running


def attend_back(
    queries,
    gathered,
    prefix_keys,
    prefix_values,
    grad_out,
    attended,
    totals,
    query_docs,
    key_docs,
    query_first,
    causal,
):
    query_count = queries.shape[0]
    key_count = gathered.shape[0]
    key_width = gathered.shape[1] // 2
    block_len = math.gcd(key_count, 512)
    query_pos = query_first + jnp.arange(query_count, dtype=jnp.int32)
    grad_heads = heads_of(grad_out)
    grad_summed = (grad_heads / totals.T[:, :, None]).astype(jnp.bfloat16)
    row_dot = jnp.sum(grad_heads * heads_of(attended), axis=-1).T / totals
    prefix_key_heads = heads_of(prefix_keys)
    prefix_value_heads = heads_of(prefix_values)
    prefix_weights = jnp.exp(
        jnp.einsum("qhd,phd->hqp", queries, prefix_key_heads, preferred_element_type=jnp.float32)
        * score_scale
    )
    prefix_dots = jnp.einsum(
        "qhd,phd->hqp", grad_summed, prefix_value_heads, preferred_element_type=jnp.float32
    )
    prefix_slopes = (prefix_weights * (prefix_dots - row_dot[:, :, None])).astype(jnp.bfloat16)
    query_grad = jnp.einsum(
        "hqp,phd->qhd", prefix_slopes, prefix_key_heads, preferred_element_type=jnp.float32
    )
    key_grad_prefix = (
        jnp.einsum("hqp,qhd->phd", prefix_slopes, queries, preferred_element_type=jnp.float32)
        * score_scale
    ).reshape(-1, D)
    value_grad_prefix = jnp.einsum(
        "hqp,qhd->phd",
        prefix_weights.astype(jnp.bfloat16),
        grad_summed,
        preferred_element_type=jnp.float32,
    ).reshape(-1, D)

    def attend_one_block(current, element):
        key_block, block_index = element
        key_first = block_index * block_len

        def compute(present):
            block_docs = lax.dynamic_slice_in_dim(key_docs, key_first, block_len, 0)
            allowed = allowed_keys(
                query_docs,
                block_docs,
                query_pos,
                key_first + jnp.arange(block_len, dtype=jnp.int32),
                causal,
            )
            key_heads = heads_of(key_block[:, :key_width])
            value_heads = heads_of(key_block[:, key_width:])
            scores = (
                jnp.einsum("qhd,khd->hqk", queries, key_heads, preferred_element_type=jnp.float32)
                * score_scale
            )
            weights = jnp.exp(jnp.where(allowed[None], scores, masked_score))
            dots = jnp.einsum(
                "qhd,khd->hqk", grad_summed, value_heads, preferred_element_type=jnp.float32
            )
            slopes = (weights * (dots - row_dot[:, :, None])).astype(jnp.bfloat16)
            present = present + jnp.einsum(
                "hqk,khd->qhd", slopes, key_heads, preferred_element_type=jnp.float32
            )
            key_grad = (
                jnp.einsum("hqk,qhd->khd", slopes, queries, preferred_element_type=jnp.float32)
                * score_scale
            )
            value_grad = jnp.einsum(
                "hqk,qhd->khd",
                weights.astype(jnp.bfloat16),
                grad_summed,
                preferred_element_type=jnp.float32,
            )
            return (
                present,
                jnp.concatenate(
                    [key_grad.reshape(block_len, D), value_grad.reshape(block_len, D)], axis=1
                ),
            )

        if causal:
            return lax.cond(
                key_first <= query_first + query_count - 1,
                compute,
                lambda held: (held, jnp.zeros((block_len, 2 * D), jnp.float32)),
                current,
            )
        return compute(current)

    query_grad, key_terms = lax.scan(
        attend_one_block,
        query_grad,
        (
            gathered.reshape(key_count // block_len, block_len, gathered.shape[1]),
            jnp.arange(key_count // block_len, dtype=jnp.int32),
        ),
    )
    query_low = (query_grad * score_scale).astype(jnp.bfloat16).reshape(query_count, D)
    key_terms = key_terms.reshape(key_count, 2 * D)
    return (query_low, key_terms, key_grad_prefix, value_grad_prefix, grad_summed, row_dot)


def fetch_all(
    self_project,
    self_output,
    cross_query,
    cross_memory,
    cross_output,
    inner_weight,
    outer_weight,
    adapter_down,
    adapter_up,
    norm_gains,
    prefixes,
):
    return (
        lax.all_gather(self_project, ("seq", "rows"), axis=0, tiled=True),
        lax.all_gather(self_output, ("seq", "rows"), axis=0, tiled=True),
        lax.all_gather(cross_query, ("seq", "rows"), axis=0, tiled=True),
        lax.all_gather(cross_memory, ("seq", "rows"), axis=0, tiled=True),
        lax.all_gather(cross_output, ("seq", "rows"), axis=0, tiled=True),
        lax.all_gather(inner_weight, ("seq", "rows"), axis=0, tiled=True),
        lax.all_gather(outer_weight, ("seq", "rows"), axis=0, tiled=True),
        lax.all_gather(adapter_down, ("seq", "rows"), axis=0, tiled=True),
        lax.all_gather(adapter_up, ("seq", "rows"), axis=0, tiled=True),
        lax.all_gather(norm_gains, ("seq", "rows"), axis=1, tiled=True),
        lax.all_gather(prefixes, ("seq", "rows"), axis=2, tiled=True),
    )


def fetch_again(
    self_project,
    self_output,
    cross_query,
    cross_memory,
    cross_output,
    inner_weight,
    outer_weight,
    adapter_down,
    adapter_up,
    norm_gains,
    prefixes,
):
    return (
        lax.all_gather(self_project, ("seq", "rows"), axis=0, tiled=True),
        lax.all_gather(self_output, ("seq", "rows"), axis=0, tiled=True),
        lax.all_gather(cross_query, ("seq", "rows"), axis=0, tiled=True),
        lax.all_gather(cross_memory, ("seq", "rows"), axis=0, tiled=True),
        lax.all_gather(cross_output, ("seq", "rows"), axis=0, tiled=True),
        lax.all_gather(inner_weight, ("seq", "rows"), axis=0, tiled=True),
        lax.all_gather(outer_weight, ("seq", "rows"), axis=0, tiled=True),
        lax.all_gather(adapter_down, ("seq", "rows"), axis=0, tiled=True),
        lax.all_gather(adapter_up, ("seq", "rows"), axis=0, tiled=True),
        lax.all_gather(norm_gains, ("seq", "rows"), axis=1, tiled=True),
        lax.all_gather(prefixes, ("seq", "rows"), axis=2, tiled=True),
    )


def forward_row(tokens, memory_rows, query_docs, token_docs, memory_docs, query_first, weights):
    (
        self_project,
        self_output,
        cross_query,
        cross_memory,
        cross_output,
        inner_weight,
        outer_weight,
        adapter_down,
        adapter_up,
        norm_gains,
        prefixes,
    ) = weights
    gains = norm_gains.astype(jnp.float32)
    projected = jnp.dot(tokens, self_project, preferred_element_type=jnp.float32).astype(
        jnp.bfloat16
    )
    queries = heads_of(projected[:, :D])
    local_pairs = projected[:, D:]
    start_self = prefix_terms(queries, prefixes[0], prefixes[1])
    totals, summed = fold_keys(
        start_self,
        lax.all_gather(local_pairs, "seq", axis=0, tiled=True),
        queries,
        query_docs,
        token_docs,
        query_first,
        True,
    )
    attended = (summed / totals.T[:, :, None]).reshape(-1, D)
    first_resid = tokens.astype(jnp.float32) + jnp.dot(
        attended.astype(jnp.bfloat16), self_output, preferred_element_type=jnp.float32
    )
    first_norm = norm_rows(first_resid, gains[0])
    first_low = first_norm.astype(jnp.bfloat16)
    cross_queries = heads_of(
        jnp.dot(first_low, cross_query, preferred_element_type=jnp.float32).astype(jnp.bfloat16)
    )
    memory_pairs = jnp.dot(memory_rows, cross_memory, preferred_element_type=jnp.float32).astype(
        jnp.bfloat16
    )
    start_cross = prefix_terms(cross_queries, prefixes[2], prefixes[3])
    cross_totals, cross_summed = fold_keys(
        start_cross,
        lax.all_gather(memory_pairs, "seq", axis=0, tiled=True),
        cross_queries,
        query_docs,
        memory_docs,
        query_first,
        False,
    )
    crossed = (cross_summed / cross_totals.T[:, :, None]).reshape(-1, D)
    second_resid = first_norm + jnp.dot(
        crossed.astype(jnp.bfloat16), cross_output, preferred_element_type=jnp.float32
    )
    second_norm = norm_rows(second_resid, gains[1])
    second_low = second_norm.astype(jnp.bfloat16)
    hidden_pre = jnp.dot(second_low, inner_weight, preferred_element_type=jnp.float32)
    hidden_act = jax.nn.gelu(hidden_pre, approximate=False).astype(jnp.bfloat16)
    adapter_pre = jnp.dot(second_low, adapter_down, preferred_element_type=jnp.float32)
    adapter_act = jax.nn.gelu(adapter_pre, approximate=False).astype(jnp.bfloat16)
    third_resid = (
        second_norm
        + jnp.dot(hidden_act, outer_weight, preferred_element_type=jnp.float32)
        + 4.0 * jnp.dot(adapter_act, adapter_up, preferred_element_type=jnp.float32)
    )
    layer_out = norm_rows(third_resid, gains[2]).astype(jnp.bfloat16)
    saved = (
        queries,
        local_pairs,
        totals,
        attended,
        first_resid,
        cross_queries,
        memory_pairs,
        cross_totals,
        crossed,
        second_resid,
        second_low,
        hidden_pre,
        adapter_pre,
        adapter_act,
        third_resid,
    )
    return (layer_out, saved)


def backward_row(cotangent, saved, weights, query_docs, token_docs, memory_docs, query_first):
    (
        self_project,
        self_output,
        cross_query,
        cross_memory,
        cross_output,
        inner_weight,
        outer_weight,
        adapter_down,
        adapter_up,
        norm_gains,
        prefixes,
    ) = weights
    (
        queries,
        local_pairs,
        totals,
        attended,
        first_resid,
        cross_queries,
        memory_pairs,
        cross_totals,
        crossed,
        second_resid,
        second_low,
        hidden_pre,
        adapter_pre,
        adapter_act,
        third_resid,
    ) = saved
    gains = norm_gains.astype(jnp.float32)
    third_grad = norm_back(third_resid, gains[2], cotangent.astype(jnp.float32))
    feed_low = third_grad.astype(jnp.bfloat16)
    adapter_low = (4.0 * third_grad).astype(jnp.bfloat16)
    hidden_grad = gelu_back(hidden_pre, dot_right(feed_low, outer_weight)).astype(jnp.bfloat16)
    up_grad = dot_left(adapter_act, adapter_low)
    adapter_grad = gelu_back(adapter_pre, dot_right(adapter_low, adapter_up)).astype(jnp.bfloat16)
    down_grad = dot_left(second_low, adapter_grad)
    second_grad = (
        third_grad + dot_right(hidden_grad, inner_weight) + dot_right(adapter_grad, adapter_down)
    )
    second_resid_grad = norm_back(second_resid, gains[1], second_grad)
    self_all, memory_all = (
        lax.all_gather(local_pairs, "seq", axis=0, tiled=True),
        lax.all_gather(memory_pairs, "seq", axis=0, tiled=True),
    )
    cross_out_grad = dot_right(second_resid_grad.astype(jnp.bfloat16), cross_output)
    (
        cross_query_low,
        memory_terms,
        cross_key_prefix,
        cross_value_prefix,
        cross_summed_grad,
        cross_dot,
    ) = attend_back(
        cross_queries,
        memory_all,
        prefixes[2],
        prefixes[3],
        cross_out_grad,
        crossed,
        cross_totals,
        query_docs,
        memory_docs,
        query_first,
        False,
    )
    first_grad = second_resid_grad + dot_right(cross_query_low, cross_query)
    first_resid_grad = norm_back(first_resid, gains[0], first_grad)
    self_out_grad = dot_right(first_resid_grad.astype(jnp.bfloat16), self_output)
    query_low, self_terms, self_key_prefix, self_value_prefix, self_summed_grad, self_dot = (
        attend_back(
            queries,
            self_all,
            prefixes[0],
            prefixes[1],
            self_out_grad,
            attended,
            totals,
            query_docs,
            token_docs,
            query_first,
            True,
        )
    )
    self_sums, memory_sums = (
        lax.psum_scatter(
            self_terms.astype(jnp.bfloat16), "seq", scatter_dimension=0, tiled=True
        ).astype(jnp.float32),
        lax.psum_scatter(
            memory_terms.astype(jnp.bfloat16), "seq", scatter_dimension=0, tiled=True
        ).astype(jnp.float32),
    )
    project_grad = jnp.concatenate([query_low, self_sums.astype(jnp.bfloat16)], axis=1)
    input_grad = first_resid_grad + dot_right(project_grad, self_project)
    memory_grad = dot_right(memory_sums.astype(jnp.bfloat16), cross_memory)
    prefix_grad = jnp.stack(
        [self_key_prefix, self_value_prefix, cross_key_prefix, cross_value_prefix]
    )
    return (input_grad, memory_grad, (down_grad, up_grad, prefix_grad))


def per_device(
    inputs,
    memory,
    out_grad,
    token_docs,
    memory_docs,
    self_project,
    self_output,
    cross_query,
    cross_memory,
    cross_output,
    inner_weight,
    outer_weight,
    adapter_down,
    adapter_up,
    norm_gains,
    prefixes,
):
    docs_full, memory_full = (
        lax.all_gather(token_docs, "seq", axis=1, tiled=True),
        lax.all_gather(memory_docs, "seq", axis=1, tiled=True),
    )
    query_first = lax.axis_index("seq") * inputs.shape[1]
    outputs = []
    input_grads = []
    memory_grads = []
    adjusted_grads = None
    for row_index in range(inputs.shape[0]):
        weights = fetch_all(
            self_project,
            self_output,
            cross_query,
            cross_memory,
            cross_output,
            inner_weight,
            outer_weight,
            adapter_down,
            adapter_up,
            norm_gains,
            prefixes,
        )
        layer_out, saved = forward_row(
            inputs[row_index],
            memory[row_index],
            token_docs[row_index],
            docs_full[row_index],
            memory_full[row_index],
            query_first,
            weights,
        )
        weights_back = fetch_again(
            self_project,
            self_output,
            cross_query,
            cross_memory,
            cross_output,
            inner_weight,
            outer_weight,
            adapter_down,
            adapter_up,
            norm_gains,
            prefixes,
        )
        input_grad, memory_grad, row_grads = backward_row(
            out_grad[row_index],
            saved,
            weights_back,
            token_docs[row_index],
            docs_full[row_index],
            memory_full[row_index],
            query_first,
        )
        shares = (
            lax.psum_scatter(row_grads[0], ("seq", "rows"), scatter_dimension=0, tiled=True),
            lax.psum_scatter(row_grads[1], ("seq", "rows"), scatter_dimension=0, tiled=True),
            lax.psum_scatter(row_grads[2], ("seq", "rows"), scatter_dimension=2, tiled=True),
        )
        if adjusted_grads is None:
            adjusted_grads = shares
        else:
            adjusted_grads = tuple(
                (former + latter for former, latter in zip(adjusted_grads, shares))
            )
        outputs.append(layer_out)
        input_grads.append(input_grad)
        memory_grads.append(memory_grad)
    return (
        jnp.stack(outputs),
        jnp.stack(input_grads),
        jnp.stack(memory_grads),
        adjusted_grads[2],
        adjusted_grads[0],
        adjusted_grads[1],
    )


MESH_ID = pl.DeviceIdType.MESH
F32 = jnp.float32
BF16 = jnp.bfloat16
VMEM_BYTES = 60 * 1024 * 1024
PAIRS = HEADS // 2
LANES = 2 * HEAD_DIM
Q_AT, K_AT, V_AT, SELF_OUT_AT, CROSS_Q_AT, MEM_K_AT, MEM_V_AT, CROSS_OUT_AT = range(0, 256, 32)
INNER_AT, OUTER_AT, MIXED_AT = 256, 384, 512
ALL_ROWS = 544
SMALL_ROWS = 144
PIECE_ROWS = 16
GAP = 2
LEAD = 4
SENDS = 2
Z_LAST = ()
WAIT_TICKS = 4
STEP_TICKS = 2


def whole(space=pltpu.VMEM):
    return pl.BlockSpec(memory_space=space)


def params(collective_id=None):
    if collective_id is None:
        return pltpu.CompilerParams(vmem_limit_bytes=VMEM_BYTES)
    return pltpu.CompilerParams(
        vmem_limit_bytes=VMEM_BYTES, collective_id=collective_id, has_side_effects=True
    )


def remote(src, dst, send_sem, recv_sem, device):
    return pltpu.make_async_remote_copy(
        src_ref=src, dst_ref=dst, send_sem=send_sem, recv_sem=recv_sem,
        device_id=device, device_id_type=MESH_ID,
    )


def greet(peers):
    barrier = pltpu.get_barrier_semaphore()
    for peer in peers:
        pl.semaphore_signal(barrier, inc=1, device_id=peer, device_id_type=MESH_ID)
    pl.semaphore_wait(barrier, len(peers))


def dot_nn(left, right):
    return lax.dot_general(left, right, (((1,), (0,)), ((), ())), preferred_element_type=F32)


class Place:
    def __init__(self):
        self.seq, self.x = lax.axis_index("seq"), lax.axis_index("rows")
        self.z, self.y, self.core = self.seq // 4, (self.seq // 2) % 2, self.seq % 2
        self.pair, self.row = self.seq // 2, self.seq % 2

    def device(self, z, y, core, x):
        return ((z * 2 + y) * 2 + core, x)

    def along_z(self, step):
        return self.device((self.z + step) % 4, self.y, self.core, self.x)

    def along_y(self):
        return self.device(self.z, 1 - self.y, self.core, self.x)

    def along_x(self):
        return self.device(self.z, self.y, self.core, 1 - self.x)

    def other_core(self):
        return self.device(self.z, self.y, 1 - self.core, self.x)

    def diagonal(self):
        return self.device(self.z, self.y, 1 - self.core, 1 - self.x)

    def others(self):
        return [((self.seq + step) % 16, self.x) for step in range(1, 16)]


class Gather:
    def __init__(self, place, full, local_sem, sems, gap):
        self.place, self.full, self.local_sem, self.sems, self.gap = place, full, local_sem, sems, gap
        self.stages = []
        self.waiting = []
        self.tick_at = 0

    def copies(self, level, source, target, device, slot):
        k = len(self.stages)
        return remote(source, target, self.sems[2 * level].at[k, slot], self.sems[2 * level + 1].at[k, slot], device)

    def add(self, source, first, count, piece=PIECE_ROWS):
        for from_row in range(0, count, piece):
            self.add_piece(source.at[pl.ds(from_row, piece)], first + from_row, piece)
        return len(self.stages) - 1

    def add_piece(self, source, first, count):
        at, full = self.place, self.full
        z, y, core, x = at.z, at.y, at.core, at.x
        rows = pl.ds(first, count)
        mine = full.at[z, y, core, x, rows]
        k = len(self.stages)
        if k in Z_LAST:
            plane = full.at[z, :, core, :, rows]
            first_way, then_way = (at.along_x(), at.along_y()) if k % 2 else (at.along_y(), at.along_x())
            line = full.at[z, y, core, :, rows] if k % 2 else full.at[z, :, core, x, rows]
            self.stages.append((
                pltpu.make_async_copy(source, mine, self.local_sem.at[k]),
                [self.copies(0, source, mine, first_way, 0)],
                [self.copies(1, line, line, then_way, 0)],
                [self.copies(2, plane, plane, at.along_z(d + 1), d) for d in range(3)],
                [self.copies(3, full.at[:, :, core, :, rows], full.at[:, :, core, :, rows], at.other_core(), 0)],
            ))
            return
        cut = 2 if k % 3 == 0 else 1
        near, far = pl.ds(0, cut), pl.ds(cut, 4 - cut)
        near1, far1 = full.at[near, y, core, x, rows], full.at[far, y, core, x, rows]
        near2, far2 = full.at[near, y, core, :, rows], full.at[far, :, core, x, rows]
        half = full.at[:, :, core, :, rows]
        self.stages.append((
            pltpu.make_async_copy(source, mine, self.local_sem.at[len(self.stages)]),
            [self.copies(0, source, mine, at.along_z(d + 1), d) for d in range(3)],
            [self.copies(1, near1, near1, at.along_x(), 0), self.copies(1, far1, far1, at.along_y(), 1)],
            [self.copies(2, near2, near2, at.along_y(), 0), self.copies(2, far2, far2, at.along_x(), 1)],
            [self.copies(3, half, half, at.other_core(), 0)],
        ))

    def add_memory(self, source, full):
        for row in range(2):
            self.add_memory_row(source.at[row], full.at[:, :, :, row])
        return len(self.stages) - 1

    def add_memory_row(self, source, full):
        at = self.place
        mine, column, half = full.at[at.z, at.y, at.core], full.at[:, at.y, at.core], full.at[:, :, at.core]
        self.stages.append((
            pltpu.make_async_copy(source, mine, self.local_sem.at[len(self.stages)]),
            [self.copies(0, source, mine, at.along_z(d + 1), d) for d in range(3)],
            [self.copies(1, column, column, at.along_y(), 1)],
            [],
            [self.copies(3, half, half, at.other_core(), 0)],
        ))

    def start(self):
        for stage in self.stages:
            stage[0].start()

    def tick(self, count=1):
        for _ in range(count):
            for level in range(5):
                k = self.tick_at - self.after(level)
                if not 0 <= k < len(self.stages):
                    continue
                if level == 1:
                    self.stages[k][0].wait()
                if level > 0:
                    for copy in self.stages[k][level]:
                        copy.wait_recv()
                if level < 4:
                    for copy in self.stages[k][level + 1]:
                        copy.start()
            self.tick_at += 1
            for _ in range(SENDS):
                if self.waiting:
                    self.waiting.pop(0).start()

    def after(self, level):
        return 0 if level == 0 else LEAD + (level - 1) * self.gap

    def until(self, k):
        while self.tick_at <= k + self.after(4):
            self.tick()

    def finish(self):
        self.until(len(self.stages) - 1)
        for _, *levels in self.stages:
            for level in levels:
                for copy in level:
                    copy.wait_send()


def head_masks():
    lane = lax.broadcasted_iota(jnp.int32, (1, LANES), 1)
    first = (lane < HEAD_DIM).astype(F32).astype(BF16)
    return first, (1.0 - first.astype(F32)).astype(BF16)


def stack_heads(block):
    first, second = head_masks()
    return jnp.concatenate([block * first, block * second], axis=0)


def merge_heads(stacked):
    half = stacked.shape[0] // 2
    lane = lax.broadcasted_iota(jnp.int32, (half, LANES), 1)
    return jnp.where(lane < HEAD_DIM, stacked[:half], stacked[half:])


def rows_in_lanes(values):
    lane = lax.broadcasted_iota(jnp.int32, (8, LANES), 1)
    row = lax.broadcasted_iota(jnp.int32, (8, LANES), 0)
    picks = (lane // HEAD_DIM == row).astype(F32)
    return lax.dot_general(
        picks, values, (((1,), (1,)), ((), ())),
        precision=lax.Precision.HIGHEST, preferred_element_type=F32,
    )


def first_kernel(
    tokens, memory, small, docs,
    project, self_out, cross_q, cross_mem, cross_out, inner, outer, mixed,
    full, memory_full, memory_pairs, small_full, docs_all, docs_row, docs_column, arrived, attended, inverse,
    first_resid, cross_queries, crossed, cross_inverse, second_resid, second_norm,
    gathered, first_norm, weights, staged, quad, memory_held, result_staged, sums, parts,
    local_sem, send0, recv0, send1, recv1, send2, recv2, send3, recv3,
    fetch_sem, own_sem, quad_send, quad_recv, small_send, small_recv, docs_send, docs_recv,
    head_send, head_recv, out_send, out_recv,
):
    place = Place()
    seq, x, pair, row = place.seq, place.x, place.pair, place.row
    others = place.others()
    quad_peers = [place.other_core(), place.along_x(), place.diagonal()]
    greet(others + quad_peers[1:])

    engine = Gather(place, full, local_sem, (send0, recv0, send1, recv1, send2, recv2, send3, recv3), GAP)
    project_done = [
        engine.add(project.at[:, pl.ds(part * D, D)], at, 32) for part, at in enumerate((Q_AT, K_AT, V_AT))
    ]
    engine.add_memory(memory, memory_full)
    for part, at in enumerate((MEM_K_AT, MEM_V_AT)):
        memory_done = engine.add(cross_mem.at[:, pl.ds(part * D, D)], at, 32)
    out_done = engine.add(self_out, SELF_OUT_AT, 32)
    query_done = engine.add(cross_q, CROSS_Q_AT, 32)
    cross_done = engine.add(cross_out, CROSS_OUT_AT, 32)
    for part in range(4):
        engine.add(inner.at[:, pl.ds(part * D, D)], INNER_AT + 32 * part, 32)
    for part in range(4):
        engine.add(outer.at[pl.ds(32 * part, 32)], OUTER_AT + 32 * part, 32)
    engine.add(mixed, MIXED_AT, 32)
    engine.start()
    engine.tick()

    mine = place.core * 2 + x
    quad_copies = [
        remote(small, quad.at[mine], quad_send.at[k], quad_recv.at[k], quad_peers[k]) for k in range(3)
    ]
    own_small = pltpu.make_async_copy(small, quad.at[mine], own_sem.at[0])
    docs_copies = [
        remote(docs, docs_all.at[seq], docs_send.at[k], docs_recv.at[k], others[k]) for k in range(15)
    ]
    own_docs = pltpu.make_async_copy(docs, docs_all.at[seq], own_sem.at[1])
    own_small.start()
    own_docs.start()
    for copy in quad_copies + docs_copies:
        copy.start()
    engine.tick()
    own_small.wait()
    for copy in quad_copies:
        copy.wait()
    small_full[pair] = (quad[0] + quad[1]) + (quad[2] + quad[3])
    small_copies = []
    for k in range(1, 8):
        to = (((pair + k) % 8) * 2 + place.core, x)
        small_copies.append(
            remote(small_full.at[pair], small_full.at[pair], small_send.at[k], small_recv.at[k], to)
        )
        small_copies[-1].start()
    own_docs.wait()
    for copy in docs_copies:
        copy.wait()

    def spread_docs(at, carry):
        tile = docs_all[at]
        line = jnp.where(row == 0, tile[0:1], tile[1:2])
        docs_row[:, pl.ds(pl.multiple_of(at * S_DEV, S_DEV), S_DEV)] = jnp.broadcast_to(line, (8, S_DEV))
        docs_column[pl.ds(at * S_DEV, S_DEV)] = jnp.transpose(jnp.broadcast_to(line, (S_DEV, LANES)))
        return carry

    lax.fori_loop(0, 16, spread_docs, 0)

    rows = tokens[...].reshape(2 * S_DEV, D)
    for part in range(3):
        engine.until(project_done[part])
        fetch = pltpu.make_async_copy(full_rows(full, 32 * part), weights.at[part], fetch_sem.at[part])
        fetch.start()
        fetch.wait()
        result = dot_nn(rows, weights[part].reshape(D, D)).astype(BF16)
        for at_row in range(2):
            for at_pair in range(PAIRS):
                staged[at_pair, at_row, part] = result[
                    at_row * S_DEV:(at_row + 1) * S_DEV, at_pair * LANES:(at_pair + 1) * LANES
                ]
    head_copies = []
    for k in range(15):
        to = (seq + k + 1) % 16
        head_copies.append(
            remote(staged.at[to // 2, to % 2], arrived.at[seq], head_send.at[k], head_recv.at[k], others[k])
        )
    own_heads = pltpu.make_async_copy(staged.at[pair, row], arrived.at[seq], own_sem.at[2])
    own_heads.start()
    engine.waiting = list(head_copies)

    engine.until(memory_done)
    fetch_memory = pltpu.make_async_copy(memory_full, memory_held, own_sem.at[3])
    fetch_memory.start()
    fetches = [
        pltpu.make_async_copy(full_rows(full, at), weights.at[part], fetch_sem.at[part])
        for part, at in enumerate((MEM_K_AT, MEM_V_AT))
    ]
    for fetch in fetches:
        fetch.start()
    fetch_memory.wait()
    for part in range(2):
        fetches[part].wait()

        def project_memory(at, carry):
            held = memory_held[at].reshape(4 * 2 * M_DEV, D)
            result = dot_nn(held, weights[part].reshape(D, D)).astype(BF16)
            memory_pairs[pl.ds(4 * at, 4), :, :, pl.ds(part * D, D)] = result.reshape(4, 2, M_DEV, D)
            return carry

        lax.fori_loop(0, 4, project_memory, 0)
    engine.tick(max(WAIT_TICKS, -(-len(engine.waiting) // SENDS)))
    own_heads.wait()
    for copy in head_copies:
        copy.wait()

    block = 2 * S_DEV
    columns = pl.ds(pl.multiple_of(pair * LANES, LANES), LANES)
    target = gathered.at[row, :, columns]
    away = (
        lax.broadcasted_iota(jnp.int32, (block, block), 1)
        - lax.broadcasted_iota(jnp.int32, (block, block), 0)
    )
    prefix_lane = lax.broadcasted_iota(jnp.int32, (2 * block, 32), 1)
    prefix_keys, prefix_values = small_full[pair, 0:32], small_full[pair, 32:64]

    for step in range(8):
        at = (step + pair) % 8
        queries = stack_heads(arrived[pl.ds(2 * at, 2), 0].reshape(block, LANES))
        query_docs = docs_column[pl.ds(at * block, block)]
        scores = dot_right(queries, prefix_keys) * score_scale
        e = jnp.where(prefix_lane < PREFIX, jnp.exp(scores), 0.0)
        sums[...] = jnp.concatenate([e, jnp.zeros((2 * block, LANES - 32), F32)], axis=1)
        parts[...] = dot_nn(e.astype(BF16), prefix_values)

        def one_tile(key_at, carry):
            keys = arrived[pl.ds(2 * key_at, 2), 1].reshape(block, LANES)
            values = arrived[pl.ds(2 * key_at, 2), 2].reshape(block, LANES)
            key_docs = docs_row[0:1, pl.ds(pl.multiple_of(key_at * block, block), block)]
            same = jnp.concatenate([query_docs, query_docs], axis=1) == key_docs
            allowed = same & (away <= (at - key_at) * block)
            scores = dot_right(queries, keys) * score_scale
            e = jnp.where(allowed[None], jnp.exp(scores).reshape(2, block, block), 0.0)
            e = e.reshape(2 * block, block)
            sums[...] += e[:, :LANES] + e[:, LANES:]
            parts[...] += dot_nn(e.astype(BF16), values)
            return carry

        lax.fori_loop(0, at + 1, one_tile, 0)
        totals = 1.0 / jnp.sum(sums[...], axis=1, keepdims=True)
        result = merge_heads(parts[...] * totals)
        here = pl.ds(at * block, block)
        attended[here] = result
        inverse[here] = merge_heads(jnp.broadcast_to(totals, (2 * block, LANES)))
        result_staged[pl.ds(2 * at, 2)] = result.astype(BF16).reshape(2, S_DEV, LANES)
        for half in range(2):
            to = 2 * at + half

            @pl.when(to != seq)
            def _():
                remote(result_staged.at[to], target, out_send.at[to], out_recv.at[seq], (to, x)).start()

            @pl.when(to == seq)
            def _():
                pltpu.make_async_copy(result_staged.at[to], target, own_sem.at[4]).start()

        engine.tick(STEP_TICKS)

    for copy in small_copies:
        copy.wait()
    engine.until(cross_done)
    fetches = [
        pltpu.make_async_copy(full_rows(full, at), weights.at[part], fetch_sem.at[part])
        for part, at in enumerate((SELF_OUT_AT, CROSS_Q_AT, CROSS_OUT_AT))
    ]
    for fetch in fetches:
        fetch.start()
    gains = [
        jnp.concatenate(
            [small_full[at_pair, 128:144].astype(F32)[part:part + 1] for at_pair in range(PAIRS)], axis=1
        )
        for part in range(2)
    ]
    pltpu.make_async_copy(result_staged.at[seq], target, own_sem.at[4]).wait()
    for other, _ in others:
        remote(result_staged.at[other], target, out_send.at[other], out_recv.at[other], (other, x)).wait()
    fetches[0].wait()
    resid = tokens[...].reshape(2 * S_DEV, D).astype(F32) + dot_nn(
        gathered[...].reshape(2 * S_DEV, D), weights[0].reshape(D, D)
    )
    first_resid[...] = resid
    normed = norm_rows(resid, gains[0])
    first_norm[...] = normed
    engine.tick(STEP_TICKS)
    fetches[1].wait()
    cross_queries[...] = dot_nn(normed.astype(BF16), weights[1].reshape(D, D)).astype(BF16).reshape(2, S_DEV, D)
    engine.tick(STEP_TICKS)
    memory_len = 16 * M_DEV
    cross_prefix_lane = lax.broadcasted_iota(jnp.int32, (2 * S_DEV, 32), 1)
    for at_row in range(2):
        own = jnp.transpose(jnp.broadcast_to(docs[at_row:at_row + 1], (LANES, S_DEV)))
        own = jnp.concatenate([own] * (memory_len // LANES), axis=1)
        lines = [
            sum(docs_all[4 * at + k, 2 + at_row:3 + at_row] for k in range(4)) for at in range(4)
        ]
        allowed = own == jnp.concatenate(lines, axis=1)

        def one_pair(at_pair, carry):
            first = pl.multiple_of(at_pair * LANES, LANES)
            columns, value_columns = pl.ds(first, LANES), pl.ds(pl.multiple_of(first + D, LANES), LANES)
            stacked = stack_heads(cross_queries[at_row, :, columns])
            keys = memory_pairs[:, at_row, :, columns].reshape(memory_len, LANES)
            values = memory_pairs[:, at_row, :, value_columns].reshape(memory_len, LANES)
            scores = dot_right(stacked, small_full[at_pair, 64:96]) * score_scale
            prefix_e = jnp.where(cross_prefix_lane < PREFIX, jnp.exp(scores), 0.0)
            scores = dot_right(stacked, keys) * score_scale
            e = jnp.where(allowed[None], jnp.exp(scores).reshape(2, S_DEV, memory_len), 0.0)
            e = e.reshape(2 * S_DEV, memory_len)
            totals = jnp.sum(e, axis=1, keepdims=True) + jnp.sum(prefix_e, axis=1, keepdims=True)
            totals = 1.0 / totals
            summed = dot_nn(e.astype(BF16), values) + dot_nn(prefix_e.astype(BF16), small_full[at_pair, 96:128])
            crossed[at_row, :, columns] = merge_heads(summed * totals)
            cross_inverse[at_row, :, columns] = merge_heads(jnp.broadcast_to(totals, (2 * S_DEV, LANES)))
            return carry

        lax.fori_loop(0, PAIRS // 2, one_pair, 0)
        engine.tick(STEP_TICKS)
        lax.fori_loop(PAIRS // 2, PAIRS, one_pair, 0)
        engine.tick(STEP_TICKS)
    fetches[2].wait()
    resid = first_norm[...] + dot_nn(
        crossed[...].reshape(2 * S_DEV, D).astype(BF16), weights[2].reshape(D, D)
    )
    second_resid[...] = resid
    second_norm[...] = norm_rows(resid, gains[1])
    engine.finish()


def full_rows(full, first):
    return full.at[:, :, :, :, pl.ds(first, 32)]


def first_call(tokens, memory, small, docs, *weights):
    length = 16 * S_DEV
    chunks = 16 * 32 // PIECE_ROWS + 32 // PIECE_ROWS + 2
    dma = pltpu.SemaphoreType.DMA
    shape = jax.ShapeDtypeStruct
    outs = pl.pallas_call(
        first_kernel,
        out_shape=(
            shape((4, 2, 2, 2, ALL_ROWS, D), BF16),
            shape((4, 2, 2, 2, M_DEV, D), BF16),
            shape((16, 2, M_DEV, 2 * D), BF16),
            shape((8, SMALL_ROWS, LANES), BF16),
            shape((16, 8, LANES), F32),
            shape((8, length), F32),
            shape((length, LANES), F32),
            shape((16, 3, S_DEV, LANES), BF16),
            shape((length, LANES), F32),
            shape((length, LANES), F32),
            shape((2 * S_DEV, D), F32),
            shape((2, S_DEV, D), BF16),
            shape((2, S_DEV, D), F32),
            shape((2, S_DEV, D), F32),
            shape((2 * S_DEV, D), F32),
            shape((2 * S_DEV, D), F32),
        ),
        in_specs=[whole(), whole(pl.ANY), whole(), whole()] + [whole(pl.ANY)] * 8,
        out_specs=(whole(pl.ANY), whole(pl.ANY)) + (whole(),) * 14,
        scratch_shapes=[
            pltpu.VMEM((2, S_DEV, D), BF16),
            pltpu.VMEM((2 * S_DEV, D), F32),
            pltpu.VMEM((3, 4, 2, 2, 2, 32, D), BF16),
            pltpu.VMEM((PAIRS, 2, 3, S_DEV, LANES), BF16),
            pltpu.VMEM((4, SMALL_ROWS, LANES), BF16),
            pltpu.VMEM((4, 2, 2, 2, M_DEV, D), BF16),
            pltpu.VMEM((16, S_DEV, LANES), BF16),
            pltpu.VMEM((4 * S_DEV, LANES), F32),
            pltpu.VMEM((4 * S_DEV, LANES), F32),
            dma((chunks,)),
            dma((chunks, 3)), dma((chunks, 3)), dma((chunks, 2)), dma((chunks, 2)),
            dma((chunks, 3)), dma((chunks, 3)), dma((chunks, 1)), dma((chunks, 1)),
            dma((3,)), dma((5,)), dma((3,)), dma((3,)), dma((8,)), dma((8,)), dma((15,)), dma((15,)),
            dma((15,)), dma((15,)), dma((16,)), dma((16,)),
        ],
        compiler_params=params(0),
        name="first",
    )(tokens, memory, small, docs, *weights)
    return (outs[0].reshape(32, ALL_ROWS, D),) + tuple(outs[2:])


def self_backward_kernel(
    arrived, grad_out, attended, inverse, docs_row, docs_column, prefix_keys, prefix_values,
    gathered, prefix_grads,
    grads, grad_low, delta, query_grads, key_grads, value_grads, staged,
    local_sem, in_send, in_recv, out_send, out_recv, query_send, query_recv,
):
    seq, x = lax.axis_index("seq"), lax.axis_index("rows")
    block = 2 * S_DEV
    pair, row = seq // 2, seq % 2
    greet([((seq + step) % 16, x) for step in range(1, 16)])

    def heads_for(to):
        return grad_out.at[to % 2, :, pl.ds(pl.multiple_of((to // 2) * LANES, LANES), LANES)]

    own = pltpu.make_async_copy(heads_for(seq), grads.at[seq], local_sem.at[0])
    own.start()
    arrivals = []
    for step in range(1, 16):
        to = (seq + step) % 16
        arrivals.append(remote(heads_for(to), grads.at[seq], in_send.at[step], in_recv.at[step], (to, x)))
        arrivals[-1].start()
    own.wait()
    for copy in arrivals:
        copy.wait()

    pad_row = lax.broadcasted_iota(jnp.int32, (64, block), 0) % 32
    prefix_key_stack = stack_heads(prefix_keys[...])
    prefix_value_stack = stack_heads(prefix_values[...])

    def head_rows(at, count):
        there = delta[:, pl.ds(pl.multiple_of(at * block, block), block)]
        return jnp.concatenate(
            [jnp.broadcast_to(there[0:1], (count, block)), jnp.broadcast_to(there[1:2], (count, block))],
            axis=0,
        )

    prefix_grads[...] = jnp.zeros(prefix_grads.shape, F32)

    def prepare(at, carry):
        here = pl.ds(at * block, block)
        grad = grads[pl.ds(2 * at, 2)].reshape(block, LANES).astype(F32) * inverse[here]
        low = grad.astype(BF16)
        grad_low[here] = low
        delta[:, pl.ds(pl.multiple_of(at * block, block), block)] = rows_in_lanes(grad * attended[here])
        queries = arrived[pl.ds(2 * at, 2), 0].reshape(block, LANES)
        weights = jnp.exp(dot_right(prefix_key_stack, queries) * score_scale)
        weights = jnp.where(pad_row < PREFIX, weights, 0.0)
        slopes = (weights * (dot_right(prefix_value_stack, low) - head_rows(at, 32))).astype(BF16)
        prefix_grads[0] += merge_heads(dot_nn(slopes, queries)) * score_scale
        prefix_grads[1] += merge_heads(dot_nn(weights.astype(BF16), low))
        query_grads[here] = dot_left(slopes, prefix_key_stack)
        return carry

    lax.fori_loop(0, 8, prepare, 0)
    away = (
        lax.broadcasted_iota(jnp.int32, (block, block), 0)
        - lax.broadcasted_iota(jnp.int32, (block, block), 1)
    )

    def send_block(part, count, at, send, recv):
        for half in range(2):
            to = 2 * at + half
            source = staged.at[to, pl.ds(part, count)]
            mine = gathered.at[pair, row, pl.ds(part, count)]

            @pl.when(to != seq)
            def _():
                remote(source, mine, send.at[to], recv.at[seq], (to, x)).start()

            @pl.when(to == seq)
            def _():
                pltpu.make_async_copy(source, mine, local_sem.at[1 + part]).start()

    def one_block(step, carry):
        key_at = (step + seq // 2) % 8
        keys = stack_heads(arrived[pl.ds(2 * key_at, 2), 1].reshape(block, LANES))
        values = stack_heads(arrived[pl.ds(2 * key_at, 2), 2].reshape(block, LANES))
        key_docs = docs_column[pl.ds(key_at * block, block)]
        key_docs = jnp.concatenate([key_docs, key_docs], axis=1)
        key_grads[...] = jnp.zeros(key_grads.shape, F32)
        value_grads[...] = jnp.zeros(value_grads.shape, F32)

        def one_tile(at, carry):
            here = pl.ds(at * block, block)
            queries = arrived[pl.ds(2 * at, 2), 0].reshape(block, LANES)
            low = grad_low[here]
            query_docs = docs_row[0:1, pl.ds(pl.multiple_of(at * block, block), block)]
            allowed = (key_docs == query_docs) & (away <= (at - key_at) * block)
            weights = jnp.exp(dot_right(keys, queries) * score_scale).reshape(2, block, block)
            weights = jnp.where(allowed[None], weights, 0.0).reshape(2 * block, block)
            slopes = (weights * (dot_right(values, low) - head_rows(at, block))).astype(BF16)
            key_grads[...] += dot_nn(slopes, queries)
            value_grads[...] += dot_nn(weights.astype(BF16), low)
            query_grads[here] += dot_left(slopes, keys)
            return carry

        lax.fori_loop(key_at, 8, one_tile, 0)
        there = pl.ds(2 * key_at, 2)
        staged[there, 1] = (merge_heads(key_grads[...]) * score_scale).astype(BF16).reshape(2, S_DEV, LANES)
        staged[there, 2] = merge_heads(value_grads[...]).astype(BF16).reshape(2, S_DEV, LANES)
        send_block(1, 2, key_at, out_send, out_recv)
        return carry

    lax.fori_loop(0, 8, one_block, 0)

    def last_block(step, carry):
        at = (step + seq // 2) % 8
        result = (query_grads[pl.ds(at * block, block)] * score_scale).astype(BF16)
        staged[pl.ds(2 * at, 2), 0] = result.reshape(2, S_DEV, LANES)
        send_block(0, 1, at, query_send, query_recv)
        return carry

    lax.fori_loop(0, 8, last_block, 0)
    pltpu.make_async_copy(staged.at[seq, pl.ds(1, 2)], gathered.at[pair, row, pl.ds(1, 2)], local_sem.at[2]).wait()
    pltpu.make_async_copy(staged.at[seq, pl.ds(0, 1)], gathered.at[pair, row, pl.ds(0, 1)], local_sem.at[1]).wait()
    for step in range(1, 16):
        other = (seq + step) % 16
        mine = gathered.at[other // 2, other % 2]
        remote(
            staged.at[other, pl.ds(1, 2)], mine.at[pl.ds(1, 2)], out_send.at[other], out_recv.at[other], (other, x)
        ).wait()
        remote(
            staged.at[other, pl.ds(0, 1)], mine.at[pl.ds(0, 1)], query_send.at[other], query_recv.at[other], (other, x)
        ).wait()


def self_backward(arrived, grad_out, attended, inverse, docs_row, docs_column, prefix_keys, prefix_values):
    length = 16 * S_DEV
    dma = pltpu.SemaphoreType.DMA
    return pl.pallas_call(
        self_backward_kernel,
        out_shape=(
            jax.ShapeDtypeStruct((PAIRS, 2, 3, S_DEV, LANES), BF16),
            jax.ShapeDtypeStruct((2, 32, LANES), F32),
        ),
        in_specs=[whole()] * 8,
        out_specs=(whole(), whole()),
        scratch_shapes=[
            pltpu.VMEM((16, S_DEV, LANES), BF16),
            pltpu.VMEM((length, LANES), BF16),
            pltpu.VMEM((8, length), F32),
            pltpu.VMEM((length, LANES), F32),
            pltpu.VMEM((4 * S_DEV, LANES), F32),
            pltpu.VMEM((4 * S_DEV, LANES), F32),
            pltpu.VMEM((16, 3, S_DEV, LANES), BF16),
            dma((3,)), dma((16,)), dma((16,)), dma((16,)), dma((16,)), dma((16,)), dma((16,)),
        ],
        compiler_params=params(3),
        name="self_backward",
    )(arrived, grad_out, attended, inverse, docs_row, docs_column, prefix_keys, prefix_values)


def cross_backward_kernel(
    queries, keys, values, query_docs, key_docs, prefix_keys, prefix_values, grad_out, crossed, inverse,
    query_grad, key_grad, value_grad, prefix_grads,
):
    row = pl.program_id(1)
    memory_len = keys.shape[0] * keys.shape[2]
    heads = queries[0]
    grad = grad_out[0] * inverse[0]
    low = grad.astype(BF16)
    delta = rows_in_lanes(grad * crossed[0])

    def head_rows(count):
        return jnp.concatenate(
            [jnp.broadcast_to(delta[0:1], (count, S_DEV)), jnp.broadcast_to(delta[1:2], (count, S_DEV))],
            axis=0,
        )

    pad_row = lax.broadcasted_iota(jnp.int32, (64, S_DEV), 0) % 32
    prefix_key_stack = stack_heads(prefix_keys[...])
    weights = jnp.exp(dot_right(prefix_key_stack, heads) * score_scale)
    weights = jnp.where(pad_row < PREFIX, weights, 0.0)
    slopes = (weights * (dot_right(stack_heads(prefix_values[...]), low) - head_rows(32))).astype(BF16)
    from_prefix = dot_left(slopes, prefix_key_stack)
    prefix_key_grad = merge_heads(dot_nn(slopes, heads)) * score_scale
    prefix_value_grad = merge_heads(dot_nn(weights.astype(BF16), low))

    @pl.when(row == 0)
    def _():
        prefix_grads[0] = prefix_key_grad
        prefix_grads[1] = prefix_value_grad

    @pl.when(row > 0)
    def _():
        prefix_grads[0] += prefix_key_grad
        prefix_grads[1] += prefix_value_grad

    key_stack = stack_heads(keys[...].reshape(memory_len, LANES))
    value_stack = stack_heads(values[...].reshape(memory_len, LANES))
    allowed = key_docs[0] == query_docs[0]
    weights = jnp.exp(dot_right(key_stack, heads) * score_scale).reshape(2, memory_len, S_DEV)
    weights = jnp.where(allowed[None], weights, 0.0).reshape(2 * memory_len, S_DEV)
    slopes = (weights * (dot_right(value_stack, low) - head_rows(memory_len))).astype(BF16)
    key_grad[...] = (merge_heads(dot_nn(slopes, heads)) * score_scale).astype(BF16).reshape(key_grad.shape)
    value_grad[...] = merge_heads(dot_nn(weights.astype(BF16), low)).astype(BF16).reshape(value_grad.shape)
    query_grad[0] = ((from_prefix + dot_left(slopes, key_stack)) * score_scale).astype(BF16)


def cross_backward(queries, memory_pairs, query_docs, key_docs, prefix_keys, prefix_values, grad_out, crossed, inverse):
    memory_len = 16 * M_DEV
    head_block = pl.BlockSpec((1, S_DEV, LANES), lambda pair, row: (row, 0, pair))
    keys = pl.BlockSpec((16, 1, M_DEV, LANES), lambda pair, row: (0, row, 0, pair))
    values = pl.BlockSpec((16, 1, M_DEV, LANES), lambda pair, row: (0, row, 0, PAIRS + pair))
    prefix = pl.BlockSpec((32, LANES), lambda pair, row: (0, pair))
    terms = jax.ShapeDtypeStruct((16, 2, M_DEV, D), BF16)
    return pl.pallas_call(
        cross_backward_kernel,
        grid=(PAIRS, 2),
        out_shape=(
            jax.ShapeDtypeStruct((2, S_DEV, D), BF16), terms, terms,
            jax.ShapeDtypeStruct((2, 32, D), F32),
        ),
        in_specs=[
            head_block, keys, values,
            pl.BlockSpec((1, 1, S_DEV), lambda pair, row: (row, 0, 0)),
            pl.BlockSpec((1, memory_len, LANES), lambda pair, row: (row, 0, 0)),
            prefix, prefix, head_block, head_block, head_block,
        ],
        out_specs=(
            head_block, keys, keys, pl.BlockSpec((2, 32, LANES), lambda pair, row: (0, 0, pair)),
        ),
        compiler_params=params(),
        name="cross_backward",
    )(queries, memory_pairs, memory_pairs, query_docs, key_docs, prefix_keys, prefix_values, grad_out, crossed, inverse)


def gelu_parts(pre):
    upper = 0.5 * (1.0 + lax.erf(pre * (0.5 ** 0.5)))
    return upper


def gelu_slope(pre):
    return gelu_parts(pre) + pre * jnp.exp(-0.5 * pre * pre) * (1.0 / math.sqrt(2.0 * math.pi))


def norm_back_rows(resid, gain, upstream):
    middle = jnp.mean(resid, axis=-1, keepdims=True)
    centred = resid - middle
    scale = lax.rsqrt(jnp.mean(centred * centred, axis=-1, keepdims=True) + 1e-05)
    unit = centred * scale
    pulled = upstream * gain
    return scale * (
        pulled - jnp.mean(pulled, axis=-1, keepdims=True) - unit * jnp.mean(pulled * unit, axis=-1, keepdims=True)
    )


def feed_kernel(
    normed, cotangent, gain, inner, outer, mixed,
    layer_out, second_grad, small_grads,
    low, pre, adapter_pre, total, feed_low,
):
    step = pl.program_id(0)
    down = mixed[:, :, :ADAPTER].reshape(D, ADAPTER)
    up_left = mixed[:, :16, ADAPTER:].reshape(ADAPTER, ADAPTER)
    up_right = mixed[:, 16:, ADAPTER:].reshape(ADAPTER, ADAPTER)
    half = ADAPTER

    @pl.when(step == 0)
    def _():
        low[...] = normed[...].astype(BF16)
        adapter_pre[...] = dot_nn(low[...], down)
        act = adapter_pre[...]
        act = (act * gelu_parts(act)).astype(BF16)
        total[:, :half] = normed[:, :half] + 4.0 * dot_nn(act, up_left)
        total[:, half:] = normed[:, half:] + 4.0 * dot_nn(act, up_right)

    @pl.when(step < 4)
    def _():
        hidden = dot_nn(low[...], inner[...].reshape(D, D))
        pre[jnp.minimum(step, 3)] = hidden
        act = (hidden * gelu_parts(hidden)).astype(BF16)
        total[...] += dot_nn(act, outer[...].reshape(D, D))

    @pl.when(step == 3)
    def _():
        resid = total[...]
        layer_out[...] = norm_rows(resid, gain[...]).astype(BF16)
        third_grad = norm_back_rows(resid, gain[...], cotangent[...].astype(F32))
        feed_low[...] = third_grad.astype(BF16)
        adapter_low = (4.0 * third_grad).astype(BF16)
        act = adapter_pre[...]
        upper = gelu_parts(act)
        slope = gelu_slope(act)
        act = (act * upper).astype(BF16)
        grad = dot_right(adapter_low[:, :half], up_left) + dot_right(adapter_low[:, half:], up_right)
        grad = (slope * grad).astype(BF16)
        second_grad[...] = third_grad + dot_right(grad, down)
        small_grads[:, :, :half] = dot_left(low[...], grad).astype(BF16).reshape(32, 32, half)
        small_grads[:, :16, half:] = dot_left(act, adapter_low[:, :half]).astype(BF16).reshape(32, 16, half)
        small_grads[:, 16:, half:] = dot_left(act, adapter_low[:, half:]).astype(BF16).reshape(32, 16, half)

    @pl.when(step >= 4)
    def _():
        hidden = pre[jnp.clip(7 - step, 0, 3)]
        grad = dot_right(feed_low[...], outer[...].reshape(D, D))
        grad = (gelu_slope(hidden) * grad).astype(BF16)
        second_grad[...] += dot_right(grad, inner[...].reshape(D, D))


def feed_forward_backward(normed, cotangent, gain, weights):
    tokens = normed.shape[0]
    at = lambda step: jnp.minimum(step, 7 - step)
    still = lambda step: (0, 0)
    rows = pl.BlockSpec((tokens, D), still)
    return pl.pallas_call(
        feed_kernel,
        grid=(8,),
        out_shape=(
            jax.ShapeDtypeStruct((tokens, D), BF16),
            jax.ShapeDtypeStruct((tokens, D), F32),
            jax.ShapeDtypeStruct((32, 32, D), BF16),
        ),
        in_specs=[
            rows, rows, pl.BlockSpec((1, D), still),
            pl.BlockSpec((32, 32, D), lambda step: (0, INNER_AT // 32 + at(step), 0)),
            pl.BlockSpec((8, 128, D), lambda step: (at(step), OUTER_AT // 128, 0)),
            pl.BlockSpec((32, 32, D), lambda step: (0, MIXED_AT // 32, 0)),
        ],
        out_specs=(rows, rows, pl.BlockSpec((32, 32, D), lambda step: (0, 0, 0))),
        scratch_shapes=[
            pltpu.VMEM((tokens, D), BF16),
            pltpu.VMEM((4, tokens, D), F32),
            pltpu.VMEM((tokens, ADAPTER), F32),
            pltpu.VMEM((tokens, D), F32),
            pltpu.VMEM((tokens, D), BF16),
        ],
        compiler_params=params(),
        name="feed",
    )(normed, cotangent, gain, weights, weights, weights)


def fast_device(
    inputs, memory, out_grad, token_docs, memory_docs, self_project, self_output, cross_query,
    cross_memory, cross_output, inner_weight, outer_weight, adapter_down, adapter_up, norm_gains, prefixes,
):
    seq, x = lax.axis_index("seq"), lax.axis_index("rows")
    tokens = 2 * S_DEV
    mixed = jnp.concatenate(
        [adapter_down, jnp.concatenate([adapter_up[:, :ADAPTER], adapter_up[:, ADAPTER:]], axis=0)], axis=1
    )
    lane_group = lax.broadcasted_iota(jnp.int32, (1, LANES), 1) // 32
    small = jnp.concatenate([
        jnp.pad(prefixes, ((0, 0), (0, 2), (0, 0))).reshape(128, 32), jnp.pad(norm_gains, ((0, 13), (0, 0)))
    ])
    small = jnp.where(lane_group == (seq % 2) * 2 + x, jnp.tile(small, (1, 4)), jnp.zeros((), BF16))
    memory_line = jnp.where(lane_group == seq % 4, jnp.tile(memory_docs, (1, 4)), 0)
    docs = jnp.concatenate([token_docs, memory_line, jnp.zeros((4, LANES), jnp.int32)]).astype(F32)
    (
        full, memory_pairs, small_full, docs_all, docs_row, docs_column, arrived, pair_attended, pair_inverse,
        first_resid, cross_queries, crossed, cross_inverse, second_resid, second_norm,
    ) = first_call(
        inputs, memory.reshape(2, M_DEV, D), small, docs,
        self_project, self_output, cross_query, cross_memory, cross_output, inner_weight, outer_weight, mixed,
    )

    def weight(first):
        return full[:, first:first + 32].reshape(D, D)

    gains = small_full[:, 128:131].transpose(1, 0, 2).reshape(3, D).astype(F32)
    cross_prefixes = small_full[:, 64:128].reshape(8, 2, 32, LANES).transpose(1, 2, 0, 3).reshape(2, 32, D)
    pair_prefixes = lax.dynamic_index_in_dim(small_full, seq // 2, 0, False)[:64].reshape(2, 32, LANES)
    memory_row = docs_all[:, 2:4].reshape(4, 4, 2, LANES).sum(axis=1).transpose(1, 0, 2).reshape(2, 1, 16 * M_DEV)
    memory_column = jnp.broadcast_to(memory_row.reshape(2, -1, 1), (2, 16 * M_DEV, LANES))
    query_row = token_docs.astype(F32).reshape(2, 1, S_DEV)

    layer_out, second_grad, small_grads = feed_forward_backward(
        second_norm, out_grad.reshape(tokens, D), gains[2:3], full
    )
    small_sums = lax.psum_scatter(small_grads.reshape(1024, D), "seq", scatter_dimension=0, tiled=True)

    second_resid_grad = norm_back_rows(second_resid, gains[1], second_grad)
    cross_out_grad = dot_right(second_resid_grad.astype(BF16), weight(CROSS_OUT_AT))
    cross_query_grad, key_terms, value_terms, cross_prefix_grads = cross_backward(
        cross_queries, memory_pairs, query_row, memory_column, cross_prefixes[0], cross_prefixes[1],
        cross_out_grad.reshape(2, S_DEV, D), crossed, cross_inverse,
    )
    memory_terms = dot_right(key_terms.reshape(-1, D), weight(MEM_K_AT)) + dot_right(
        value_terms.reshape(-1, D), weight(MEM_V_AT)
    )
    prefix_flat = cross_prefix_grads[:, :PREFIX].reshape(2 * PREFIX, 16, 64).transpose(1, 0, 2).reshape(16, -1)
    prefix_flat = jnp.pad(prefix_flat, ((0, 0), (0, 8 * D - prefix_flat.shape[1]))).reshape(16, 8, D)
    memory_terms = jnp.concatenate(
        [memory_terms.astype(BF16).reshape(16, 64, D), prefix_flat.astype(BF16)], axis=1
    )
    memory_sums = lax.psum_scatter(memory_terms, "seq", scatter_dimension=0, tiled=False)

    first_grad = second_resid_grad + dot_right(cross_query_grad.reshape(tokens, D), weight(CROSS_Q_AT))
    first_resid_grad = norm_back_rows(first_resid, gains[0], first_grad)
    self_out_grad = dot_right(first_resid_grad.astype(BF16), weight(SELF_OUT_AT))
    project_grads, self_prefix_grads = self_backward(
        arrived, self_out_grad.astype(BF16).reshape(2, S_DEV, D), pair_attended, pair_inverse,
        docs_row, docs_column, pair_prefixes[0], pair_prefixes[1],
    )
    project_grads = project_grads.transpose(2, 1, 3, 0, 4).reshape(3, tokens, D)
    input_grad = first_resid_grad
    for part in range(3):
        input_grad = input_grad + dot_right(project_grads[part], weight(32 * part))

    def swapped(values):
        return lax.ppermute(values, "rows", [(0, 1), (1, 0)])

    halves = small_sums.astype(F32).reshape(2, 32, D)
    give = lax.dynamic_index_in_dim(halves, 1 - x, 0, False)
    keep = lax.dynamic_index_in_dim(halves, x, 0, False)
    prefix_half = memory_sums[64:].astype(F32).reshape(-1)[:60 * 64].reshape(60, 2, 32)
    cross_give = lax.dynamic_index_in_dim(prefix_half, 1 - x, 1, False)
    cross_keep = lax.dynamic_index_in_dim(prefix_half, x, 1, False)
    pair_sum = self_prefix_grads + lax.ppermute(
        self_prefix_grads, "seq", [(at, at ^ 1) for at in range(16)]
    )
    pair_sum = pair_sum[:, :PREFIX].reshape(60, 2, 2, 32)
    pair_sum = lax.dynamic_index_in_dim(pair_sum, seq % 2, 1, False)
    self_give = lax.dynamic_index_in_dim(pair_sum, 1 - x, 1, False)
    self_keep = lax.dynamic_index_in_dim(pair_sum, x, 1, False)
    keep = keep + swapped(give)
    prefix_grad = jnp.concatenate([self_keep, cross_keep], axis=0) + swapped(
        jnp.concatenate([self_give, cross_give], axis=0)
    )
    return (
        layer_out.reshape(2, S_DEV, D),
        input_grad.reshape(2, S_DEV, D),
        memory_sums[:64].astype(F32).reshape(2, M_DEV, D),
        prefix_grad.reshape(4, PREFIX, 32),
        keep[:, :ADAPTER],
        jnp.concatenate([keep[:16, ADAPTER:], keep[16:, ADAPTER:]], axis=1),
    )


def solution(mesh):
    placed = (
        P("rows", "seq", None),
        P("rows", "seq", None),
        P("rows", "seq", None),
        P("rows", "seq"),
        P("rows", "seq"),
        P(("seq", "rows"), None),
        P(("seq", "rows"), None),
        P(("seq", "rows"), None),
        P(("seq", "rows"), None),
        P(("seq", "rows"), None),
        P(("seq", "rows"), None),
        P(("seq", "rows"), None),
        P(("seq", "rows"), None),
        P(("seq", "rows"), None),
        P(None, ("seq", "rows")),
        P(None, None, ("seq", "rows")),
    )
    small_slice = mesh.shape["seq"] == 16 and mesh.shape["rows"] == 2
    return jax.shard_map(
        fast_device if small_slice else per_device,
        mesh=mesh,
        in_specs=placed,
        out_specs=(
            P("rows", "seq", None),
            P("rows", "seq", None),
            P("rows", "seq", None),
            P(None, None, ("seq", "rows")),
            P(("seq", "rows"), None),
            P(("seq", "rows"), None),
        ),
        check_vma=False,
    )
```

```python
import math

import jax
import jax.numpy as jnp
from jax import lax
from jax.experimental import pallas as pl
from jax.experimental.pallas import tpu as pltpu
from jax.sharding import PartitionSpec as P

D = 1024
HEADS = 16
HEAD_DIM = 64
ADAPTER = 512
PREFIX = 30
S_DEV = 128
M_DEV = 32


score_scale = 0.125
masked_score = -1000000000.0


def heads_of(matrix):
    return matrix.reshape(matrix.shape[0], HEADS, HEAD_DIM)


def dot_right(left, right):
    return lax.dot_general(
        left, right, (((1,), (1,)), ((), ())), preferred_element_type=jnp.float32
    )


def dot_left(left, right):
    return lax.dot_general(
        left, right, (((0,), (0,)), ((), ())), preferred_element_type=jnp.float32
    )


def norm_rows(resid, gain):
    middle = jnp.mean(resid, axis=-1, keepdims=True)
    centred = resid - middle
    spread = jnp.mean(centred * centred, axis=-1, keepdims=True)
    return centred * lax.rsqrt(spread + 1e-05) * gain


def norm_back(resid, gain, upstream):
    unused, pullback = jax.vjp(lambda values: norm_rows(values, gain), resid)
    return pullback(upstream)[0]


def gelu_back(pre_act, upstream):
    unused, pullback = jax.vjp(lambda values: jax.nn.gelu(values, approximate=False), pre_act)
    return pullback(upstream)[0]


def allowed_keys(query_docs, key_docs, query_pos, key_pos, causal):
    allowed = query_docs[:, None] == key_docs[None, :]
    if causal:
        allowed = allowed & (key_pos[None, :] <= query_pos[:, None])
    return allowed


def prefix_terms(queries, prefix_keys, prefix_values):
    scores = (
        jnp.einsum(
            "qhd,phd->hqp", queries, heads_of(prefix_keys), preferred_element_type=jnp.float32
        )
        * score_scale
    )
    weights = jnp.exp(scores)
    summed = jnp.einsum(
        "hqp,phd->qhd",
        weights.astype(jnp.bfloat16),
        heads_of(prefix_values),
        preferred_element_type=jnp.float32,
    )
    return (jnp.sum(weights, axis=-1), summed)


def fold_keys(running, arrived, queries, query_docs, key_docs, query_first, causal):
    key_count = arrived.shape[0]
    block_len = math.gcd(key_count, 512)
    query_count = queries.shape[0]
    query_pos = query_first + jnp.arange(query_count, dtype=jnp.int32)
    key_width = arrived.shape[1] // 2

    def fold_one_block(current, element):
        key_block, block_index = element
        key_first = block_index * block_len

        def compute(present):
            block_docs = lax.dynamic_slice_in_dim(key_docs, key_first, block_len, 0)
            allowed = allowed_keys(
                query_docs,
                block_docs,
                query_pos,
                key_first + jnp.arange(block_len, dtype=jnp.int32),
                causal,
            )
            scores = (
                jnp.einsum(
                    "qhd,khd->hqk",
                    queries,
                    heads_of(key_block[:, :key_width]),
                    preferred_element_type=jnp.float32,
                )
                * score_scale
            )
            weights = jnp.exp(jnp.where(allowed[None], scores, masked_score))
            summed = jnp.einsum(
                "hqk,khd->qhd",
                weights.astype(jnp.bfloat16),
                heads_of(key_block[:, key_width:]),
                preferred_element_type=jnp.float32,
            )
            return (present[0] + jnp.sum(weights, axis=-1), present[1] + summed)

        if causal:
            return (
                lax.cond(
                    key_first <= query_first + query_count - 1, compute, lambda held: held, current
                ),
                None,
            )
        return (compute(current), None)

    running, unused = lax.scan(
        fold_one_block,
        running,
        (
            arrived.reshape(key_count // block_len, block_len, arrived.shape[1]),
            jnp.arange(key_count // block_len, dtype=jnp.int32),
        ),
    )
    return running


def attend_back(
    queries,
    gathered,
    prefix_keys,
    prefix_values,
    grad_out,
    attended,
    totals,
    query_docs,
    key_docs,
    query_first,
    causal,
):
    query_count = queries.shape[0]
    key_count = gathered.shape[0]
    key_width = gathered.shape[1] // 2
    block_len = math.gcd(key_count, 512)
    query_pos = query_first + jnp.arange(query_count, dtype=jnp.int32)
    grad_heads = heads_of(grad_out)
    grad_summed = (grad_heads / totals.T[:, :, None]).astype(jnp.bfloat16)
    row_dot = jnp.sum(grad_heads * heads_of(attended), axis=-1).T / totals
    prefix_key_heads = heads_of(prefix_keys)
    prefix_value_heads = heads_of(prefix_values)
    prefix_weights = jnp.exp(
        jnp.einsum("qhd,phd->hqp", queries, prefix_key_heads, preferred_element_type=jnp.float32)
        * score_scale
    )
    prefix_dots = jnp.einsum(
        "qhd,phd->hqp", grad_summed, prefix_value_heads, preferred_element_type=jnp.float32
    )
    prefix_slopes = (prefix_weights * (prefix_dots - row_dot[:, :, None])).astype(jnp.bfloat16)
    query_grad = jnp.einsum(
        "hqp,phd->qhd", prefix_slopes, prefix_key_heads, preferred_element_type=jnp.float32
    )
    key_grad_prefix = (
        jnp.einsum("hqp,qhd->phd", prefix_slopes, queries, preferred_element_type=jnp.float32)
        * score_scale
    ).reshape(-1, D)
    value_grad_prefix = jnp.einsum(
        "hqp,qhd->phd",
        prefix_weights.astype(jnp.bfloat16),
        grad_summed,
        preferred_element_type=jnp.float32,
    ).reshape(-1, D)

    def attend_one_block(current, element):
        key_block, block_index = element
        key_first = block_index * block_len

        def compute(present):
            block_docs = lax.dynamic_slice_in_dim(key_docs, key_first, block_len, 0)
            allowed = allowed_keys(
                query_docs,
                block_docs,
                query_pos,
                key_first + jnp.arange(block_len, dtype=jnp.int32),
                causal,
            )
            key_heads = heads_of(key_block[:, :key_width])
            value_heads = heads_of(key_block[:, key_width:])
            scores = (
                jnp.einsum("qhd,khd->hqk", queries, key_heads, preferred_element_type=jnp.float32)
                * score_scale
            )
            weights = jnp.exp(jnp.where(allowed[None], scores, masked_score))
            dots = jnp.einsum(
                "qhd,khd->hqk", grad_summed, value_heads, preferred_element_type=jnp.float32
            )
            slopes = (weights * (dots - row_dot[:, :, None])).astype(jnp.bfloat16)
            present = present + jnp.einsum(
                "hqk,khd->qhd", slopes, key_heads, preferred_element_type=jnp.float32
            )
            key_grad = (
                jnp.einsum("hqk,qhd->khd", slopes, queries, preferred_element_type=jnp.float32)
                * score_scale
            )
            value_grad = jnp.einsum(
                "hqk,qhd->khd",
                weights.astype(jnp.bfloat16),
                grad_summed,
                preferred_element_type=jnp.float32,
            )
            return (
                present,
                jnp.concatenate(
                    [key_grad.reshape(block_len, D), value_grad.reshape(block_len, D)], axis=1
                ),
            )

        if causal:
            return lax.cond(
                key_first <= query_first + query_count - 1,
                compute,
                lambda held: (held, jnp.zeros((block_len, 2 * D), jnp.float32)),
                current,
            )
        return compute(current)

    query_grad, key_terms = lax.scan(
        attend_one_block,
        query_grad,
        (
            gathered.reshape(key_count // block_len, block_len, gathered.shape[1]),
            jnp.arange(key_count // block_len, dtype=jnp.int32),
        ),
    )
    query_low = (query_grad * score_scale).astype(jnp.bfloat16).reshape(query_count, D)
    key_terms = key_terms.reshape(key_count, 2 * D)
    return (query_low, key_terms, key_grad_prefix, value_grad_prefix, grad_summed, row_dot)


def fetch_all(
    self_project,
    self_output,
    cross_query,
    cross_memory,
    cross_output,
    inner_weight,
    outer_weight,
    adapter_down,
    adapter_up,
    norm_gains,
    prefixes,
):
    return (
        lax.all_gather(self_project, ("seq", "rows"), axis=0, tiled=True),
        lax.all_gather(self_output, ("seq", "rows"), axis=0, tiled=True),
        lax.all_gather(cross_query, ("seq", "rows"), axis=0, tiled=True),
        lax.all_gather(cross_memory, ("seq", "rows"), axis=0, tiled=True),
        lax.all_gather(cross_output, ("seq", "rows"), axis=0, tiled=True),
        lax.all_gather(inner_weight, ("seq", "rows"), axis=0, tiled=True),
        lax.all_gather(outer_weight, ("seq", "rows"), axis=0, tiled=True),
        lax.all_gather(adapter_down, ("seq", "rows"), axis=0, tiled=True),
        lax.all_gather(adapter_up, ("seq", "rows"), axis=0, tiled=True),
        lax.all_gather(norm_gains, ("seq", "rows"), axis=1, tiled=True),
        lax.all_gather(prefixes, ("seq", "rows"), axis=2, tiled=True),
    )


def fetch_again(
    self_project,
    self_output,
    cross_query,
    cross_memory,
    cross_output,
    inner_weight,
    outer_weight,
    adapter_down,
    adapter_up,
    norm_gains,
    prefixes,
):
    return (
        lax.all_gather(self_project, ("seq", "rows"), axis=0, tiled=True),
        lax.all_gather(self_output, ("seq", "rows"), axis=0, tiled=True),
        lax.all_gather(cross_query, ("seq", "rows"), axis=0, tiled=True),
        lax.all_gather(cross_memory, ("seq", "rows"), axis=0, tiled=True),
        lax.all_gather(cross_output, ("seq", "rows"), axis=0, tiled=True),
        lax.all_gather(inner_weight, ("seq", "rows"), axis=0, tiled=True),
        lax.all_gather(outer_weight, ("seq", "rows"), axis=0, tiled=True),
        lax.all_gather(adapter_down, ("seq", "rows"), axis=0, tiled=True),
        lax.all_gather(adapter_up, ("seq", "rows"), axis=0, tiled=True),
        lax.all_gather(norm_gains, ("seq", "rows"), axis=1, tiled=True),
        lax.all_gather(prefixes, ("seq", "rows"), axis=2, tiled=True),
    )


def forward_row(tokens, memory_rows, query_docs, token_docs, memory_docs, query_first, weights):
    (
        self_project,
        self_output,
        cross_query,
        cross_memory,
        cross_output,
        inner_weight,
        outer_weight,
        adapter_down,
        adapter_up,
        norm_gains,
        prefixes,
    ) = weights
    gains = norm_gains.astype(jnp.float32)
    projected = jnp.dot(tokens, self_project, preferred_element_type=jnp.float32).astype(
        jnp.bfloat16
    )
    queries = heads_of(projected[:, :D])
    local_pairs = projected[:, D:]
    start_self = prefix_terms(queries, prefixes[0], prefixes[1])
    totals, summed = fold_keys(
        start_self,
        lax.all_gather(local_pairs, "seq", axis=0, tiled=True),
        queries,
        query_docs,
        token_docs,
        query_first,
        True,
    )
    attended = (summed / totals.T[:, :, None]).reshape(-1, D)
    first_resid = tokens.astype(jnp.float32) + jnp.dot(
        attended.astype(jnp.bfloat16), self_output, preferred_element_type=jnp.float32
    )
    first_norm = norm_rows(first_resid, gains[0])
    first_low = first_norm.astype(jnp.bfloat16)
    cross_queries = heads_of(
        jnp.dot(first_low, cross_query, preferred_element_type=jnp.float32).astype(jnp.bfloat16)
    )
    memory_pairs = jnp.dot(memory_rows, cross_memory, preferred_element_type=jnp.float32).astype(
        jnp.bfloat16
    )
    start_cross = prefix_terms(cross_queries, prefixes[2], prefixes[3])
    cross_totals, cross_summed = fold_keys(
        start_cross,
        lax.all_gather(memory_pairs, "seq", axis=0, tiled=True),
        cross_queries,
        query_docs,
        memory_docs,
        query_first,
        False,
    )
    crossed = (cross_summed / cross_totals.T[:, :, None]).reshape(-1, D)
    second_resid = first_norm + jnp.dot(
        crossed.astype(jnp.bfloat16), cross_output, preferred_element_type=jnp.float32
    )
    second_norm = norm_rows(second_resid, gains[1])
    second_low = second_norm.astype(jnp.bfloat16)
    hidden_pre = jnp.dot(second_low, inner_weight, preferred_element_type=jnp.float32)
    hidden_act = jax.nn.gelu(hidden_pre, approximate=False).astype(jnp.bfloat16)
    adapter_pre = jnp.dot(second_low, adapter_down, preferred_element_type=jnp.float32)
    adapter_act = jax.nn.gelu(adapter_pre, approximate=False).astype(jnp.bfloat16)
    third_resid = (
        second_norm
        + jnp.dot(hidden_act, outer_weight, preferred_element_type=jnp.float32)
        + 4.0 * jnp.dot(adapter_act, adapter_up, preferred_element_type=jnp.float32)
    )
    layer_out = norm_rows(third_resid, gains[2]).astype(jnp.bfloat16)
    saved = (
        queries,
        local_pairs,
        totals,
        attended,
        first_resid,
        cross_queries,
        memory_pairs,
        cross_totals,
        crossed,
        second_resid,
        second_low,
        hidden_pre,
        adapter_pre,
        adapter_act,
        third_resid,
    )
    return (layer_out, saved)


def backward_row(cotangent, saved, weights, query_docs, token_docs, memory_docs, query_first):
    (
        self_project,
        self_output,
        cross_query,
        cross_memory,
        cross_output,
        inner_weight,
        outer_weight,
        adapter_down,
        adapter_up,
        norm_gains,
        prefixes,
    ) = weights
    (
        queries,
        local_pairs,
        totals,
        attended,
        first_resid,
        cross_queries,
        memory_pairs,
        cross_totals,
        crossed,
        second_resid,
        second_low,
        hidden_pre,
        adapter_pre,
        adapter_act,
        third_resid,
    ) = saved
    gains = norm_gains.astype(jnp.float32)
    third_grad = norm_back(third_resid, gains[2], cotangent.astype(jnp.float32))
    feed_low = third_grad.astype(jnp.bfloat16)
    adapter_low = (4.0 * third_grad).astype(jnp.bfloat16)
    hidden_grad = gelu_back(hidden_pre, dot_right(feed_low, outer_weight)).astype(jnp.bfloat16)
    up_grad = dot_left(adapter_act, adapter_low)
    adapter_grad = gelu_back(adapter_pre, dot_right(adapter_low, adapter_up)).astype(jnp.bfloat16)
    down_grad = dot_left(second_low, adapter_grad)
    second_grad = (
        third_grad + dot_right(hidden_grad, inner_weight) + dot_right(adapter_grad, adapter_down)
    )
    second_resid_grad = norm_back(second_resid, gains[1], second_grad)
    self_all, memory_all = (
        lax.all_gather(local_pairs, "seq", axis=0, tiled=True),
        lax.all_gather(memory_pairs, "seq", axis=0, tiled=True),
    )
    cross_out_grad = dot_right(second_resid_grad.astype(jnp.bfloat16), cross_output)
    (
        cross_query_low,
        memory_terms,
        cross_key_prefix,
        cross_value_prefix,
        cross_summed_grad,
        cross_dot,
    ) = attend_back(
        cross_queries,
        memory_all,
        prefixes[2],
        prefixes[3],
        cross_out_grad,
        crossed,
        cross_totals,
        query_docs,
        memory_docs,
        query_first,
        False,
    )
    first_grad = second_resid_grad + dot_right(cross_query_low, cross_query)
    first_resid_grad = norm_back(first_resid, gains[0], first_grad)
    self_out_grad = dot_right(first_resid_grad.astype(jnp.bfloat16), self_output)
    query_low, self_terms, self_key_prefix, self_value_prefix, self_summed_grad, self_dot = (
        attend_back(
            queries,
            self_all,
            prefixes[0],
            prefixes[1],
            self_out_grad,
            attended,
            totals,
            query_docs,
            token_docs,
            query_first,
            True,
        )
    )
    self_sums, memory_sums = (
        lax.psum_scatter(
            self_terms.astype(jnp.bfloat16), "seq", scatter_dimension=0, tiled=True
        ).astype(jnp.float32),
        lax.psum_scatter(
            memory_terms.astype(jnp.bfloat16), "seq", scatter_dimension=0, tiled=True
        ).astype(jnp.float32),
    )
    project_grad = jnp.concatenate([query_low, self_sums.astype(jnp.bfloat16)], axis=1)
    input_grad = first_resid_grad + dot_right(project_grad, self_project)
    memory_grad = dot_right(memory_sums.astype(jnp.bfloat16), cross_memory)
    prefix_grad = jnp.stack(
        [self_key_prefix, self_value_prefix, cross_key_prefix, cross_value_prefix]
    )
    return (input_grad, memory_grad, (down_grad, up_grad, prefix_grad))


def per_device(
    inputs,
    memory,
    out_grad,
    token_docs,
    memory_docs,
    self_project,
    self_output,
    cross_query,
    cross_memory,
    cross_output,
    inner_weight,
    outer_weight,
    adapter_down,
    adapter_up,
    norm_gains,
    prefixes,
):
    docs_full, memory_full = (
        lax.all_gather(token_docs, "seq", axis=1, tiled=True),
        lax.all_gather(memory_docs, "seq", axis=1, tiled=True),
    )
    query_first = lax.axis_index("seq") * inputs.shape[1]
    outputs = []
    input_grads = []
    memory_grads = []
    adjusted_grads = None
    for row_index in range(inputs.shape[0]):
        weights = fetch_all(
            self_project,
            self_output,
            cross_query,
            cross_memory,
            cross_output,
            inner_weight,
            outer_weight,
            adapter_down,
            adapter_up,
            norm_gains,
            prefixes,
        )
        layer_out, saved = forward_row(
            inputs[row_index],
            memory[row_index],
            token_docs[row_index],
            docs_full[row_index],
            memory_full[row_index],
            query_first,
            weights,
        )
        weights_back = fetch_again(
            self_project,
            self_output,
            cross_query,
            cross_memory,
            cross_output,
            inner_weight,
            outer_weight,
            adapter_down,
            adapter_up,
            norm_gains,
            prefixes,
        )
        input_grad, memory_grad, row_grads = backward_row(
            out_grad[row_index],
            saved,
            weights_back,
            token_docs[row_index],
            docs_full[row_index],
            memory_full[row_index],
            query_first,
        )
        shares = (
            lax.psum_scatter(row_grads[0], ("seq", "rows"), scatter_dimension=0, tiled=True),
            lax.psum_scatter(row_grads[1], ("seq", "rows"), scatter_dimension=0, tiled=True),
            lax.psum_scatter(row_grads[2], ("seq", "rows"), scatter_dimension=2, tiled=True),
        )
        if adjusted_grads is None:
            adjusted_grads = shares
        else:
            adjusted_grads = tuple(
                (former + latter for former, latter in zip(adjusted_grads, shares))
            )
        outputs.append(layer_out)
        input_grads.append(input_grad)
        memory_grads.append(memory_grad)
    return (
        jnp.stack(outputs),
        jnp.stack(input_grads),
        jnp.stack(memory_grads),
        adjusted_grads[2],
        adjusted_grads[0],
        adjusted_grads[1],
    )


MESH_ID = pl.DeviceIdType.MESH
F32 = jnp.float32
BF16 = jnp.bfloat16
VMEM_BYTES = 60 * 1024 * 1024
PAIRS = HEADS // 2
LANES = 2 * HEAD_DIM
Q_AT, K_AT, V_AT, SELF_OUT_AT, CROSS_Q_AT, MEM_K_AT, MEM_V_AT, CROSS_OUT_AT = range(0, 256, 32)
INNER_AT, OUTER_AT, MIXED_AT = 256, 384, 512
ALL_ROWS = 544
SMALL_ROWS = 144
PIECE_ROWS = 16
GAP = 2
LEAD = 4
SENDS = 2
Z_LAST = ()
WAIT_TICKS = 4
STEP_TICKS = 2


def whole(space=pltpu.VMEM):
    return pl.BlockSpec(memory_space=space)


def params(collective_id=None):
    if collective_id is None:
        return pltpu.CompilerParams(vmem_limit_bytes=VMEM_BYTES)
    return pltpu.CompilerParams(
        vmem_limit_bytes=VMEM_BYTES, collective_id=collective_id, has_side_effects=True
    )


def remote(src, dst, send_sem, recv_sem, device):
    return pltpu.make_async_remote_copy(
        src_ref=src, dst_ref=dst, send_sem=send_sem, recv_sem=recv_sem,
        device_id=device, device_id_type=MESH_ID,
    )


def greet(peers):
    barrier = pltpu.get_barrier_semaphore()
    for peer in peers:
        pl.semaphore_signal(barrier, inc=1, device_id=peer, device_id_type=MESH_ID)
    pl.semaphore_wait(barrier, len(peers))


def dot_nn(left, right):
    return lax.dot_general(left, right, (((1,), (0,)), ((), ())), preferred_element_type=F32)


class Place:
    def __init__(self):
        self.seq, self.x = lax.axis_index("seq"), lax.axis_index("rows")
        self.z, self.y, self.core = self.seq // 4, (self.seq // 2) % 2, self.seq % 2
        self.pair, self.row = self.seq // 2, self.seq % 2

    def device(self, z, y, core, x):
        return ((z * 2 + y) * 2 + core, x)

    def along_z(self, step):
        return self.device((self.z + step) % 4, self.y, self.core, self.x)

    def along_y(self):
        return self.device(self.z, 1 - self.y, self.core, self.x)

    def along_x(self):
        return self.device(self.z, self.y, self.core, 1 - self.x)

    def other_core(self):
        return self.device(self.z, self.y, 1 - self.core, self.x)

    def diagonal(self):
        return self.device(self.z, self.y, 1 - self.core, 1 - self.x)

    def others(self):
        return [((self.seq + step) % 16, self.x) for step in range(1, 16)]


class Gather:
    def __init__(self, place, full, local_sem, sems, gap):
        self.place, self.full, self.local_sem, self.sems, self.gap = place, full, local_sem, sems, gap
        self.stages = []
        self.waiting = []
        self.tick_at = 0

    def copies(self, level, source, target, device, slot):
        k = len(self.stages)
        return remote(source, target, self.sems[2 * level].at[k, slot], self.sems[2 * level + 1].at[k, slot], device)

    def add(self, source, first, count, piece=PIECE_ROWS):
        for from_row in range(0, count, piece):
            self.add_piece(source.at[pl.ds(from_row, piece)], first + from_row, piece)
        return len(self.stages) - 1

    def add_piece(self, source, first, count):
        at, full = self.place, self.full
        z, y, core, x = at.z, at.y, at.core, at.x
        rows = pl.ds(first, count)
        mine = full.at[z, y, core, x, rows]
        k = len(self.stages)
        if k in Z_LAST:
            plane = full.at[z, :, core, :, rows]
            first_way, then_way = (at.along_x(), at.along_y()) if k % 2 else (at.along_y(), at.along_x())
            line = full.at[z, y, core, :, rows] if k % 2 else full.at[z, :, core, x, rows]
            self.stages.append((
                pltpu.make_async_copy(source, mine, self.local_sem.at[k]),
                [self.copies(0, source, mine, first_way, 0)],
                [self.copies(1, line, line, then_way, 0)],
                [self.copies(2, plane, plane, at.along_z(d + 1), d) for d in range(3)],
                [self.copies(3, full.at[:, :, core, :, rows], full.at[:, :, core, :, rows], at.other_core(), 0)],
            ))
            return
        cut = 2 if k % 3 == 0 else 1
        near, far = pl.ds(0, cut), pl.ds(cut, 4 - cut)
        near1, far1 = full.at[near, y, core, x, rows], full.at[far, y, core, x, rows]
        near2, far2 = full.at[near, y, core, :, rows], full.at[far, :, core, x, rows]
        half = full.at[:, :, core, :, rows]
        self.stages.append((
            pltpu.make_async_copy(source, mine, self.local_sem.at[len(self.stages)]),
            [self.copies(0, source, mine, at.along_z(d + 1), d) for d in range(3)],
            [self.copies(1, near1, near1, at.along_x(), 0), self.copies(1, far1, far1, at.along_y(), 1)],
            [self.copies(2, near2, near2, at.along_y(), 0), self.copies(2, far2, far2, at.along_x(), 1)],
            [self.copies(3, half, half, at.other_core(), 0)],
        ))

    def add_memory(self, source, full):
        for row in range(2):
            self.add_memory_row(source.at[row], full.at[:, :, :, row])
        return len(self.stages) - 1

    def add_memory_row(self, source, full):
        at = self.place
        mine, column, half = full.at[at.z, at.y, at.core], full.at[:, at.y, at.core], full.at[:, :, at.core]
        self.stages.append((
            pltpu.make_async_copy(source, mine, self.local_sem.at[len(self.stages)]),
            [self.copies(0, source, mine, at.along_z(d + 1), d) for d in range(3)],
            [self.copies(1, column, column, at.along_y(), 1)],
            [],
            [self.copies(3, half, half, at.other_core(), 0)],
        ))

    def start(self):
        for stage in self.stages:
            stage[0].start()

    def tick(self, count=1):
        for _ in range(count):
            for level in range(5):
                k = self.tick_at - self.after(level)
                if not 0 <= k < len(self.stages):
                    continue
                if level == 1:
                    self.stages[k][0].wait()
                if level > 0:
                    for copy in self.stages[k][level]:
                        copy.wait_recv()
                if level < 4:
                    for copy in self.stages[k][level + 1]:
                        copy.start()
            self.tick_at += 1
            for _ in range(SENDS):
                if self.waiting:
                    self.waiting.pop(0).start()

    def after(self, level):
        return 0 if level == 0 else LEAD + (level - 1) * self.gap

    def until(self, k):
        while self.tick_at <= k + self.after(4):
            self.tick()

    def finish(self):
        self.until(len(self.stages) - 1)
        for _, *levels in self.stages:
            for level in levels:
                for copy in level:
                    copy.wait_send()


def head_masks():
    lane = lax.broadcasted_iota(jnp.int32, (1, LANES), 1)
    first = (lane < HEAD_DIM).astype(F32).astype(BF16)
    return first, (1.0 - first.astype(F32)).astype(BF16)


def stack_heads(block):
    first, second = head_masks()
    return jnp.concatenate([block * first, block * second], axis=0)


def merge_heads(stacked):
    half = stacked.shape[0] // 2
    lane = lax.broadcasted_iota(jnp.int32, (half, LANES), 1)
    return jnp.where(lane < HEAD_DIM, stacked[:half], stacked[half:])


def rows_in_lanes(values):
    lane = lax.broadcasted_iota(jnp.int32, (8, LANES), 1)
    row = lax.broadcasted_iota(jnp.int32, (8, LANES), 0)
    picks = (lane // HEAD_DIM == row).astype(F32)
    return lax.dot_general(
        picks, values, (((1,), (1,)), ((), ())),
        precision=lax.Precision.HIGHEST, preferred_element_type=F32,
    )


def first_kernel(
    tokens, memory, small, docs,
    project, self_out, cross_q, cross_mem, cross_out, inner, outer, mixed,
    full, memory_full, memory_pairs, small_full, docs_all, docs_row, docs_column, arrived, attended, inverse,
    first_resid, cross_queries, crossed, cross_inverse, second_resid, second_norm,
    gathered, first_norm, weights, staged, quad, memory_held, result_staged, sums, parts,
    local_sem, send0, recv0, send1, recv1, send2, recv2, send3, recv3,
    fetch_sem, own_sem, quad_send, quad_recv, small_send, small_recv, docs_send, docs_recv,
    head_send, head_recv, out_send, out_recv,
):
    place = Place()
    seq, x, pair, row = place.seq, place.x, place.pair, place.row
    others = place.others()
    quad_peers = [place.other_core(), place.along_x(), place.diagonal()]
    greet(others + quad_peers[1:])

    engine = Gather(place, full, local_sem, (send0, recv0, send1, recv1, send2, recv2, send3, recv3), GAP)
    project_done = [
        engine.add(project.at[:, pl.ds(part * D, D)], at, 32) for part, at in enumerate((Q_AT, K_AT, V_AT))
    ]
    engine.add_memory(memory, memory_full)
    for part, at in enumerate((MEM_K_AT, MEM_V_AT)):
        memory_done = engine.add(cross_mem.at[:, pl.ds(part * D, D)], at, 32)
    out_done = engine.add(self_out, SELF_OUT_AT, 32)
    query_done = engine.add(cross_q, CROSS_Q_AT, 32)
    cross_done = engine.add(cross_out, CROSS_OUT_AT, 32)
    for part in range(4):
        engine.add(inner.at[:, pl.ds(part * D, D)], INNER_AT + 32 * part, 32)
    for part in range(4):
        engine.add(outer.at[pl.ds(32 * part, 32)], OUTER_AT + 32 * part, 32)
    engine.add(mixed, MIXED_AT, 32)
    engine.start()
    engine.tick()

    mine = place.core * 2 + x
    quad_copies = [
        remote(small, quad.at[mine], quad_send.at[k], quad_recv.at[k], quad_peers[k]) for k in range(3)
    ]
    own_small = pltpu.make_async_copy(small, quad.at[mine], own_sem.at[0])
    docs_copies = [
        remote(docs, docs_all.at[seq], docs_send.at[k], docs_recv.at[k], others[k]) for k in range(15)
    ]
    own_docs = pltpu.make_async_copy(docs, docs_all.at[seq], own_sem.at[1])
    own_small.start()
    own_docs.start()
    for copy in quad_copies + docs_copies:
        copy.start()
    engine.tick()
    own_small.wait()
    for copy in quad_copies:
        copy.wait()
    small_full[pair] = (quad[0] + quad[1]) + (quad[2] + quad[3])
    small_copies = []
    for k in range(1, 8):
        to = (((pair + k) % 8) * 2 + place.core, x)
        small_copies.append(
            remote(small_full.at[pair], small_full.at[pair], small_send.at[k], small_recv.at[k], to)
        )
        small_copies[-1].start()
    own_docs.wait()
    for copy in docs_copies:
        copy.wait()

    def spread_docs(at, carry):
        tile = docs_all[at]
        line = jnp.where(row == 0, tile[0:1], tile[1:2])
        docs_row[:, pl.ds(pl.multiple_of(at * S_DEV, S_DEV), S_DEV)] = jnp.broadcast_to(line, (8, S_DEV))
        docs_column[pl.ds(at * S_DEV, S_DEV)] = jnp.transpose(jnp.broadcast_to(line, (S_DEV, LANES)))
        return carry

    lax.fori_loop(0, 16, spread_docs, 0)

    rows = tokens[...].reshape(2 * S_DEV, D)
    for part in range(3):
        engine.until(project_done[part])
        fetch = pltpu.make_async_copy(full_rows(full, 32 * part), weights.at[part], fetch_sem.at[part])
        fetch.start()
        fetch.wait()
        result = dot_nn(rows, weights[part].reshape(D, D)).astype(BF16)
        for at_row in range(2):
            for at_pair in range(PAIRS):
                staged[at_pair, at_row, part] = result[
                    at_row * S_DEV:(at_row + 1) * S_DEV, at_pair * LANES:(at_pair + 1) * LANES
                ]
    head_copies = []
    for k in range(15):
        to = (seq + k + 1) % 16
        head_copies.append(
            remote(staged.at[to // 2, to % 2], arrived.at[seq], head_send.at[k], head_recv.at[k], others[k])
        )
    own_heads = pltpu.make_async_copy(staged.at[pair, row], arrived.at[seq], own_sem.at[2])
    own_heads.start()
    engine.waiting = list(head_copies)

    engine.until(memory_done)
    fetch_memory = pltpu.make_async_copy(memory_full, memory_held, own_sem.at[3])
    fetch_memory.start()
    fetches = [
        pltpu.make_async_copy(full_rows(full, at), weights.at[part], fetch_sem.at[part])
        for part, at in enumerate((MEM_K_AT, MEM_V_AT))
    ]
    for fetch in fetches:
        fetch.start()
    fetch_memory.wait()
    for part in range(2):
        fetches[part].wait()

        def project_memory(at, carry):
            held = memory_held[at].reshape(4 * 2 * M_DEV, D)
            result = dot_nn(held, weights[part].reshape(D, D)).astype(BF16)
            memory_pairs[pl.ds(4 * at, 4), :, :, pl.ds(part * D, D)] = result.reshape(4, 2, M_DEV, D)
            return carry

        lax.fori_loop(0, 4, project_memory, 0)
    engine.tick(max(WAIT_TICKS, -(-len(engine.waiting) // SENDS)))
    own_heads.wait()
    for copy in head_copies:
        copy.wait()

    block = 2 * S_DEV
    columns = pl.ds(pl.multiple_of(pair * LANES, LANES), LANES)
    target = gathered.at[row, :, columns]
    away = (
        lax.broadcasted_iota(jnp.int32, (block, block), 1)
        - lax.broadcasted_iota(jnp.int32, (block, block), 0)
    )
    prefix_lane = lax.broadcasted_iota(jnp.int32, (2 * block, 32), 1)
    prefix_keys, prefix_values = small_full[pair, 0:32], small_full[pair, 32:64]

    for step in range(8):
        at = (step + pair) % 8
        queries = stack_heads(arrived[pl.ds(2 * at, 2), 0].reshape(block, LANES))
        query_docs = docs_column[pl.ds(at * block, block)]
        scores = dot_right(queries, prefix_keys) * score_scale
        e = jnp.where(prefix_lane < PREFIX, jnp.exp(scores), 0.0)
        sums[...] = jnp.concatenate([e, jnp.zeros((2 * block, LANES - 32), F32)], axis=1)
        parts[...] = dot_nn(e.astype(BF16), prefix_values)

        def one_tile(key_at, carry):
            keys = arrived[pl.ds(2 * key_at, 2), 1].reshape(block, LANES)
            values = arrived[pl.ds(2 * key_at, 2), 2].reshape(block, LANES)
            key_docs = docs_row[0:1, pl.ds(pl.multiple_of(key_at * block, block), block)]
            same = jnp.concatenate([query_docs, query_docs], axis=1) == key_docs
            allowed = same & (away <= (at - key_at) * block)
            scores = dot_right(queries, keys) * score_scale
            e = jnp.where(allowed[None], jnp.exp(scores).reshape(2, block, block), 0.0)
            e = e.reshape(2 * block, block)
            sums[...] += e[:, :LANES] + e[:, LANES:]
            parts[...] += dot_nn(e.astype(BF16), values)
            return carry

        lax.fori_loop(0, at + 1, one_tile, 0)
        totals = 1.0 / jnp.sum(sums[...], axis=1, keepdims=True)
        result = merge_heads(parts[...] * totals)
        here = pl.ds(at * block, block)
        attended[here] = result
        inverse[here] = merge_heads(jnp.broadcast_to(totals, (2 * block, LANES)))
        result_staged[pl.ds(2 * at, 2)] = result.astype(BF16).reshape(2, S_DEV, LANES)
        for half in range(2):
            to = 2 * at + half

            @pl.when(to != seq)
            def _():
                remote(result_staged.at[to], target, out_send.at[to], out_recv.at[seq], (to, x)).start()

            @pl.when(to == seq)
            def _():
                pltpu.make_async_copy(result_staged.at[to], target, own_sem.at[4]).start()

        engine.tick(STEP_TICKS)

    for copy in small_copies:
        copy.wait()
    engine.until(cross_done)
    fetches = [
        pltpu.make_async_copy(full_rows(full, at), weights.at[part], fetch_sem.at[part])
        for part, at in enumerate((SELF_OUT_AT, CROSS_Q_AT, CROSS_OUT_AT))
    ]
    for fetch in fetches:
        fetch.start()
    gains = [
        jnp.concatenate(
            [small_full[at_pair, 128:144].astype(F32)[part:part + 1] for at_pair in range(PAIRS)], axis=1
        )
        for part in range(2)
    ]
    pltpu.make_async_copy(result_staged.at[seq], target, own_sem.at[4]).wait()
    for other, _ in others:
        remote(result_staged.at[other], target, out_send.at[other], out_recv.at[other], (other, x)).wait()
    fetches[0].wait()
    resid = tokens[...].reshape(2 * S_DEV, D).astype(F32) + dot_nn(
        gathered[...].reshape(2 * S_DEV, D), weights[0].reshape(D, D)
    )
    first_resid[...] = resid
    normed = norm_rows(resid, gains[0])
    first_norm[...] = normed
    engine.tick(STEP_TICKS)
    fetches[1].wait()
    cross_queries[...] = dot_nn(normed.astype(BF16), weights[1].reshape(D, D)).astype(BF16).reshape(2, S_DEV, D)
    engine.tick(STEP_TICKS)
    memory_len = 16 * M_DEV
    cross_prefix_lane = lax.broadcasted_iota(jnp.int32, (2 * S_DEV, 32), 1)
    for at_row in range(2):
        own = jnp.transpose(jnp.broadcast_to(docs[at_row:at_row + 1], (LANES, S_DEV)))
        own = jnp.concatenate([own] * (memory_len // LANES), axis=1)
        lines = [
            sum(docs_all[4 * at + k, 2 + at_row:3 + at_row] for k in range(4)) for at in range(4)
        ]
        allowed = own == jnp.concatenate(lines, axis=1)

        def one_pair(at_pair, carry):
            first = pl.multiple_of(at_pair * LANES, LANES)
            columns, value_columns = pl.ds(first, LANES), pl.ds(pl.multiple_of(first + D, LANES), LANES)
            stacked = stack_heads(cross_queries[at_row, :, columns])
            keys = memory_pairs[:, at_row, :, columns].reshape(memory_len, LANES)
            values = memory_pairs[:, at_row, :, value_columns].reshape(memory_len, LANES)
            scores = dot_right(stacked, small_full[at_pair, 64:96]) * score_scale
            prefix_e = jnp.where(cross_prefix_lane < PREFIX, jnp.exp(scores), 0.0)
            scores = dot_right(stacked, keys) * score_scale
            e = jnp.where(allowed[None], jnp.exp(scores).reshape(2, S_DEV, memory_len), 0.0)
            e = e.reshape(2 * S_DEV, memory_len)
            totals = jnp.sum(e, axis=1, keepdims=True) + jnp.sum(prefix_e, axis=1, keepdims=True)
            totals = 1.0 / totals
            summed = dot_nn(e.astype(BF16), values) + dot_nn(prefix_e.astype(BF16), small_full[at_pair, 96:128])
            crossed[at_row, :, columns] = merge_heads(summed * totals)
            cross_inverse[at_row, :, columns] = merge_heads(jnp.broadcast_to(totals, (2 * S_DEV, LANES)))
            return carry

        lax.fori_loop(0, PAIRS // 2, one_pair, 0)
        engine.tick(STEP_TICKS)
        lax.fori_loop(PAIRS // 2, PAIRS, one_pair, 0)
        engine.tick(STEP_TICKS)
    fetches[2].wait()
    resid = first_norm[...] + dot_nn(
        crossed[...].reshape(2 * S_DEV, D).astype(BF16), weights[2].reshape(D, D)
    )
    second_resid[...] = resid
    second_norm[...] = norm_rows(resid, gains[1])
    engine.finish()


def full_rows(full, first):
    return full.at[:, :, :, :, pl.ds(first, 32)]


def first_call(tokens, memory, small, docs, *weights):
    length = 16 * S_DEV
    chunks = 16 * 32 // PIECE_ROWS + 32 // PIECE_ROWS + 2
    dma = pltpu.SemaphoreType.DMA
    shape = jax.ShapeDtypeStruct
    outs = pl.pallas_call(
        first_kernel,
        out_shape=(
            shape((4, 2, 2, 2, ALL_ROWS, D), BF16),
            shape((4, 2, 2, 2, M_DEV, D), BF16),
            shape((16, 2, M_DEV, 2 * D), BF16),
            shape((8, SMALL_ROWS, LANES), BF16),
            shape((16, 8, LANES), F32),
            shape((8, length), F32),
            shape((length, LANES), F32),
            shape((16, 3, S_DEV, LANES), BF16),
            shape((length, LANES), F32),
            shape((length, LANES), F32),
            shape((2 * S_DEV, D), F32),
            shape((2, S_DEV, D), BF16),
            shape((2, S_DEV, D), F32),
            shape((2, S_DEV, D), F32),
            shape((2 * S_DEV, D), F32),
            shape((2 * S_DEV, D), F32),
        ),
        in_specs=[whole(), whole(pl.ANY), whole(), whole()] + [whole(pl.ANY)] * 8,
        out_specs=(whole(pl.ANY), whole(pl.ANY)) + (whole(),) * 14,
        scratch_shapes=[
            pltpu.VMEM((2, S_DEV, D), BF16),
            pltpu.VMEM((2 * S_DEV, D), F32),
            pltpu.VMEM((3, 4, 2, 2, 2, 32, D), BF16),
            pltpu.VMEM((PAIRS, 2, 3, S_DEV, LANES), BF16),
            pltpu.VMEM((4, SMALL_ROWS, LANES), BF16),
            pltpu.VMEM((4, 2, 2, 2, M_DEV, D), BF16),
            pltpu.VMEM((16, S_DEV, LANES), BF16),
            pltpu.VMEM((4 * S_DEV, LANES), F32),
            pltpu.VMEM((4 * S_DEV, LANES), F32),
            dma((chunks,)),
            dma((chunks, 3)), dma((chunks, 3)), dma((chunks, 2)), dma((chunks, 2)),
            dma((chunks, 3)), dma((chunks, 3)), dma((chunks, 1)), dma((chunks, 1)),
            dma((3,)), dma((5,)), dma((3,)), dma((3,)), dma((8,)), dma((8,)), dma((15,)), dma((15,)),
            dma((15,)), dma((15,)), dma((16,)), dma((16,)),
        ],
        compiler_params=params(0),
        name="first",
    )(tokens, memory, small, docs, *weights)
    return (outs[0].reshape(32, ALL_ROWS, D),) + tuple(outs[2:])


def second_kernel(
    second_grad, second_resid, small_full, docs, docs_all, docs_row, crossed, cross_inverse, cross_queries,
    full, memory_pairs_far, first_resid_far, arrived_far, attended_far, inverse_far, docs_column_far, small_grads,
    input_grad, memory_grad, down_grad, up_grad, prefix_sum,
    weights, memory_pairs, first_resid, arrived, attended, inverse, docs_column,
    pull, cross_grad, cross_query_grad, key_terms, value_terms, cross_prefix,
    small_core, small_mine, small_x, small_pair, small_all,
    memory_part, memory_core, memory_mine, memory_all, prefix_all, prefix_mine, prefix_quad,
    heads_out, grads, grad_low, delta, query_grads, key_grads, value_grads, staged, gathered,
    fetch_sem, own_sem, near_send, near_recv, small_send, small_recv, memory_send, memory_recv,
    prefix_send, prefix_recv, quad_send, quad_recv,
    in_send, in_recv, out_send, out_recv, query_send, query_recv,
):
    place = Place()
    seq, x, pair, row, core = place.seq, place.x, place.pair, place.row, place.core
    z, y = place.z, place.y
    others = place.others()
    tokens = 2 * S_DEV
    memory_len = 16 * M_DEV
    block = 2 * S_DEV

    fetches = {}

    def fetch(name, source, target):
        fetches[name] = pltpu.make_async_copy(source, target, fetch_sem.at[len(fetches)])
        fetches[name].start()

    firsts = (CROSS_OUT_AT, CROSS_Q_AT, SELF_OUT_AT, MEM_K_AT, MEM_V_AT, Q_AT, K_AT, V_AT)

    def fetch_weight(at):
        fetch(at, full.at[:, pl.ds(at, 32)], weights.at[firsts.index(at)])

    def weight(at):
        return weights[firsts.index(at)].reshape(D, D)

    fetch_weight(CROSS_OUT_AT)
    fetch("pairs", memory_pairs_far, memory_pairs)
    fetch_weight(CROSS_Q_AT)
    fetch("resid", first_resid_far, first_resid)
    fetch_weight(SELF_OUT_AT)
    fetch_weight(MEM_K_AT)
    fetch_weight(MEM_V_AT)
    fetch("arrived", arrived_far, arrived)
    fetch("attended", attended_far, attended)
    fetch("inverse", inverse_far, inverse)
    fetch("docs", docs_column_far, docs_column)
    for at in (K_AT, V_AT, Q_AT):
        fetch_weight(at)
    greet(others + [place.along_x(), place.diagonal()])

    small_first = remote(
        small_grads.at[:, :, 1 - core], small_core, near_send.at[0], near_recv.at[0], place.other_core()
    )
    small_own = pltpu.make_async_copy(small_grads.at[:, :, core], small_mine, own_sem.at[0])
    small_second = remote(small_mine.at[:, :, 1 - x], small_x, near_send.at[1], near_recv.at[1], place.along_x())
    plane = z * 2 + y

    def chips(source, target, sends, recvs):
        copies = []
        for k in range(1, 8):
            to = (plane + k) % 8
            copies.append(
                remote(source.at[to // 2, to % 2], target.at[plane], sends.at[k], recvs.at[k], (to * 2 + core, x))
            )
        return copies

    small_third = chips(small_pair, small_all, small_send, small_recv)
    memory_first = remote(
        memory_part.at[:, :, 1 - core], memory_core, near_send.at[2], near_recv.at[2], place.other_core()
    )
    memory_second = chips(memory_mine, memory_all, memory_send, memory_recv)
    small_first.start()
    small_own.start()

    gains = [
        jnp.concatenate(
            [small_full[at_pair, 128:144].astype(F32)[part:part + 1] for at_pair in range(PAIRS)], axis=1
        )
        for part in range(2)
    ]
    pulled = norm_back_rows(second_resid[...], gains[1], second_grad[...])
    pull[...] = pulled
    fetches[CROSS_OUT_AT].wait()
    cross_grad[...] = dot_right(pulled.astype(BF16), weight(CROSS_OUT_AT)).reshape(2, S_DEV, D)
    fetches["pairs"].wait()

    cross_pad = lax.broadcasted_iota(jnp.int32, (64, S_DEV), 0) % 32
    for at_row in range(2):
        lines = [sum(docs_all[4 * at + k, 2 + at_row:3 + at_row] for k in range(4)) for at in range(4)]
        key_docs = jnp.concatenate(
            [jnp.transpose(jnp.broadcast_to(line, (S_DEV, LANES))) for line in lines], axis=0
        )
        allowed = key_docs == docs[at_row:at_row + 1]

        def one_pair(at_pair, carry):
            first = pl.multiple_of(at_pair * LANES, LANES)
            columns, value_columns = pl.ds(first, LANES), pl.ds(pl.multiple_of(first + D, LANES), LANES)
            heads = cross_queries[at_row, :, columns]
            grad = cross_grad[at_row, :, columns] * cross_inverse[at_row, :, columns]
            low = grad.astype(BF16)
            lines = rows_in_lanes(grad * crossed[at_row, :, columns])

            def head_rows(count):
                return jnp.concatenate(
                    [jnp.broadcast_to(lines[0:1], (count, S_DEV)), jnp.broadcast_to(lines[1:2], (count, S_DEV))],
                    axis=0,
                )

            prefix_key_stack = stack_heads(small_full[at_pair, 64:96])
            prefix_value_stack = stack_heads(small_full[at_pair, 96:128])
            e = jnp.exp(dot_right(prefix_key_stack, heads) * score_scale)
            e = jnp.where(cross_pad < PREFIX, e, 0.0)
            slopes = (e * (dot_right(prefix_value_stack, low) - head_rows(32))).astype(BF16)
            from_prefix = dot_left(slopes, prefix_key_stack)
            key_grad = merge_heads(dot_nn(slopes, heads)) * score_scale
            value_grad = merge_heads(dot_nn(e.astype(BF16), low))
            if at_row == 0:
                cross_prefix[at_pair, 0] = key_grad
                cross_prefix[at_pair, 1] = value_grad
            else:
                cross_prefix[at_pair, 0] += key_grad
                cross_prefix[at_pair, 1] += value_grad
            key_stack = stack_heads(memory_pairs[:, at_row, :, columns].reshape(memory_len, LANES))
            value_stack = stack_heads(memory_pairs[:, at_row, :, value_columns].reshape(memory_len, LANES))
            e = jnp.exp(dot_right(key_stack, heads) * score_scale).reshape(2, memory_len, S_DEV)
            e = jnp.where(allowed[None], e, 0.0).reshape(2 * memory_len, S_DEV)
            slopes = (e * (dot_right(value_stack, low) - head_rows(memory_len))).astype(BF16)
            terms = merge_heads(dot_nn(slopes, heads)) * score_scale
            key_terms[:, at_row, :, columns] = terms.astype(BF16).reshape(16, M_DEV, LANES)
            terms = merge_heads(dot_nn(e.astype(BF16), low))
            value_terms[:, at_row, :, columns] = terms.astype(BF16).reshape(16, M_DEV, LANES)
            query_grad = (from_prefix + dot_left(slopes, key_stack)) * score_scale
            cross_query_grad[at_row, :, columns] = query_grad.astype(BF16)
            return carry

        lax.fori_loop(0, PAIRS, one_pair, 0)
        if at_row == 0:
            small_own.wait()
            small_first.wait_recv()
            small_mine[...] = small_mine[...] + small_core[...]
            small_second.start()
    small_second.wait()
    small_pair[...] = small_mine[:, :, x] + small_x[...]
    for copy in small_third:
        copy.start()
    small_all[plane] = small_pair[z, y]

    prefix_copies = []
    for k in range(1, 8):
        to = (pair + k) % 8
        prefix_copies.append(
            remote(cross_prefix.at[to], prefix_all.at[pair], prefix_send.at[k], prefix_recv.at[k], (to * 2 + core, x))
        )
        prefix_copies[-1].start()
    prefix_all[pair] = cross_prefix[pair]

    fetches[CROSS_Q_AT].wait()
    fetches["resid"].wait()
    first_grad = pull[...] + dot_right(cross_query_grad[...].reshape(tokens, D), weight(CROSS_Q_AT))
    resid_grad = norm_back_rows(first_resid[...], gains[0], first_grad)
    pull[...] = resid_grad
    fetches[SELF_OUT_AT].wait()
    out_grad = dot_right(resid_grad.astype(BF16), weight(SELF_OUT_AT)).astype(BF16)
    for at_pair in range(PAIRS):
        for at_row in range(2):
            heads_out[at_pair, at_row] = out_grad[
                at_row * S_DEV:(at_row + 1) * S_DEV, at_pair * LANES:(at_pair + 1) * LANES
            ]
    arrivals = []
    for k in range(15):
        to = (seq + k + 1) % 16
        arrivals.append(remote(heads_out.at[to // 2, to % 2], grads.at[seq], in_send.at[k], in_recv.at[k], others[k]))
        arrivals[-1].start()
    own_heads = pltpu.make_async_copy(heads_out.at[pair, row], grads.at[seq], own_sem.at[1])
    own_heads.start()

    fetches[MEM_K_AT].wait()
    fetches[MEM_V_AT].wait()

    def memory_block(at, carry):
        there = pl.ds(4 * at, 4)
        terms = dot_right(key_terms[there].reshape(8 * M_DEV, D), weight(MEM_K_AT))
        terms += dot_right(value_terms[there].reshape(8 * M_DEV, D), weight(MEM_V_AT))
        memory_part[at] = terms.astype(BF16).reshape(2, 2, 2 * M_DEV, D)
        return carry

    lax.fori_loop(0, 4, memory_block, 0)
    memory_first.start()
    for copy in small_third:
        copy.wait()
    total = small_all[0].astype(F32)
    for k in range(1, 8):
        total += small_all[k].astype(F32)
    down_grad[...] = total[:, :ADAPTER]
    up_grad[:, :ADAPTER] = total[:16, ADAPTER:]
    up_grad[:, ADAPTER:] = total[16:, ADAPTER:]
    for name in ("arrived", "attended", "inverse", "docs"):
        fetches[name].wait()
    own_heads.wait()
    for copy in arrivals:
        copy.wait()

    pad_row = lax.broadcasted_iota(jnp.int32, (64, block), 0) % 32
    prefix_key_stack = stack_heads(small_full[pair, 0:32])
    prefix_value_stack = stack_heads(small_full[pair, 32:64])

    def head_rows(at, count):
        there = delta[:, pl.ds(pl.multiple_of(at * block, block), block)]
        return jnp.concatenate(
            [jnp.broadcast_to(there[0:1], (count, block)), jnp.broadcast_to(there[1:2], (count, block))],
            axis=0,
        )

    prefix_mine[...] = jnp.zeros(prefix_mine.shape, F32)

    def prepare(at, carry):
        here = pl.ds(at * block, block)
        grad = grads[pl.ds(2 * at, 2)].reshape(block, LANES).astype(F32) * inverse[here]
        low = grad.astype(BF16)
        grad_low[here] = low
        delta[:, pl.ds(pl.multiple_of(at * block, block), block)] = rows_in_lanes(grad * attended[here])
        queries = arrived[pl.ds(2 * at, 2), 0].reshape(block, LANES)
        e = jnp.exp(dot_right(prefix_key_stack, queries) * score_scale)
        e = jnp.where(pad_row < PREFIX, e, 0.0)
        slopes = (e * (dot_right(prefix_value_stack, low) - head_rows(at, 32))).astype(BF16)
        prefix_mine[0] += merge_heads(dot_nn(slopes, queries)) * score_scale
        prefix_mine[1] += merge_heads(dot_nn(e.astype(BF16), low))
        query_grads[here] = dot_left(slopes, prefix_key_stack)
        return carry

    lax.fori_loop(0, 8, prepare, 0)
    memory_first.wait()
    memory_mine[...] = memory_part[:, :, core] + memory_core[...]
    for copy in memory_second:
        copy.start()
    memory_all[plane] = memory_mine[z, y]
    for copy in prefix_copies:
        copy.wait()
    for part in range(2):
        prefix_mine[2 + part] = sum(prefix_all[k, part] for k in range(8))
    prefix_quad[core * 2 + x] = prefix_mine[...]
    quad_copies = [
        remote(prefix_mine, prefix_quad.at[core * 2 + x], quad_send.at[k], quad_recv.at[k], peer)
        for k, peer in enumerate((place.other_core(), place.along_x(), place.diagonal()))
    ]
    for copy in quad_copies:
        copy.start()

    away = (
        lax.broadcasted_iota(jnp.int32, (block, block), 0)
        - lax.broadcasted_iota(jnp.int32, (block, block), 1)
    )

    def send_block(part, count, at, send, recv):
        for half in range(2):
            to = 2 * at + half
            source = staged.at[to, pl.ds(part, count)]
            mine = gathered.at[pair, row, pl.ds(part, count)]

            @pl.when(to != seq)
            def _():
                remote(source, mine, send.at[to], recv.at[seq], (to, x)).start()

            @pl.when(to == seq)
            def _():
                pltpu.make_async_copy(source, mine, own_sem.at[2 + part]).start()

    def one_block(step, carry):
        key_at = (step + pair) % 8
        keys = stack_heads(arrived[pl.ds(2 * key_at, 2), 1].reshape(block, LANES))
        values = stack_heads(arrived[pl.ds(2 * key_at, 2), 2].reshape(block, LANES))
        key_docs = docs_column[pl.ds(key_at * block, block)]
        key_docs = jnp.concatenate([key_docs, key_docs], axis=1)
        key_grads[...] = jnp.zeros(key_grads.shape, F32)
        value_grads[...] = jnp.zeros(value_grads.shape, F32)

        def one_tile(at, carry):
            here = pl.ds(at * block, block)
            queries = arrived[pl.ds(2 * at, 2), 0].reshape(block, LANES)
            low = grad_low[here]
            query_docs = docs_row[0:1, pl.ds(pl.multiple_of(at * block, block), block)]
            allowed = (key_docs == query_docs) & (away <= (at - key_at) * block)
            e = jnp.exp(dot_right(keys, queries) * score_scale).reshape(2, block, block)
            e = jnp.where(allowed[None], e, 0.0).reshape(2 * block, block)
            slopes = (e * (dot_right(values, low) - head_rows(at, block))).astype(BF16)
            key_grads[...] += dot_nn(slopes, queries)
            value_grads[...] += dot_nn(e.astype(BF16), low)
            query_grads[here] += dot_left(slopes, keys)
            return carry

        lax.fori_loop(key_at, 8, one_tile, 0)
        there = pl.ds(2 * key_at, 2)
        staged[there, 1] = (merge_heads(key_grads[...]) * score_scale).astype(BF16).reshape(2, S_DEV, LANES)
        staged[there, 2] = merge_heads(value_grads[...]).astype(BF16).reshape(2, S_DEV, LANES)
        send_block(1, 2, key_at, out_send, out_recv)
        return carry

    lax.fori_loop(0, 8, one_block, 0)

    def last_block(step, carry):
        at = (step + pair) % 8
        result = (query_grads[pl.ds(at * block, block)] * score_scale).astype(BF16)
        staged[pl.ds(2 * at, 2), 0] = result.reshape(2, S_DEV, LANES)
        send_block(0, 1, at, query_send, query_recv)
        return carry

    lax.fori_loop(0, 8, last_block, 0)
    small_first.wait_send()
    for copy in memory_second:
        copy.wait()
    total = memory_all[0].astype(F32)
    for k in range(1, 8):
        total += memory_all[k].astype(F32)
    memory_grad[...] = total
    for copy in quad_copies:
        copy.wait()
    prefix_sum[...] = (prefix_quad[0] + prefix_quad[1]) + (prefix_quad[2] + prefix_quad[3])

    pltpu.make_async_copy(staged.at[seq, pl.ds(1, 2)], gathered.at[pair, row, pl.ds(1, 2)], own_sem.at[3]).wait()
    for other, _ in others:
        remote(
            staged.at[other, pl.ds(1, 2)], gathered.at[other // 2, other % 2, pl.ds(1, 2)],
            out_send.at[other], out_recv.at[other], (other, x),
        ).wait()

    def part_grad(part, at):
        fetches[at].wait()
        joined = jnp.concatenate([gathered[k, :, part].reshape(tokens, LANES) for k in range(PAIRS)], axis=1)
        return dot_right(joined, weight(at))

    input_grad[...] = pull[...] + part_grad(1, K_AT) + part_grad(2, V_AT)
    pltpu.make_async_copy(staged.at[seq, pl.ds(0, 1)], gathered.at[pair, row, pl.ds(0, 1)], own_sem.at[2]).wait()
    for other, _ in others:
        remote(
            staged.at[other, pl.ds(0, 1)], gathered.at[other // 2, other % 2, pl.ds(0, 1)],
            query_send.at[other], query_recv.at[other], (other, x),
        ).wait()
    input_grad[...] += part_grad(0, Q_AT)


def second_call(*operands):
    length = 16 * S_DEV
    tokens = 2 * S_DEV
    dma = pltpu.SemaphoreType.DMA
    shape = jax.ShapeDtypeStruct
    return pl.pallas_call(
        second_kernel,
        out_shape=(
            shape((tokens, D), F32),
            shape((2 * M_DEV, D), F32),
            shape((32, ADAPTER), F32),
            shape((16, D), F32),
            shape((4, 32, LANES), F32),
        ),
        in_specs=[whole()] * 9 + [whole(pl.ANY)] * 8,
        out_specs=(whole(),) * 5,
        scratch_shapes=[
            pltpu.VMEM((8, 32, 32, D), BF16),
            pltpu.VMEM((16, 2, M_DEV, 2 * D), BF16),
            pltpu.VMEM((tokens, D), F32),
            pltpu.VMEM((16, 3, S_DEV, LANES), BF16),
            pltpu.VMEM((length, LANES), F32),
            pltpu.VMEM((length, LANES), F32),
            pltpu.VMEM((length, LANES), F32),
            pltpu.VMEM((tokens, D), F32),
            pltpu.VMEM((2, S_DEV, D), F32),
            pltpu.VMEM((2, S_DEV, D), BF16),
            pltpu.VMEM((16, 2, M_DEV, D), BF16),
            pltpu.VMEM((16, 2, M_DEV, D), BF16),
            pltpu.VMEM((PAIRS, 2, 32, LANES), F32),
            pltpu.VMEM((4, 2, 2, 32, D), BF16),
            pltpu.VMEM((4, 2, 2, 32, D), BF16),
            pltpu.VMEM((4, 2, 32, D), BF16),
            pltpu.VMEM((4, 2, 32, D), BF16),
            pltpu.VMEM((8, 32, D), BF16),
            pltpu.VMEM((4, 2, 2, 2 * M_DEV, D), BF16),
            pltpu.VMEM((4, 2, 2 * M_DEV, D), BF16),
            pltpu.VMEM((4, 2, 2 * M_DEV, D), BF16),
            pltpu.VMEM((8, 2 * M_DEV, D), BF16),
            pltpu.VMEM((8, 2, 32, LANES), F32),
            pltpu.VMEM((4, 32, LANES), F32),
            pltpu.VMEM((4, 4, 32, LANES), F32),
            pltpu.VMEM((PAIRS, 2, S_DEV, LANES), BF16),
            pltpu.VMEM((16, S_DEV, LANES), BF16),
            pltpu.VMEM((length, LANES), BF16),
            pltpu.VMEM((8, length), F32),
            pltpu.VMEM((length, LANES), F32),
            pltpu.VMEM((4 * S_DEV, LANES), F32),
            pltpu.VMEM((4 * S_DEV, LANES), F32),
            pltpu.VMEM((16, 3, S_DEV, LANES), BF16),
            pltpu.VMEM((PAIRS, 2, 3, S_DEV, LANES), BF16),
            dma((14,)), dma((4,)), dma((3,)), dma((3,)), dma((8,)), dma((8,)), dma((8,)), dma((8,)),
            dma((8,)), dma((8,)), dma((3,)), dma((3,)),
            dma((15,)), dma((15,)), dma((16,)), dma((16,)), dma((16,)), dma((16,)),
        ],
        compiler_params=params(1),
        name="second",
    )(*operands)


def gelu_parts(pre):
    upper = 0.5 * (1.0 + lax.erf(pre * (0.5 ** 0.5)))
    return upper


def gelu_slope(pre):
    return gelu_parts(pre) + pre * jnp.exp(-0.5 * pre * pre) * (1.0 / math.sqrt(2.0 * math.pi))


def norm_back_rows(resid, gain, upstream):
    middle = jnp.mean(resid, axis=-1, keepdims=True)
    centred = resid - middle
    scale = lax.rsqrt(jnp.mean(centred * centred, axis=-1, keepdims=True) + 1e-05)
    unit = centred * scale
    pulled = upstream * gain
    return scale * (
        pulled - jnp.mean(pulled, axis=-1, keepdims=True) - unit * jnp.mean(pulled * unit, axis=-1, keepdims=True)
    )


def feed_kernel(
    normed, cotangent, gain, inner, outer, mixed,
    layer_out, second_grad, small_grads,
    low, pre, adapter_pre, total, feed_low,
):
    step = pl.program_id(0)
    down = mixed[:, :, :ADAPTER].reshape(D, ADAPTER)
    up_left = mixed[:, :16, ADAPTER:].reshape(ADAPTER, ADAPTER)
    up_right = mixed[:, 16:, ADAPTER:].reshape(ADAPTER, ADAPTER)
    half = ADAPTER

    @pl.when(step == 0)
    def _():
        low[...] = normed[...].astype(BF16)
        adapter_pre[...] = dot_nn(low[...], down)
        act = adapter_pre[...]
        act = (act * gelu_parts(act)).astype(BF16)
        total[:, :half] = normed[:, :half] + 4.0 * dot_nn(act, up_left)
        total[:, half:] = normed[:, half:] + 4.0 * dot_nn(act, up_right)

    @pl.when(step < 4)
    def _():
        hidden = dot_nn(low[...], inner[...].reshape(D, D))
        pre[jnp.minimum(step, 3)] = hidden
        act = (hidden * gelu_parts(hidden)).astype(BF16)
        total[...] += dot_nn(act, outer[...].reshape(D, D))

    @pl.when(step == 3)
    def _():
        resid = total[...]
        layer_out[...] = norm_rows(resid, gain[...]).astype(BF16)
        third_grad = norm_back_rows(resid, gain[...], cotangent[...].astype(F32))
        feed_low[...] = third_grad.astype(BF16)
        adapter_low = (4.0 * third_grad).astype(BF16)
        act = adapter_pre[...]
        upper = gelu_parts(act)
        slope = gelu_slope(act)
        act = (act * upper).astype(BF16)
        grad = dot_right(adapter_low[:, :half], up_left) + dot_right(adapter_low[:, half:], up_right)
        grad = (slope * grad).astype(BF16)
        second_grad[...] = third_grad + dot_right(grad, down)
        small_grads[:, :, :half] = dot_left(low[...], grad).astype(BF16).reshape(32, 32, half)
        small_grads[:, :16, half:] = dot_left(act, adapter_low[:, :half]).astype(BF16).reshape(32, 16, half)
        small_grads[:, 16:, half:] = dot_left(act, adapter_low[:, half:]).astype(BF16).reshape(32, 16, half)

    @pl.when(step >= 4)
    def _():
        hidden = pre[jnp.clip(7 - step, 0, 3)]
        grad = dot_right(feed_low[...], outer[...].reshape(D, D))
        grad = (gelu_slope(hidden) * grad).astype(BF16)
        second_grad[...] += dot_right(grad, inner[...].reshape(D, D))


def feed_forward_backward(normed, cotangent, gain, weights):
    tokens = normed.shape[0]
    at = lambda step: jnp.minimum(step, 7 - step)
    still = lambda step: (0, 0)
    rows = pl.BlockSpec((tokens, D), still)
    return pl.pallas_call(
        feed_kernel,
        grid=(8,),
        out_shape=(
            jax.ShapeDtypeStruct((tokens, D), BF16),
            jax.ShapeDtypeStruct((tokens, D), F32),
            jax.ShapeDtypeStruct((32, 32, D), BF16),
        ),
        in_specs=[
            rows, rows, pl.BlockSpec((1, D), still),
            pl.BlockSpec((32, 32, D), lambda step: (0, INNER_AT // 32 + at(step), 0)),
            pl.BlockSpec((8, 128, D), lambda step: (at(step), OUTER_AT // 128, 0)),
            pl.BlockSpec((32, 32, D), lambda step: (0, MIXED_AT // 32, 0)),
        ],
        out_specs=(rows, rows, pl.BlockSpec((32, 32, D), lambda step: (0, 0, 0))),
        scratch_shapes=[
            pltpu.VMEM((tokens, D), BF16),
            pltpu.VMEM((4, tokens, D), F32),
            pltpu.VMEM((tokens, ADAPTER), F32),
            pltpu.VMEM((tokens, D), F32),
            pltpu.VMEM((tokens, D), BF16),
        ],
        compiler_params=params(),
        name="feed",
    )(normed, cotangent, gain, weights, weights, weights)


def fast_device(
    inputs, memory, out_grad, token_docs, memory_docs, self_project, self_output, cross_query,
    cross_memory, cross_output, inner_weight, outer_weight, adapter_down, adapter_up, norm_gains, prefixes,
):
    seq, x = lax.axis_index("seq"), lax.axis_index("rows")
    tokens = 2 * S_DEV
    mixed = jnp.concatenate(
        [adapter_down, jnp.concatenate([adapter_up[:, :ADAPTER], adapter_up[:, ADAPTER:]], axis=0)], axis=1
    )
    lane_group = lax.broadcasted_iota(jnp.int32, (1, LANES), 1) // 32
    small = jnp.concatenate([
        jnp.pad(prefixes, ((0, 0), (0, 2), (0, 0))).reshape(128, 32), jnp.pad(norm_gains, ((0, 13), (0, 0)))
    ])
    small = jnp.where(lane_group == (seq % 2) * 2 + x, jnp.tile(small, (1, 4)), jnp.zeros((), BF16))
    memory_line = jnp.where(lane_group == seq % 4, jnp.tile(memory_docs, (1, 4)), 0)
    docs = jnp.concatenate([token_docs, memory_line, jnp.zeros((4, LANES), jnp.int32)]).astype(F32)
    (
        full, memory_pairs, small_full, docs_all, docs_row, docs_column, arrived, pair_attended, pair_inverse,
        first_resid, cross_queries, crossed, cross_inverse, second_resid, second_norm,
    ) = first_call(
        inputs, memory.reshape(2, M_DEV, D), small, docs,
        self_project, self_output, cross_query, cross_memory, cross_output, inner_weight, outer_weight, mixed,
    )

    third_gain = small_full[:, 130].reshape(1, D).astype(F32)
    layer_out, second_grad, small_grads = feed_forward_backward(
        second_norm, out_grad.reshape(tokens, D), third_gain, full
    )
    input_grad, memory_grad, down_grad, up_grad, prefix_sum = second_call(
        second_grad, second_resid, small_full, docs, docs_all, docs_row, crossed, cross_inverse, cross_queries,
        full, memory_pairs, first_resid, arrived, pair_attended, pair_inverse, docs_column,
        small_grads.reshape(4, 2, 2, 2, 32, D),
    )
    prefix_grad = lax.dynamic_slice_in_dim(prefix_sum[:, :PREFIX], 32 * ((seq % 2) * 2 + x), 32, 2)
    return (
        layer_out.reshape(2, S_DEV, D),
        input_grad.reshape(2, S_DEV, D),
        memory_grad.reshape(2, M_DEV, D),
        prefix_grad,
        down_grad,
        up_grad,
    )


def solution(mesh):
    placed = (
        P("rows", "seq", None),
        P("rows", "seq", None),
        P("rows", "seq", None),
        P("rows", "seq"),
        P("rows", "seq"),
        P(("seq", "rows"), None),
        P(("seq", "rows"), None),
        P(("seq", "rows"), None),
        P(("seq", "rows"), None),
        P(("seq", "rows"), None),
        P(("seq", "rows"), None),
        P(("seq", "rows"), None),
        P(("seq", "rows"), None),
        P(("seq", "rows"), None),
        P(None, ("seq", "rows")),
        P(None, None, ("seq", "rows")),
    )
    small_slice = mesh.shape["seq"] == 16 and mesh.shape["rows"] == 2
    return jax.shard_map(
        fast_device if small_slice else per_device,
        mesh=mesh,
        in_specs=placed,
        out_specs=(
            P("rows", "seq", None),
            P("rows", "seq", None),
            P("rows", "seq", None),
            P(None, None, ("seq", "rows")),
            P(("seq", "rows"), None),
            P(("seq", "rows"), None),
        ),
        check_vma=False,
    )
```

```python
import math

import jax
import jax.numpy as jnp
from jax import lax
from jax.experimental import pallas as pl
from jax.experimental.pallas import tpu as pltpu
from jax.sharding import PartitionSpec as P

D = 1024
HEADS = 16
HEAD_DIM = 64
ADAPTER = 512
PREFIX = 30
S_DEV = 128
M_DEV = 32


score_scale = 0.125
masked_score = -1000000000.0


def heads_of(matrix):
    return matrix.reshape(matrix.shape[0], HEADS, HEAD_DIM)


def dot_right(left, right):
    return lax.dot_general(
        left, right, (((1,), (1,)), ((), ())), preferred_element_type=jnp.float32
    )


def dot_left(left, right):
    return lax.dot_general(
        left, right, (((0,), (0,)), ((), ())), preferred_element_type=jnp.float32
    )


def norm_rows(resid, gain):
    middle = jnp.mean(resid, axis=-1, keepdims=True)
    centred = resid - middle
    spread = jnp.mean(centred * centred, axis=-1, keepdims=True)
    return centred * lax.rsqrt(spread + 1e-05) * gain


def norm_back(resid, gain, upstream):
    unused, pullback = jax.vjp(lambda values: norm_rows(values, gain), resid)
    return pullback(upstream)[0]


def gelu_back(pre_act, upstream):
    unused, pullback = jax.vjp(lambda values: jax.nn.gelu(values, approximate=False), pre_act)
    return pullback(upstream)[0]


def allowed_keys(query_docs, key_docs, query_pos, key_pos, causal):
    allowed = query_docs[:, None] == key_docs[None, :]
    if causal:
        allowed = allowed & (key_pos[None, :] <= query_pos[:, None])
    return allowed


def prefix_terms(queries, prefix_keys, prefix_values):
    scores = (
        jnp.einsum(
            "qhd,phd->hqp", queries, heads_of(prefix_keys), preferred_element_type=jnp.float32
        )
        * score_scale
    )
    weights = jnp.exp(scores)
    summed = jnp.einsum(
        "hqp,phd->qhd",
        weights.astype(jnp.bfloat16),
        heads_of(prefix_values),
        preferred_element_type=jnp.float32,
    )
    return (jnp.sum(weights, axis=-1), summed)


def fold_keys(running, arrived, queries, query_docs, key_docs, query_first, causal):
    key_count = arrived.shape[0]
    block_len = math.gcd(key_count, 512)
    query_count = queries.shape[0]
    query_pos = query_first + jnp.arange(query_count, dtype=jnp.int32)
    key_width = arrived.shape[1] // 2

    def fold_one_block(current, element):
        key_block, block_index = element
        key_first = block_index * block_len

        def compute(present):
            block_docs = lax.dynamic_slice_in_dim(key_docs, key_first, block_len, 0)
            allowed = allowed_keys(
                query_docs,
                block_docs,
                query_pos,
                key_first + jnp.arange(block_len, dtype=jnp.int32),
                causal,
            )
            scores = (
                jnp.einsum(
                    "qhd,khd->hqk",
                    queries,
                    heads_of(key_block[:, :key_width]),
                    preferred_element_type=jnp.float32,
                )
                * score_scale
            )
            weights = jnp.exp(jnp.where(allowed[None], scores, masked_score))
            summed = jnp.einsum(
                "hqk,khd->qhd",
                weights.astype(jnp.bfloat16),
                heads_of(key_block[:, key_width:]),
                preferred_element_type=jnp.float32,
            )
            return (present[0] + jnp.sum(weights, axis=-1), present[1] + summed)

        if causal:
            return (
                lax.cond(
                    key_first <= query_first + query_count - 1, compute, lambda held: held, current
                ),
                None,
            )
        return (compute(current), None)

    running, unused = lax.scan(
        fold_one_block,
        running,
        (
            arrived.reshape(key_count // block_len, block_len, arrived.shape[1]),
            jnp.arange(key_count // block_len, dtype=jnp.int32),
        ),
    )
    return running


def attend_back(
    queries,
    gathered,
    prefix_keys,
    prefix_values,
    grad_out,
    attended,
    totals,
    query_docs,
    key_docs,
    query_first,
    causal,
):
    query_count = queries.shape[0]
    key_count = gathered.shape[0]
    key_width = gathered.shape[1] // 2
    block_len = math.gcd(key_count, 512)
    query_pos = query_first + jnp.arange(query_count, dtype=jnp.int32)
    grad_heads = heads_of(grad_out)
    grad_summed = (grad_heads / totals.T[:, :, None]).astype(jnp.bfloat16)
    row_dot = jnp.sum(grad_heads * heads_of(attended), axis=-1).T / totals
    prefix_key_heads = heads_of(prefix_keys)
    prefix_value_heads = heads_of(prefix_values)
    prefix_weights = jnp.exp(
        jnp.einsum("qhd,phd->hqp", queries, prefix_key_heads, preferred_element_type=jnp.float32)
        * score_scale
    )
    prefix_dots = jnp.einsum(
        "qhd,phd->hqp", grad_summed, prefix_value_heads, preferred_element_type=jnp.float32
    )
    prefix_slopes = (prefix_weights * (prefix_dots - row_dot[:, :, None])).astype(jnp.bfloat16)
    query_grad = jnp.einsum(
        "hqp,phd->qhd", prefix_slopes, prefix_key_heads, preferred_element_type=jnp.float32
    )
    key_grad_prefix = (
        jnp.einsum("hqp,qhd->phd", prefix_slopes, queries, preferred_element_type=jnp.float32)
        * score_scale
    ).reshape(-1, D)
    value_grad_prefix = jnp.einsum(
        "hqp,qhd->phd",
        prefix_weights.astype(jnp.bfloat16),
        grad_summed,
        preferred_element_type=jnp.float32,
    ).reshape(-1, D)

    def attend_one_block(current, element):
        key_block, block_index = element
        key_first = block_index * block_len

        def compute(present):
            block_docs = lax.dynamic_slice_in_dim(key_docs, key_first, block_len, 0)
            allowed = allowed_keys(
                query_docs,
                block_docs,
                query_pos,
                key_first + jnp.arange(block_len, dtype=jnp.int32),
                causal,
            )
            key_heads = heads_of(key_block[:, :key_width])
            value_heads = heads_of(key_block[:, key_width:])
            scores = (
                jnp.einsum("qhd,khd->hqk", queries, key_heads, preferred_element_type=jnp.float32)
                * score_scale
            )
            weights = jnp.exp(jnp.where(allowed[None], scores, masked_score))
            dots = jnp.einsum(
                "qhd,khd->hqk", grad_summed, value_heads, preferred_element_type=jnp.float32
            )
            slopes = (weights * (dots - row_dot[:, :, None])).astype(jnp.bfloat16)
            present = present + jnp.einsum(
                "hqk,khd->qhd", slopes, key_heads, preferred_element_type=jnp.float32
            )
            key_grad = (
                jnp.einsum("hqk,qhd->khd", slopes, queries, preferred_element_type=jnp.float32)
                * score_scale
            )
            value_grad = jnp.einsum(
                "hqk,qhd->khd",
                weights.astype(jnp.bfloat16),
                grad_summed,
                preferred_element_type=jnp.float32,
            )
            return (
                present,
                jnp.concatenate(
                    [key_grad.reshape(block_len, D), value_grad.reshape(block_len, D)], axis=1
                ),
            )

        if causal:
            return lax.cond(
                key_first <= query_first + query_count - 1,
                compute,
                lambda held: (held, jnp.zeros((block_len, 2 * D), jnp.float32)),
                current,
            )
        return compute(current)

    query_grad, key_terms = lax.scan(
        attend_one_block,
        query_grad,
        (
            gathered.reshape(key_count // block_len, block_len, gathered.shape[1]),
            jnp.arange(key_count // block_len, dtype=jnp.int32),
        ),
    )
    query_low = (query_grad * score_scale).astype(jnp.bfloat16).reshape(query_count, D)
    key_terms = key_terms.reshape(key_count, 2 * D)
    return (query_low, key_terms, key_grad_prefix, value_grad_prefix, grad_summed, row_dot)


def fetch_all(
    self_project,
    self_output,
    cross_query,
    cross_memory,
    cross_output,
    inner_weight,
    outer_weight,
    adapter_down,
    adapter_up,
    norm_gains,
    prefixes,
):
    return (
        lax.all_gather(self_project, ("seq", "rows"), axis=0, tiled=True),
        lax.all_gather(self_output, ("seq", "rows"), axis=0, tiled=True),
        lax.all_gather(cross_query, ("seq", "rows"), axis=0, tiled=True),
        lax.all_gather(cross_memory, ("seq", "rows"), axis=0, tiled=True),
        lax.all_gather(cross_output, ("seq", "rows"), axis=0, tiled=True),
        lax.all_gather(inner_weight, ("seq", "rows"), axis=0, tiled=True),
        lax.all_gather(outer_weight, ("seq", "rows"), axis=0, tiled=True),
        lax.all_gather(adapter_down, ("seq", "rows"), axis=0, tiled=True),
        lax.all_gather(adapter_up, ("seq", "rows"), axis=0, tiled=True),
        lax.all_gather(norm_gains, ("seq", "rows"), axis=1, tiled=True),
        lax.all_gather(prefixes, ("seq", "rows"), axis=2, tiled=True),
    )


def fetch_again(
    self_project,
    self_output,
    cross_query,
    cross_memory,
    cross_output,
    inner_weight,
    outer_weight,
    adapter_down,
    adapter_up,
    norm_gains,
    prefixes,
):
    return (
        lax.all_gather(self_project, ("seq", "rows"), axis=0, tiled=True),
        lax.all_gather(self_output, ("seq", "rows"), axis=0, tiled=True),
        lax.all_gather(cross_query, ("seq", "rows"), axis=0, tiled=True),
        lax.all_gather(cross_memory, ("seq", "rows"), axis=0, tiled=True),
        lax.all_gather(cross_output, ("seq", "rows"), axis=0, tiled=True),
        lax.all_gather(inner_weight, ("seq", "rows"), axis=0, tiled=True),
        lax.all_gather(outer_weight, ("seq", "rows"), axis=0, tiled=True),
        lax.all_gather(adapter_down, ("seq", "rows"), axis=0, tiled=True),
        lax.all_gather(adapter_up, ("seq", "rows"), axis=0, tiled=True),
        lax.all_gather(norm_gains, ("seq", "rows"), axis=1, tiled=True),
        lax.all_gather(prefixes, ("seq", "rows"), axis=2, tiled=True),
    )


def forward_row(tokens, memory_rows, query_docs, token_docs, memory_docs, query_first, weights):
    (
        self_project,
        self_output,
        cross_query,
        cross_memory,
        cross_output,
        inner_weight,
        outer_weight,
        adapter_down,
        adapter_up,
        norm_gains,
        prefixes,
    ) = weights
    gains = norm_gains.astype(jnp.float32)
    projected = jnp.dot(tokens, self_project, preferred_element_type=jnp.float32).astype(
        jnp.bfloat16
    )
    queries = heads_of(projected[:, :D])
    local_pairs = projected[:, D:]
    start_self = prefix_terms(queries, prefixes[0], prefixes[1])
    totals, summed = fold_keys(
        start_self,
        lax.all_gather(local_pairs, "seq", axis=0, tiled=True),
        queries,
        query_docs,
        token_docs,
        query_first,
        True,
    )
    attended = (summed / totals.T[:, :, None]).reshape(-1, D)
    first_resid = tokens.astype(jnp.float32) + jnp.dot(
        attended.astype(jnp.bfloat16), self_output, preferred_element_type=jnp.float32
    )
    first_norm = norm_rows(first_resid, gains[0])
    first_low = first_norm.astype(jnp.bfloat16)
    cross_queries = heads_of(
        jnp.dot(first_low, cross_query, preferred_element_type=jnp.float32).astype(jnp.bfloat16)
    )
    memory_pairs = jnp.dot(memory_rows, cross_memory, preferred_element_type=jnp.float32).astype(
        jnp.bfloat16
    )
    start_cross = prefix_terms(cross_queries, prefixes[2], prefixes[3])
    cross_totals, cross_summed = fold_keys(
        start_cross,
        lax.all_gather(memory_pairs, "seq", axis=0, tiled=True),
        cross_queries,
        query_docs,
        memory_docs,
        query_first,
        False,
    )
    crossed = (cross_summed / cross_totals.T[:, :, None]).reshape(-1, D)
    second_resid = first_norm + jnp.dot(
        crossed.astype(jnp.bfloat16), cross_output, preferred_element_type=jnp.float32
    )
    second_norm = norm_rows(second_resid, gains[1])
    second_low = second_norm.astype(jnp.bfloat16)
    hidden_pre = jnp.dot(second_low, inner_weight, preferred_element_type=jnp.float32)
    hidden_act = jax.nn.gelu(hidden_pre, approximate=False).astype(jnp.bfloat16)
    adapter_pre = jnp.dot(second_low, adapter_down, preferred_element_type=jnp.float32)
    adapter_act = jax.nn.gelu(adapter_pre, approximate=False).astype(jnp.bfloat16)
    third_resid = (
        second_norm
        + jnp.dot(hidden_act, outer_weight, preferred_element_type=jnp.float32)
        + 4.0 * jnp.dot(adapter_act, adapter_up, preferred_element_type=jnp.float32)
    )
    layer_out = norm_rows(third_resid, gains[2]).astype(jnp.bfloat16)
    saved = (
        queries,
        local_pairs,
        totals,
        attended,
        first_resid,
        cross_queries,
        memory_pairs,
        cross_totals,
        crossed,
        second_resid,
        second_low,
        hidden_pre,
        adapter_pre,
        adapter_act,
        third_resid,
    )
    return (layer_out, saved)


def backward_row(cotangent, saved, weights, query_docs, token_docs, memory_docs, query_first):
    (
        self_project,
        self_output,
        cross_query,
        cross_memory,
        cross_output,
        inner_weight,
        outer_weight,
        adapter_down,
        adapter_up,
        norm_gains,
        prefixes,
    ) = weights
    (
        queries,
        local_pairs,
        totals,
        attended,
        first_resid,
        cross_queries,
        memory_pairs,
        cross_totals,
        crossed,
        second_resid,
        second_low,
        hidden_pre,
        adapter_pre,
        adapter_act,
        third_resid,
    ) = saved
    gains = norm_gains.astype(jnp.float32)
    third_grad = norm_back(third_resid, gains[2], cotangent.astype(jnp.float32))
    feed_low = third_grad.astype(jnp.bfloat16)
    adapter_low = (4.0 * third_grad).astype(jnp.bfloat16)
    hidden_grad = gelu_back(hidden_pre, dot_right(feed_low, outer_weight)).astype(jnp.bfloat16)
    up_grad = dot_left(adapter_act, adapter_low)
    adapter_grad = gelu_back(adapter_pre, dot_right(adapter_low, adapter_up)).astype(jnp.bfloat16)
    down_grad = dot_left(second_low, adapter_grad)
    second_grad = (
        third_grad + dot_right(hidden_grad, inner_weight) + dot_right(adapter_grad, adapter_down)
    )
    second_resid_grad = norm_back(second_resid, gains[1], second_grad)
    self_all, memory_all = (
        lax.all_gather(local_pairs, "seq", axis=0, tiled=True),
        lax.all_gather(memory_pairs, "seq", axis=0, tiled=True),
    )
    cross_out_grad = dot_right(second_resid_grad.astype(jnp.bfloat16), cross_output)
    (
        cross_query_low,
        memory_terms,
        cross_key_prefix,
        cross_value_prefix,
        cross_summed_grad,
        cross_dot,
    ) = attend_back(
        cross_queries,
        memory_all,
        prefixes[2],
        prefixes[3],
        cross_out_grad,
        crossed,
        cross_totals,
        query_docs,
        memory_docs,
        query_first,
        False,
    )
    first_grad = second_resid_grad + dot_right(cross_query_low, cross_query)
    first_resid_grad = norm_back(first_resid, gains[0], first_grad)
    self_out_grad = dot_right(first_resid_grad.astype(jnp.bfloat16), self_output)
    query_low, self_terms, self_key_prefix, self_value_prefix, self_summed_grad, self_dot = (
        attend_back(
            queries,
            self_all,
            prefixes[0],
            prefixes[1],
            self_out_grad,
            attended,
            totals,
            query_docs,
            token_docs,
            query_first,
            True,
        )
    )
    self_sums, memory_sums = (
        lax.psum_scatter(
            self_terms.astype(jnp.bfloat16), "seq", scatter_dimension=0, tiled=True
        ).astype(jnp.float32),
        lax.psum_scatter(
            memory_terms.astype(jnp.bfloat16), "seq", scatter_dimension=0, tiled=True
        ).astype(jnp.float32),
    )
    project_grad = jnp.concatenate([query_low, self_sums.astype(jnp.bfloat16)], axis=1)
    input_grad = first_resid_grad + dot_right(project_grad, self_project)
    memory_grad = dot_right(memory_sums.astype(jnp.bfloat16), cross_memory)
    prefix_grad = jnp.stack(
        [self_key_prefix, self_value_prefix, cross_key_prefix, cross_value_prefix]
    )
    return (input_grad, memory_grad, (down_grad, up_grad, prefix_grad))


def per_device(
    inputs,
    memory,
    out_grad,
    token_docs,
    memory_docs,
    self_project,
    self_output,
    cross_query,
    cross_memory,
    cross_output,
    inner_weight,
    outer_weight,
    adapter_down,
    adapter_up,
    norm_gains,
    prefixes,
):
    docs_full, memory_full = (
        lax.all_gather(token_docs, "seq", axis=1, tiled=True),
        lax.all_gather(memory_docs, "seq", axis=1, tiled=True),
    )
    query_first = lax.axis_index("seq") * inputs.shape[1]
    outputs = []
    input_grads = []
    memory_grads = []
    adjusted_grads = None
    for row_index in range(inputs.shape[0]):
        weights = fetch_all(
            self_project,
            self_output,
            cross_query,
            cross_memory,
            cross_output,
            inner_weight,
            outer_weight,
            adapter_down,
            adapter_up,
            norm_gains,
            prefixes,
        )
        layer_out, saved = forward_row(
            inputs[row_index],
            memory[row_index],
            token_docs[row_index],
            docs_full[row_index],
            memory_full[row_index],
            query_first,
            weights,
        )
        weights_back = fetch_again(
            self_project,
            self_output,
            cross_query,
            cross_memory,
            cross_output,
            inner_weight,
            outer_weight,
            adapter_down,
            adapter_up,
            norm_gains,
            prefixes,
        )
        input_grad, memory_grad, row_grads = backward_row(
            out_grad[row_index],
            saved,
            weights_back,
            token_docs[row_index],
            docs_full[row_index],
            memory_full[row_index],
            query_first,
        )
        shares = (
            lax.psum_scatter(row_grads[0], ("seq", "rows"), scatter_dimension=0, tiled=True),
            lax.psum_scatter(row_grads[1], ("seq", "rows"), scatter_dimension=0, tiled=True),
            lax.psum_scatter(row_grads[2], ("seq", "rows"), scatter_dimension=2, tiled=True),
        )
        if adjusted_grads is None:
            adjusted_grads = shares
        else:
            adjusted_grads = tuple(
                (former + latter for former, latter in zip(adjusted_grads, shares))
            )
        outputs.append(layer_out)
        input_grads.append(input_grad)
        memory_grads.append(memory_grad)
    return (
        jnp.stack(outputs),
        jnp.stack(input_grads),
        jnp.stack(memory_grads),
        adjusted_grads[2],
        adjusted_grads[0],
        adjusted_grads[1],
    )


MESH_ID = pl.DeviceIdType.MESH
F32 = jnp.float32
BF16 = jnp.bfloat16
VMEM_BYTES = 60 * 1024 * 1024
PAIRS = HEADS // 2
LANES = 2 * HEAD_DIM
Q_AT, K_AT, V_AT, SELF_OUT_AT, CROSS_Q_AT, MEM_K_AT, MEM_V_AT, CROSS_OUT_AT = range(0, 256, 32)
INNER_AT, OUTER_AT, MIXED_AT = 256, 384, 512
ALL_ROWS = 544
SMALL_ROWS = 144
PIECE_ROWS = 16
GAP = 3
LEAD = 4
SENDS = 2
Z_LAST = ()
WAIT_TICKS = 4
STEP_TICKS = 2


def whole(space=pltpu.VMEM):
    return pl.BlockSpec(memory_space=space)


def params(collective_id=None):
    if collective_id is None:
        return pltpu.CompilerParams(vmem_limit_bytes=VMEM_BYTES)
    return pltpu.CompilerParams(
        vmem_limit_bytes=VMEM_BYTES, collective_id=collective_id, has_side_effects=True
    )


def remote(src, dst, send_sem, recv_sem, device):
    return pltpu.make_async_remote_copy(
        src_ref=src, dst_ref=dst, send_sem=send_sem, recv_sem=recv_sem,
        device_id=device, device_id_type=MESH_ID,
    )


def greet(peers):
    barrier = pltpu.get_barrier_semaphore()
    for peer in peers:
        pl.semaphore_signal(barrier, inc=1, device_id=peer, device_id_type=MESH_ID)
    pl.semaphore_wait(barrier, len(peers))


def dot_nn(left, right):
    return lax.dot_general(left, right, (((1,), (0,)), ((), ())), preferred_element_type=F32)


class Place:
    def __init__(self):
        self.seq, self.x = lax.axis_index("seq"), lax.axis_index("rows")
        self.z, self.y, self.core = self.seq // 4, (self.seq // 2) % 2, self.seq % 2
        self.pair, self.row = self.seq // 2, self.seq % 2

    def device(self, z, y, core, x):
        return ((z * 2 + y) * 2 + core, x)

    def along_z(self, step):
        return self.device((self.z + step) % 4, self.y, self.core, self.x)

    def along_y(self):
        return self.device(self.z, 1 - self.y, self.core, self.x)

    def along_x(self):
        return self.device(self.z, self.y, self.core, 1 - self.x)

    def other_core(self):
        return self.device(self.z, self.y, 1 - self.core, self.x)

    def diagonal(self):
        return self.device(self.z, self.y, 1 - self.core, 1 - self.x)

    def others(self):
        return [((self.seq + step) % 16, self.x) for step in range(1, 16)]


class Gather:
    def __init__(self, place, full, local_sem, sems, gap):
        self.place, self.full, self.local_sem, self.sems, self.gap = place, full, local_sem, sems, gap
        self.stages = []
        self.waiting = []
        self.cut = 1
        self.tick_at = 0

    def copies(self, level, source, target, device, slot):
        k = len(self.stages)
        return remote(source, target, self.sems[2 * level].at[k, slot], self.sems[2 * level + 1].at[k, slot], device)

    def add(self, source, first, count, piece=PIECE_ROWS):
        for from_row in range(0, count, piece):
            self.add_piece(source.at[pl.ds(from_row, piece)], first + from_row, piece)
        return len(self.stages) - 1

    def add_piece(self, source, first, count):
        at, full = self.place, self.full
        z, y, core, x = at.z, at.y, at.core, at.x
        rows = pl.ds(first, count)
        mine = full.at[z, y, core, x, rows]
        k = len(self.stages)
        if k in Z_LAST:
            plane = full.at[z, :, core, :, rows]
            first_way, then_way = (at.along_x(), at.along_y()) if k % 2 else (at.along_y(), at.along_x())
            line = full.at[z, y, core, :, rows] if k % 2 else full.at[z, :, core, x, rows]
            self.stages.append((
                pltpu.make_async_copy(source, mine, self.local_sem.at[k]),
                [self.copies(0, source, mine, first_way, 0)],
                [self.copies(1, line, line, then_way, 0)],
                [self.copies(2, plane, plane, at.along_z(d + 1), d) for d in range(3)],
                [self.copies(3, full.at[:, :, core, :, rows], full.at[:, :, core, :, rows], at.other_core(), 0)],
            ))
            return
        cut = self.cut
        near, far = pl.ds(0, cut), pl.ds(cut, 4 - cut)
        near1, far1 = full.at[near, y, core, x, rows], full.at[far, y, core, x, rows]
        near2, far2 = full.at[near, y, core, :, rows], full.at[far, :, core, x, rows]
        half = full.at[:, :, core, :, rows]
        self.stages.append((
            pltpu.make_async_copy(source, mine, self.local_sem.at[len(self.stages)]),
            [self.copies(0, source, mine, at.along_z(d + 1), d) for d in range(3)],
            [self.copies(1, near1, near1, at.along_x(), 0), self.copies(1, far1, far1, at.along_y(), 1)],
            [self.copies(2, near2, near2, at.along_y(), 0), self.copies(2, far2, far2, at.along_x(), 1)],
            [self.copies(3, half, half, at.other_core(), 0)],
        ))

    def add_memory_row(self, source, full):
        at = self.place
        mine, column, half = full.at[at.z, at.y, at.core], full.at[:, at.y, at.core], full.at[:, :, at.core]
        self.stages.append((
            pltpu.make_async_copy(source, mine, self.local_sem.at[len(self.stages)]),
            [self.copies(0, source, mine, at.along_z(d + 1), d) for d in range(3)],
            [self.copies(1, column, column, at.along_y(), 1)],
            [],
            [self.copies(3, half, half, at.other_core(), 0)],
        ))

    def start(self):
        for stage in self.stages:
            stage[0].start()

    def tick(self, count=1):
        for _ in range(count):
            for level in range(5):
                k = self.tick_at - self.after(level)
                if not 0 <= k < len(self.stages):
                    continue
                if level == 1:
                    self.stages[k][0].wait()
                if level > 0:
                    for copy in self.stages[k][level]:
                        copy.wait_recv()
                if level < 4:
                    for copy in self.stages[k][level + 1]:
                        copy.start()
            self.tick_at += 1
            for _ in range(SENDS):
                if self.waiting:
                    self.waiting.pop(0).start()

    def after(self, level):
        return 0 if level == 0 else LEAD + (level - 1) * self.gap

    def until(self, k):
        while self.tick_at <= k + self.after(4):
            self.tick()

    def finish(self):
        self.until(len(self.stages) - 1)
        for _, *levels in self.stages:
            for level in levels:
                for copy in level:
                    copy.wait_send()


def head_masks():
    lane = lax.broadcasted_iota(jnp.int32, (1, LANES), 1)
    first = (lane < HEAD_DIM).astype(F32).astype(BF16)
    return first, (1.0 - first.astype(F32)).astype(BF16)


def stack_heads(block):
    first, second = head_masks()
    return jnp.concatenate([block * first, block * second], axis=0)


def merge_heads(stacked):
    half = stacked.shape[0] // 2
    lane = lax.broadcasted_iota(jnp.int32, (half, LANES), 1)
    return jnp.where(lane < HEAD_DIM, stacked[:half], stacked[half:])


def rows_in_lanes(values):
    lane = lax.broadcasted_iota(jnp.int32, (8, LANES), 1)
    row = lax.broadcasted_iota(jnp.int32, (8, LANES), 0)
    picks = (lane // HEAD_DIM == row).astype(F32)
    return lax.dot_general(
        picks, values, (((1,), (1,)), ((), ())),
        precision=lax.Precision.HIGHEST, preferred_element_type=F32,
    )


def first_kernel(
    tokens, memory, small, docs,
    project, self_out, cross_q, cross_mem, cross_out, inner, outer, mixed,
    full, memory_full, memory_pairs_far, docs_column_far, arrived_far, attended_far, inverse_far,
    first_resid_far, cross_queries_far, crossed_far, cross_inverse_far,
    small_full, docs_all, docs_row, second_resid, second_norm,
    memory_pairs, docs_column, arrived, attended, inverse, first_resid, cross_queries, crossed, cross_inverse,
    gathered, first_norm, weights, staged, quad, memory_held, result_staged, sums, parts,
    local_sem, send0, recv0, send1, recv1, send2, recv2, send3, recv3,
    fetch_sem, own_sem, quad_send, quad_recv, small_send, small_recv, docs_send, docs_recv,
    head_send, head_recv, out_send, out_recv, leave_sem,
):
    leaving = []

    def leave(*arrays):
        for held, target in arrays:
            leaving.append(pltpu.make_async_copy(held, target, leave_sem.at[len(leaving)]))
            leaving[-1].start()

    place = Place()
    seq, x, pair, row = place.seq, place.x, place.pair, place.row
    others = place.others()
    quad_peers = [place.other_core(), place.along_x(), place.diagonal()]
    greet(others + quad_peers[1:])

    engine = Gather(place, full, local_sem, (send0, recv0, send1, recv1, send2, recv2, send3, recv3), GAP)
    project_done = [
        engine.add(project.at[:, pl.ds(part * D, D)], at, 32) for part, at in enumerate((Q_AT, K_AT, V_AT))
    ]
    for part, at in enumerate((MEM_K_AT, MEM_V_AT)):
        for half in range(2):
            held = pl.ds(16 * half, 16)
            engine.add_memory_row(memory.at[part, held], memory_full.at[:, :, :, part, held])
            memory_done = engine.add(cross_mem.at[held, pl.ds(part * D, D)], at + 16 * half, 16)
    out_done = engine.add(self_out, SELF_OUT_AT, 32)
    query_done = engine.add(cross_q, CROSS_Q_AT, 32)
    cross_done = engine.add(cross_out, CROSS_OUT_AT, 32)
    engine.cut = 2
    for part in range(4):
        engine.add(inner.at[:, pl.ds(part * D, D)], INNER_AT + 32 * part, 32)
    for part in range(4):
        engine.add(outer.at[pl.ds(32 * part, 32)], OUTER_AT + 32 * part, 32)
    engine.add(mixed, MIXED_AT, 32)
    engine.start()
    engine.tick()

    mine = place.core * 2 + x
    quad_copies = [
        remote(small, quad.at[mine], quad_send.at[k], quad_recv.at[k], quad_peers[k]) for k in range(3)
    ]
    own_small = pltpu.make_async_copy(small, quad.at[mine], own_sem.at[0])
    docs_copies = [
        remote(docs, docs_all.at[seq], docs_send.at[k], docs_recv.at[k], others[k]) for k in range(15)
    ]
    own_docs = pltpu.make_async_copy(docs, docs_all.at[seq], own_sem.at[1])
    own_small.start()
    own_docs.start()
    for copy in quad_copies + docs_copies:
        copy.start()
    rows = tokens[...].reshape(2 * S_DEV, D)
    fetches = []
    for part in range(3):
        engine.until(project_done[part])
        fetches.append(pltpu.make_async_copy(full_rows(full, 32 * part), weights.at[part], fetch_sem.at[part]))
        fetches[part].start()
    for part in range(3):
        fetches[part].wait()
        result = dot_nn(rows, weights[part].reshape(D, D)).astype(BF16)
        for at_row in range(2):
            for at_pair in range(PAIRS):
                staged[at_pair, at_row, part] = result[
                    at_row * S_DEV:(at_row + 1) * S_DEV, at_pair * LANES:(at_pair + 1) * LANES
                ]
        engine.tick()
    head_copies = []
    for k in range(15):
        to = (seq + k + 1) % 16
        head_copies.append(
            remote(staged.at[to // 2, to % 2], arrived.at[seq], head_send.at[k], head_recv.at[k], others[k])
        )
    own_heads = pltpu.make_async_copy(staged.at[pair, row], arrived.at[seq], own_sem.at[2])
    own_heads.start()
    engine.waiting = list(head_copies)
    engine.tick(2)
    own_small.wait()
    for copy in quad_copies:
        copy.wait()
    small_full[pair] = (quad[0] + quad[1]) + (quad[2] + quad[3])
    small_copies = []
    for k in range(1, 8):
        to = (((pair + k) % 8) * 2 + place.core, x)
        small_copies.append(
            remote(small_full.at[pair], small_full.at[pair], small_send.at[k], small_recv.at[k], to)
        )
        small_copies[-1].start()
    own_docs.wait()
    for copy in docs_copies:
        copy.wait()

    def spread_docs(at, carry):
        tile = docs_all[at]
        line = jnp.where(row == 0, tile[0:1], tile[1:2])
        docs_row[:, pl.ds(pl.multiple_of(at * S_DEV, S_DEV), S_DEV)] = jnp.broadcast_to(line, (8, S_DEV))
        docs_column[pl.ds(at * S_DEV, S_DEV)] = jnp.transpose(jnp.broadcast_to(line, (S_DEV, LANES)))
        return carry

    lax.fori_loop(0, 16, spread_docs, 0)

    engine.until(memory_done)
    fetch_memory = pltpu.make_async_copy(memory_full, memory_held, own_sem.at[3])
    fetch_memory.start()
    fetches = [
        pltpu.make_async_copy(full_rows(full, at), weights.at[part], fetch_sem.at[part])
        for part, at in enumerate((MEM_K_AT, MEM_V_AT))
    ]
    for fetch in fetches:
        fetch.start()
    fetch_memory.wait()
    for part in range(2):
        fetches[part].wait()

        def project_memory(at, carry):
            held = memory_held[at].reshape(4 * 2 * M_DEV, D)
            result = dot_nn(held, weights[part].reshape(D, D)).astype(BF16)
            memory_pairs[pl.ds(4 * at, 4), :, :, pl.ds(part * D, D)] = result.reshape(4, 2, M_DEV, D)
            return carry

        lax.fori_loop(0, 4, project_memory, 0)
    engine.tick(max(WAIT_TICKS, -(-len(engine.waiting) // SENDS)))
    own_heads.wait()
    for copy in head_copies:
        copy.wait()

    leave((memory_pairs, memory_pairs_far), (docs_column, docs_column_far), (arrived, arrived_far))

    block = 2 * S_DEV
    columns = pl.ds(pl.multiple_of(pair * LANES, LANES), LANES)
    target = gathered.at[row, :, columns]
    away = (
        lax.broadcasted_iota(jnp.int32, (block, block), 1)
        - lax.broadcasted_iota(jnp.int32, (block, block), 0)
    )
    prefix_lane = lax.broadcasted_iota(jnp.int32, (2 * block, 32), 1)
    prefix_keys, prefix_values = small_full[pair, 0:32], small_full[pair, 32:64]

    for step in range(8):
        at = (step + pair) % 8
        queries = stack_heads(arrived[pl.ds(2 * at, 2), 0].reshape(block, LANES))
        query_docs = docs_column[pl.ds(at * block, block)]
        scores = dot_right(queries, prefix_keys) * score_scale
        e = jnp.where(prefix_lane < PREFIX, jnp.exp(scores), 0.0)
        sums[...] = jnp.concatenate([e, jnp.zeros((2 * block, LANES - 32), F32)], axis=1)
        parts[...] = dot_nn(e.astype(BF16), prefix_values)

        def one_tile(key_at, carry):
            keys = arrived[pl.ds(2 * key_at, 2), 1].reshape(block, LANES)
            values = arrived[pl.ds(2 * key_at, 2), 2].reshape(block, LANES)
            key_docs = docs_row[0:1, pl.ds(pl.multiple_of(key_at * block, block), block)]
            same = jnp.concatenate([query_docs, query_docs], axis=1) == key_docs
            allowed = same & (away <= (at - key_at) * block)
            scores = dot_right(queries, keys) * score_scale
            e = jnp.where(allowed[None], jnp.exp(scores).reshape(2, block, block), 0.0)
            e = e.reshape(2 * block, block)
            sums[...] += e[:, :LANES] + e[:, LANES:]
            parts[...] += dot_nn(e.astype(BF16), values)
            return carry

        lax.fori_loop(0, at + 1, one_tile, 0)
        totals = 1.0 / jnp.sum(sums[...], axis=1, keepdims=True)
        result = merge_heads(parts[...] * totals)
        here = pl.ds(at * block, block)
        attended[here] = result
        inverse[here] = merge_heads(jnp.broadcast_to(totals, (2 * block, LANES)))
        result_staged[pl.ds(2 * at, 2)] = result.astype(BF16).reshape(2, S_DEV, LANES)
        for half in range(2):
            to = 2 * at + half

            @pl.when(to != seq)
            def _():
                remote(result_staged.at[to], target, out_send.at[to], out_recv.at[seq], (to, x)).start()

            @pl.when(to == seq)
            def _():
                pltpu.make_async_copy(result_staged.at[to], target, own_sem.at[4]).start()

        engine.tick(STEP_TICKS)

    leave((attended, attended_far), (inverse, inverse_far))

    for copy in small_copies:
        copy.wait()
    engine.until(cross_done)
    fetches = [
        pltpu.make_async_copy(full_rows(full, at), weights.at[part], fetch_sem.at[part])
        for part, at in enumerate((SELF_OUT_AT, CROSS_Q_AT, CROSS_OUT_AT))
    ]
    for fetch in fetches:
        fetch.start()
    gains = [
        jnp.concatenate(
            [small_full[at_pair, 128:144].astype(F32)[part:part + 1] for at_pair in range(PAIRS)], axis=1
        )
        for part in range(2)
    ]
    pltpu.make_async_copy(result_staged.at[seq], target, own_sem.at[4]).wait()
    for other, _ in others:
        remote(result_staged.at[other], target, out_send.at[other], out_recv.at[other], (other, x)).wait()
    fetches[0].wait()
    resid = tokens[...].reshape(2 * S_DEV, D).astype(F32) + dot_nn(
        gathered[...].reshape(2 * S_DEV, D), weights[0].reshape(D, D)
    )
    first_resid[...] = resid
    normed = norm_rows(resid, gains[0])
    first_norm[...] = normed
    engine.tick(STEP_TICKS)
    fetches[1].wait()
    cross_queries[...] = dot_nn(normed.astype(BF16), weights[1].reshape(D, D)).astype(BF16).reshape(2, S_DEV, D)
    engine.tick(STEP_TICKS)
    memory_len = 16 * M_DEV
    cross_prefix_lane = lax.broadcasted_iota(jnp.int32, (2 * S_DEV, 32), 1)
    for at_row in range(2):
        own = jnp.transpose(jnp.broadcast_to(docs[at_row:at_row + 1], (LANES, S_DEV)))
        own = jnp.concatenate([own] * (memory_len // LANES), axis=1)
        lines = [
            sum(docs_all[4 * at + k, 2 + at_row:3 + at_row] for k in range(4)) for at in range(4)
        ]
        allowed = own == jnp.concatenate(lines, axis=1)

        def one_pair(at_pair, carry):
            first = pl.multiple_of(at_pair * LANES, LANES)
            columns, value_columns = pl.ds(first, LANES), pl.ds(pl.multiple_of(first + D, LANES), LANES)
            stacked = stack_heads(cross_queries[at_row, :, columns])
            keys = memory_pairs[:, at_row, :, columns].reshape(memory_len, LANES)
            values = memory_pairs[:, at_row, :, value_columns].reshape(memory_len, LANES)
            scores = dot_right(stacked, small_full[at_pair, 64:96]) * score_scale
            prefix_e = jnp.where(cross_prefix_lane < PREFIX, jnp.exp(scores), 0.0)
            scores = dot_right(stacked, keys) * score_scale
            e = jnp.where(allowed[None], jnp.exp(scores).reshape(2, S_DEV, memory_len), 0.0)
            e = e.reshape(2 * S_DEV, memory_len)
            totals = jnp.sum(e, axis=1, keepdims=True) + jnp.sum(prefix_e, axis=1, keepdims=True)
            totals = 1.0 / totals
            summed = dot_nn(e.astype(BF16), values) + dot_nn(prefix_e.astype(BF16), small_full[at_pair, 96:128])
            crossed[at_row, :, columns] = merge_heads(summed * totals)
            cross_inverse[at_row, :, columns] = merge_heads(jnp.broadcast_to(totals, (2 * S_DEV, LANES)))
            return carry

        lax.fori_loop(0, PAIRS // 2, one_pair, 0)
        engine.tick(STEP_TICKS)
        lax.fori_loop(PAIRS // 2, PAIRS, one_pair, 0)
        engine.tick(STEP_TICKS)
    leave(
        (first_resid, first_resid_far), (cross_queries, cross_queries_far),
        (crossed, crossed_far), (cross_inverse, cross_inverse_far),
    )
    fetches[2].wait()
    resid = first_norm[...] + dot_nn(
        crossed[...].reshape(2 * S_DEV, D).astype(BF16), weights[2].reshape(D, D)
    )
    second_resid[...] = resid
    second_norm[...] = norm_rows(resid, gains[1])
    for copy in leaving:
        copy.wait()
    engine.finish()


def full_rows(full, first):
    return full.at[:, :, :, :, pl.ds(first, 32)]


def first_call(tokens, memory, small, docs, *weights):
    length = 16 * S_DEV
    chunks = 16 * 32 // PIECE_ROWS + 32 // PIECE_ROWS + 4
    dma = pltpu.SemaphoreType.DMA
    shape = jax.ShapeDtypeStruct
    outs = pl.pallas_call(
        first_kernel,
        out_shape=(
            shape((4, 2, 2, 2, ALL_ROWS, D), BF16),
            shape((4, 2, 2, 2, M_DEV, D), BF16),
            shape((16, 2, M_DEV, 2 * D), BF16),
            shape((length, LANES), F32),
            shape((16, 3, S_DEV, LANES), BF16),
            shape((length, LANES), F32),
            shape((length, LANES), F32),
            shape((2 * S_DEV, D), F32),
            shape((2, S_DEV, D), BF16),
            shape((2, S_DEV, D), F32),
            shape((2, S_DEV, D), F32),
            shape((8, SMALL_ROWS, LANES), BF16),
            shape((16, 8, LANES), F32),
            shape((8, length), F32),
            shape((2 * S_DEV, D), F32),
            shape((2 * S_DEV, D), F32),
        ),
        in_specs=[whole(), whole(pl.ANY), whole(), whole()] + [whole(pl.ANY)] * 8,
        out_specs=(whole(pl.ANY),) * 11 + (whole(),) * 5,
        scratch_shapes=[
            pltpu.VMEM((16, 2, M_DEV, 2 * D), BF16),
            pltpu.VMEM((length, LANES), F32),
            pltpu.VMEM((16, 3, S_DEV, LANES), BF16),
            pltpu.VMEM((length, LANES), F32),
            pltpu.VMEM((length, LANES), F32),
            pltpu.VMEM((2 * S_DEV, D), F32),
            pltpu.VMEM((2, S_DEV, D), BF16),
            pltpu.VMEM((2, S_DEV, D), F32),
            pltpu.VMEM((2, S_DEV, D), F32),
            pltpu.VMEM((2, S_DEV, D), BF16),
            pltpu.VMEM((2 * S_DEV, D), F32),
            pltpu.VMEM((3, 4, 2, 2, 2, 32, D), BF16),
            pltpu.VMEM((PAIRS, 2, 3, S_DEV, LANES), BF16),
            pltpu.VMEM((4, SMALL_ROWS, LANES), BF16),
            pltpu.VMEM((4, 2, 2, 2, M_DEV, D), BF16),
            pltpu.VMEM((16, S_DEV, LANES), BF16),
            pltpu.VMEM((4 * S_DEV, LANES), F32),
            pltpu.VMEM((4 * S_DEV, LANES), F32),
            dma((chunks,)),
            dma((chunks, 3)), dma((chunks, 3)), dma((chunks, 2)), dma((chunks, 2)),
            dma((chunks, 3)), dma((chunks, 3)), dma((chunks, 1)), dma((chunks, 1)),
            dma((3,)), dma((5,)), dma((3,)), dma((3,)), dma((8,)), dma((8,)), dma((15,)), dma((15,)),
            dma((15,)), dma((15,)), dma((16,)), dma((16,)), dma((9,)),
        ],
        compiler_params=params(0),
        name="first",
    )(tokens, memory, small, docs, *weights)
    return (outs[0].reshape(32, ALL_ROWS, D),) + tuple(outs[2:])


def second_kernel(
    second_grad, second_resid, small_full, docs, docs_all, docs_row, crossed, cross_inverse, cross_queries,
    full, memory_pairs_far, first_resid_far, arrived_far, attended_far, inverse_far, docs_column_far, small_grads,
    input_grad, memory_grad, down_grad, up_grad, prefix_sum,
    weights, memory_pairs, first_resid, arrived, attended, inverse, docs_column,
    pull, cross_grad, cross_query_grad, key_terms, value_terms, cross_prefix,
    small_core, small_mine, small_x, small_pair, small_y, small_line, small_all,
    memory_part, memory_core, memory_mine, memory_y, memory_line, memory_all,
    prefix_y, prefix_line, prefix_all, prefix_mine, prefix_quad,
    heads_out, grads, grad_low, delta, query_grads, key_grads, value_grads, staged, gathered,
    fetch_sem, own_sem, near_send, near_recv, line_send, line_recv, small_send, small_recv, memory_send, memory_recv,
    prefix_send, prefix_recv, quad_send, quad_recv,
    in_send, in_recv, out_send, out_recv, query_send, query_recv,
):
    place = Place()
    seq, x, pair, row, core = place.seq, place.x, place.pair, place.row, place.core
    z, y = place.z, place.y
    others = place.others()
    tokens = 2 * S_DEV
    memory_len = 16 * M_DEV
    block = 2 * S_DEV

    fetches = {}

    def fetch(name, source, target):
        fetches[name] = pltpu.make_async_copy(source, target, fetch_sem.at[len(fetches)])
        fetches[name].start()

    firsts = (CROSS_OUT_AT, CROSS_Q_AT, SELF_OUT_AT, MEM_K_AT, MEM_V_AT, Q_AT, K_AT, V_AT)

    def fetch_weight(at):
        fetch(at, full.at[:, pl.ds(at, 32)], weights.at[firsts.index(at)])

    def weight(at):
        return weights[firsts.index(at)].reshape(D, D)

    fetch_weight(CROSS_OUT_AT)
    fetch("pairs", memory_pairs_far, memory_pairs)
    fetch_weight(CROSS_Q_AT)
    fetch("resid", first_resid_far, first_resid)
    fetch_weight(SELF_OUT_AT)
    fetch_weight(MEM_K_AT)
    fetch_weight(MEM_V_AT)
    fetch("arrived", arrived_far, arrived)
    fetch("attended", attended_far, attended)
    fetch("inverse", inverse_far, inverse)
    fetch("docs", docs_column_far, docs_column)
    for at in (K_AT, V_AT, Q_AT):
        fetch_weight(at)
    greet(others + [place.along_x(), place.diagonal()])

    small_first = remote(
        small_grads.at[:, :, 1 - core], small_core, near_send.at[0], near_recv.at[0], place.other_core()
    )
    small_own = pltpu.make_async_copy(small_grads.at[:, :, core], small_mine, own_sem.at[0])
    small_second = remote(small_mine.at[:, :, 1 - x], small_x, near_send.at[1], near_recv.at[1], place.along_x())

    def along_y(k, source, target):
        return remote(source.at[:, 1 - y], target, line_send.at[k], line_recv.at[k], place.along_y())

    def along_z(source, target, sends, recvs):
        return [
            remote(source.at[(z + k) % 4], target.at[z], sends.at[k], recvs.at[k], place.along_z(k))
            for k in range(1, 4)
        ]

    small_third = along_y(0, small_pair, small_y)
    small_fourth = along_z(small_line, small_all, small_send, small_recv)
    memory_first = remote(
        memory_part.at[:, :, 1 - core], memory_core, near_send.at[2], near_recv.at[2], place.other_core()
    )
    memory_second = along_y(1, memory_mine, memory_y)
    memory_third = along_z(memory_line, memory_all, memory_send, memory_recv)
    prefix_first = along_y(2, cross_prefix, prefix_y)
    prefix_second = along_z(prefix_line, prefix_all, prefix_send, prefix_recv)
    small_first.start()
    small_own.start()

    gains = [
        jnp.concatenate(
            [small_full[at_pair, 128:144].astype(F32)[part:part + 1] for at_pair in range(PAIRS)], axis=1
        )
        for part in range(2)
    ]
    pulled = norm_back_rows(second_resid[...], gains[1], second_grad[...])
    pull[...] = pulled
    fetches[CROSS_OUT_AT].wait()
    cross_grad[...] = dot_right(pulled.astype(BF16), weight(CROSS_OUT_AT)).reshape(2, S_DEV, D)
    fetches["pairs"].wait()

    cross_pad = lax.broadcasted_iota(jnp.int32, (64, S_DEV), 0) % 32
    for at_row in range(2):
        lines = [sum(docs_all[4 * at + k, 2 + at_row:3 + at_row] for k in range(4)) for at in range(4)]
        key_docs = jnp.concatenate(
            [jnp.transpose(jnp.broadcast_to(line, (S_DEV, LANES))) for line in lines], axis=0
        )
        allowed = key_docs == docs[at_row:at_row + 1]

        def one_pair(at_pair, carry):
            first = pl.multiple_of(at_pair * LANES, LANES)
            columns, value_columns = pl.ds(first, LANES), pl.ds(pl.multiple_of(first + D, LANES), LANES)
            heads = cross_queries[at_row, :, columns]
            grad = cross_grad[at_row, :, columns] * cross_inverse[at_row, :, columns]
            low = grad.astype(BF16)
            lines = rows_in_lanes(grad * crossed[at_row, :, columns])

            def head_rows(count):
                return jnp.concatenate(
                    [jnp.broadcast_to(lines[0:1], (count, S_DEV)), jnp.broadcast_to(lines[1:2], (count, S_DEV))],
                    axis=0,
                )

            prefix_key_stack = stack_heads(small_full[at_pair, 64:96])
            prefix_value_stack = stack_heads(small_full[at_pair, 96:128])
            e = jnp.exp(dot_right(prefix_key_stack, heads) * score_scale)
            e = jnp.where(cross_pad < PREFIX, e, 0.0)
            slopes = (e * (dot_right(prefix_value_stack, low) - head_rows(32))).astype(BF16)
            from_prefix = dot_left(slopes, prefix_key_stack)
            key_grad = merge_heads(dot_nn(slopes, heads)) * score_scale
            value_grad = merge_heads(dot_nn(e.astype(BF16), low))
            held = cross_prefix.at[at_pair // 2, at_pair % 2]
            if at_row == 0:
                held[0] = key_grad
                held[1] = value_grad
            else:
                held[0] += key_grad
                held[1] += value_grad
            key_stack = stack_heads(memory_pairs[:, at_row, :, columns].reshape(memory_len, LANES))
            value_stack = stack_heads(memory_pairs[:, at_row, :, value_columns].reshape(memory_len, LANES))
            e = jnp.exp(dot_right(key_stack, heads) * score_scale).reshape(2, memory_len, S_DEV)
            e = jnp.where(allowed[None], e, 0.0).reshape(2 * memory_len, S_DEV)
            slopes = (e * (dot_right(value_stack, low) - head_rows(memory_len))).astype(BF16)
            terms = merge_heads(dot_nn(slopes, heads)) * score_scale
            key_terms[:, at_row, :, columns] = terms.astype(BF16).reshape(16, M_DEV, LANES)
            terms = merge_heads(dot_nn(e.astype(BF16), low))
            value_terms[:, at_row, :, columns] = terms.astype(BF16).reshape(16, M_DEV, LANES)
            query_grad = (from_prefix + dot_left(slopes, key_stack)) * score_scale
            cross_query_grad[at_row, :, columns] = query_grad.astype(BF16)
            return carry

        lax.fori_loop(0, PAIRS, one_pair, 0)
        if at_row == 0:
            small_own.wait()
            small_first.wait_recv()
            small_mine[...] = small_mine[...] + small_core[...]
            small_second.start()
    prefix_first.start()

    fetches[CROSS_Q_AT].wait()
    fetches["resid"].wait()
    first_grad = pull[...] + dot_right(cross_query_grad[...].reshape(tokens, D), weight(CROSS_Q_AT))
    resid_grad = norm_back_rows(first_resid[...], gains[0], first_grad)
    pull[...] = resid_grad
    fetches[SELF_OUT_AT].wait()
    out_grad = dot_right(resid_grad.astype(BF16), weight(SELF_OUT_AT)).astype(BF16)
    for at_pair in range(PAIRS):
        for at_row in range(2):
            heads_out[at_pair, at_row] = out_grad[
                at_row * S_DEV:(at_row + 1) * S_DEV, at_pair * LANES:(at_pair + 1) * LANES
            ]
    arrivals = []
    for k in range(15):
        to = (seq + k + 1) % 16
        arrivals.append(remote(heads_out.at[to // 2, to % 2], grads.at[seq], in_send.at[k], in_recv.at[k], others[k]))
        arrivals[-1].start()
    own_heads = pltpu.make_async_copy(heads_out.at[pair, row], grads.at[seq], own_sem.at[1])
    own_heads.start()

    fetches[MEM_K_AT].wait()
    fetches[MEM_V_AT].wait()

    def memory_block(at, carry):
        there = pl.ds(4 * at, 4)
        terms = dot_right(key_terms[there].reshape(8 * M_DEV, D), weight(MEM_K_AT))
        terms += dot_right(value_terms[there].reshape(8 * M_DEV, D), weight(MEM_V_AT))
        memory_part[at] = terms.astype(BF16).reshape(2, 2, 2 * M_DEV, D)
        return carry

    lax.fori_loop(0, 4, memory_block, 0)
    memory_first.start()
    small_second.wait()
    small_pair[...] = small_mine[:, :, x] + small_x[...]
    small_third.start()
    memory_first.wait()
    memory_mine[...] = memory_part[:, :, core] + memory_core[...]
    memory_second.start()
    for name in ("arrived", "attended", "inverse", "docs"):
        fetches[name].wait()
    own_heads.wait()
    for copy in arrivals:
        copy.wait()

    pad_row = lax.broadcasted_iota(jnp.int32, (64, block), 0) % 32
    prefix_key_stack = stack_heads(small_full[pair, 0:32])
    prefix_value_stack = stack_heads(small_full[pair, 32:64])

    def head_rows(at, count):
        there = delta[:, pl.ds(pl.multiple_of(at * block, block), block)]
        return jnp.concatenate(
            [jnp.broadcast_to(there[0:1], (count, block)), jnp.broadcast_to(there[1:2], (count, block))],
            axis=0,
        )

    prefix_mine[...] = jnp.zeros(prefix_mine.shape, F32)

    def prepare(at, carry):
        here = pl.ds(at * block, block)
        grad = grads[pl.ds(2 * at, 2)].reshape(block, LANES).astype(F32) * inverse[here]
        low = grad.astype(BF16)
        grad_low[here] = low
        delta[:, pl.ds(pl.multiple_of(at * block, block), block)] = rows_in_lanes(grad * attended[here])
        queries = arrived[pl.ds(2 * at, 2), 0].reshape(block, LANES)
        e = jnp.exp(dot_right(prefix_key_stack, queries) * score_scale)
        e = jnp.where(pad_row < PREFIX, e, 0.0)
        slopes = (e * (dot_right(prefix_value_stack, low) - head_rows(at, 32))).astype(BF16)
        prefix_mine[0] += merge_heads(dot_nn(slopes, queries)) * score_scale
        prefix_mine[1] += merge_heads(dot_nn(e.astype(BF16), low))
        query_grads[here] = dot_left(slopes, prefix_key_stack)
        return carry

    lax.fori_loop(0, 8, prepare, 0)
    prefix_first.wait()
    prefix_line[...] = cross_prefix[:, y] + prefix_y[...]
    for copy in prefix_second:
        copy.start()
    prefix_all[z] = prefix_line[z]
    small_third.wait()
    small_line[...] = small_pair[:, y] + small_y[...]
    for copy in small_fourth:
        copy.start()
    small_all[z] = small_line[z]

    away = (
        lax.broadcasted_iota(jnp.int32, (block, block), 0)
        - lax.broadcasted_iota(jnp.int32, (block, block), 1)
    )

    def send_block(part, count, at, send, recv):
        for half in range(2):
            to = 2 * at + half
            source = staged.at[to, pl.ds(part, count)]
            mine = gathered.at[pair, row, pl.ds(part, count)]

            @pl.when(to != seq)
            def _():
                remote(source, mine, send.at[to], recv.at[seq], (to, x)).start()

            @pl.when(to == seq)
            def _():
                pltpu.make_async_copy(source, mine, own_sem.at[2 + part]).start()

    def one_block(step, carry):
        key_at = (step + pair) % 8
        keys = stack_heads(arrived[pl.ds(2 * key_at, 2), 1].reshape(block, LANES))
        values = stack_heads(arrived[pl.ds(2 * key_at, 2), 2].reshape(block, LANES))
        key_docs = docs_column[pl.ds(key_at * block, block)]
        key_docs = jnp.concatenate([key_docs, key_docs], axis=1)
        key_grads[...] = jnp.zeros(key_grads.shape, F32)
        value_grads[...] = jnp.zeros(value_grads.shape, F32)

        def one_tile(at, carry):
            here = pl.ds(at * block, block)
            queries = arrived[pl.ds(2 * at, 2), 0].reshape(block, LANES)
            low = grad_low[here]
            query_docs = docs_row[0:1, pl.ds(pl.multiple_of(at * block, block), block)]
            allowed = (key_docs == query_docs) & (away <= (at - key_at) * block)
            e = jnp.exp(dot_right(keys, queries) * score_scale).reshape(2, block, block)
            e = jnp.where(allowed[None], e, 0.0).reshape(2 * block, block)
            slopes = (e * (dot_right(values, low) - head_rows(at, block))).astype(BF16)
            key_grads[...] += dot_nn(slopes, queries)
            value_grads[...] += dot_nn(e.astype(BF16), low)
            query_grads[here] += dot_left(slopes, keys)
            return carry

        lax.fori_loop(key_at, 8, one_tile, 0)
        there = pl.ds(2 * key_at, 2)
        staged[there, 1] = (merge_heads(key_grads[...]) * score_scale).astype(BF16).reshape(2, S_DEV, LANES)
        staged[there, 2] = merge_heads(value_grads[...]).astype(BF16).reshape(2, S_DEV, LANES)
        send_block(1, 2, key_at, out_send, out_recv)
        return carry

    lax.fori_loop(0, 2, one_block, 0)
    memory_second.wait()
    memory_line[...] = memory_mine[:, y] + memory_y[...]
    for copy in memory_third:
        copy.start()
    memory_all[z] = memory_line[z]
    lax.fori_loop(2, 8, one_block, 0)

    def last_block(step, carry):
        at = (step + pair) % 8
        result = (query_grads[pl.ds(at * block, block)] * score_scale).astype(BF16)
        staged[pl.ds(2 * at, 2), 0] = result.reshape(2, S_DEV, LANES)
        send_block(0, 1, at, query_send, query_recv)
        return carry

    lax.fori_loop(0, 8, last_block, 0)
    small_first.wait_send()
    for copy in prefix_second:
        copy.wait()
    for part in range(2):
        prefix_mine[2 + part] = sum(prefix_all[k, part] for k in range(4))
    prefix_quad[core * 2 + x] = prefix_mine[...]
    quad_copies = [
        remote(prefix_mine, prefix_quad.at[core * 2 + x], quad_send.at[k], quad_recv.at[k], peer)
        for k, peer in enumerate((place.other_core(), place.along_x(), place.diagonal()))
    ]
    for copy in quad_copies:
        copy.start()
    for copy in small_fourth:
        copy.wait()
    total = small_all[0].astype(F32)
    for k in range(1, 4):
        total += small_all[k].astype(F32)
    down_grad[...] = total[:, :ADAPTER]
    up_grad[:, :ADAPTER] = total[:16, ADAPTER:]
    up_grad[:, ADAPTER:] = total[16:, ADAPTER:]
    for copy in memory_third:
        copy.wait()
    total = memory_all[0].astype(F32)
    for k in range(1, 4):
        total += memory_all[k].astype(F32)
    memory_grad[...] = total
    for copy in quad_copies:
        copy.wait()
    prefix_sum[...] = (prefix_quad[0] + prefix_quad[1]) + (prefix_quad[2] + prefix_quad[3])

    pltpu.make_async_copy(staged.at[seq, pl.ds(1, 2)], gathered.at[pair, row, pl.ds(1, 2)], own_sem.at[3]).wait()
    for other, _ in others:
        remote(
            staged.at[other, pl.ds(1, 2)], gathered.at[other // 2, other % 2, pl.ds(1, 2)],
            out_send.at[other], out_recv.at[other], (other, x),
        ).wait()

    def part_grad(part, at):
        fetches[at].wait()
        joined = jnp.concatenate([gathered[k, :, part].reshape(tokens, LANES) for k in range(PAIRS)], axis=1)
        return dot_right(joined, weight(at))

    input_grad[...] = pull[...] + part_grad(1, K_AT) + part_grad(2, V_AT)
    pltpu.make_async_copy(staged.at[seq, pl.ds(0, 1)], gathered.at[pair, row, pl.ds(0, 1)], own_sem.at[2]).wait()
    for other, _ in others:
        remote(
            staged.at[other, pl.ds(0, 1)], gathered.at[other // 2, other % 2, pl.ds(0, 1)],
            query_send.at[other], query_recv.at[other], (other, x),
        ).wait()
    input_grad[...] += part_grad(0, Q_AT)


def second_call(*operands):
    length = 16 * S_DEV
    tokens = 2 * S_DEV
    dma = pltpu.SemaphoreType.DMA
    shape = jax.ShapeDtypeStruct
    return pl.pallas_call(
        second_kernel,
        out_shape=(
            shape((tokens, D), F32),
            shape((2 * M_DEV, D), F32),
            shape((32, ADAPTER), F32),
            shape((16, D), F32),
            shape((4, 32, LANES), F32),
        ),
        in_specs=[whole()] * 9 + [whole(pl.ANY)] * 8,
        out_specs=(whole(),) * 5,
        scratch_shapes=[
            pltpu.VMEM((8, 32, 32, D), BF16),
            pltpu.VMEM((16, 2, M_DEV, 2 * D), BF16),
            pltpu.VMEM((tokens, D), F32),
            pltpu.VMEM((16, 3, S_DEV, LANES), BF16),
            pltpu.VMEM((length, LANES), F32),
            pltpu.VMEM((length, LANES), F32),
            pltpu.VMEM((length, LANES), F32),
            pltpu.VMEM((tokens, D), F32),
            pltpu.VMEM((2, S_DEV, D), F32),
            pltpu.VMEM((2, S_DEV, D), BF16),
            pltpu.VMEM((16, 2, M_DEV, D), BF16),
            pltpu.VMEM((16, 2, M_DEV, D), BF16),
            pltpu.VMEM((4, 2, 2, 32, LANES), F32),
            pltpu.VMEM((4, 2, 2, 32, D), BF16),
            pltpu.VMEM((4, 2, 2, 32, D), BF16),
            pltpu.VMEM((4, 2, 32, D), BF16),
            pltpu.VMEM((4, 2, 32, D), BF16),
            pltpu.VMEM((4, 32, D), BF16),
            pltpu.VMEM((4, 32, D), BF16),
            pltpu.VMEM((4, 32, D), BF16),
            pltpu.VMEM((4, 2, 2, 2 * M_DEV, D), BF16),
            pltpu.VMEM((4, 2, 2 * M_DEV, D), BF16),
            pltpu.VMEM((4, 2, 2 * M_DEV, D), BF16),
            pltpu.VMEM((4, 2 * M_DEV, D), BF16),
            pltpu.VMEM((4, 2 * M_DEV, D), BF16),
            pltpu.VMEM((4, 2 * M_DEV, D), BF16),
            pltpu.VMEM((4, 2, 32, LANES), F32),
            pltpu.VMEM((4, 2, 32, LANES), F32),
            pltpu.VMEM((4, 2, 32, LANES), F32),
            pltpu.VMEM((4, 32, LANES), F32),
            pltpu.VMEM((4, 4, 32, LANES), F32),
            pltpu.VMEM((PAIRS, 2, S_DEV, LANES), BF16),
            pltpu.VMEM((16, S_DEV, LANES), BF16),
            pltpu.VMEM((length, LANES), BF16),
            pltpu.VMEM((8, length), F32),
            pltpu.VMEM((length, LANES), F32),
            pltpu.VMEM((4 * S_DEV, LANES), F32),
            pltpu.VMEM((4 * S_DEV, LANES), F32),
            pltpu.VMEM((16, 3, S_DEV, LANES), BF16),
            pltpu.VMEM((PAIRS, 2, 3, S_DEV, LANES), BF16),
            dma((14,)), dma((4,)), dma((3,)), dma((3,)), dma((3,)), dma((3,)), dma((4,)), dma((4,)), dma((4,)), dma((4,)),
            dma((4,)), dma((4,)), dma((3,)), dma((3,)),
            dma((15,)), dma((15,)), dma((16,)), dma((16,)), dma((16,)), dma((16,)),
        ],
        compiler_params=params(1),
        name="second",
    )(*operands)


def gelu_parts(pre):
    upper = 0.5 * (1.0 + lax.erf(pre * (0.5 ** 0.5)))
    return upper


def gelu_slope(pre):
    return gelu_parts(pre) + pre * jnp.exp(-0.5 * pre * pre) * (1.0 / math.sqrt(2.0 * math.pi))


def norm_back_rows(resid, gain, upstream):
    middle = jnp.mean(resid, axis=-1, keepdims=True)
    centred = resid - middle
    scale = lax.rsqrt(jnp.mean(centred * centred, axis=-1, keepdims=True) + 1e-05)
    unit = centred * scale
    pulled = upstream * gain
    return scale * (
        pulled - jnp.mean(pulled, axis=-1, keepdims=True) - unit * jnp.mean(pulled * unit, axis=-1, keepdims=True)
    )


def feed_kernel(
    normed, cotangent, gain, inner, outer, mixed,
    layer_out, second_grad, small_grads,
    low, pre, adapter_pre, total, feed_low,
):
    step = pl.program_id(0)
    down = mixed[:, :, :ADAPTER].reshape(D, ADAPTER)
    up_left = mixed[:, :16, ADAPTER:].reshape(ADAPTER, ADAPTER)
    up_right = mixed[:, 16:, ADAPTER:].reshape(ADAPTER, ADAPTER)
    half = ADAPTER

    @pl.when(step == 0)
    def _():
        low[...] = normed[...].astype(BF16)
        adapter_pre[...] = dot_nn(low[...], down)
        act = adapter_pre[...]
        act = (act * gelu_parts(act)).astype(BF16)
        total[:, :half] = normed[:, :half] + 4.0 * dot_nn(act, up_left)
        total[:, half:] = normed[:, half:] + 4.0 * dot_nn(act, up_right)

    @pl.when(step < 4)
    def _():
        hidden = dot_nn(low[...], inner[...].reshape(D, D))
        pre[jnp.minimum(step, 3)] = hidden
        act = (hidden * gelu_parts(hidden)).astype(BF16)
        total[...] += dot_nn(act, outer[...].reshape(D, D))

    @pl.when(step == 3)
    def _():
        resid = total[...]
        layer_out[...] = norm_rows(resid, gain[...]).astype(BF16)
        third_grad = norm_back_rows(resid, gain[...], cotangent[...].astype(F32))
        feed_low[...] = third_grad.astype(BF16)
        adapter_low = (4.0 * third_grad).astype(BF16)
        act = adapter_pre[...]
        upper = gelu_parts(act)
        slope = gelu_slope(act)
        act = (act * upper).astype(BF16)
        grad = dot_right(adapter_low[:, :half], up_left) + dot_right(adapter_low[:, half:], up_right)
        grad = (slope * grad).astype(BF16)
        second_grad[...] = third_grad + dot_right(grad, down)
        small_grads[:, :, :half] = dot_left(low[...], grad).astype(BF16).reshape(32, 32, half)
        small_grads[:, :16, half:] = dot_left(act, adapter_low[:, :half]).astype(BF16).reshape(32, 16, half)
        small_grads[:, 16:, half:] = dot_left(act, adapter_low[:, half:]).astype(BF16).reshape(32, 16, half)

    @pl.when(step >= 4)
    def _():
        hidden = pre[jnp.clip(7 - step, 0, 3)]
        grad = dot_right(feed_low[...], outer[...].reshape(D, D))
        grad = (gelu_slope(hidden) * grad).astype(BF16)
        second_grad[...] += dot_right(grad, inner[...].reshape(D, D))


def feed_forward_backward(normed, cotangent, gain, weights):
    tokens = normed.shape[0]
    at = lambda step: jnp.minimum(step, 7 - step)
    still = lambda step: (0, 0)
    rows = pl.BlockSpec((tokens, D), still)
    return pl.pallas_call(
        feed_kernel,
        grid=(8,),
        out_shape=(
            jax.ShapeDtypeStruct((tokens, D), BF16),
            jax.ShapeDtypeStruct((tokens, D), F32),
            jax.ShapeDtypeStruct((32, 32, D), BF16),
        ),
        in_specs=[
            rows, rows, pl.BlockSpec((1, D), still),
            pl.BlockSpec((32, 32, D), lambda step: (0, INNER_AT // 32 + at(step), 0)),
            pl.BlockSpec((8, 128, D), lambda step: (at(step), OUTER_AT // 128, 0)),
            pl.BlockSpec((32, 32, D), lambda step: (0, MIXED_AT // 32, 0)),
        ],
        out_specs=(rows, rows, pl.BlockSpec((32, 32, D), lambda step: (0, 0, 0))),
        scratch_shapes=[
            pltpu.VMEM((tokens, D), BF16),
            pltpu.VMEM((4, tokens, D), F32),
            pltpu.VMEM((tokens, ADAPTER), F32),
            pltpu.VMEM((tokens, D), F32),
            pltpu.VMEM((tokens, D), BF16),
        ],
        compiler_params=params(),
        name="feed",
    )(normed, cotangent, gain, weights, weights, weights)


def fast_device(
    inputs, memory, out_grad, token_docs, memory_docs, self_project, self_output, cross_query,
    cross_memory, cross_output, inner_weight, outer_weight, adapter_down, adapter_up, norm_gains, prefixes,
):
    seq, x = lax.axis_index("seq"), lax.axis_index("rows")
    tokens = 2 * S_DEV
    mixed = jnp.concatenate(
        [adapter_down, jnp.concatenate([adapter_up[:, :ADAPTER], adapter_up[:, ADAPTER:]], axis=0)], axis=1
    )
    lane_group = lax.broadcasted_iota(jnp.int32, (1, LANES), 1) // 32
    small = jnp.concatenate([
        jnp.pad(prefixes, ((0, 0), (0, 2), (0, 0))).reshape(128, 32), jnp.pad(norm_gains, ((0, 13), (0, 0)))
    ])
    small = jnp.where(lane_group == (seq % 2) * 2 + x, jnp.tile(small, (1, 4)), jnp.zeros((), BF16))
    memory_line = jnp.where(lane_group == seq % 4, jnp.tile(memory_docs, (1, 4)), 0)
    docs = jnp.concatenate([token_docs, memory_line, jnp.zeros((4, LANES), jnp.int32)]).astype(F32)
    (
        full, memory_pairs, docs_column, arrived, pair_attended, pair_inverse,
        first_resid, cross_queries, crossed, cross_inverse, small_full, docs_all, docs_row, second_resid, second_norm,
    ) = first_call(
        inputs, memory.reshape(2, M_DEV, D), small, docs,
        self_project, self_output, cross_query, cross_memory, cross_output, inner_weight, outer_weight, mixed,
    )

    third_gain = small_full[:, 130].reshape(1, D).astype(F32)
    layer_out, second_grad, small_grads = feed_forward_backward(
        second_norm, out_grad.reshape(tokens, D), third_gain, full
    )
    input_grad, memory_grad, down_grad, up_grad, prefix_sum = second_call(
        second_grad, second_resid, small_full, docs, docs_all, docs_row, crossed, cross_inverse, cross_queries,
        full, memory_pairs, first_resid, arrived, pair_attended, pair_inverse, docs_column,
        small_grads.reshape(4, 2, 2, 2, 32, D),
    )
    prefix_grad = lax.dynamic_slice_in_dim(prefix_sum[:, :PREFIX], 32 * ((seq % 2) * 2 + x), 32, 2)
    return (
        layer_out.reshape(2, S_DEV, D),
        input_grad.reshape(2, S_DEV, D),
        memory_grad.reshape(2, M_DEV, D),
        prefix_grad,
        down_grad,
        up_grad,
    )


def solution(mesh):
    placed = (
        P("rows", "seq", None),
        P("rows", "seq", None),
        P("rows", "seq", None),
        P("rows", "seq"),
        P("rows", "seq"),
        P(("seq", "rows"), None),
        P(("seq", "rows"), None),
        P(("seq", "rows"), None),
        P(("seq", "rows"), None),
        P(("seq", "rows"), None),
        P(("seq", "rows"), None),
        P(("seq", "rows"), None),
        P(("seq", "rows"), None),
        P(("seq", "rows"), None),
        P(None, ("seq", "rows")),
        P(None, None, ("seq", "rows")),
    )
    small_slice = mesh.shape["seq"] == 16 and mesh.shape["rows"] == 2
    return jax.shard_map(
        fast_device if small_slice else per_device,
        mesh=mesh,
        in_specs=placed,
        out_specs=(
            P("rows", "seq", None),
            P("rows", "seq", None),
            P("rows", "seq", None),
            P(None, None, ("seq", "rows")),
            P(("seq", "rows"), None),
            P(("seq", "rows"), None),
        ),
        check_vma=False,
    )
```

```python
import math

import jax
import jax.numpy as jnp
from jax import lax
from jax.experimental import pallas as pl
from jax.experimental.pallas import tpu as pltpu
from jax.sharding import PartitionSpec as P

D = 1024
HEADS = 16
HEAD_DIM = 64
ADAPTER = 512
PREFIX = 30
S_DEV = 128
M_DEV = 32


score_scale = 0.125
masked_score = -1000000000.0


def heads_of(matrix):
    return matrix.reshape(matrix.shape[0], HEADS, HEAD_DIM)


def dot_right(left, right):
    return lax.dot_general(
        left, right, (((1,), (1,)), ((), ())), preferred_element_type=jnp.float32
    )


def dot_left(left, right):
    return lax.dot_general(
        left, right, (((0,), (0,)), ((), ())), preferred_element_type=jnp.float32
    )


def norm_rows(resid, gain):
    middle = jnp.mean(resid, axis=-1, keepdims=True)
    centred = resid - middle
    spread = jnp.mean(centred * centred, axis=-1, keepdims=True)
    return centred * lax.rsqrt(spread + 1e-05) * gain


def norm_back(resid, gain, upstream):
    unused, pullback = jax.vjp(lambda values: norm_rows(values, gain), resid)
    return pullback(upstream)[0]


def gelu_back(pre_act, upstream):
    unused, pullback = jax.vjp(lambda values: jax.nn.gelu(values, approximate=False), pre_act)
    return pullback(upstream)[0]


def allowed_keys(query_docs, key_docs, query_pos, key_pos, causal):
    allowed = query_docs[:, None] == key_docs[None, :]
    if causal:
        allowed = allowed & (key_pos[None, :] <= query_pos[:, None])
    return allowed


def prefix_terms(queries, prefix_keys, prefix_values):
    scores = (
        jnp.einsum(
            "qhd,phd->hqp", queries, heads_of(prefix_keys), preferred_element_type=jnp.float32
        )
        * score_scale
    )
    weights = jnp.exp(scores)
    summed = jnp.einsum(
        "hqp,phd->qhd",
        weights.astype(jnp.bfloat16),
        heads_of(prefix_values),
        preferred_element_type=jnp.float32,
    )
    return (jnp.sum(weights, axis=-1), summed)


def fold_keys(running, arrived, queries, query_docs, key_docs, query_first, causal):
    key_count = arrived.shape[0]
    block_len = math.gcd(key_count, 512)
    query_count = queries.shape[0]
    query_pos = query_first + jnp.arange(query_count, dtype=jnp.int32)
    key_width = arrived.shape[1] // 2

    def fold_one_block(current, element):
        key_block, block_index = element
        key_first = block_index * block_len

        def compute(present):
            block_docs = lax.dynamic_slice_in_dim(key_docs, key_first, block_len, 0)
            allowed = allowed_keys(
                query_docs,
                block_docs,
                query_pos,
                key_first + jnp.arange(block_len, dtype=jnp.int32),
                causal,
            )
            scores = (
                jnp.einsum(
                    "qhd,khd->hqk",
                    queries,
                    heads_of(key_block[:, :key_width]),
                    preferred_element_type=jnp.float32,
                )
                * score_scale
            )
            weights = jnp.exp(jnp.where(allowed[None], scores, masked_score))
            summed = jnp.einsum(
                "hqk,khd->qhd",
                weights.astype(jnp.bfloat16),
                heads_of(key_block[:, key_width:]),
                preferred_element_type=jnp.float32,
            )
            return (present[0] + jnp.sum(weights, axis=-1), present[1] + summed)

        if causal:
            return (
                lax.cond(
                    key_first <= query_first + query_count - 1, compute, lambda held: held, current
                ),
                None,
            )
        return (compute(current), None)

    running, unused = lax.scan(
        fold_one_block,
        running,
        (
            arrived.reshape(key_count // block_len, block_len, arrived.shape[1]),
            jnp.arange(key_count // block_len, dtype=jnp.int32),
        ),
    )
    return running


def attend_back(
    queries,
    gathered,
    prefix_keys,
    prefix_values,
    grad_out,
    attended,
    totals,
    query_docs,
    key_docs,
    query_first,
    causal,
):
    query_count = queries.shape[0]
    key_count = gathered.shape[0]
    key_width = gathered.shape[1] // 2
    block_len = math.gcd(key_count, 512)
    query_pos = query_first + jnp.arange(query_count, dtype=jnp.int32)
    grad_heads = heads_of(grad_out)
    grad_summed = (grad_heads / totals.T[:, :, None]).astype(jnp.bfloat16)
    row_dot = jnp.sum(grad_heads * heads_of(attended), axis=-1).T / totals
    prefix_key_heads = heads_of(prefix_keys)
    prefix_value_heads = heads_of(prefix_values)
    prefix_weights = jnp.exp(
        jnp.einsum("qhd,phd->hqp", queries, prefix_key_heads, preferred_element_type=jnp.float32)
        * score_scale
    )
    prefix_dots = jnp.einsum(
        "qhd,phd->hqp", grad_summed, prefix_value_heads, preferred_element_type=jnp.float32
    )
    prefix_slopes = (prefix_weights * (prefix_dots - row_dot[:, :, None])).astype(jnp.bfloat16)
    query_grad = jnp.einsum(
        "hqp,phd->qhd", prefix_slopes, prefix_key_heads, preferred_element_type=jnp.float32
    )
    key_grad_prefix = (
        jnp.einsum("hqp,qhd->phd", prefix_slopes, queries, preferred_element_type=jnp.float32)
        * score_scale
    ).reshape(-1, D)
    value_grad_prefix = jnp.einsum(
        "hqp,qhd->phd",
        prefix_weights.astype(jnp.bfloat16),
        grad_summed,
        preferred_element_type=jnp.float32,
    ).reshape(-1, D)

    def attend_one_block(current, element):
        key_block, block_index = element
        key_first = block_index * block_len

        def compute(present):
            block_docs = lax.dynamic_slice_in_dim(key_docs, key_first, block_len, 0)
            allowed = allowed_keys(
                query_docs,
                block_docs,
                query_pos,
                key_first + jnp.arange(block_len, dtype=jnp.int32),
                causal,
            )
            key_heads = heads_of(key_block[:, :key_width])
            value_heads = heads_of(key_block[:, key_width:])
            scores = (
                jnp.einsum("qhd,khd->hqk", queries, key_heads, preferred_element_type=jnp.float32)
                * score_scale
            )
            weights = jnp.exp(jnp.where(allowed[None], scores, masked_score))
            dots = jnp.einsum(
                "qhd,khd->hqk", grad_summed, value_heads, preferred_element_type=jnp.float32
            )
            slopes = (weights * (dots - row_dot[:, :, None])).astype(jnp.bfloat16)
            present = present + jnp.einsum(
                "hqk,khd->qhd", slopes, key_heads, preferred_element_type=jnp.float32
            )
            key_grad = (
                jnp.einsum("hqk,qhd->khd", slopes, queries, preferred_element_type=jnp.float32)
                * score_scale
            )
            value_grad = jnp.einsum(
                "hqk,qhd->khd",
                weights.astype(jnp.bfloat16),
                grad_summed,
                preferred_element_type=jnp.float32,
            )
            return (
                present,
                jnp.concatenate(
                    [key_grad.reshape(block_len, D), value_grad.reshape(block_len, D)], axis=1
                ),
            )

        if causal:
            return lax.cond(
                key_first <= query_first + query_count - 1,
                compute,
                lambda held: (held, jnp.zeros((block_len, 2 * D), jnp.float32)),
                current,
            )
        return compute(current)

    query_grad, key_terms = lax.scan(
        attend_one_block,
        query_grad,
        (
            gathered.reshape(key_count // block_len, block_len, gathered.shape[1]),
            jnp.arange(key_count // block_len, dtype=jnp.int32),
        ),
    )
    query_low = (query_grad * score_scale).astype(jnp.bfloat16).reshape(query_count, D)
    key_terms = key_terms.reshape(key_count, 2 * D)
    return (query_low, key_terms, key_grad_prefix, value_grad_prefix, grad_summed, row_dot)


def fetch_all(
    self_project,
    self_output,
    cross_query,
    cross_memory,
    cross_output,
    inner_weight,
    outer_weight,
    adapter_down,
    adapter_up,
    norm_gains,
    prefixes,
):
    return (
        lax.all_gather(self_project, ("seq", "rows"), axis=0, tiled=True),
        lax.all_gather(self_output, ("seq", "rows"), axis=0, tiled=True),
        lax.all_gather(cross_query, ("seq", "rows"), axis=0, tiled=True),
        lax.all_gather(cross_memory, ("seq", "rows"), axis=0, tiled=True),
        lax.all_gather(cross_output, ("seq", "rows"), axis=0, tiled=True),
        lax.all_gather(inner_weight, ("seq", "rows"), axis=0, tiled=True),
        lax.all_gather(outer_weight, ("seq", "rows"), axis=0, tiled=True),
        lax.all_gather(adapter_down, ("seq", "rows"), axis=0, tiled=True),
        lax.all_gather(adapter_up, ("seq", "rows"), axis=0, tiled=True),
        lax.all_gather(norm_gains, ("seq", "rows"), axis=1, tiled=True),
        lax.all_gather(prefixes, ("seq", "rows"), axis=2, tiled=True),
    )


def fetch_again(
    self_project,
    self_output,
    cross_query,
    cross_memory,
    cross_output,
    inner_weight,
    outer_weight,
    adapter_down,
    adapter_up,
    norm_gains,
    prefixes,
):
    return (
        lax.all_gather(self_project, ("seq", "rows"), axis=0, tiled=True),
        lax.all_gather(self_output, ("seq", "rows"), axis=0, tiled=True),
        lax.all_gather(cross_query, ("seq", "rows"), axis=0, tiled=True),
        lax.all_gather(cross_memory, ("seq", "rows"), axis=0, tiled=True),
        lax.all_gather(cross_output, ("seq", "rows"), axis=0, tiled=True),
        lax.all_gather(inner_weight, ("seq", "rows"), axis=0, tiled=True),
        lax.all_gather(outer_weight, ("seq", "rows"), axis=0, tiled=True),
        lax.all_gather(adapter_down, ("seq", "rows"), axis=0, tiled=True),
        lax.all_gather(adapter_up, ("seq", "rows"), axis=0, tiled=True),
        lax.all_gather(norm_gains, ("seq", "rows"), axis=1, tiled=True),
        lax.all_gather(prefixes, ("seq", "rows"), axis=2, tiled=True),
    )


def forward_row(tokens, memory_rows, query_docs, token_docs, memory_docs, query_first, weights):
    (
        self_project,
        self_output,
        cross_query,
        cross_memory,
        cross_output,
        inner_weight,
        outer_weight,
        adapter_down,
        adapter_up,
        norm_gains,
        prefixes,
    ) = weights
    gains = norm_gains.astype(jnp.float32)
    projected = jnp.dot(tokens, self_project, preferred_element_type=jnp.float32).astype(
        jnp.bfloat16
    )
    queries = heads_of(projected[:, :D])
    local_pairs = projected[:, D:]
    start_self = prefix_terms(queries, prefixes[0], prefixes[1])
    totals, summed = fold_keys(
        start_self,
        lax.all_gather(local_pairs, "seq", axis=0, tiled=True),
        queries,
        query_docs,
        token_docs,
        query_first,
        True,
    )
    attended = (summed / totals.T[:, :, None]).reshape(-1, D)
    first_resid = tokens.astype(jnp.float32) + jnp.dot(
        attended.astype(jnp.bfloat16), self_output, preferred_element_type=jnp.float32
    )
    first_norm = norm_rows(first_resid, gains[0])
    first_low = first_norm.astype(jnp.bfloat16)
    cross_queries = heads_of(
        jnp.dot(first_low, cross_query, preferred_element_type=jnp.float32).astype(jnp.bfloat16)
    )
    memory_pairs = jnp.dot(memory_rows, cross_memory, preferred_element_type=jnp.float32).astype(
        jnp.bfloat16
    )
    start_cross = prefix_terms(cross_queries, prefixes[2], prefixes[3])
    cross_totals, cross_summed = fold_keys(
        start_cross,
        lax.all_gather(memory_pairs, "seq", axis=0, tiled=True),
        cross_queries,
        query_docs,
        memory_docs,
        query_first,
        False,
    )
    crossed = (cross_summed / cross_totals.T[:, :, None]).reshape(-1, D)
    second_resid = first_norm + jnp.dot(
        crossed.astype(jnp.bfloat16), cross_output, preferred_element_type=jnp.float32
    )
    second_norm = norm_rows(second_resid, gains[1])
    second_low = second_norm.astype(jnp.bfloat16)
    hidden_pre = jnp.dot(second_low, inner_weight, preferred_element_type=jnp.float32)
    hidden_act = jax.nn.gelu(hidden_pre, approximate=False).astype(jnp.bfloat16)
    adapter_pre = jnp.dot(second_low, adapter_down, preferred_element_type=jnp.float32)
    adapter_act = jax.nn.gelu(adapter_pre, approximate=False).astype(jnp.bfloat16)
    third_resid = (
        second_norm
        + jnp.dot(hidden_act, outer_weight, preferred_element_type=jnp.float32)
        + 4.0 * jnp.dot(adapter_act, adapter_up, preferred_element_type=jnp.float32)
    )
    layer_out = norm_rows(third_resid, gains[2]).astype(jnp.bfloat16)
    saved = (
        queries,
        local_pairs,
        totals,
        attended,
        first_resid,
        cross_queries,
        memory_pairs,
        cross_totals,
        crossed,
        second_resid,
        second_low,
        hidden_pre,
        adapter_pre,
        adapter_act,
        third_resid,
    )
    return (layer_out, saved)


def backward_row(cotangent, saved, weights, query_docs, token_docs, memory_docs, query_first):
    (
        self_project,
        self_output,
        cross_query,
        cross_memory,
        cross_output,
        inner_weight,
        outer_weight,
        adapter_down,
        adapter_up,
        norm_gains,
        prefixes,
    ) = weights
    (
        queries,
        local_pairs,
        totals,
        attended,
        first_resid,
        cross_queries,
        memory_pairs,
        cross_totals,
        crossed,
        second_resid,
        second_low,
        hidden_pre,
        adapter_pre,
        adapter_act,
        third_resid,
    ) = saved
    gains = norm_gains.astype(jnp.float32)
    third_grad = norm_back(third_resid, gains[2], cotangent.astype(jnp.float32))
    feed_low = third_grad.astype(jnp.bfloat16)
    adapter_low = (4.0 * third_grad).astype(jnp.bfloat16)
    hidden_grad = gelu_back(hidden_pre, dot_right(feed_low, outer_weight)).astype(jnp.bfloat16)
    up_grad = dot_left(adapter_act, adapter_low)
    adapter_grad = gelu_back(adapter_pre, dot_right(adapter_low, adapter_up)).astype(jnp.bfloat16)
    down_grad = dot_left(second_low, adapter_grad)
    second_grad = (
        third_grad + dot_right(hidden_grad, inner_weight) + dot_right(adapter_grad, adapter_down)
    )
    second_resid_grad = norm_back(second_resid, gains[1], second_grad)
    self_all, memory_all = (
        lax.all_gather(local_pairs, "seq", axis=0, tiled=True),
        lax.all_gather(memory_pairs, "seq", axis=0, tiled=True),
    )
    cross_out_grad = dot_right(second_resid_grad.astype(jnp.bfloat16), cross_output)
    (
        cross_query_low,
        memory_terms,
        cross_key_prefix,
        cross_value_prefix,
        cross_summed_grad,
        cross_dot,
    ) = attend_back(
        cross_queries,
        memory_all,
        prefixes[2],
        prefixes[3],
        cross_out_grad,
        crossed,
        cross_totals,
        query_docs,
        memory_docs,
        query_first,
        False,
    )
    first_grad = second_resid_grad + dot_right(cross_query_low, cross_query)
    first_resid_grad = norm_back(first_resid, gains[0], first_grad)
    self_out_grad = dot_right(first_resid_grad.astype(jnp.bfloat16), self_output)
    query_low, self_terms, self_key_prefix, self_value_prefix, self_summed_grad, self_dot = (
        attend_back(
            queries,
            self_all,
            prefixes[0],
            prefixes[1],
            self_out_grad,
            attended,
            totals,
            query_docs,
            token_docs,
            query_first,
            True,
        )
    )
    self_sums, memory_sums = (
        lax.psum_scatter(
            self_terms.astype(jnp.bfloat16), "seq", scatter_dimension=0, tiled=True
        ).astype(jnp.float32),
        lax.psum_scatter(
            memory_terms.astype(jnp.bfloat16), "seq", scatter_dimension=0, tiled=True
        ).astype(jnp.float32),
    )
    project_grad = jnp.concatenate([query_low, self_sums.astype(jnp.bfloat16)], axis=1)
    input_grad = first_resid_grad + dot_right(project_grad, self_project)
    memory_grad = dot_right(memory_sums.astype(jnp.bfloat16), cross_memory)
    prefix_grad = jnp.stack(
        [self_key_prefix, self_value_prefix, cross_key_prefix, cross_value_prefix]
    )
    return (input_grad, memory_grad, (down_grad, up_grad, prefix_grad))


def per_device(
    inputs,
    memory,
    out_grad,
    token_docs,
    memory_docs,
    self_project,
    self_output,
    cross_query,
    cross_memory,
    cross_output,
    inner_weight,
    outer_weight,
    adapter_down,
    adapter_up,
    norm_gains,
    prefixes,
):
    docs_full, memory_full = (
        lax.all_gather(token_docs, "seq", axis=1, tiled=True),
        lax.all_gather(memory_docs, "seq", axis=1, tiled=True),
    )
    query_first = lax.axis_index("seq") * inputs.shape[1]
    outputs = []
    input_grads = []
    memory_grads = []
    adjusted_grads = None
    for row_index in range(inputs.shape[0]):
        weights = fetch_all(
            self_project,
            self_output,
            cross_query,
            cross_memory,
            cross_output,
            inner_weight,
            outer_weight,
            adapter_down,
            adapter_up,
            norm_gains,
            prefixes,
        )
        layer_out, saved = forward_row(
            inputs[row_index],
            memory[row_index],
            token_docs[row_index],
            docs_full[row_index],
            memory_full[row_index],
            query_first,
            weights,
        )
        weights_back = fetch_again(
            self_project,
            self_output,
            cross_query,
            cross_memory,
            cross_output,
            inner_weight,
            outer_weight,
            adapter_down,
            adapter_up,
            norm_gains,
            prefixes,
        )
        input_grad, memory_grad, row_grads = backward_row(
            out_grad[row_index],
            saved,
            weights_back,
            token_docs[row_index],
            docs_full[row_index],
            memory_full[row_index],
            query_first,
        )
        shares = (
            lax.psum_scatter(row_grads[0], ("seq", "rows"), scatter_dimension=0, tiled=True),
            lax.psum_scatter(row_grads[1], ("seq", "rows"), scatter_dimension=0, tiled=True),
            lax.psum_scatter(row_grads[2], ("seq", "rows"), scatter_dimension=2, tiled=True),
        )
        if adjusted_grads is None:
            adjusted_grads = shares
        else:
            adjusted_grads = tuple(
                (former + latter for former, latter in zip(adjusted_grads, shares))
            )
        outputs.append(layer_out)
        input_grads.append(input_grad)
        memory_grads.append(memory_grad)
    return (
        jnp.stack(outputs),
        jnp.stack(input_grads),
        jnp.stack(memory_grads),
        adjusted_grads[2],
        adjusted_grads[0],
        adjusted_grads[1],
    )


MESH_ID = pl.DeviceIdType.MESH
F32 = jnp.float32
BF16 = jnp.bfloat16
VMEM_BYTES = 60 * 1024 * 1024
PAIRS = HEADS // 2
LANES = 2 * HEAD_DIM
Q_AT, K_AT, V_AT, SELF_OUT_AT, CROSS_Q_AT, MEM_K_AT, MEM_V_AT, CROSS_OUT_AT = range(0, 256, 32)
INNER_AT, OUTER_AT, MIXED_AT = 256, 384, 512
ALL_ROWS = 544
SMALL_ROWS = 144
PIECE_ROWS = 16
GAP = 6
LEAD = 4
SENDS = 2
Z_LAST = ()
WAIT_TICKS = 4
STEP_TICKS = 2


def whole(space=pltpu.VMEM):
    return pl.BlockSpec(memory_space=space)


def params(collective_id=None):
    if collective_id is None:
        return pltpu.CompilerParams(vmem_limit_bytes=VMEM_BYTES)
    return pltpu.CompilerParams(
        vmem_limit_bytes=VMEM_BYTES, collective_id=collective_id, has_side_effects=True
    )


def remote(src, dst, send_sem, recv_sem, device):
    return pltpu.make_async_remote_copy(
        src_ref=src, dst_ref=dst, send_sem=send_sem, recv_sem=recv_sem,
        device_id=device, device_id_type=MESH_ID,
    )


def greet(peers):
    barrier = pltpu.get_barrier_semaphore()
    for peer in peers:
        pl.semaphore_signal(barrier, inc=1, device_id=peer, device_id_type=MESH_ID)
    pl.semaphore_wait(barrier, len(peers))


def dot_nn(left, right):
    return lax.dot_general(left, right, (((1,), (0,)), ((), ())), preferred_element_type=F32)


class Place:
    def __init__(self):
        self.seq, self.x = lax.axis_index("seq"), lax.axis_index("rows")
        self.z, self.y, self.core = self.seq // 4, (self.seq // 2) % 2, self.seq % 2
        self.pair, self.row = self.seq // 2, self.seq % 2

    def device(self, z, y, core, x):
        return ((z * 2 + y) * 2 + core, x)

    def along_z(self, step):
        return self.device((self.z + step) % 4, self.y, self.core, self.x)

    def along_y(self):
        return self.device(self.z, 1 - self.y, self.core, self.x)

    def along_x(self):
        return self.device(self.z, self.y, self.core, 1 - self.x)

    def other_core(self):
        return self.device(self.z, self.y, 1 - self.core, self.x)

    def diagonal(self):
        return self.device(self.z, self.y, 1 - self.core, 1 - self.x)

    def others(self):
        return [((self.seq + step) % 16, self.x) for step in range(1, 16)]


class Gather:
    def __init__(self, place, full, local_sem, sems, gap):
        self.place, self.full, self.local_sem, self.sems, self.gap = place, full, local_sem, sems, gap
        self.stages = []
        self.waiting = []
        self.cut = 1
        self.tick_at = 0

    def copies(self, level, source, target, device, slot):
        k = len(self.stages)
        return remote(source, target, self.sems[2 * level].at[k, slot], self.sems[2 * level + 1].at[k, slot], device)

    def add(self, source, first, count, piece=PIECE_ROWS):
        for from_row in range(0, count, piece):
            self.add_piece(source.at[pl.ds(from_row, piece)], first + from_row, piece)
        return len(self.stages) - 1

    def add_piece(self, source, first, count):
        at, full = self.place, self.full
        z, y, core, x = at.z, at.y, at.core, at.x
        rows = pl.ds(first, count)
        mine = full.at[z, y, core, x, rows]
        k = len(self.stages)
        if k in Z_LAST:
            plane = full.at[z, :, core, :, rows]
            first_way, then_way = (at.along_x(), at.along_y()) if k % 2 else (at.along_y(), at.along_x())
            line = full.at[z, y, core, :, rows] if k % 2 else full.at[z, :, core, x, rows]
            self.stages.append((
                pltpu.make_async_copy(source, mine, self.local_sem.at[k]),
                [self.copies(0, source, mine, first_way, 0)],
                [self.copies(1, line, line, then_way, 0)],
                [self.copies(2, plane, plane, at.along_z(d + 1), d) for d in range(3)],
                [self.copies(3, full.at[:, :, core, :, rows], full.at[:, :, core, :, rows], at.other_core(), 0)],
            ))
            return
        cut = self.cut
        near, far = pl.ds(0, cut), pl.ds(cut, 4 - cut)
        near1, far1 = full.at[near, y, core, x, rows], full.at[far, y, core, x, rows]
        near2, far2 = full.at[near, y, core, :, rows], full.at[far, :, core, x, rows]
        half = full.at[:, :, core, :, rows]
        self.stages.append((
            pltpu.make_async_copy(source, mine, self.local_sem.at[len(self.stages)]),
            [self.copies(0, source, mine, at.along_z(d + 1), d) for d in range(3)],
            [self.copies(1, near1, near1, at.along_x(), 0), self.copies(1, far1, far1, at.along_y(), 1)],
            [self.copies(2, near2, near2, at.along_y(), 0), self.copies(2, far2, far2, at.along_x(), 1)],
            [self.copies(3, half, half, at.other_core(), 0)],
        ))

    def add_memory_row(self, source, full):
        at = self.place
        mine, column, half = full.at[at.z, at.y, at.core], full.at[:, at.y, at.core], full.at[:, :, at.core]
        self.stages.append((
            pltpu.make_async_copy(source, mine, self.local_sem.at[len(self.stages)]),
            [self.copies(0, source, mine, at.along_z(d + 1), d) for d in range(3)],
            [self.copies(1, column, column, at.along_y(), 1)],
            [],
            [self.copies(3, half, half, at.other_core(), 0)],
        ))

    def start(self):
        for stage in self.stages:
            stage[0].start()

    def tick(self, count=1):
        for _ in range(count):
            for level in range(5):
                k = self.tick_at - self.after(level)
                if not 0 <= k < len(self.stages):
                    continue
                if level == 1:
                    self.stages[k][0].wait()
                if level > 0:
                    for copy in self.stages[k][level]:
                        copy.wait_recv()
                if level < 4:
                    for copy in self.stages[k][level + 1]:
                        copy.start()
            self.tick_at += 1
            for _ in range(SENDS):
                if self.waiting:
                    self.waiting.pop(0).start()

    def after(self, level):
        return 0 if level == 0 else LEAD + (level - 1) * self.gap

    def until(self, k):
        while self.tick_at <= k + self.after(4):
            self.tick()

    def finish(self):
        self.until(len(self.stages) - 1)
        for _, *levels in self.stages:
            for level in levels:
                for copy in level:
                    copy.wait_send()


def head_masks():
    lane = lax.broadcasted_iota(jnp.int32, (1, LANES), 1)
    first = (lane < HEAD_DIM).astype(F32).astype(BF16)
    return first, (1.0 - first.astype(F32)).astype(BF16)


def stack_heads(block):
    first, second = head_masks()
    return jnp.concatenate([block * first, block * second], axis=0)


def merge_heads(stacked):
    half = stacked.shape[0] // 2
    lane = lax.broadcasted_iota(jnp.int32, (half, LANES), 1)
    return jnp.where(lane < HEAD_DIM, stacked[:half], stacked[half:])


def rows_in_lanes(values):
    lane = lax.broadcasted_iota(jnp.int32, (8, LANES), 1)
    row = lax.broadcasted_iota(jnp.int32, (8, LANES), 0)
    picks = (lane // HEAD_DIM == row).astype(F32)
    return lax.dot_general(
        picks, values, (((1,), (1,)), ((), ())),
        precision=lax.Precision.HIGHEST, preferred_element_type=F32,
    )


def first_kernel(
    tokens, memory, small, docs,
    project, self_out, cross_q, cross_mem, cross_out, inner, outer, mixed,
    full, memory_full, memory_pairs_far, docs_column_far, arrived_far, attended_far, inverse_far,
    first_resid_far, cross_queries_far, crossed_far, cross_inverse_far,
    small_full, docs_all, docs_row, second_resid, second_norm,
    memory_pairs, docs_column, arrived, attended, inverse, first_resid, cross_queries, crossed, cross_inverse,
    gathered, first_norm, weights, staged, quad, memory_held, result_staged, sums, parts,
    local_sem, send0, recv0, send1, recv1, send2, recv2, send3, recv3,
    fetch_sem, own_sem, quad_send, quad_recv, small_send, small_recv, docs_send, docs_recv,
    head_send, head_recv, out_send, out_recv, leave_sem,
):
    leaving = []

    def leave(*arrays):
        for held, target in arrays:
            leaving.append(pltpu.make_async_copy(held, target, leave_sem.at[len(leaving)]))
            leaving[-1].start()

    place = Place()
    seq, x, pair, row = place.seq, place.x, place.pair, place.row
    others = place.others()
    quad_peers = [place.other_core(), place.along_x(), place.diagonal()]
    greet(others + quad_peers[1:])

    engine = Gather(place, full, local_sem, (send0, recv0, send1, recv1, send2, recv2, send3, recv3), GAP)
    project_done = [
        engine.add(project.at[:, pl.ds(part * D, D)], at, 32) for part, at in enumerate((Q_AT, K_AT, V_AT))
    ]
    for part, at in enumerate((MEM_K_AT, MEM_V_AT)):
        for half in range(2):
            held = pl.ds(16 * half, 16)
            engine.add_memory_row(memory.at[part, held], memory_full.at[:, :, :, part, held])
            memory_done = engine.add(cross_mem.at[held, pl.ds(part * D, D)], at + 16 * half, 16)
    out_done = engine.add(self_out, SELF_OUT_AT, 32)
    query_done = engine.add(cross_q, CROSS_Q_AT, 32)
    cross_done = engine.add(cross_out, CROSS_OUT_AT, 32)
    engine.cut = 2
    for part in range(4):
        engine.add(inner.at[:, pl.ds(part * D, D)], INNER_AT + 32 * part, 32)
    for part in range(4):
        engine.add(outer.at[pl.ds(32 * part, 32)], OUTER_AT + 32 * part, 32)
    engine.add(mixed, MIXED_AT, 32)
    engine.start()
    engine.tick()

    mine = place.core * 2 + x
    quad_copies = [
        remote(small, quad.at[mine], quad_send.at[k], quad_recv.at[k], quad_peers[k]) for k in range(3)
    ]
    own_small = pltpu.make_async_copy(small, quad.at[mine], own_sem.at[0])
    docs_copies = [
        remote(docs, docs_all.at[seq], docs_send.at[k], docs_recv.at[k], others[k]) for k in range(15)
    ]
    own_docs = pltpu.make_async_copy(docs, docs_all.at[seq], own_sem.at[1])
    own_small.start()
    own_docs.start()
    for copy in quad_copies + docs_copies:
        copy.start()
    rows = tokens[...].reshape(2 * S_DEV, D)
    fetches = []
    for part in range(3):
        engine.until(project_done[part])
        fetches.append(pltpu.make_async_copy(full_rows(full, 32 * part), weights.at[part], fetch_sem.at[part]))
        fetches[part].start()
    for part in range(3):
        fetches[part].wait()
        result = dot_nn(rows, weights[part].reshape(D, D)).astype(BF16)
        for at_row in range(2):
            for at_pair in range(PAIRS):
                staged[at_pair, at_row, part] = result[
                    at_row * S_DEV:(at_row + 1) * S_DEV, at_pair * LANES:(at_pair + 1) * LANES
                ]
        engine.tick()
    head_copies = []
    for k in range(15):
        to = (seq + k + 1) % 16
        head_copies.append(
            remote(staged.at[to // 2, to % 2], arrived.at[seq], head_send.at[k], head_recv.at[k], others[k])
        )
    own_heads = pltpu.make_async_copy(staged.at[pair, row], arrived.at[seq], own_sem.at[2])
    own_heads.start()
    engine.waiting = list(head_copies)
    engine.tick(2)
    own_small.wait()
    for copy in quad_copies:
        copy.wait()
    small_full[pair] = (quad[0] + quad[1]) + (quad[2] + quad[3])
    small_copies = []
    for k in range(1, 8):
        to = (((pair + k) % 8) * 2 + place.core, x)
        small_copies.append(
            remote(small_full.at[pair], small_full.at[pair], small_send.at[k], small_recv.at[k], to)
        )
        small_copies[-1].start()
    own_docs.wait()
    for copy in docs_copies:
        copy.wait()

    def spread_docs(at, carry):
        tile = docs_all[at]
        line = jnp.where(row == 0, tile[0:1], tile[1:2])
        docs_row[:, pl.ds(pl.multiple_of(at * S_DEV, S_DEV), S_DEV)] = jnp.broadcast_to(line, (8, S_DEV))
        docs_column[pl.ds(at * S_DEV, S_DEV)] = jnp.transpose(jnp.broadcast_to(line, (S_DEV, LANES)))
        return carry

    lax.fori_loop(0, 16, spread_docs, 0)

    engine.until(memory_done)
    fetch_memory = pltpu.make_async_copy(memory_full, memory_held, own_sem.at[3])
    fetch_memory.start()
    fetches = [
        pltpu.make_async_copy(full_rows(full, at), weights.at[part], fetch_sem.at[part])
        for part, at in enumerate((MEM_K_AT, MEM_V_AT))
    ]
    for fetch in fetches:
        fetch.start()
    fetch_memory.wait()
    for part in range(2):
        fetches[part].wait()

        def project_memory(at, carry):
            held = memory_held[at].reshape(4 * 2 * M_DEV, D)
            result = dot_nn(held, weights[part].reshape(D, D)).astype(BF16)
            memory_pairs[pl.ds(4 * at, 4), :, :, pl.ds(part * D, D)] = result.reshape(4, 2, M_DEV, D)
            return carry

        lax.fori_loop(0, 4, project_memory, 0)
    engine.tick(max(WAIT_TICKS, -(-len(engine.waiting) // SENDS)))
    own_heads.wait()
    for copy in head_copies:
        copy.wait()

    leave((memory_pairs, memory_pairs_far), (docs_column, docs_column_far), (arrived, arrived_far))

    block = 2 * S_DEV
    columns = pl.ds(pl.multiple_of(pair * LANES, LANES), LANES)
    target = gathered.at[row, :, columns]
    away = (
        lax.broadcasted_iota(jnp.int32, (block, block), 1)
        - lax.broadcasted_iota(jnp.int32, (block, block), 0)
    )
    prefix_lane = lax.broadcasted_iota(jnp.int32, (2 * block, 32), 1)
    prefix_keys, prefix_values = small_full[pair, 0:32], small_full[pair, 32:64]

    for step in range(8):
        at = (step + pair) % 8
        queries = stack_heads(arrived[pl.ds(2 * at, 2), 0].reshape(block, LANES))
        query_docs = docs_column[pl.ds(at * block, block)]
        scores = dot_right(queries, prefix_keys) * score_scale
        e = jnp.where(prefix_lane < PREFIX, jnp.exp(scores), 0.0)
        sums[...] = jnp.concatenate([e, jnp.zeros((2 * block, LANES - 32), F32)], axis=1)
        parts[...] = dot_nn(e.astype(BF16), prefix_values)

        def one_tile(key_at, carry):
            keys = arrived[pl.ds(2 * key_at, 2), 1].reshape(block, LANES)
            values = arrived[pl.ds(2 * key_at, 2), 2].reshape(block, LANES)
            key_docs = docs_row[0:1, pl.ds(pl.multiple_of(key_at * block, block), block)]
            same = jnp.concatenate([query_docs, query_docs], axis=1) == key_docs
            allowed = same & (away <= (at - key_at) * block)
            scores = dot_right(queries, keys) * score_scale
            e = jnp.where(allowed[None], jnp.exp(scores).reshape(2, block, block), 0.0)
            e = e.reshape(2 * block, block)
            sums[...] += e[:, :LANES] + e[:, LANES:]
            parts[...] += dot_nn(e.astype(BF16), values)
            return carry

        lax.fori_loop(0, at + 1, one_tile, 0)
        totals = 1.0 / jnp.sum(sums[...], axis=1, keepdims=True)
        result = merge_heads(parts[...] * totals)
        here = pl.ds(at * block, block)
        attended[here] = result
        inverse[here] = merge_heads(jnp.broadcast_to(totals, (2 * block, LANES)))
        result_staged[pl.ds(2 * at, 2)] = result.astype(BF16).reshape(2, S_DEV, LANES)
        for half in range(2):
            to = 2 * at + half

            @pl.when(to != seq)
            def _():
                remote(result_staged.at[to], target, out_send.at[to], out_recv.at[seq], (to, x)).start()

            @pl.when(to == seq)
            def _():
                pltpu.make_async_copy(result_staged.at[to], target, own_sem.at[4]).start()

        engine.tick(STEP_TICKS)

    leave((attended, attended_far), (inverse, inverse_far))

    for copy in small_copies:
        copy.wait()
    engine.until(cross_done)
    fetches = [
        pltpu.make_async_copy(full_rows(full, at), weights.at[part], fetch_sem.at[part])
        for part, at in enumerate((SELF_OUT_AT, CROSS_Q_AT, CROSS_OUT_AT))
    ]
    for fetch in fetches:
        fetch.start()
    gains = [
        jnp.concatenate(
            [small_full[at_pair, 128:144].astype(F32)[part:part + 1] for at_pair in range(PAIRS)], axis=1
        )
        for part in range(2)
    ]
    pltpu.make_async_copy(result_staged.at[seq], target, own_sem.at[4]).wait()
    for other, _ in others:
        remote(result_staged.at[other], target, out_send.at[other], out_recv.at[other], (other, x)).wait()
    fetches[0].wait()
    resid = tokens[...].reshape(2 * S_DEV, D).astype(F32) + dot_nn(
        gathered[...].reshape(2 * S_DEV, D), weights[0].reshape(D, D)
    )
    first_resid[...] = resid
    normed = norm_rows(resid, gains[0])
    first_norm[...] = normed
    engine.tick(STEP_TICKS)
    fetches[1].wait()
    cross_queries[...] = dot_nn(normed.astype(BF16), weights[1].reshape(D, D)).astype(BF16).reshape(2, S_DEV, D)
    engine.tick(STEP_TICKS)
    memory_len = 16 * M_DEV
    cross_prefix_lane = lax.broadcasted_iota(jnp.int32, (2 * S_DEV, 32), 1)
    for at_row in range(2):
        own = jnp.transpose(jnp.broadcast_to(docs[at_row:at_row + 1], (LANES, S_DEV)))
        own = jnp.concatenate([own] * (memory_len // LANES), axis=1)
        lines = [
            sum(docs_all[4 * at + k, 2 + at_row:3 + at_row] for k in range(4)) for at in range(4)
        ]
        allowed = own == jnp.concatenate(lines, axis=1)

        def one_pair(at_pair, carry):
            first = pl.multiple_of(at_pair * LANES, LANES)
            columns, value_columns = pl.ds(first, LANES), pl.ds(pl.multiple_of(first + D, LANES), LANES)
            stacked = stack_heads(cross_queries[at_row, :, columns])
            keys = memory_pairs[:, at_row, :, columns].reshape(memory_len, LANES)
            values = memory_pairs[:, at_row, :, value_columns].reshape(memory_len, LANES)
            scores = dot_right(stacked, small_full[at_pair, 64:96]) * score_scale
            prefix_e = jnp.where(cross_prefix_lane < PREFIX, jnp.exp(scores), 0.0)
            scores = dot_right(stacked, keys) * score_scale
            e = jnp.where(allowed[None], jnp.exp(scores).reshape(2, S_DEV, memory_len), 0.0)
            e = e.reshape(2 * S_DEV, memory_len)
            totals = jnp.sum(e, axis=1, keepdims=True) + jnp.sum(prefix_e, axis=1, keepdims=True)
            totals = 1.0 / totals
            summed = dot_nn(e.astype(BF16), values) + dot_nn(prefix_e.astype(BF16), small_full[at_pair, 96:128])
            crossed[at_row, :, columns] = merge_heads(summed * totals)
            cross_inverse[at_row, :, columns] = merge_heads(jnp.broadcast_to(totals, (2 * S_DEV, LANES)))
            return carry

        lax.fori_loop(0, PAIRS // 2, one_pair, 0)
        engine.tick(STEP_TICKS)
        lax.fori_loop(PAIRS // 2, PAIRS, one_pair, 0)
        engine.tick(STEP_TICKS)
    leave(
        (first_resid, first_resid_far), (cross_queries, cross_queries_far),
        (crossed, crossed_far), (cross_inverse, cross_inverse_far),
    )
    fetches[2].wait()
    resid = first_norm[...] + dot_nn(
        crossed[...].reshape(2 * S_DEV, D).astype(BF16), weights[2].reshape(D, D)
    )
    second_resid[...] = resid
    second_norm[...] = norm_rows(resid, gains[1])
    for copy in leaving:
        copy.wait()
    engine.finish()


def full_rows(full, first):
    return full.at[:, :, :, :, pl.ds(first, 32)]


def first_call(tokens, memory, small, docs, *weights):
    length = 16 * S_DEV
    chunks = 16 * 32 // PIECE_ROWS + 32 // PIECE_ROWS + 4
    dma = pltpu.SemaphoreType.DMA
    shape = jax.ShapeDtypeStruct
    outs = pl.pallas_call(
        first_kernel,
        out_shape=(
            shape((4, 2, 2, 2, ALL_ROWS, D), BF16),
            shape((4, 2, 2, 2, M_DEV, D), BF16),
            shape((16, 2, M_DEV, 2 * D), BF16),
            shape((length, LANES), F32),
            shape((16, 3, S_DEV, LANES), BF16),
            shape((length, LANES), F32),
            shape((length, LANES), F32),
            shape((2 * S_DEV, D), F32),
            shape((2, S_DEV, D), BF16),
            shape((2, S_DEV, D), F32),
            shape((2, S_DEV, D), F32),
            shape((8, SMALL_ROWS, LANES), BF16),
            shape((16, 8, LANES), F32),
            shape((8, length), F32),
            shape((2 * S_DEV, D), F32),
            shape((2 * S_DEV, D), F32),
        ),
        in_specs=[whole(), whole(pl.ANY), whole(), whole()] + [whole(pl.ANY)] * 8,
        out_specs=(whole(pl.ANY),) * 11 + (whole(),) * 5,
        scratch_shapes=[
            pltpu.VMEM((16, 2, M_DEV, 2 * D), BF16),
            pltpu.VMEM((length, LANES), F32),
            pltpu.VMEM((16, 3, S_DEV, LANES), BF16),
            pltpu.VMEM((length, LANES), F32),
            pltpu.VMEM((length, LANES), F32),
            pltpu.VMEM((2 * S_DEV, D), F32),
            pltpu.VMEM((2, S_DEV, D), BF16),
            pltpu.VMEM((2, S_DEV, D), F32),
            pltpu.VMEM((2, S_DEV, D), F32),
            pltpu.VMEM((2, S_DEV, D), BF16),
            pltpu.VMEM((2 * S_DEV, D), F32),
            pltpu.VMEM((3, 4, 2, 2, 2, 32, D), BF16),
            pltpu.VMEM((PAIRS, 2, 3, S_DEV, LANES), BF16),
            pltpu.VMEM((4, SMALL_ROWS, LANES), BF16),
            pltpu.VMEM((4, 2, 2, 2, M_DEV, D), BF16),
            pltpu.VMEM((16, S_DEV, LANES), BF16),
            pltpu.VMEM((4 * S_DEV, LANES), F32),
            pltpu.VMEM((4 * S_DEV, LANES), F32),
            dma((chunks,)),
            dma((chunks, 3)), dma((chunks, 3)), dma((chunks, 2)), dma((chunks, 2)),
            dma((chunks, 3)), dma((chunks, 3)), dma((chunks, 1)), dma((chunks, 1)),
            dma((3,)), dma((5,)), dma((3,)), dma((3,)), dma((8,)), dma((8,)), dma((15,)), dma((15,)),
            dma((15,)), dma((15,)), dma((16,)), dma((16,)), dma((9,)),
        ],
        compiler_params=params(0),
        name="first",
    )(tokens, memory, small, docs, *weights)
    return (outs[0].reshape(32, ALL_ROWS, D),) + tuple(outs[2:])


def second_kernel(
    second_grad, second_resid, small_full, docs, docs_all, docs_row, crossed, cross_inverse, cross_queries,
    full, memory_pairs_far, first_resid_far, arrived_far, attended_far, inverse_far, docs_column_far, small_grads,
    input_grad, memory_grad, down_grad, up_grad, prefix_sum,
    weights, memory_pairs, first_resid, arrived, attended, inverse, docs_column,
    pull, cross_grad, cross_query_grad, key_terms, value_terms, cross_prefix,
    small_core, small_mine, small_x, small_pair, small_y, small_line, small_all,
    memory_part, memory_core, memory_mine, memory_y, memory_line, memory_all,
    prefix_y, prefix_line, prefix_all, prefix_mine, prefix_quad,
    heads_out, grads, grad_low, delta, query_grads, key_grads, value_grads, staged, gathered,
    fetch_sem, own_sem, near_send, near_recv, line_send, line_recv, small_send, small_recv, memory_send, memory_recv,
    prefix_send, prefix_recv, quad_send, quad_recv,
    in_send, in_recv, out_send, out_recv, query_send, query_recv,
):
    place = Place()
    seq, x, pair, row, core = place.seq, place.x, place.pair, place.row, place.core
    z, y = place.z, place.y
    others = place.others()
    tokens = 2 * S_DEV
    memory_len = 16 * M_DEV
    block = 2 * S_DEV

    fetches = {}

    def fetch(name, source, target):
        fetches[name] = pltpu.make_async_copy(source, target, fetch_sem.at[len(fetches)])
        fetches[name].start()

    firsts = (CROSS_OUT_AT, CROSS_Q_AT, SELF_OUT_AT, MEM_K_AT, MEM_V_AT, Q_AT, K_AT, V_AT)

    def fetch_weight(at):
        fetch(at, full.at[:, pl.ds(at, 32)], weights.at[firsts.index(at)])

    def weight(at):
        return weights[firsts.index(at)].reshape(D, D)

    fetch_weight(CROSS_OUT_AT)
    fetch("pairs", memory_pairs_far, memory_pairs)
    fetch_weight(CROSS_Q_AT)
    fetch("resid", first_resid_far, first_resid)
    fetch_weight(SELF_OUT_AT)
    fetch_weight(MEM_K_AT)
    fetch_weight(MEM_V_AT)
    fetch("arrived", arrived_far, arrived)
    fetch("attended", attended_far, attended)
    fetch("inverse", inverse_far, inverse)
    fetch("docs", docs_column_far, docs_column)
    for at in (K_AT, V_AT, Q_AT):
        fetch_weight(at)
    greet(others + [place.along_x(), place.diagonal()])

    small_first = remote(
        small_grads.at[:, :, 1 - core], small_core, near_send.at[0], near_recv.at[0], place.other_core()
    )
    small_own = pltpu.make_async_copy(small_grads.at[:, :, core], small_mine, own_sem.at[0])
    small_second = remote(small_mine.at[:, :, 1 - x], small_x, near_send.at[1], near_recv.at[1], place.along_x())

    def along_y(k, source, target):
        return remote(source.at[:, 1 - y], target, line_send.at[k], line_recv.at[k], place.along_y())

    def along_z(source, target, sends, recvs):
        return [
            remote(source.at[(z + k) % 4], target.at[z], sends.at[k], recvs.at[k], place.along_z(k))
            for k in range(1, 4)
        ]

    small_third = along_y(0, small_pair, small_y)
    small_fourth = along_z(small_line, small_all, small_send, small_recv)
    memory_first = remote(
        memory_part.at[:, :, 1 - core], memory_core, near_send.at[2], near_recv.at[2], place.other_core()
    )
    memory_second = along_y(1, memory_mine, memory_y)
    memory_third = along_z(memory_line, memory_all, memory_send, memory_recv)
    prefix_first = along_y(2, cross_prefix, prefix_y)
    prefix_second = along_z(prefix_line, prefix_all, prefix_send, prefix_recv)
    small_first.start()
    small_own.start()

    gains = [
        jnp.concatenate(
            [small_full[at_pair, 128:144].astype(F32)[part:part + 1] for at_pair in range(PAIRS)], axis=1
        )
        for part in range(2)
    ]
    pulled = norm_back_rows(second_resid[...], gains[1], second_grad[...])
    pull[...] = pulled
    fetches[CROSS_OUT_AT].wait()
    cross_grad[...] = dot_right(pulled.astype(BF16), weight(CROSS_OUT_AT)).reshape(2, S_DEV, D)
    fetches["pairs"].wait()

    cross_pad = lax.broadcasted_iota(jnp.int32, (64, S_DEV), 0) % 32
    for at_row in range(2):
        lines = [sum(docs_all[4 * at + k, 2 + at_row:3 + at_row] for k in range(4)) for at in range(4)]
        key_docs = jnp.concatenate(
            [jnp.transpose(jnp.broadcast_to(line, (S_DEV, LANES))) for line in lines], axis=0
        )
        allowed = key_docs == docs[at_row:at_row + 1]

        def one_pair(at_pair, carry):
            first = pl.multiple_of(at_pair * LANES, LANES)
            columns, value_columns = pl.ds(first, LANES), pl.ds(pl.multiple_of(first + D, LANES), LANES)
            heads = cross_queries[at_row, :, columns]
            grad = cross_grad[at_row, :, columns] * cross_inverse[at_row, :, columns]
            low = grad.astype(BF16)
            lines = rows_in_lanes(grad * crossed[at_row, :, columns])

            def head_rows(count):
                return jnp.concatenate(
                    [jnp.broadcast_to(lines[0:1], (count, S_DEV)), jnp.broadcast_to(lines[1:2], (count, S_DEV))],
                    axis=0,
                )

            prefix_key_stack = stack_heads(small_full[at_pair, 64:96])
            prefix_value_stack = stack_heads(small_full[at_pair, 96:128])
            e = jnp.exp(dot_right(prefix_key_stack, heads) * score_scale)
            e = jnp.where(cross_pad < PREFIX, e, 0.0)
            slopes = (e * (dot_right(prefix_value_stack, low) - head_rows(32))).astype(BF16)
            from_prefix = dot_left(slopes, prefix_key_stack)
            key_grad = merge_heads(dot_nn(slopes, heads)) * score_scale
            value_grad = merge_heads(dot_nn(e.astype(BF16), low))
            held = cross_prefix.at[at_pair // 2, at_pair % 2]
            if at_row == 0:
                held[0] = key_grad
                held[1] = value_grad
            else:
                held[0] += key_grad
                held[1] += value_grad
            key_stack = stack_heads(memory_pairs[:, at_row, :, columns].reshape(memory_len, LANES))
            value_stack = stack_heads(memory_pairs[:, at_row, :, value_columns].reshape(memory_len, LANES))
            e = jnp.exp(dot_right(key_stack, heads) * score_scale).reshape(2, memory_len, S_DEV)
            e = jnp.where(allowed[None], e, 0.0).reshape(2 * memory_len, S_DEV)
            slopes = (e * (dot_right(value_stack, low) - head_rows(memory_len))).astype(BF16)
            terms = merge_heads(dot_nn(slopes, heads)) * score_scale
            key_terms[:, at_row, :, columns] = terms.astype(BF16).reshape(16, M_DEV, LANES)
            terms = merge_heads(dot_nn(e.astype(BF16), low))
            value_terms[:, at_row, :, columns] = terms.astype(BF16).reshape(16, M_DEV, LANES)
            query_grad = (from_prefix + dot_left(slopes, key_stack)) * score_scale
            cross_query_grad[at_row, :, columns] = query_grad.astype(BF16)
            return carry

        lax.fori_loop(0, PAIRS, one_pair, 0)
        if at_row == 0:
            small_own.wait()
            small_first.wait_recv()
            small_mine[...] = small_mine[...] + small_core[...]
            small_second.start()
    prefix_first.start()

    fetches[CROSS_Q_AT].wait()
    fetches["resid"].wait()
    first_grad = pull[...] + dot_right(cross_query_grad[...].reshape(tokens, D), weight(CROSS_Q_AT))
    resid_grad = norm_back_rows(first_resid[...], gains[0], first_grad)
    pull[...] = resid_grad
    fetches[SELF_OUT_AT].wait()
    out_grad = dot_right(resid_grad.astype(BF16), weight(SELF_OUT_AT)).astype(BF16)
    for at_pair in range(PAIRS):
        for at_row in range(2):
            heads_out[at_pair, at_row] = out_grad[
                at_row * S_DEV:(at_row + 1) * S_DEV, at_pair * LANES:(at_pair + 1) * LANES
            ]
    arrivals = []
    for k in range(15):
        to = (seq + k + 1) % 16
        arrivals.append(remote(heads_out.at[to // 2, to % 2], grads.at[seq], in_send.at[k], in_recv.at[k], others[k]))
        arrivals[-1].start()
    own_heads = pltpu.make_async_copy(heads_out.at[pair, row], grads.at[seq], own_sem.at[1])
    own_heads.start()

    fetches[MEM_K_AT].wait()
    fetches[MEM_V_AT].wait()

    def memory_block(at, carry):
        there = pl.ds(4 * at, 4)
        terms = dot_right(key_terms[there].reshape(8 * M_DEV, D), weight(MEM_K_AT))
        terms += dot_right(value_terms[there].reshape(8 * M_DEV, D), weight(MEM_V_AT))
        memory_part[at] = terms.astype(BF16).reshape(2, 2, 2 * M_DEV, D)
        return carry

    lax.fori_loop(0, 4, memory_block, 0)
    memory_first.start()
    small_second.wait()
    small_pair[...] = small_mine[:, :, x] + small_x[...]
    small_third.start()
    memory_first.wait()
    memory_mine[...] = memory_part[:, :, core] + memory_core[...]
    memory_second.start()
    for name in ("arrived", "attended", "inverse", "docs"):
        fetches[name].wait()
    own_heads.wait()
    for copy in arrivals:
        copy.wait()

    pad_row = lax.broadcasted_iota(jnp.int32, (64, block), 0) % 32
    prefix_key_stack = stack_heads(small_full[pair, 0:32])
    prefix_value_stack = stack_heads(small_full[pair, 32:64])

    def head_rows(at, count):
        there = delta[:, pl.ds(pl.multiple_of(at * block, block), block)]
        return jnp.concatenate(
            [jnp.broadcast_to(there[0:1], (count, block)), jnp.broadcast_to(there[1:2], (count, block))],
            axis=0,
        )

    prefix_mine[...] = jnp.zeros(prefix_mine.shape, F32)

    def prepare(at, carry):
        here = pl.ds(at * block, block)
        grad = grads[pl.ds(2 * at, 2)].reshape(block, LANES).astype(F32) * inverse[here]
        low = grad.astype(BF16)
        grad_low[here] = low
        delta[:, pl.ds(pl.multiple_of(at * block, block), block)] = rows_in_lanes(grad * attended[here])
        queries = arrived[pl.ds(2 * at, 2), 0].reshape(block, LANES)
        e = jnp.exp(dot_right(prefix_key_stack, queries) * score_scale)
        e = jnp.where(pad_row < PREFIX, e, 0.0)
        slopes = (e * (dot_right(prefix_value_stack, low) - head_rows(at, 32))).astype(BF16)
        prefix_mine[0] += merge_heads(dot_nn(slopes, queries)) * score_scale
        prefix_mine[1] += merge_heads(dot_nn(e.astype(BF16), low))
        query_grads[here] = dot_left(slopes, prefix_key_stack)
        return carry

    lax.fori_loop(0, 8, prepare, 0)
    prefix_first.wait()
    prefix_line[...] = cross_prefix[:, y] + prefix_y[...]
    for copy in prefix_second:
        copy.start()
    prefix_all[z] = prefix_line[z]
    small_third.wait()
    small_line[...] = small_pair[:, y] + small_y[...]
    for copy in small_fourth:
        copy.start()
    small_all[z] = small_line[z]

    away = (
        lax.broadcasted_iota(jnp.int32, (block, block), 0)
        - lax.broadcasted_iota(jnp.int32, (block, block), 1)
    )

    def send_block(part, count, at, send, recv):
        for half in range(2):
            to = 2 * at + half
            source = staged.at[to, pl.ds(part, count)]
            mine = gathered.at[pair, row, pl.ds(part, count)]

            @pl.when(to != seq)
            def _():
                remote(source, mine, send.at[to], recv.at[seq], (to, x)).start()

            @pl.when(to == seq)
            def _():
                pltpu.make_async_copy(source, mine, own_sem.at[2 + part]).start()

    def one_block(step, carry):
        key_at = (step + pair) % 8
        keys = stack_heads(arrived[pl.ds(2 * key_at, 2), 1].reshape(block, LANES))
        values = stack_heads(arrived[pl.ds(2 * key_at, 2), 2].reshape(block, LANES))
        key_docs = docs_column[pl.ds(key_at * block, block)]
        key_docs = jnp.concatenate([key_docs, key_docs], axis=1)
        key_grads[...] = jnp.zeros(key_grads.shape, F32)
        value_grads[...] = jnp.zeros(value_grads.shape, F32)

        def one_tile(at, carry):
            here = pl.ds(at * block, block)
            queries = arrived[pl.ds(2 * at, 2), 0].reshape(block, LANES)
            low = grad_low[here]
            query_docs = docs_row[0:1, pl.ds(pl.multiple_of(at * block, block), block)]
            allowed = (key_docs == query_docs) & (away <= (at - key_at) * block)
            e = jnp.exp(dot_right(keys, queries) * score_scale).reshape(2, block, block)
            e = jnp.where(allowed[None], e, 0.0).reshape(2 * block, block)
            slopes = (e * (dot_right(values, low) - head_rows(at, block))).astype(BF16)
            key_grads[...] += dot_nn(slopes, queries)
            value_grads[...] += dot_nn(e.astype(BF16), low)
            query_grads[here] += dot_left(slopes, keys)
            return carry

        lax.fori_loop(key_at, 8, one_tile, 0)
        there = pl.ds(2 * key_at, 2)
        staged[there, 1] = (merge_heads(key_grads[...]) * score_scale).astype(BF16).reshape(2, S_DEV, LANES)
        staged[there, 2] = merge_heads(value_grads[...]).astype(BF16).reshape(2, S_DEV, LANES)
        send_block(1, 2, key_at, out_send, out_recv)
        return carry

    lax.fori_loop(0, 2, one_block, 0)
    memory_second.wait()
    memory_line[...] = memory_mine[:, y] + memory_y[...]
    for copy in memory_third:
        copy.start()
    memory_all[z] = memory_line[z]
    lax.fori_loop(2, 8, one_block, 0)

    def last_block(step, carry):
        at = (step + pair) % 8
        result = (query_grads[pl.ds(at * block, block)] * score_scale).astype(BF16)
        staged[pl.ds(2 * at, 2), 0] = result.reshape(2, S_DEV, LANES)
        send_block(0, 1, at, query_send, query_recv)
        return carry

    lax.fori_loop(0, 8, last_block, 0)
    small_first.wait_send()
    for copy in prefix_second:
        copy.wait()
    for part in range(2):
        prefix_mine[2 + part] = sum(prefix_all[k, part] for k in range(4))
    prefix_quad[core * 2 + x] = prefix_mine[...]
    quad_copies = [
        remote(prefix_mine, prefix_quad.at[core * 2 + x], quad_send.at[k], quad_recv.at[k], peer)
        for k, peer in enumerate((place.other_core(), place.along_x(), place.diagonal()))
    ]
    for copy in quad_copies:
        copy.start()
    for copy in small_fourth:
        copy.wait()
    total = small_all[0].astype(F32)
    for k in range(1, 4):
        total += small_all[k].astype(F32)
    down_grad[...] = total[:, :ADAPTER]
    up_grad[:, :ADAPTER] = total[:16, ADAPTER:]
    up_grad[:, ADAPTER:] = total[16:, ADAPTER:]
    for copy in memory_third:
        copy.wait()
    total = memory_all[0].astype(F32)
    for k in range(1, 4):
        total += memory_all[k].astype(F32)
    memory_grad[...] = total
    for copy in quad_copies:
        copy.wait()
    prefix_sum[...] = (prefix_quad[0] + prefix_quad[1]) + (prefix_quad[2] + prefix_quad[3])

    pltpu.make_async_copy(staged.at[seq, pl.ds(1, 2)], gathered.at[pair, row, pl.ds(1, 2)], own_sem.at[3]).wait()
    for other, _ in others:
        remote(
            staged.at[other, pl.ds(1, 2)], gathered.at[other // 2, other % 2, pl.ds(1, 2)],
            out_send.at[other], out_recv.at[other], (other, x),
        ).wait()

    def part_grad(part, at):
        fetches[at].wait()
        joined = jnp.concatenate([gathered[k, :, part].reshape(tokens, LANES) for k in range(PAIRS)], axis=1)
        return dot_right(joined, weight(at))

    input_grad[...] = pull[...] + part_grad(1, K_AT) + part_grad(2, V_AT)
    pltpu.make_async_copy(staged.at[seq, pl.ds(0, 1)], gathered.at[pair, row, pl.ds(0, 1)], own_sem.at[2]).wait()
    for other, _ in others:
        remote(
            staged.at[other, pl.ds(0, 1)], gathered.at[other // 2, other % 2, pl.ds(0, 1)],
            query_send.at[other], query_recv.at[other], (other, x),
        ).wait()
    input_grad[...] += part_grad(0, Q_AT)


def second_call(*operands):
    length = 16 * S_DEV
    tokens = 2 * S_DEV
    dma = pltpu.SemaphoreType.DMA
    shape = jax.ShapeDtypeStruct
    return pl.pallas_call(
        second_kernel,
        out_shape=(
            shape((tokens, D), F32),
            shape((2 * M_DEV, D), F32),
            shape((32, ADAPTER), F32),
            shape((16, D), F32),
            shape((4, 32, LANES), F32),
        ),
        in_specs=[whole()] * 9 + [whole(pl.ANY)] * 8,
        out_specs=(whole(),) * 5,
        scratch_shapes=[
            pltpu.VMEM((8, 32, 32, D), BF16),
            pltpu.VMEM((16, 2, M_DEV, 2 * D), BF16),
            pltpu.VMEM((tokens, D), F32),
            pltpu.VMEM((16, 3, S_DEV, LANES), BF16),
            pltpu.VMEM((length, LANES), F32),
            pltpu.VMEM((length, LANES), F32),
            pltpu.VMEM((length, LANES), F32),
            pltpu.VMEM((tokens, D), F32),
            pltpu.VMEM((2, S_DEV, D), F32),
            pltpu.VMEM((2, S_DEV, D), BF16),
            pltpu.VMEM((16, 2, M_DEV, D), BF16),
            pltpu.VMEM((16, 2, M_DEV, D), BF16),
            pltpu.VMEM((4, 2, 2, 32, LANES), F32),
            pltpu.VMEM((4, 2, 2, 32, D), BF16),
            pltpu.VMEM((4, 2, 2, 32, D), BF16),
            pltpu.VMEM((4, 2, 32, D), BF16),
            pltpu.VMEM((4, 2, 32, D), BF16),
            pltpu.VMEM((4, 32, D), BF16),
            pltpu.VMEM((4, 32, D), BF16),
            pltpu.VMEM((4, 32, D), BF16),
            pltpu.VMEM((4, 2, 2, 2 * M_DEV, D), BF16),
            pltpu.VMEM((4, 2, 2 * M_DEV, D), BF16),
            pltpu.VMEM((4, 2, 2 * M_DEV, D), BF16),
            pltpu.VMEM((4, 2 * M_DEV, D), BF16),
            pltpu.VMEM((4, 2 * M_DEV, D), BF16),
            pltpu.VMEM((4, 2 * M_DEV, D), BF16),
            pltpu.VMEM((4, 2, 32, LANES), F32),
            pltpu.VMEM((4, 2, 32, LANES), F32),
            pltpu.VMEM((4, 2, 32, LANES), F32),
            pltpu.VMEM((4, 32, LANES), F32),
            pltpu.VMEM((4, 4, 32, LANES), F32),
            pltpu.VMEM((PAIRS, 2, S_DEV, LANES), BF16),
            pltpu.VMEM((16, S_DEV, LANES), BF16),
            pltpu.VMEM((length, LANES), BF16),
            pltpu.VMEM((8, length), F32),
            pltpu.VMEM((length, LANES), F32),
            pltpu.VMEM((4 * S_DEV, LANES), F32),
            pltpu.VMEM((4 * S_DEV, LANES), F32),
            pltpu.VMEM((16, 3, S_DEV, LANES), BF16),
            pltpu.VMEM((PAIRS, 2, 3, S_DEV, LANES), BF16),
            dma((14,)), dma((4,)), dma((3,)), dma((3,)), dma((3,)), dma((3,)), dma((4,)), dma((4,)), dma((4,)), dma((4,)),
            dma((4,)), dma((4,)), dma((3,)), dma((3,)),
            dma((15,)), dma((15,)), dma((16,)), dma((16,)), dma((16,)), dma((16,)),
        ],
        compiler_params=params(1),
        name="second",
    )(*operands)


def gelu_parts(pre):
    upper = 0.5 * (1.0 + lax.erf(pre * (0.5 ** 0.5)))
    return upper


def gelu_slope(pre):
    return gelu_parts(pre) + pre * jnp.exp(-0.5 * pre * pre) * (1.0 / math.sqrt(2.0 * math.pi))


def norm_back_rows(resid, gain, upstream):
    middle = jnp.mean(resid, axis=-1, keepdims=True)
    centred = resid - middle
    scale = lax.rsqrt(jnp.mean(centred * centred, axis=-1, keepdims=True) + 1e-05)
    unit = centred * scale
    pulled = upstream * gain
    return scale * (
        pulled - jnp.mean(pulled, axis=-1, keepdims=True) - unit * jnp.mean(pulled * unit, axis=-1, keepdims=True)
    )


def feed_kernel(
    normed, cotangent, gain, inner, outer, mixed,
    layer_out, second_grad, small_grads,
    low, pre, adapter_pre, total, feed_low,
):
    step = pl.program_id(0)
    down = mixed[:, :, :ADAPTER].reshape(D, ADAPTER)
    up_left = mixed[:, :16, ADAPTER:].reshape(ADAPTER, ADAPTER)
    up_right = mixed[:, 16:, ADAPTER:].reshape(ADAPTER, ADAPTER)
    half = ADAPTER

    @pl.when(step == 0)
    def _():
        low[...] = normed[...].astype(BF16)
        adapter_pre[...] = dot_nn(low[...], down)
        act = adapter_pre[...]
        act = (act * gelu_parts(act)).astype(BF16)
        total[:, :half] = normed[:, :half] + 4.0 * dot_nn(act, up_left)
        total[:, half:] = normed[:, half:] + 4.0 * dot_nn(act, up_right)

    @pl.when(step < 4)
    def _():
        hidden = dot_nn(low[...], inner[...].reshape(D, D))
        pre[jnp.minimum(step, 3)] = hidden
        act = (hidden * gelu_parts(hidden)).astype(BF16)
        total[...] += dot_nn(act, outer[...].reshape(D, D))

    @pl.when(step == 3)
    def _():
        resid = total[...]
        layer_out[...] = norm_rows(resid, gain[...]).astype(BF16)
        third_grad = norm_back_rows(resid, gain[...], cotangent[...].astype(F32))
        feed_low[...] = third_grad.astype(BF16)
        adapter_low = (4.0 * third_grad).astype(BF16)
        act = adapter_pre[...]
        upper = gelu_parts(act)
        slope = gelu_slope(act)
        act = (act * upper).astype(BF16)
        grad = dot_right(adapter_low[:, :half], up_left) + dot_right(adapter_low[:, half:], up_right)
        grad = (slope * grad).astype(BF16)
        second_grad[...] = third_grad + dot_right(grad, down)
        small_grads[:, :, :half] = dot_left(low[...], grad).astype(BF16).reshape(32, 32, half)
        small_grads[:, :16, half:] = dot_left(act, adapter_low[:, :half]).astype(BF16).reshape(32, 16, half)
        small_grads[:, 16:, half:] = dot_left(act, adapter_low[:, half:]).astype(BF16).reshape(32, 16, half)

    @pl.when(step >= 4)
    def _():
        hidden = pre[jnp.clip(7 - step, 0, 3)]
        grad = dot_right(feed_low[...], outer[...].reshape(D, D))
        grad = (gelu_slope(hidden) * grad).astype(BF16)
        second_grad[...] += dot_right(grad, inner[...].reshape(D, D))


def feed_forward_backward(normed, cotangent, gain, weights):
    tokens = normed.shape[0]
    at = lambda step: jnp.minimum(step, 7 - step)
    still = lambda step: (0, 0)
    rows = pl.BlockSpec((tokens, D), still)
    return pl.pallas_call(
        feed_kernel,
        grid=(8,),
        out_shape=(
            jax.ShapeDtypeStruct((tokens, D), BF16),
            jax.ShapeDtypeStruct((tokens, D), F32),
            jax.ShapeDtypeStruct((32, 32, D), BF16),
        ),
        in_specs=[
            rows, rows, pl.BlockSpec((1, D), still),
            pl.BlockSpec((32, 32, D), lambda step: (0, INNER_AT // 32 + at(step), 0)),
            pl.BlockSpec((8, 128, D), lambda step: (at(step), OUTER_AT // 128, 0)),
            pl.BlockSpec((32, 32, D), lambda step: (0, MIXED_AT // 32, 0)),
        ],
        out_specs=(rows, rows, pl.BlockSpec((32, 32, D), lambda step: (0, 0, 0))),
        scratch_shapes=[
            pltpu.VMEM((tokens, D), BF16),
            pltpu.VMEM((4, tokens, D), F32),
            pltpu.VMEM((tokens, ADAPTER), F32),
            pltpu.VMEM((tokens, D), F32),
            pltpu.VMEM((tokens, D), BF16),
        ],
        compiler_params=params(),
        name="feed",
    )(normed, cotangent, gain, weights, weights, weights)


def fast_device(
    inputs, memory, out_grad, token_docs, memory_docs, self_project, self_output, cross_query,
    cross_memory, cross_output, inner_weight, outer_weight, adapter_down, adapter_up, norm_gains, prefixes,
):
    seq, x = lax.axis_index("seq"), lax.axis_index("rows")
    tokens = 2 * S_DEV
    mixed = jnp.concatenate(
        [adapter_down, jnp.concatenate([adapter_up[:, :ADAPTER], adapter_up[:, ADAPTER:]], axis=0)], axis=1
    )
    lane_group = lax.broadcasted_iota(jnp.int32, (1, LANES), 1) // 32
    small = jnp.concatenate([
        jnp.pad(prefixes, ((0, 0), (0, 2), (0, 0))).reshape(128, 32), jnp.pad(norm_gains, ((0, 13), (0, 0)))
    ])
    small = jnp.where(lane_group == (seq % 2) * 2 + x, jnp.tile(small, (1, 4)), jnp.zeros((), BF16))
    memory_line = jnp.where(lane_group == seq % 4, jnp.tile(memory_docs, (1, 4)), 0)
    docs = jnp.concatenate([token_docs, memory_line, jnp.zeros((4, LANES), jnp.int32)]).astype(F32)
    (
        full, memory_pairs, docs_column, arrived, pair_attended, pair_inverse,
        first_resid, cross_queries, crossed, cross_inverse, small_full, docs_all, docs_row, second_resid, second_norm,
    ) = first_call(
        inputs, memory.reshape(2, M_DEV, D), small, docs,
        self_project, self_output, cross_query, cross_memory, cross_output, inner_weight, outer_weight, mixed,
    )

    third_gain = small_full[:, 130].reshape(1, D).astype(F32)
    layer_out, second_grad, small_grads = feed_forward_backward(
        second_norm, out_grad.reshape(tokens, D), third_gain, full
    )
    input_grad, memory_grad, down_grad, up_grad, prefix_sum = second_call(
        second_grad, second_resid, small_full, docs, docs_all, docs_row, crossed, cross_inverse, cross_queries,
        full, memory_pairs, first_resid, arrived, pair_attended, pair_inverse, docs_column,
        small_grads.reshape(4, 2, 2, 2, 32, D),
    )
    prefix_grad = lax.dynamic_slice_in_dim(prefix_sum[:, :PREFIX], 32 * ((seq % 2) * 2 + x), 32, 2)
    return (
        layer_out.reshape(2, S_DEV, D),
        input_grad.reshape(2, S_DEV, D),
        memory_grad.reshape(2, M_DEV, D),
        prefix_grad,
        down_grad,
        up_grad,
    )


def solution(mesh):
    placed = (
        P("rows", "seq", None),
        P("rows", "seq", None),
        P("rows", "seq", None),
        P("rows", "seq"),
        P("rows", "seq"),
        P(("seq", "rows"), None),
        P(("seq", "rows"), None),
        P(("seq", "rows"), None),
        P(("seq", "rows"), None),
        P(("seq", "rows"), None),
        P(("seq", "rows"), None),
        P(("seq", "rows"), None),
        P(("seq", "rows"), None),
        P(("seq", "rows"), None),
        P(None, ("seq", "rows")),
        P(None, None, ("seq", "rows")),
    )
    small_slice = mesh.shape["seq"] == 16 and mesh.shape["rows"] == 2
    return jax.shard_map(
        fast_device if small_slice else per_device,
        mesh=mesh,
        in_specs=placed,
        out_specs=(
            P("rows", "seq", None),
            P("rows", "seq", None),
            P("rows", "seq", None),
            P(None, None, ("seq", "rows")),
            P(("seq", "rows"), None),
            P(("seq", "rows"), None),
        ),
        check_vma=False,
    )
```

```python
import math

import jax
import jax.numpy as jnp
from jax import lax
from jax.experimental import pallas as pl
from jax.experimental.pallas import tpu as pltpu
from jax.sharding import PartitionSpec as P

D = 1024
HEADS = 16
HEAD_DIM = 64
ADAPTER = 512
PREFIX = 30
S_DEV = 128
M_DEV = 32


score_scale = 0.125
masked_score = -1000000000.0


def heads_of(matrix):
    return matrix.reshape(matrix.shape[0], HEADS, HEAD_DIM)


def dot_right(left, right):
    return lax.dot_general(
        left, right, (((1,), (1,)), ((), ())), preferred_element_type=jnp.float32
    )


def dot_left(left, right):
    return lax.dot_general(
        left, right, (((0,), (0,)), ((), ())), preferred_element_type=jnp.float32
    )


def norm_rows(resid, gain):
    middle = jnp.mean(resid, axis=-1, keepdims=True)
    centred = resid - middle
    spread = jnp.mean(centred * centred, axis=-1, keepdims=True)
    return centred * lax.rsqrt(spread + 1e-05) * gain


def norm_back(resid, gain, upstream):
    unused, pullback = jax.vjp(lambda values: norm_rows(values, gain), resid)
    return pullback(upstream)[0]


def gelu_back(pre_act, upstream):
    unused, pullback = jax.vjp(lambda values: jax.nn.gelu(values, approximate=False), pre_act)
    return pullback(upstream)[0]


def allowed_keys(query_docs, key_docs, query_pos, key_pos, causal):
    allowed = query_docs[:, None] == key_docs[None, :]
    if causal:
        allowed = allowed & (key_pos[None, :] <= query_pos[:, None])
    return allowed


def prefix_terms(queries, prefix_keys, prefix_values):
    scores = (
        jnp.einsum(
            "qhd,phd->hqp", queries, heads_of(prefix_keys), preferred_element_type=jnp.float32
        )
        * score_scale
    )
    weights = jnp.exp(scores)
    summed = jnp.einsum(
        "hqp,phd->qhd",
        weights.astype(jnp.bfloat16),
        heads_of(prefix_values),
        preferred_element_type=jnp.float32,
    )
    return (jnp.sum(weights, axis=-1), summed)


def fold_keys(running, arrived, queries, query_docs, key_docs, query_first, causal):
    key_count = arrived.shape[0]
    block_len = math.gcd(key_count, 512)
    query_count = queries.shape[0]
    query_pos = query_first + jnp.arange(query_count, dtype=jnp.int32)
    key_width = arrived.shape[1] // 2

    def fold_one_block(current, element):
        key_block, block_index = element
        key_first = block_index * block_len

        def compute(present):
            block_docs = lax.dynamic_slice_in_dim(key_docs, key_first, block_len, 0)
            allowed = allowed_keys(
                query_docs,
                block_docs,
                query_pos,
                key_first + jnp.arange(block_len, dtype=jnp.int32),
                causal,
            )
            scores = (
                jnp.einsum(
                    "qhd,khd->hqk",
                    queries,
                    heads_of(key_block[:, :key_width]),
                    preferred_element_type=jnp.float32,
                )
                * score_scale
            )
            weights = jnp.exp(jnp.where(allowed[None], scores, masked_score))
            summed = jnp.einsum(
                "hqk,khd->qhd",
                weights.astype(jnp.bfloat16),
                heads_of(key_block[:, key_width:]),
                preferred_element_type=jnp.float32,
            )
            return (present[0] + jnp.sum(weights, axis=-1), present[1] + summed)

        if causal:
            return (
                lax.cond(
                    key_first <= query_first + query_count - 1, compute, lambda held: held, current
                ),
                None,
            )
        return (compute(current), None)

    running, unused = lax.scan(
        fold_one_block,
        running,
        (
            arrived.reshape(key_count // block_len, block_len, arrived.shape[1]),
            jnp.arange(key_count // block_len, dtype=jnp.int32),
        ),
    )
    return running


def attend_back(
    queries,
    gathered,
    prefix_keys,
    prefix_values,
    grad_out,
    attended,
    totals,
    query_docs,
    key_docs,
    query_first,
    causal,
):
    query_count = queries.shape[0]
    key_count = gathered.shape[0]
    key_width = gathered.shape[1] // 2
    block_len = math.gcd(key_count, 512)
    query_pos = query_first + jnp.arange(query_count, dtype=jnp.int32)
    grad_heads = heads_of(grad_out)
    grad_summed = (grad_heads / totals.T[:, :, None]).astype(jnp.bfloat16)
    row_dot = jnp.sum(grad_heads * heads_of(attended), axis=-1).T / totals
    prefix_key_heads = heads_of(prefix_keys)
    prefix_value_heads = heads_of(prefix_values)
    prefix_weights = jnp.exp(
        jnp.einsum("qhd,phd->hqp", queries, prefix_key_heads, preferred_element_type=jnp.float32)
        * score_scale
    )
    prefix_dots = jnp.einsum(
        "qhd,phd->hqp", grad_summed, prefix_value_heads, preferred_element_type=jnp.float32
    )
    prefix_slopes = (prefix_weights * (prefix_dots - row_dot[:, :, None])).astype(jnp.bfloat16)
    query_grad = jnp.einsum(
        "hqp,phd->qhd", prefix_slopes, prefix_key_heads, preferred_element_type=jnp.float32
    )
    key_grad_prefix = (
        jnp.einsum("hqp,qhd->phd", prefix_slopes, queries, preferred_element_type=jnp.float32)
        * score_scale
    ).reshape(-1, D)
    value_grad_prefix = jnp.einsum(
        "hqp,qhd->phd",
        prefix_weights.astype(jnp.bfloat16),
        grad_summed,
        preferred_element_type=jnp.float32,
    ).reshape(-1, D)

    def attend_one_block(current, element):
        key_block, block_index = element
        key_first = block_index * block_len

        def compute(present):
            block_docs = lax.dynamic_slice_in_dim(key_docs, key_first, block_len, 0)
            allowed = allowed_keys(
                query_docs,
                block_docs,
                query_pos,
                key_first + jnp.arange(block_len, dtype=jnp.int32),
                causal,
            )
            key_heads = heads_of(key_block[:, :key_width])
            value_heads = heads_of(key_block[:, key_width:])
            scores = (
                jnp.einsum("qhd,khd->hqk", queries, key_heads, preferred_element_type=jnp.float32)
                * score_scale
            )
            weights = jnp.exp(jnp.where(allowed[None], scores, masked_score))
            dots = jnp.einsum(
                "qhd,khd->hqk", grad_summed, value_heads, preferred_element_type=jnp.float32
            )
            slopes = (weights * (dots - row_dot[:, :, None])).astype(jnp.bfloat16)
            present = present + jnp.einsum(
                "hqk,khd->qhd", slopes, key_heads, preferred_element_type=jnp.float32
            )
            key_grad = (
                jnp.einsum("hqk,qhd->khd", slopes, queries, preferred_element_type=jnp.float32)
                * score_scale
            )
            value_grad = jnp.einsum(
                "hqk,qhd->khd",
                weights.astype(jnp.bfloat16),
                grad_summed,
                preferred_element_type=jnp.float32,
            )
            return (
                present,
                jnp.concatenate(
                    [key_grad.reshape(block_len, D), value_grad.reshape(block_len, D)], axis=1
                ),
            )

        if causal:
            return lax.cond(
                key_first <= query_first + query_count - 1,
                compute,
                lambda held: (held, jnp.zeros((block_len, 2 * D), jnp.float32)),
                current,
            )
        return compute(current)

    query_grad, key_terms = lax.scan(
        attend_one_block,
        query_grad,
        (
            gathered.reshape(key_count // block_len, block_len, gathered.shape[1]),
            jnp.arange(key_count // block_len, dtype=jnp.int32),
        ),
    )
    query_low = (query_grad * score_scale).astype(jnp.bfloat16).reshape(query_count, D)
    key_terms = key_terms.reshape(key_count, 2 * D)
    return (query_low, key_terms, key_grad_prefix, value_grad_prefix, grad_summed, row_dot)


def fetch_all(
    self_project,
    self_output,
    cross_query,
    cross_memory,
    cross_output,
    inner_weight,
    outer_weight,
    adapter_down,
    adapter_up,
    norm_gains,
    prefixes,
):
    return (
        lax.all_gather(self_project, ("seq", "rows"), axis=0, tiled=True),
        lax.all_gather(self_output, ("seq", "rows"), axis=0, tiled=True),
        lax.all_gather(cross_query, ("seq", "rows"), axis=0, tiled=True),
        lax.all_gather(cross_memory, ("seq", "rows"), axis=0, tiled=True),
        lax.all_gather(cross_output, ("seq", "rows"), axis=0, tiled=True),
        lax.all_gather(inner_weight, ("seq", "rows"), axis=0, tiled=True),
        lax.all_gather(outer_weight, ("seq", "rows"), axis=0, tiled=True),
        lax.all_gather(adapter_down, ("seq", "rows"), axis=0, tiled=True),
        lax.all_gather(adapter_up, ("seq", "rows"), axis=0, tiled=True),
        lax.all_gather(norm_gains, ("seq", "rows"), axis=1, tiled=True),
        lax.all_gather(prefixes, ("seq", "rows"), axis=2, tiled=True),
    )


def fetch_again(
    self_project,
    self_output,
    cross_query,
    cross_memory,
    cross_output,
    inner_weight,
    outer_weight,
    adapter_down,
    adapter_up,
    norm_gains,
    prefixes,
):
    return (
        lax.all_gather(self_project, ("seq", "rows"), axis=0, tiled=True),
        lax.all_gather(self_output, ("seq", "rows"), axis=0, tiled=True),
        lax.all_gather(cross_query, ("seq", "rows"), axis=0, tiled=True),
        lax.all_gather(cross_memory, ("seq", "rows"), axis=0, tiled=True),
        lax.all_gather(cross_output, ("seq", "rows"), axis=0, tiled=True),
        lax.all_gather(inner_weight, ("seq", "rows"), axis=0, tiled=True),
        lax.all_gather(outer_weight, ("seq", "rows"), axis=0, tiled=True),
        lax.all_gather(adapter_down, ("seq", "rows"), axis=0, tiled=True),
        lax.all_gather(adapter_up, ("seq", "rows"), axis=0, tiled=True),
        lax.all_gather(norm_gains, ("seq", "rows"), axis=1, tiled=True),
        lax.all_gather(prefixes, ("seq", "rows"), axis=2, tiled=True),
    )


def forward_row(tokens, memory_rows, query_docs, token_docs, memory_docs, query_first, weights):
    (
        self_project,
        self_output,
        cross_query,
        cross_memory,
        cross_output,
        inner_weight,
        outer_weight,
        adapter_down,
        adapter_up,
        norm_gains,
        prefixes,
    ) = weights
    gains = norm_gains.astype(jnp.float32)
    projected = jnp.dot(tokens, self_project, preferred_element_type=jnp.float32).astype(
        jnp.bfloat16
    )
    queries = heads_of(projected[:, :D])
    local_pairs = projected[:, D:]
    start_self = prefix_terms(queries, prefixes[0], prefixes[1])
    totals, summed = fold_keys(
        start_self,
        lax.all_gather(local_pairs, "seq", axis=0, tiled=True),
        queries,
        query_docs,
        token_docs,
        query_first,
        True,
    )
    attended = (summed / totals.T[:, :, None]).reshape(-1, D)
    first_resid = tokens.astype(jnp.float32) + jnp.dot(
        attended.astype(jnp.bfloat16), self_output, preferred_element_type=jnp.float32
    )
    first_norm = norm_rows(first_resid, gains[0])
    first_low = first_norm.astype(jnp.bfloat16)
    cross_queries = heads_of(
        jnp.dot(first_low, cross_query, preferred_element_type=jnp.float32).astype(jnp.bfloat16)
    )
    memory_pairs = jnp.dot(memory_rows, cross_memory, preferred_element_type=jnp.float32).astype(
        jnp.bfloat16
    )
    start_cross = prefix_terms(cross_queries, prefixes[2], prefixes[3])
    cross_totals, cross_summed = fold_keys(
        start_cross,
        lax.all_gather(memory_pairs, "seq", axis=0, tiled=True),
        cross_queries,
        query_docs,
        memory_docs,
        query_first,
        False,
    )
    crossed = (cross_summed / cross_totals.T[:, :, None]).reshape(-1, D)
    second_resid = first_norm + jnp.dot(
        crossed.astype(jnp.bfloat16), cross_output, preferred_element_type=jnp.float32
    )
    second_norm = norm_rows(second_resid, gains[1])
    second_low = second_norm.astype(jnp.bfloat16)
    hidden_pre = jnp.dot(second_low, inner_weight, preferred_element_type=jnp.float32)
    hidden_act = jax.nn.gelu(hidden_pre, approximate=False).astype(jnp.bfloat16)
    adapter_pre = jnp.dot(second_low, adapter_down, preferred_element_type=jnp.float32)
    adapter_act = jax.nn.gelu(adapter_pre, approximate=False).astype(jnp.bfloat16)
    third_resid = (
        second_norm
        + jnp.dot(hidden_act, outer_weight, preferred_element_type=jnp.float32)
        + 4.0 * jnp.dot(adapter_act, adapter_up, preferred_element_type=jnp.float32)
    )
    layer_out = norm_rows(third_resid, gains[2]).astype(jnp.bfloat16)
    saved = (
        queries,
        local_pairs,
        totals,
        attended,
        first_resid,
        cross_queries,
        memory_pairs,
        cross_totals,
        crossed,
        second_resid,
        second_low,
        hidden_pre,
        adapter_pre,
        adapter_act,
        third_resid,
    )
    return (layer_out, saved)


def backward_row(cotangent, saved, weights, query_docs, token_docs, memory_docs, query_first):
    (
        self_project,
        self_output,
        cross_query,
        cross_memory,
        cross_output,
        inner_weight,
        outer_weight,
        adapter_down,
        adapter_up,
        norm_gains,
        prefixes,
    ) = weights
    (
        queries,
        local_pairs,
        totals,
        attended,
        first_resid,
        cross_queries,
        memory_pairs,
        cross_totals,
        crossed,
        second_resid,
        second_low,
        hidden_pre,
        adapter_pre,
        adapter_act,
        third_resid,
    ) = saved
    gains = norm_gains.astype(jnp.float32)
    third_grad = norm_back(third_resid, gains[2], cotangent.astype(jnp.float32))
    feed_low = third_grad.astype(jnp.bfloat16)
    adapter_low = (4.0 * third_grad).astype(jnp.bfloat16)
    hidden_grad = gelu_back(hidden_pre, dot_right(feed_low, outer_weight)).astype(jnp.bfloat16)
    up_grad = dot_left(adapter_act, adapter_low)
    adapter_grad = gelu_back(adapter_pre, dot_right(adapter_low, adapter_up)).astype(jnp.bfloat16)
    down_grad = dot_left(second_low, adapter_grad)
    second_grad = (
        third_grad + dot_right(hidden_grad, inner_weight) + dot_right(adapter_grad, adapter_down)
    )
    second_resid_grad = norm_back(second_resid, gains[1], second_grad)
    self_all, memory_all = (
        lax.all_gather(local_pairs, "seq", axis=0, tiled=True),
        lax.all_gather(memory_pairs, "seq", axis=0, tiled=True),
    )
    cross_out_grad = dot_right(second_resid_grad.astype(jnp.bfloat16), cross_output)
    (
        cross_query_low,
        memory_terms,
        cross_key_prefix,
        cross_value_prefix,
        cross_summed_grad,
        cross_dot,
    ) = attend_back(
        cross_queries,
        memory_all,
        prefixes[2],
        prefixes[3],
        cross_out_grad,
        crossed,
        cross_totals,
        query_docs,
        memory_docs,
        query_first,
        False,
    )
    first_grad = second_resid_grad + dot_right(cross_query_low, cross_query)
    first_resid_grad = norm_back(first_resid, gains[0], first_grad)
    self_out_grad = dot_right(first_resid_grad.astype(jnp.bfloat16), self_output)
    query_low, self_terms, self_key_prefix, self_value_prefix, self_summed_grad, self_dot = (
        attend_back(
            queries,
            self_all,
            prefixes[0],
            prefixes[1],
            self_out_grad,
            attended,
            totals,
            query_docs,
            token_docs,
            query_first,
            True,
        )
    )
    self_sums, memory_sums = (
        lax.psum_scatter(
            self_terms.astype(jnp.bfloat16), "seq", scatter_dimension=0, tiled=True
        ).astype(jnp.float32),
        lax.psum_scatter(
            memory_terms.astype(jnp.bfloat16), "seq", scatter_dimension=0, tiled=True
        ).astype(jnp.float32),
    )
    project_grad = jnp.concatenate([query_low, self_sums.astype(jnp.bfloat16)], axis=1)
    input_grad = first_resid_grad + dot_right(project_grad, self_project)
    memory_grad = dot_right(memory_sums.astype(jnp.bfloat16), cross_memory)
    prefix_grad = jnp.stack(
        [self_key_prefix, self_value_prefix, cross_key_prefix, cross_value_prefix]
    )
    return (input_grad, memory_grad, (down_grad, up_grad, prefix_grad))


def per_device(
    inputs,
    memory,
    out_grad,
    token_docs,
    memory_docs,
    self_project,
    self_output,
    cross_query,
    cross_memory,
    cross_output,
    inner_weight,
    outer_weight,
    adapter_down,
    adapter_up,
    norm_gains,
    prefixes,
):
    docs_full, memory_full = (
        lax.all_gather(token_docs, "seq", axis=1, tiled=True),
        lax.all_gather(memory_docs, "seq", axis=1, tiled=True),
    )
    query_first = lax.axis_index("seq") * inputs.shape[1]
    outputs = []
    input_grads = []
    memory_grads = []
    adjusted_grads = None
    for row_index in range(inputs.shape[0]):
        weights = fetch_all(
            self_project,
            self_output,
            cross_query,
            cross_memory,
            cross_output,
            inner_weight,
            outer_weight,
            adapter_down,
            adapter_up,
            norm_gains,
            prefixes,
        )
        layer_out, saved = forward_row(
            inputs[row_index],
            memory[row_index],
            token_docs[row_index],
            docs_full[row_index],
            memory_full[row_index],
            query_first,
            weights,
        )
        weights_back = fetch_again(
            self_project,
            self_output,
            cross_query,
            cross_memory,
            cross_output,
            inner_weight,
            outer_weight,
            adapter_down,
            adapter_up,
            norm_gains,
            prefixes,
        )
        input_grad, memory_grad, row_grads = backward_row(
            out_grad[row_index],
            saved,
            weights_back,
            token_docs[row_index],
            docs_full[row_index],
            memory_full[row_index],
            query_first,
        )
        shares = (
            lax.psum_scatter(row_grads[0], ("seq", "rows"), scatter_dimension=0, tiled=True),
            lax.psum_scatter(row_grads[1], ("seq", "rows"), scatter_dimension=0, tiled=True),
            lax.psum_scatter(row_grads[2], ("seq", "rows"), scatter_dimension=2, tiled=True),
        )
        if adjusted_grads is None:
            adjusted_grads = shares
        else:
            adjusted_grads = tuple(
                (former + latter for former, latter in zip(adjusted_grads, shares))
            )
        outputs.append(layer_out)
        input_grads.append(input_grad)
        memory_grads.append(memory_grad)
    return (
        jnp.stack(outputs),
        jnp.stack(input_grads),
        jnp.stack(memory_grads),
        adjusted_grads[2],
        adjusted_grads[0],
        adjusted_grads[1],
    )


MESH_ID = pl.DeviceIdType.MESH
F32 = jnp.float32
BF16 = jnp.bfloat16
VMEM_BYTES = 60 * 1024 * 1024
PAIRS = HEADS // 2
LANES = 2 * HEAD_DIM
Q_AT, K_AT, V_AT, SELF_OUT_AT, CROSS_Q_AT, MEM_K_AT, MEM_V_AT, CROSS_OUT_AT = range(0, 256, 32)
INNER_AT, OUTER_AT, MIXED_AT = 256, 384, 512
ALL_ROWS = 544
SMALL_ROWS = 144
PIECE_ROWS = 16
GAP = 6
LEAD = 4
SENDS = 3
Z_LAST = ()
WAIT_TICKS = 4
STEP_TICKS = 1


def whole(space=pltpu.VMEM):
    return pl.BlockSpec(memory_space=space)


def params(collective_id=None):
    if collective_id is None:
        return pltpu.CompilerParams(vmem_limit_bytes=VMEM_BYTES)
    return pltpu.CompilerParams(
        vmem_limit_bytes=VMEM_BYTES, collective_id=collective_id, has_side_effects=True
    )


def remote(src, dst, send_sem, recv_sem, device):
    return pltpu.make_async_remote_copy(
        src_ref=src, dst_ref=dst, send_sem=send_sem, recv_sem=recv_sem,
        device_id=device, device_id_type=MESH_ID,
    )


def greet(peers):
    barrier = pltpu.get_barrier_semaphore()
    for peer in peers:
        pl.semaphore_signal(barrier, inc=1, device_id=peer, device_id_type=MESH_ID)
    pl.semaphore_wait(barrier, len(peers))


def dot_nn(left, right):
    return lax.dot_general(left, right, (((1,), (0,)), ((), ())), preferred_element_type=F32)


class Place:
    def __init__(self):
        self.seq, self.x = lax.axis_index("seq"), lax.axis_index("rows")
        self.z, self.y, self.core = self.seq // 4, (self.seq // 2) % 2, self.seq % 2
        self.pair, self.row = self.seq // 2, self.seq % 2

    def device(self, z, y, core, x):
        return ((z * 2 + y) * 2 + core, x)

    def along_z(self, step):
        return self.device((self.z + step) % 4, self.y, self.core, self.x)

    def along_y(self):
        return self.device(self.z, 1 - self.y, self.core, self.x)

    def along_x(self):
        return self.device(self.z, self.y, self.core, 1 - self.x)

    def other_core(self):
        return self.device(self.z, self.y, 1 - self.core, self.x)

    def diagonal(self):
        return self.device(self.z, self.y, 1 - self.core, 1 - self.x)

    def others(self):
        return [((self.seq + step) % 16, self.x) for step in range(1, 16)]


class Gather:
    def __init__(self, place, full, local_sem, sems, gap):
        self.place, self.full, self.local_sem, self.sems, self.gap = place, full, local_sem, sems, gap
        self.stages = []
        self.waiting = []
        self.cut = 1
        self.tick_at = 0

    def copies(self, level, source, target, device, slot):
        k = len(self.stages)
        return remote(source, target, self.sems[2 * level].at[k, slot], self.sems[2 * level + 1].at[k, slot], device)

    def add(self, source, first, count, piece=PIECE_ROWS):
        for from_row in range(0, count, piece):
            self.add_piece(source.at[pl.ds(from_row, piece)], first + from_row, piece)
        return len(self.stages) - 1

    def add_piece(self, source, first, count):
        at, full = self.place, self.full
        z, y, core, x = at.z, at.y, at.core, at.x
        rows = pl.ds(first, count)
        mine = full.at[z, y, core, x, rows]
        k = len(self.stages)
        if k in Z_LAST:
            plane = full.at[z, :, core, :, rows]
            first_way, then_way = (at.along_x(), at.along_y()) if k % 2 else (at.along_y(), at.along_x())
            line = full.at[z, y, core, :, rows] if k % 2 else full.at[z, :, core, x, rows]
            self.stages.append((
                pltpu.make_async_copy(source, mine, self.local_sem.at[k]),
                [self.copies(0, source, mine, first_way, 0)],
                [self.copies(1, line, line, then_way, 0)],
                [self.copies(2, plane, plane, at.along_z(d + 1), d) for d in range(3)],
                [self.copies(3, full.at[:, :, core, :, rows], full.at[:, :, core, :, rows], at.other_core(), 0)],
            ))
            return
        cut = self.cut
        near, far = pl.ds(0, cut), pl.ds(cut, 4 - cut)
        near1, far1 = full.at[near, y, core, x, rows], full.at[far, y, core, x, rows]
        near2, far2 = full.at[near, y, core, :, rows], full.at[far, :, core, x, rows]
        half = full.at[:, :, core, :, rows]
        self.stages.append((
            pltpu.make_async_copy(source, mine, self.local_sem.at[len(self.stages)]),
            [self.copies(0, source, mine, at.along_z(d + 1), d) for d in range(3)],
            [self.copies(1, near1, near1, at.along_x(), 0), self.copies(1, far1, far1, at.along_y(), 1)],
            [self.copies(2, near2, near2, at.along_y(), 0), self.copies(2, far2, far2, at.along_x(), 1)],
            [self.copies(3, half, half, at.other_core(), 0)],
        ))

    def add_memory_row(self, source, full):
        at = self.place
        mine, column, half = full.at[at.z, at.y, at.core], full.at[:, at.y, at.core], full.at[:, :, at.core]
        self.stages.append((
            pltpu.make_async_copy(source, mine, self.local_sem.at[len(self.stages)]),
            [self.copies(0, source, mine, at.along_z(d + 1), d) for d in range(3)],
            [self.copies(1, column, column, at.along_y(), 1)],
            [],
            [self.copies(3, half, half, at.other_core(), 0)],
        ))

    def start(self):
        for stage in self.stages:
            stage[0].start()

    def tick(self, count=1):
        for _ in range(count):
            for level in range(5):
                k = self.tick_at - self.after(level)
                if not 0 <= k < len(self.stages):
                    continue
                if level == 1:
                    self.stages[k][0].wait()
                if level > 0:
                    for copy in self.stages[k][level]:
                        copy.wait_recv()
                if level < 4:
                    for copy in self.stages[k][level + 1]:
                        copy.start()
            self.tick_at += 1
            for _ in range(SENDS):
                if self.waiting:
                    self.waiting.pop(0).start()

    def after(self, level):
        return 0 if level == 0 else LEAD + (level - 1) * self.gap

    def until(self, k):
        while self.tick_at <= k + self.after(4):
            self.tick()

    def finish(self):
        self.until(len(self.stages) - 1)
        for _, *levels in self.stages:
            for level in levels:
                for copy in level:
                    copy.wait_send()


def head_masks():
    lane = lax.broadcasted_iota(jnp.int32, (1, LANES), 1)
    first = (lane < HEAD_DIM).astype(F32).astype(BF16)
    return first, (1.0 - first.astype(F32)).astype(BF16)


def stack_heads(block):
    first, second = head_masks()
    return jnp.concatenate([block * first, block * second], axis=0)


def merge_heads(stacked):
    half = stacked.shape[0] // 2
    lane = lax.broadcasted_iota(jnp.int32, (half, LANES), 1)
    return jnp.where(lane < HEAD_DIM, stacked[:half], stacked[half:])


def rows_in_lanes(values):
    lane = lax.broadcasted_iota(jnp.int32, (8, LANES), 1)
    row = lax.broadcasted_iota(jnp.int32, (8, LANES), 0)
    picks = (lane // HEAD_DIM == row).astype(F32)
    return lax.dot_general(
        picks, values, (((1,), (1,)), ((), ())),
        precision=lax.Precision.HIGHEST, preferred_element_type=F32,
    )


def first_kernel(
    tokens, memory, small, docs,
    project, self_out, cross_q, cross_mem, cross_out, inner, outer, mixed,
    full, memory_full, memory_pairs_far, docs_column_far, arrived_far, attended_far, inverse_far,
    first_resid_far, cross_queries_far, crossed_far, cross_inverse_far,
    small_full, docs_all, docs_row, second_resid, second_norm,
    memory_pairs, docs_column, arrived, attended, inverse, first_resid, cross_queries, crossed, cross_inverse,
    gathered, first_norm, weights, staged, quad, memory_held, result_staged, sums, parts,
    local_sem, send0, recv0, send1, recv1, send2, recv2, send3, recv3,
    fetch_sem, own_sem, quad_send, quad_recv, small_send, small_recv, docs_send, docs_recv,
    head_send, head_recv, out_send, out_recv, leave_sem,
):
    leaving = []

    def leave(*arrays):
        for held, target in arrays:
            leaving.append(pltpu.make_async_copy(held, target, leave_sem.at[len(leaving)]))
            leaving[-1].start()

    place = Place()
    seq, x, pair, row = place.seq, place.x, place.pair, place.row
    others = place.others()
    quad_peers = [place.other_core(), place.along_x(), place.diagonal()]
    greet(others + quad_peers[1:])

    engine = Gather(place, full, local_sem, (send0, recv0, send1, recv1, send2, recv2, send3, recv3), GAP)
    project_done = [
        engine.add(project.at[:, pl.ds(part * D, D)], at, 32) for part, at in enumerate((Q_AT, K_AT, V_AT))
    ]
    for part, at in enumerate((MEM_K_AT, MEM_V_AT)):
        for half in range(2):
            held = pl.ds(16 * half, 16)
            engine.add_memory_row(memory.at[part, held], memory_full.at[:, :, :, part, held])
            memory_done = engine.add(cross_mem.at[held, pl.ds(part * D, D)], at + 16 * half, 16)
    out_done = engine.add(self_out, SELF_OUT_AT, 32)
    query_done = engine.add(cross_q, CROSS_Q_AT, 32)
    cross_done = engine.add(cross_out, CROSS_OUT_AT, 32)
    engine.cut = 2
    for part in range(4):
        engine.add(inner.at[:, pl.ds(part * D, D)], INNER_AT + 32 * part, 32)
    for part in range(4):
        engine.add(outer.at[pl.ds(32 * part, 32)], OUTER_AT + 32 * part, 32)
    engine.add(mixed, MIXED_AT, 32)
    engine.start()
    engine.tick()

    mine = place.core * 2 + x
    quad_copies = [
        remote(small, quad.at[mine], quad_send.at[k], quad_recv.at[k], quad_peers[k]) for k in range(3)
    ]
    own_small = pltpu.make_async_copy(small, quad.at[mine], own_sem.at[0])
    docs_copies = [
        remote(docs, docs_all.at[seq], docs_send.at[k], docs_recv.at[k], others[k]) for k in range(15)
    ]
    own_docs = pltpu.make_async_copy(docs, docs_all.at[seq], own_sem.at[1])
    own_small.start()
    own_docs.start()
    for copy in quad_copies + docs_copies:
        copy.start()
    rows = tokens[...].reshape(2 * S_DEV, D)
    fetches = []
    for part in range(3):
        engine.until(project_done[part])
        fetches.append(pltpu.make_async_copy(full_rows(full, 32 * part), weights.at[part], fetch_sem.at[part]))
        fetches[part].start()
    for part in range(3):
        fetches[part].wait()
        result = dot_nn(rows, weights[part].reshape(D, D)).astype(BF16)
        for at_row in range(2):
            for at_pair in range(PAIRS):
                staged[at_pair, at_row, part] = result[
                    at_row * S_DEV:(at_row + 1) * S_DEV, at_pair * LANES:(at_pair + 1) * LANES
                ]
        engine.tick()
    head_copies = []
    for k in range(15):
        to = (seq + k + 1) % 16
        head_copies.append(
            remote(staged.at[to // 2, to % 2], arrived.at[seq], head_send.at[k], head_recv.at[k], others[k])
        )
    own_heads = pltpu.make_async_copy(staged.at[pair, row], arrived.at[seq], own_sem.at[2])
    own_heads.start()
    engine.waiting = list(head_copies)
    engine.tick(2)
    own_small.wait()
    for copy in quad_copies:
        copy.wait()
    small_full[pair] = (quad[0] + quad[1]) + (quad[2] + quad[3])
    small_copies = []
    for k in range(1, 8):
        to = (((pair + k) % 8) * 2 + place.core, x)
        small_copies.append(
            remote(small_full.at[pair], small_full.at[pair], small_send.at[k], small_recv.at[k], to)
        )
        small_copies[-1].start()
    own_docs.wait()
    for copy in docs_copies:
        copy.wait()

    def spread_docs(at, carry):
        tile = docs_all[at]
        line = jnp.where(row == 0, tile[0:1], tile[1:2])
        docs_row[:, pl.ds(pl.multiple_of(at * S_DEV, S_DEV), S_DEV)] = jnp.broadcast_to(line, (8, S_DEV))
        docs_column[pl.ds(at * S_DEV, S_DEV)] = jnp.transpose(jnp.broadcast_to(line, (S_DEV, LANES)))
        return carry

    lax.fori_loop(0, 16, spread_docs, 0)

    engine.until(memory_done)
    fetch_memory = pltpu.make_async_copy(memory_full, memory_held, own_sem.at[3])
    fetch_memory.start()
    fetches = [
        pltpu.make_async_copy(full_rows(full, at), weights.at[part], fetch_sem.at[part])
        for part, at in enumerate((MEM_K_AT, MEM_V_AT))
    ]
    for fetch in fetches:
        fetch.start()
    fetch_memory.wait()
    for part in range(2):
        fetches[part].wait()

        def project_memory(at, carry):
            held = memory_held[at].reshape(4 * 2 * M_DEV, D)
            result = dot_nn(held, weights[part].reshape(D, D)).astype(BF16)
            memory_pairs[pl.ds(4 * at, 4), :, :, pl.ds(part * D, D)] = result.reshape(4, 2, M_DEV, D)
            return carry

        lax.fori_loop(0, 4, project_memory, 0)
    engine.tick(max(WAIT_TICKS, -(-len(engine.waiting) // SENDS)))
    own_heads.wait()
    for copy in head_copies:
        copy.wait()

    leave((memory_pairs, memory_pairs_far), (docs_column, docs_column_far), (arrived, arrived_far))

    block = 2 * S_DEV
    columns = pl.ds(pl.multiple_of(pair * LANES, LANES), LANES)
    target = gathered.at[row, :, columns]
    away = (
        lax.broadcasted_iota(jnp.int32, (block, block), 1)
        - lax.broadcasted_iota(jnp.int32, (block, block), 0)
    )
    prefix_lane = lax.broadcasted_iota(jnp.int32, (2 * block, 32), 1)
    prefix_keys, prefix_values = small_full[pair, 0:32], small_full[pair, 32:64]

    for step in range(8):
        at = (step + pair) % 8
        queries = stack_heads(arrived[pl.ds(2 * at, 2), 0].reshape(block, LANES))
        query_docs = docs_column[pl.ds(at * block, block)]
        scores = dot_right(queries, prefix_keys) * score_scale
        e = jnp.where(prefix_lane < PREFIX, jnp.exp(scores), 0.0)
        sums[...] = jnp.concatenate([e, jnp.zeros((2 * block, LANES - 32), F32)], axis=1)
        parts[...] = dot_nn(e.astype(BF16), prefix_values)

        def one_tile(key_at, carry):
            keys = arrived[pl.ds(2 * key_at, 2), 1].reshape(block, LANES)
            values = arrived[pl.ds(2 * key_at, 2), 2].reshape(block, LANES)
            key_docs = docs_row[0:1, pl.ds(pl.multiple_of(key_at * block, block), block)]
            same = jnp.concatenate([query_docs, query_docs], axis=1) == key_docs
            allowed = same & (away <= (at - key_at) * block)
            scores = dot_right(queries, keys) * score_scale
            e = jnp.where(allowed[None], jnp.exp(scores).reshape(2, block, block), 0.0)
            e = e.reshape(2 * block, block)
            sums[...] += e[:, :LANES] + e[:, LANES:]
            parts[...] += dot_nn(e.astype(BF16), values)
            return carry

        lax.fori_loop(0, at + 1, one_tile, 0)
        totals = 1.0 / jnp.sum(sums[...], axis=1, keepdims=True)
        result = merge_heads(parts[...] * totals)
        here = pl.ds(at * block, block)
        attended[here] = result
        inverse[here] = merge_heads(jnp.broadcast_to(totals, (2 * block, LANES)))
        result_staged[pl.ds(2 * at, 2)] = result.astype(BF16).reshape(2, S_DEV, LANES)
        for half in range(2):
            to = 2 * at + half

            @pl.when(to != seq)
            def _():
                remote(result_staged.at[to], target, out_send.at[to], out_recv.at[seq], (to, x)).start()

            @pl.when(to == seq)
            def _():
                pltpu.make_async_copy(result_staged.at[to], target, own_sem.at[4]).start()

        engine.tick(step % 2)

    leave((attended, attended_far), (inverse, inverse_far))

    for copy in small_copies:
        copy.wait()
    engine.until(cross_done)
    fetches = [
        pltpu.make_async_copy(full_rows(full, at), weights.at[part], fetch_sem.at[part])
        for part, at in enumerate((SELF_OUT_AT, CROSS_Q_AT, CROSS_OUT_AT))
    ]
    for fetch in fetches:
        fetch.start()
    gains = [
        jnp.concatenate(
            [small_full[at_pair, 128:144].astype(F32)[part:part + 1] for at_pair in range(PAIRS)], axis=1
        )
        for part in range(2)
    ]
    pltpu.make_async_copy(result_staged.at[seq], target, own_sem.at[4]).wait()
    for other, _ in others:
        remote(result_staged.at[other], target, out_send.at[other], out_recv.at[other], (other, x)).wait()
    fetches[0].wait()
    resid = tokens[...].reshape(2 * S_DEV, D).astype(F32) + dot_nn(
        gathered[...].reshape(2 * S_DEV, D), weights[0].reshape(D, D)
    )
    first_resid[...] = resid
    normed = norm_rows(resid, gains[0])
    first_norm[...] = normed
    engine.tick(STEP_TICKS)
    fetches[1].wait()
    cross_queries[...] = dot_nn(normed.astype(BF16), weights[1].reshape(D, D)).astype(BF16).reshape(2, S_DEV, D)
    engine.tick(STEP_TICKS)
    memory_len = 16 * M_DEV
    cross_prefix_lane = lax.broadcasted_iota(jnp.int32, (2 * S_DEV, 32), 1)
    for at_row in range(2):
        own = jnp.transpose(jnp.broadcast_to(docs[at_row:at_row + 1], (LANES, S_DEV)))
        own = jnp.concatenate([own] * (memory_len // LANES), axis=1)
        lines = [
            sum(docs_all[4 * at + k, 2 + at_row:3 + at_row] for k in range(4)) for at in range(4)
        ]
        allowed = own == jnp.concatenate(lines, axis=1)

        def one_pair(at_pair, carry):
            first = pl.multiple_of(at_pair * LANES, LANES)
            columns, value_columns = pl.ds(first, LANES), pl.ds(pl.multiple_of(first + D, LANES), LANES)
            stacked = stack_heads(cross_queries[at_row, :, columns])
            keys = memory_pairs[:, at_row, :, columns].reshape(memory_len, LANES)
            values = memory_pairs[:, at_row, :, value_columns].reshape(memory_len, LANES)
            scores = dot_right(stacked, small_full[at_pair, 64:96]) * score_scale
            prefix_e = jnp.where(cross_prefix_lane < PREFIX, jnp.exp(scores), 0.0)
            scores = dot_right(stacked, keys) * score_scale
            e = jnp.where(allowed[None], jnp.exp(scores).reshape(2, S_DEV, memory_len), 0.0)
            e = e.reshape(2 * S_DEV, memory_len)
            totals = jnp.sum(e, axis=1, keepdims=True) + jnp.sum(prefix_e, axis=1, keepdims=True)
            totals = 1.0 / totals
            summed = dot_nn(e.astype(BF16), values) + dot_nn(prefix_e.astype(BF16), small_full[at_pair, 96:128])
            crossed[at_row, :, columns] = merge_heads(summed * totals)
            cross_inverse[at_row, :, columns] = merge_heads(jnp.broadcast_to(totals, (2 * S_DEV, LANES)))
            return carry

        lax.fori_loop(0, PAIRS // 2, one_pair, 0)
        engine.tick(STEP_TICKS)
        lax.fori_loop(PAIRS // 2, PAIRS, one_pair, 0)
        engine.tick(STEP_TICKS)
    leave(
        (first_resid, first_resid_far), (cross_queries, cross_queries_far),
        (crossed, crossed_far), (cross_inverse, cross_inverse_far),
    )
    fetches[2].wait()
    resid = first_norm[...] + dot_nn(
        crossed[...].reshape(2 * S_DEV, D).astype(BF16), weights[2].reshape(D, D)
    )
    second_resid[...] = resid
    second_norm[...] = norm_rows(resid, gains[1])
    for copy in leaving:
        copy.wait()
    engine.finish()


def full_rows(full, first):
    return full.at[:, :, :, :, pl.ds(first, 32)]


def first_call(tokens, memory, small, docs, *weights):
    length = 16 * S_DEV
    chunks = 16 * 32 // PIECE_ROWS + 32 // PIECE_ROWS + 4
    dma = pltpu.SemaphoreType.DMA
    shape = jax.ShapeDtypeStruct
    outs = pl.pallas_call(
        first_kernel,
        out_shape=(
            shape((4, 2, 2, 2, ALL_ROWS, D), BF16),
            shape((4, 2, 2, 2, M_DEV, D), BF16),
            shape((16, 2, M_DEV, 2 * D), BF16),
            shape((length, LANES), F32),
            shape((16, 3, S_DEV, LANES), BF16),
            shape((length, LANES), F32),
            shape((length, LANES), F32),
            shape((2 * S_DEV, D), F32),
            shape((2, S_DEV, D), BF16),
            shape((2, S_DEV, D), F32),
            shape((2, S_DEV, D), F32),
            shape((8, SMALL_ROWS, LANES), BF16),
            shape((16, 8, LANES), F32),
            shape((8, length), F32),
            shape((2 * S_DEV, D), F32),
            shape((2 * S_DEV, D), F32),
        ),
        in_specs=[whole(), whole(pl.ANY), whole(), whole()] + [whole(pl.ANY)] * 8,
        out_specs=(whole(pl.ANY),) * 11 + (whole(),) * 5,
        scratch_shapes=[
            pltpu.VMEM((16, 2, M_DEV, 2 * D), BF16),
            pltpu.VMEM((length, LANES), F32),
            pltpu.VMEM((16, 3, S_DEV, LANES), BF16),
            pltpu.VMEM((length, LANES), F32),
            pltpu.VMEM((length, LANES), F32),
            pltpu.VMEM((2 * S_DEV, D), F32),
            pltpu.VMEM((2, S_DEV, D), BF16),
            pltpu.VMEM((2, S_DEV, D), F32),
            pltpu.VMEM((2, S_DEV, D), F32),
            pltpu.VMEM((2, S_DEV, D), BF16),
            pltpu.VMEM((2 * S_DEV, D), F32),
            pltpu.VMEM((3, 4, 2, 2, 2, 32, D), BF16),
            pltpu.VMEM((PAIRS, 2, 3, S_DEV, LANES), BF16),
            pltpu.VMEM((4, SMALL_ROWS, LANES), BF16),
            pltpu.VMEM((4, 2, 2, 2, M_DEV, D), BF16),
            pltpu.VMEM((16, S_DEV, LANES), BF16),
            pltpu.VMEM((4 * S_DEV, LANES), F32),
            pltpu.VMEM((4 * S_DEV, LANES), F32),
            dma((chunks,)),
            dma((chunks, 3)), dma((chunks, 3)), dma((chunks, 2)), dma((chunks, 2)),
            dma((chunks, 3)), dma((chunks, 3)), dma((chunks, 1)), dma((chunks, 1)),
            dma((3,)), dma((5,)), dma((3,)), dma((3,)), dma((8,)), dma((8,)), dma((15,)), dma((15,)),
            dma((15,)), dma((15,)), dma((16,)), dma((16,)), dma((9,)),
        ],
        compiler_params=params(0),
        name="first",
    )(tokens, memory, small, docs, *weights)
    return (outs[0].reshape(32, ALL_ROWS, D),) + tuple(outs[2:])


def second_kernel(
    second_grad, second_resid, small_full, docs, docs_all, docs_row, crossed, cross_inverse, cross_queries,
    full, memory_pairs_far, first_resid_far, arrived_far, attended_far, inverse_far, docs_column_far, small_grads,
    input_grad, memory_grad, down_grad, up_grad, prefix_sum,
    weights, memory_pairs, first_resid, arrived, attended, inverse, docs_column,
    pull, cross_grad, cross_query_grad, key_terms, value_terms, cross_prefix,
    small_core, small_mine, small_x, small_pair, small_y, small_line, small_all,
    memory_part, memory_core, memory_mine, memory_y, memory_line, memory_all,
    prefix_y, prefix_line, prefix_all, prefix_mine, prefix_quad,
    heads_out, grads, grad_low, delta, query_grads, key_grads, value_grads, staged, gathered,
    fetch_sem, own_sem, near_send, near_recv, line_send, line_recv, small_send, small_recv, memory_send, memory_recv,
    prefix_send, prefix_recv, quad_send, quad_recv,
    in_send, in_recv, out_send, out_recv, query_send, query_recv,
):
    place = Place()
    seq, x, pair, row, core = place.seq, place.x, place.pair, place.row, place.core
    z, y = place.z, place.y
    others = place.others()
    tokens = 2 * S_DEV
    memory_len = 16 * M_DEV
    block = 2 * S_DEV

    fetches = {}

    def fetch(name, source, target):
        fetches[name] = pltpu.make_async_copy(source, target, fetch_sem.at[len(fetches)])
        fetches[name].start()

    firsts = (CROSS_OUT_AT, CROSS_Q_AT, SELF_OUT_AT, MEM_K_AT, MEM_V_AT, Q_AT, K_AT, V_AT)

    def fetch_weight(at):
        fetch(at, full.at[:, pl.ds(at, 32)], weights.at[firsts.index(at)])

    def weight(at):
        return weights[firsts.index(at)].reshape(D, D)

    fetch_weight(CROSS_OUT_AT)
    fetch("pairs", memory_pairs_far, memory_pairs)
    fetch_weight(CROSS_Q_AT)
    fetch("resid", first_resid_far, first_resid)
    fetch_weight(SELF_OUT_AT)
    fetch_weight(MEM_K_AT)
    fetch_weight(MEM_V_AT)
    fetch("arrived", arrived_far, arrived)
    fetch("attended", attended_far, attended)
    fetch("inverse", inverse_far, inverse)
    fetch("docs", docs_column_far, docs_column)
    for at in (K_AT, V_AT, Q_AT):
        fetch_weight(at)
    greet(others + [place.along_x(), place.diagonal()])

    small_first = remote(
        small_grads.at[:, :, 1 - core], small_core, near_send.at[0], near_recv.at[0], place.other_core()
    )
    small_own = pltpu.make_async_copy(small_grads.at[:, :, core], small_mine, own_sem.at[0])
    small_second = remote(small_mine.at[:, :, 1 - x], small_x, near_send.at[1], near_recv.at[1], place.along_x())

    def along_y(k, source, target):
        return remote(source.at[:, 1 - y], target, line_send.at[k], line_recv.at[k], place.along_y())

    def along_z(source, target, sends, recvs):
        return [
            remote(source.at[(z + k) % 4], target.at[z], sends.at[k], recvs.at[k], place.along_z(k))
            for k in range(1, 4)
        ]

    small_third = along_y(0, small_pair, small_y)
    small_fourth = along_z(small_line, small_all, small_send, small_recv)
    memory_first = remote(
        memory_part.at[:, :, 1 - core], memory_core, near_send.at[2], near_recv.at[2], place.other_core()
    )
    memory_second = along_y(1, memory_mine, memory_y)
    memory_third = along_z(memory_line, memory_all, memory_send, memory_recv)
    prefix_first = along_y(2, cross_prefix, prefix_y)
    prefix_second = along_z(prefix_line, prefix_all, prefix_send, prefix_recv)
    small_first.start()
    small_own.start()

    gains = [
        jnp.concatenate(
            [small_full[at_pair, 128:144].astype(F32)[part:part + 1] for at_pair in range(PAIRS)], axis=1
        )
        for part in range(2)
    ]
    pulled = norm_back_rows(second_resid[...], gains[1], second_grad[...])
    pull[...] = pulled
    fetches[CROSS_OUT_AT].wait()
    cross_grad[...] = dot_right(pulled.astype(BF16), weight(CROSS_OUT_AT)).reshape(2, S_DEV, D)
    fetches["pairs"].wait()

    cross_pad = lax.broadcasted_iota(jnp.int32, (64, S_DEV), 0) % 32
    for at_row in range(2):
        lines = [sum(docs_all[4 * at + k, 2 + at_row:3 + at_row] for k in range(4)) for at in range(4)]
        key_docs = jnp.concatenate(
            [jnp.transpose(jnp.broadcast_to(line, (S_DEV, LANES))) for line in lines], axis=0
        )
        allowed = key_docs == docs[at_row:at_row + 1]

        def one_pair(at_pair, carry):
            first = pl.multiple_of(at_pair * LANES, LANES)
            columns, value_columns = pl.ds(first, LANES), pl.ds(pl.multiple_of(first + D, LANES), LANES)
            heads = cross_queries[at_row, :, columns]
            grad = cross_grad[at_row, :, columns] * cross_inverse[at_row, :, columns]
            low = grad.astype(BF16)
            lines = rows_in_lanes(grad * crossed[at_row, :, columns])

            def head_rows(count):
                return jnp.concatenate(
                    [jnp.broadcast_to(lines[0:1], (count, S_DEV)), jnp.broadcast_to(lines[1:2], (count, S_DEV))],
                    axis=0,
                )

            prefix_key_stack = stack_heads(small_full[at_pair, 64:96])
            prefix_value_stack = stack_heads(small_full[at_pair, 96:128])
            e = jnp.exp(dot_right(prefix_key_stack, heads) * score_scale)
            e = jnp.where(cross_pad < PREFIX, e, 0.0)
            slopes = (e * (dot_right(prefix_value_stack, low) - head_rows(32))).astype(BF16)
            from_prefix = dot_left(slopes, prefix_key_stack)
            key_grad = merge_heads(dot_nn(slopes, heads)) * score_scale
            value_grad = merge_heads(dot_nn(e.astype(BF16), low))
            held = cross_prefix.at[at_pair // 2, at_pair % 2]
            if at_row == 0:
                held[0] = key_grad
                held[1] = value_grad
            else:
                held[0] += key_grad
                held[1] += value_grad
            key_stack = stack_heads(memory_pairs[:, at_row, :, columns].reshape(memory_len, LANES))
            value_stack = stack_heads(memory_pairs[:, at_row, :, value_columns].reshape(memory_len, LANES))
            e = jnp.exp(dot_right(key_stack, heads) * score_scale).reshape(2, memory_len, S_DEV)
            e = jnp.where(allowed[None], e, 0.0).reshape(2 * memory_len, S_DEV)
            slopes = (e * (dot_right(value_stack, low) - head_rows(memory_len))).astype(BF16)
            terms = merge_heads(dot_nn(slopes, heads)) * score_scale
            key_terms[:, at_row, :, columns] = terms.astype(BF16).reshape(16, M_DEV, LANES)
            terms = merge_heads(dot_nn(e.astype(BF16), low))
            value_terms[:, at_row, :, columns] = terms.astype(BF16).reshape(16, M_DEV, LANES)
            query_grad = (from_prefix + dot_left(slopes, key_stack)) * score_scale
            cross_query_grad[at_row, :, columns] = query_grad.astype(BF16)
            return carry

        lax.fori_loop(0, PAIRS, one_pair, 0)
        if at_row == 0:
            small_own.wait()
            small_first.wait_recv()
            small_mine[...] = small_mine[...] + small_core[...]
            small_second.start()
    prefix_first.start()

    fetches[CROSS_Q_AT].wait()
    fetches["resid"].wait()
    first_grad = pull[...] + dot_right(cross_query_grad[...].reshape(tokens, D), weight(CROSS_Q_AT))
    resid_grad = norm_back_rows(first_resid[...], gains[0], first_grad)
    pull[...] = resid_grad
    fetches[SELF_OUT_AT].wait()
    out_grad = dot_right(resid_grad.astype(BF16), weight(SELF_OUT_AT)).astype(BF16)
    for at_pair in range(PAIRS):
        for at_row in range(2):
            heads_out[at_pair, at_row] = out_grad[
                at_row * S_DEV:(at_row + 1) * S_DEV, at_pair * LANES:(at_pair + 1) * LANES
            ]
    arrivals = []
    for k in range(15):
        to = (seq + k + 1) % 16
        arrivals.append(remote(heads_out.at[to // 2, to % 2], grads.at[seq], in_send.at[k], in_recv.at[k], others[k]))
        arrivals[-1].start()
    own_heads = pltpu.make_async_copy(heads_out.at[pair, row], grads.at[seq], own_sem.at[1])
    own_heads.start()

    fetches[MEM_K_AT].wait()
    fetches[MEM_V_AT].wait()

    def memory_block(at, carry):
        there = pl.ds(4 * at, 4)
        terms = dot_right(key_terms[there].reshape(8 * M_DEV, D), weight(MEM_K_AT))
        terms += dot_right(value_terms[there].reshape(8 * M_DEV, D), weight(MEM_V_AT))
        memory_part[at] = terms.astype(BF16).reshape(2, 2, 2 * M_DEV, D)
        return carry

    lax.fori_loop(0, 4, memory_block, 0)
    memory_first.start()
    small_second.wait()
    small_pair[...] = small_mine[:, :, x] + small_x[...]
    small_third.start()
    memory_first.wait()
    memory_mine[...] = memory_part[:, :, core] + memory_core[...]
    memory_second.start()
    for name in ("arrived", "attended", "inverse", "docs"):
        fetches[name].wait()
    own_heads.wait()
    for copy in arrivals:
        copy.wait()

    pad_row = lax.broadcasted_iota(jnp.int32, (64, block), 0) % 32
    prefix_key_stack = stack_heads(small_full[pair, 0:32])
    prefix_value_stack = stack_heads(small_full[pair, 32:64])

    def head_rows(at, count):
        there = delta[:, pl.ds(pl.multiple_of(at * block, block), block)]
        return jnp.concatenate(
            [jnp.broadcast_to(there[0:1], (count, block)), jnp.broadcast_to(there[1:2], (count, block))],
            axis=0,
        )

    prefix_mine[...] = jnp.zeros(prefix_mine.shape, F32)

    def prepare(at, carry):
        here = pl.ds(at * block, block)
        grad = grads[pl.ds(2 * at, 2)].reshape(block, LANES).astype(F32) * inverse[here]
        low = grad.astype(BF16)
        grad_low[here] = low
        delta[:, pl.ds(pl.multiple_of(at * block, block), block)] = rows_in_lanes(grad * attended[here])
        queries = arrived[pl.ds(2 * at, 2), 0].reshape(block, LANES)
        e = jnp.exp(dot_right(prefix_key_stack, queries) * score_scale)
        e = jnp.where(pad_row < PREFIX, e, 0.0)
        slopes = (e * (dot_right(prefix_value_stack, low) - head_rows(at, 32))).astype(BF16)
        prefix_mine[0] += merge_heads(dot_nn(slopes, queries)) * score_scale
        prefix_mine[1] += merge_heads(dot_nn(e.astype(BF16), low))
        query_grads[here] = dot_left(slopes, prefix_key_stack)
        return carry

    lax.fori_loop(0, 8, prepare, 0)
    prefix_first.wait()
    prefix_line[...] = cross_prefix[:, y] + prefix_y[...]
    for copy in prefix_second:
        copy.start()
    prefix_all[z] = prefix_line[z]
    small_third.wait()
    small_line[...] = small_pair[:, y] + small_y[...]
    for copy in small_fourth:
        copy.start()
    small_all[z] = small_line[z]

    away = (
        lax.broadcasted_iota(jnp.int32, (block, block), 0)
        - lax.broadcasted_iota(jnp.int32, (block, block), 1)
    )

    def send_block(part, count, at, send, recv):
        for half in range(2):
            to = 2 * at + half
            source = staged.at[to, pl.ds(part, count)]
            mine = gathered.at[pair, row, pl.ds(part, count)]

            @pl.when(to != seq)
            def _():
                remote(source, mine, send.at[to], recv.at[seq], (to, x)).start()

            @pl.when(to == seq)
            def _():
                pltpu.make_async_copy(source, mine, own_sem.at[2 + part]).start()

    def one_block(step, carry):
        key_at = (step + pair) % 8
        keys = stack_heads(arrived[pl.ds(2 * key_at, 2), 1].reshape(block, LANES))
        values = stack_heads(arrived[pl.ds(2 * key_at, 2), 2].reshape(block, LANES))
        key_docs = docs_column[pl.ds(key_at * block, block)]
        key_docs = jnp.concatenate([key_docs, key_docs], axis=1)
        key_grads[...] = jnp.zeros(key_grads.shape, F32)
        value_grads[...] = jnp.zeros(value_grads.shape, F32)

        def one_tile(at, carry):
            here = pl.ds(at * block, block)
            queries = arrived[pl.ds(2 * at, 2), 0].reshape(block, LANES)
            low = grad_low[here]
            query_docs = docs_row[0:1, pl.ds(pl.multiple_of(at * block, block), block)]
            allowed = (key_docs == query_docs) & (away <= (at - key_at) * block)
            e = jnp.exp(dot_right(keys, queries) * score_scale).reshape(2, block, block)
            e = jnp.where(allowed[None], e, 0.0).reshape(2 * block, block)
            slopes = (e * (dot_right(values, low) - head_rows(at, block))).astype(BF16)
            key_grads[...] += dot_nn(slopes, queries)
            value_grads[...] += dot_nn(e.astype(BF16), low)
            query_grads[here] += dot_left(slopes, keys)
            return carry

        lax.fori_loop(key_at, 8, one_tile, 0)
        there = pl.ds(2 * key_at, 2)
        staged[there, 1] = (merge_heads(key_grads[...]) * score_scale).astype(BF16).reshape(2, S_DEV, LANES)
        staged[there, 2] = merge_heads(value_grads[...]).astype(BF16).reshape(2, S_DEV, LANES)
        send_block(1, 2, key_at, out_send, out_recv)
        return carry

    lax.fori_loop(0, 2, one_block, 0)
    memory_second.wait()
    memory_line[...] = memory_mine[:, y] + memory_y[...]
    for copy in memory_third:
        copy.start()
    memory_all[z] = memory_line[z]
    lax.fori_loop(2, 8, one_block, 0)

    def last_block(step, carry):
        at = (step + pair) % 8
        result = (query_grads[pl.ds(at * block, block)] * score_scale).astype(BF16)
        staged[pl.ds(2 * at, 2), 0] = result.reshape(2, S_DEV, LANES)
        send_block(0, 1, at, query_send, query_recv)
        return carry

    lax.fori_loop(0, 8, last_block, 0)
    small_first.wait_send()
    for copy in prefix_second:
        copy.wait()
    for part in range(2):
        prefix_mine[2 + part] = sum(prefix_all[k, part] for k in range(4))
    prefix_quad[core * 2 + x] = prefix_mine[...]
    quad_copies = [
        remote(prefix_mine, prefix_quad.at[core * 2 + x], quad_send.at[k], quad_recv.at[k], peer)
        for k, peer in enumerate((place.other_core(), place.along_x(), place.diagonal()))
    ]
    for copy in quad_copies:
        copy.start()
    for copy in small_fourth:
        copy.wait()
    total = small_all[0].astype(F32)
    for k in range(1, 4):
        total += small_all[k].astype(F32)
    down_grad[...] = total[:, :ADAPTER]
    up_grad[:, :ADAPTER] = total[:16, ADAPTER:]
    up_grad[:, ADAPTER:] = total[16:, ADAPTER:]
    for copy in memory_third:
        copy.wait()
    total = memory_all[0].astype(F32)
    for k in range(1, 4):
        total += memory_all[k].astype(F32)
    memory_grad[...] = total
    for copy in quad_copies:
        copy.wait()
    prefix_sum[...] = (prefix_quad[0] + prefix_quad[1]) + (prefix_quad[2] + prefix_quad[3])

    pltpu.make_async_copy(staged.at[seq, pl.ds(1, 2)], gathered.at[pair, row, pl.ds(1, 2)], own_sem.at[3]).wait()
    for other, _ in others:
        remote(
            staged.at[other, pl.ds(1, 2)], gathered.at[other // 2, other % 2, pl.ds(1, 2)],
            out_send.at[other], out_recv.at[other], (other, x),
        ).wait()

    def part_grad(part, at):
        fetches[at].wait()
        joined = jnp.concatenate([gathered[k, :, part].reshape(tokens, LANES) for k in range(PAIRS)], axis=1)
        return dot_right(joined, weight(at))

    input_grad[...] = pull[...] + part_grad(1, K_AT) + part_grad(2, V_AT)
    pltpu.make_async_copy(staged.at[seq, pl.ds(0, 1)], gathered.at[pair, row, pl.ds(0, 1)], own_sem.at[2]).wait()
    for other, _ in others:
        remote(
            staged.at[other, pl.ds(0, 1)], gathered.at[other // 2, other % 2, pl.ds(0, 1)],
            query_send.at[other], query_recv.at[other], (other, x),
        ).wait()
    input_grad[...] += part_grad(0, Q_AT)


def second_call(*operands):
    length = 16 * S_DEV
    tokens = 2 * S_DEV
    dma = pltpu.SemaphoreType.DMA
    shape = jax.ShapeDtypeStruct
    return pl.pallas_call(
        second_kernel,
        out_shape=(
            shape((tokens, D), F32),
            shape((2 * M_DEV, D), F32),
            shape((32, ADAPTER), F32),
            shape((16, D), F32),
            shape((4, 32, LANES), F32),
        ),
        in_specs=[whole()] * 9 + [whole(pl.ANY)] * 8,
        out_specs=(whole(),) * 5,
        scratch_shapes=[
            pltpu.VMEM((8, 32, 32, D), BF16),
            pltpu.VMEM((16, 2, M_DEV, 2 * D), BF16),
            pltpu.VMEM((tokens, D), F32),
            pltpu.VMEM((16, 3, S_DEV, LANES), BF16),
            pltpu.VMEM((length, LANES), F32),
            pltpu.VMEM((length, LANES), F32),
            pltpu.VMEM((length, LANES), F32),
            pltpu.VMEM((tokens, D), F32),
            pltpu.VMEM((2, S_DEV, D), F32),
            pltpu.VMEM((2, S_DEV, D), BF16),
            pltpu.VMEM((16, 2, M_DEV, D), BF16),
            pltpu.VMEM((16, 2, M_DEV, D), BF16),
            pltpu.VMEM((4, 2, 2, 32, LANES), F32),
            pltpu.VMEM((4, 2, 2, 32, D), BF16),
            pltpu.VMEM((4, 2, 2, 32, D), BF16),
            pltpu.VMEM((4, 2, 32, D), BF16),
            pltpu.VMEM((4, 2, 32, D), BF16),
            pltpu.VMEM((4, 32, D), BF16),
            pltpu.VMEM((4, 32, D), BF16),
            pltpu.VMEM((4, 32, D), BF16),
            pltpu.VMEM((4, 2, 2, 2 * M_DEV, D), BF16),
            pltpu.VMEM((4, 2, 2 * M_DEV, D), BF16),
            pltpu.VMEM((4, 2, 2 * M_DEV, D), BF16),
            pltpu.VMEM((4, 2 * M_DEV, D), BF16),
            pltpu.VMEM((4, 2 * M_DEV, D), BF16),
            pltpu.VMEM((4, 2 * M_DEV, D), BF16),
            pltpu.VMEM((4, 2, 32, LANES), F32),
            pltpu.VMEM((4, 2, 32, LANES), F32),
            pltpu.VMEM((4, 2, 32, LANES), F32),
            pltpu.VMEM((4, 32, LANES), F32),
            pltpu.VMEM((4, 4, 32, LANES), F32),
            pltpu.VMEM((PAIRS, 2, S_DEV, LANES), BF16),
            pltpu.VMEM((16, S_DEV, LANES), BF16),
            pltpu.VMEM((length, LANES), BF16),
            pltpu.VMEM((8, length), F32),
            pltpu.VMEM((length, LANES), F32),
            pltpu.VMEM((4 * S_DEV, LANES), F32),
            pltpu.VMEM((4 * S_DEV, LANES), F32),
            pltpu.VMEM((16, 3, S_DEV, LANES), BF16),
            pltpu.VMEM((PAIRS, 2, 3, S_DEV, LANES), BF16),
            dma((14,)), dma((4,)), dma((3,)), dma((3,)), dma((3,)), dma((3,)), dma((4,)), dma((4,)), dma((4,)), dma((4,)),
            dma((4,)), dma((4,)), dma((3,)), dma((3,)),
            dma((15,)), dma((15,)), dma((16,)), dma((16,)), dma((16,)), dma((16,)),
        ],
        compiler_params=params(1),
        name="second",
    )(*operands)


def gelu_parts(pre):
    upper = 0.5 * (1.0 + lax.erf(pre * (0.5 ** 0.5)))
    return upper


def gelu_slope(pre):
    return gelu_parts(pre) + pre * jnp.exp(-0.5 * pre * pre) * (1.0 / math.sqrt(2.0 * math.pi))


def norm_back_rows(resid, gain, upstream):
    middle = jnp.mean(resid, axis=-1, keepdims=True)
    centred = resid - middle
    scale = lax.rsqrt(jnp.mean(centred * centred, axis=-1, keepdims=True) + 1e-05)
    unit = centred * scale
    pulled = upstream * gain
    return scale * (
        pulled - jnp.mean(pulled, axis=-1, keepdims=True) - unit * jnp.mean(pulled * unit, axis=-1, keepdims=True)
    )


def feed_kernel(
    normed, cotangent, gain, inner, outer, mixed,
    layer_out, second_grad, small_grads,
    low, pre, adapter_pre, total, feed_low,
):
    step = pl.program_id(0)
    down = mixed[:, :, :ADAPTER].reshape(D, ADAPTER)
    up_left = mixed[:, :16, ADAPTER:].reshape(ADAPTER, ADAPTER)
    up_right = mixed[:, 16:, ADAPTER:].reshape(ADAPTER, ADAPTER)
    half = ADAPTER

    @pl.when(step == 0)
    def _():
        low[...] = normed[...].astype(BF16)
        adapter_pre[...] = dot_nn(low[...], down)
        act = adapter_pre[...]
        act = (act * gelu_parts(act)).astype(BF16)
        total[:, :half] = normed[:, :half] + 4.0 * dot_nn(act, up_left)
        total[:, half:] = normed[:, half:] + 4.0 * dot_nn(act, up_right)

    @pl.when(step < 4)
    def _():
        hidden = dot_nn(low[...], inner[...].reshape(D, D))
        pre[jnp.minimum(step, 3)] = hidden
        act = (hidden * gelu_parts(hidden)).astype(BF16)
        total[...] += dot_nn(act, outer[...].reshape(D, D))

    @pl.when(step == 3)
    def _():
        resid = total[...]
        layer_out[...] = norm_rows(resid, gain[...]).astype(BF16)
        third_grad = norm_back_rows(resid, gain[...], cotangent[...].astype(F32))
        feed_low[...] = third_grad.astype(BF16)
        adapter_low = (4.0 * third_grad).astype(BF16)
        act = adapter_pre[...]
        upper = gelu_parts(act)
        slope = gelu_slope(act)
        act = (act * upper).astype(BF16)
        grad = dot_right(adapter_low[:, :half], up_left) + dot_right(adapter_low[:, half:], up_right)
        grad = (slope * grad).astype(BF16)
        second_grad[...] = third_grad + dot_right(grad, down)
        small_grads[:, :, :half] = dot_left(low[...], grad).astype(BF16).reshape(32, 32, half)
        small_grads[:, :16, half:] = dot_left(act, adapter_low[:, :half]).astype(BF16).reshape(32, 16, half)
        small_grads[:, 16:, half:] = dot_left(act, adapter_low[:, half:]).astype(BF16).reshape(32, 16, half)

    @pl.when(step >= 4)
    def _():
        hidden = pre[jnp.clip(7 - step, 0, 3)]
        grad = dot_right(feed_low[...], outer[...].reshape(D, D))
        grad = (gelu_slope(hidden) * grad).astype(BF16)
        second_grad[...] += dot_right(grad, inner[...].reshape(D, D))


def feed_forward_backward(normed, cotangent, gain, weights):
    tokens = normed.shape[0]
    at = lambda step: jnp.minimum(step, 7 - step)
    still = lambda step: (0, 0)
    rows = pl.BlockSpec((tokens, D), still)
    return pl.pallas_call(
        feed_kernel,
        grid=(8,),
        out_shape=(
            jax.ShapeDtypeStruct((tokens, D), BF16),
            jax.ShapeDtypeStruct((tokens, D), F32),
            jax.ShapeDtypeStruct((32, 32, D), BF16),
        ),
        in_specs=[
            rows, rows, pl.BlockSpec((1, D), still),
            pl.BlockSpec((32, 32, D), lambda step: (0, INNER_AT // 32 + at(step), 0)),
            pl.BlockSpec((8, 128, D), lambda step: (at(step), OUTER_AT // 128, 0)),
            pl.BlockSpec((32, 32, D), lambda step: (0, MIXED_AT // 32, 0)),
        ],
        out_specs=(rows, rows, pl.BlockSpec((32, 32, D), lambda step: (0, 0, 0))),
        scratch_shapes=[
            pltpu.VMEM((tokens, D), BF16),
            pltpu.VMEM((4, tokens, D), F32),
            pltpu.VMEM((tokens, ADAPTER), F32),
            pltpu.VMEM((tokens, D), F32),
            pltpu.VMEM((tokens, D), BF16),
        ],
        compiler_params=params(),
        name="feed",
    )(normed, cotangent, gain, weights, weights, weights)


def fast_device(
    inputs, memory, out_grad, token_docs, memory_docs, self_project, self_output, cross_query,
    cross_memory, cross_output, inner_weight, outer_weight, adapter_down, adapter_up, norm_gains, prefixes,
):
    seq, x = lax.axis_index("seq"), lax.axis_index("rows")
    tokens = 2 * S_DEV
    mixed = jnp.concatenate(
        [adapter_down, jnp.concatenate([adapter_up[:, :ADAPTER], adapter_up[:, ADAPTER:]], axis=0)], axis=1
    )
    lane_group = lax.broadcasted_iota(jnp.int32, (1, LANES), 1) // 32
    small = jnp.concatenate([
        jnp.pad(prefixes, ((0, 0), (0, 2), (0, 0))).reshape(128, 32), jnp.pad(norm_gains, ((0, 13), (0, 0)))
    ])
    small = jnp.where(lane_group == (seq % 2) * 2 + x, jnp.tile(small, (1, 4)), jnp.zeros((), BF16))
    memory_line = jnp.where(lane_group == seq % 4, jnp.tile(memory_docs, (1, 4)), 0)
    docs = jnp.concatenate([token_docs, memory_line, jnp.zeros((4, LANES), jnp.int32)]).astype(F32)
    (
        full, memory_pairs, docs_column, arrived, pair_attended, pair_inverse,
        first_resid, cross_queries, crossed, cross_inverse, small_full, docs_all, docs_row, second_resid, second_norm,
    ) = first_call(
        inputs, memory.reshape(2, M_DEV, D), small, docs,
        self_project, self_output, cross_query, cross_memory, cross_output, inner_weight, outer_weight, mixed,
    )

    third_gain = small_full[:, 130].reshape(1, D).astype(F32)
    layer_out, second_grad, small_grads = feed_forward_backward(
        second_norm, out_grad.reshape(tokens, D), third_gain, full
    )
    input_grad, memory_grad, down_grad, up_grad, prefix_sum = second_call(
        second_grad, second_resid, small_full, docs, docs_all, docs_row, crossed, cross_inverse, cross_queries,
        full, memory_pairs, first_resid, arrived, pair_attended, pair_inverse, docs_column,
        small_grads.reshape(4, 2, 2, 2, 32, D),
    )
    prefix_grad = lax.dynamic_slice_in_dim(prefix_sum[:, :PREFIX], 32 * ((seq % 2) * 2 + x), 32, 2)
    return (
        layer_out.reshape(2, S_DEV, D),
        input_grad.reshape(2, S_DEV, D),
        memory_grad.reshape(2, M_DEV, D),
        prefix_grad,
        down_grad,
        up_grad,
    )


def solution(mesh):
    placed = (
        P("rows", "seq", None),
        P("rows", "seq", None),
        P("rows", "seq", None),
        P("rows", "seq"),
        P("rows", "seq"),
        P(("seq", "rows"), None),
        P(("seq", "rows"), None),
        P(("seq", "rows"), None),
        P(("seq", "rows"), None),
        P(("seq", "rows"), None),
        P(("seq", "rows"), None),
        P(("seq", "rows"), None),
        P(("seq", "rows"), None),
        P(("seq", "rows"), None),
        P(None, ("seq", "rows")),
        P(None, None, ("seq", "rows")),
    )
    small_slice = mesh.shape["seq"] == 16 and mesh.shape["rows"] == 2
    return jax.shard_map(
        fast_device if small_slice else per_device,
        mesh=mesh,
        in_specs=placed,
        out_specs=(
            P("rows", "seq", None),
            P("rows", "seq", None),
            P("rows", "seq", None),
            P(None, None, ("seq", "rows")),
            P(("seq", "rows"), None),
            P(("seq", "rows"), None),
        ),
        check_vma=False,
    )
```

```python
import math

import jax
import jax.numpy as jnp
from jax import lax
from jax.experimental import pallas as pl
from jax.experimental.pallas import tpu as pltpu
from jax.sharding import PartitionSpec as P

D = 1024
HEADS = 16
HEAD_DIM = 64
ADAPTER = 512
PREFIX = 30
S_DEV = 128
M_DEV = 32


score_scale = 0.125
masked_score = -1000000000.0


def heads_of(matrix):
    return matrix.reshape(matrix.shape[0], HEADS, HEAD_DIM)


def dot_right(left, right):
    return lax.dot_general(
        left, right, (((1,), (1,)), ((), ())), preferred_element_type=jnp.float32
    )


def dot_left(left, right):
    return lax.dot_general(
        left, right, (((0,), (0,)), ((), ())), preferred_element_type=jnp.float32
    )


def norm_rows(resid, gain):
    middle = jnp.mean(resid, axis=-1, keepdims=True)
    centred = resid - middle
    spread = jnp.mean(centred * centred, axis=-1, keepdims=True)
    return centred * lax.rsqrt(spread + 1e-05) * gain


def norm_back(resid, gain, upstream):
    unused, pullback = jax.vjp(lambda values: norm_rows(values, gain), resid)
    return pullback(upstream)[0]


def gelu_back(pre_act, upstream):
    unused, pullback = jax.vjp(lambda values: jax.nn.gelu(values, approximate=False), pre_act)
    return pullback(upstream)[0]


def allowed_keys(query_docs, key_docs, query_pos, key_pos, causal):
    allowed = query_docs[:, None] == key_docs[None, :]
    if causal:
        allowed = allowed & (key_pos[None, :] <= query_pos[:, None])
    return allowed


def prefix_terms(queries, prefix_keys, prefix_values):
    scores = (
        jnp.einsum(
            "qhd,phd->hqp", queries, heads_of(prefix_keys), preferred_element_type=jnp.float32
        )
        * score_scale
    )
    weights = jnp.exp(scores)
    summed = jnp.einsum(
        "hqp,phd->qhd",
        weights.astype(jnp.bfloat16),
        heads_of(prefix_values),
        preferred_element_type=jnp.float32,
    )
    return (jnp.sum(weights, axis=-1), summed)


def fold_keys(running, arrived, queries, query_docs, key_docs, query_first, causal):
    key_count = arrived.shape[0]
    block_len = math.gcd(key_count, 512)
    query_count = queries.shape[0]
    query_pos = query_first + jnp.arange(query_count, dtype=jnp.int32)
    key_width = arrived.shape[1] // 2

    def fold_one_block(current, element):
        key_block, block_index = element
        key_first = block_index * block_len

        def compute(present):
            block_docs = lax.dynamic_slice_in_dim(key_docs, key_first, block_len, 0)
            allowed = allowed_keys(
                query_docs,
                block_docs,
                query_pos,
                key_first + jnp.arange(block_len, dtype=jnp.int32),
                causal,
            )
            scores = (
                jnp.einsum(
                    "qhd,khd->hqk",
                    queries,
                    heads_of(key_block[:, :key_width]),
                    preferred_element_type=jnp.float32,
                )
                * score_scale
            )
            weights = jnp.exp(jnp.where(allowed[None], scores, masked_score))
            summed = jnp.einsum(
                "hqk,khd->qhd",
                weights.astype(jnp.bfloat16),
                heads_of(key_block[:, key_width:]),
                preferred_element_type=jnp.float32,
            )
            return (present[0] + jnp.sum(weights, axis=-1), present[1] + summed)

        if causal:
            return (
                lax.cond(
                    key_first <= query_first + query_count - 1, compute, lambda held: held, current
                ),
                None,
            )
        return (compute(current), None)

    running, unused = lax.scan(
        fold_one_block,
        running,
        (
            arrived.reshape(key_count // block_len, block_len, arrived.shape[1]),
            jnp.arange(key_count // block_len, dtype=jnp.int32),
        ),
    )
    return running


def attend_back(
    queries,
    gathered,
    prefix_keys,
    prefix_values,
    grad_out,
    attended,
    totals,
    query_docs,
    key_docs,
    query_first,
    causal,
):
    query_count = queries.shape[0]
    key_count = gathered.shape[0]
    key_width = gathered.shape[1] // 2
    block_len = math.gcd(key_count, 512)
    query_pos = query_first + jnp.arange(query_count, dtype=jnp.int32)
    grad_heads = heads_of(grad_out)
    grad_summed = (grad_heads / totals.T[:, :, None]).astype(jnp.bfloat16)
    row_dot = jnp.sum(grad_heads * heads_of(attended), axis=-1).T / totals
    prefix_key_heads = heads_of(prefix_keys)
    prefix_value_heads = heads_of(prefix_values)
    prefix_weights = jnp.exp(
        jnp.einsum("qhd,phd->hqp", queries, prefix_key_heads, preferred_element_type=jnp.float32)
        * score_scale
    )
    prefix_dots = jnp.einsum(
        "qhd,phd->hqp", grad_summed, prefix_value_heads, preferred_element_type=jnp.float32
    )
    prefix_slopes = (prefix_weights * (prefix_dots - row_dot[:, :, None])).astype(jnp.bfloat16)
    query_grad = jnp.einsum(
        "hqp,phd->qhd", prefix_slopes, prefix_key_heads, preferred_element_type=jnp.float32
    )
    key_grad_prefix = (
        jnp.einsum("hqp,qhd->phd", prefix_slopes, queries, preferred_element_type=jnp.float32)
        * score_scale
    ).reshape(-1, D)
    value_grad_prefix = jnp.einsum(
        "hqp,qhd->phd",
        prefix_weights.astype(jnp.bfloat16),
        grad_summed,
        preferred_element_type=jnp.float32,
    ).reshape(-1, D)

    def attend_one_block(current, element):
        key_block, block_index = element
        key_first = block_index * block_len

        def compute(present):
            block_docs = lax.dynamic_slice_in_dim(key_docs, key_first, block_len, 0)
            allowed = allowed_keys(
                query_docs,
                block_docs,
                query_pos,
                key_first + jnp.arange(block_len, dtype=jnp.int32),
                causal,
            )
            key_heads = heads_of(key_block[:, :key_width])
            value_heads = heads_of(key_block[:, key_width:])
            scores = (
                jnp.einsum("qhd,khd->hqk", queries, key_heads, preferred_element_type=jnp.float32)
                * score_scale
            )
            weights = jnp.exp(jnp.where(allowed[None], scores, masked_score))
            dots = jnp.einsum(
                "qhd,khd->hqk", grad_summed, value_heads, preferred_element_type=jnp.float32
            )
            slopes = (weights * (dots - row_dot[:, :, None])).astype(jnp.bfloat16)
            present = present + jnp.einsum(
                "hqk,khd->qhd", slopes, key_heads, preferred_element_type=jnp.float32
            )
            key_grad = (
                jnp.einsum("hqk,qhd->khd", slopes, queries, preferred_element_type=jnp.float32)
                * score_scale
            )
            value_grad = jnp.einsum(
                "hqk,qhd->khd",
                weights.astype(jnp.bfloat16),
                grad_summed,
                preferred_element_type=jnp.float32,
            )
            return (
                present,
                jnp.concatenate(
                    [key_grad.reshape(block_len, D), value_grad.reshape(block_len, D)], axis=1
                ),
            )

        if causal:
            return lax.cond(
                key_first <= query_first + query_count - 1,
                compute,
                lambda held: (held, jnp.zeros((block_len, 2 * D), jnp.float32)),
                current,
            )
        return compute(current)

    query_grad, key_terms = lax.scan(
        attend_one_block,
        query_grad,
        (
            gathered.reshape(key_count // block_len, block_len, gathered.shape[1]),
            jnp.arange(key_count // block_len, dtype=jnp.int32),
        ),
    )
    query_low = (query_grad * score_scale).astype(jnp.bfloat16).reshape(query_count, D)
    key_terms = key_terms.reshape(key_count, 2 * D)
    return (query_low, key_terms, key_grad_prefix, value_grad_prefix, grad_summed, row_dot)


def fetch_all(
    self_project,
    self_output,
    cross_query,
    cross_memory,
    cross_output,
    inner_weight,
    outer_weight,
    adapter_down,
    adapter_up,
    norm_gains,
    prefixes,
):
    return (
        lax.all_gather(self_project, ("seq", "rows"), axis=0, tiled=True),
        lax.all_gather(self_output, ("seq", "rows"), axis=0, tiled=True),
        lax.all_gather(cross_query, ("seq", "rows"), axis=0, tiled=True),
        lax.all_gather(cross_memory, ("seq", "rows"), axis=0, tiled=True),
        lax.all_gather(cross_output, ("seq", "rows"), axis=0, tiled=True),
        lax.all_gather(inner_weight, ("seq", "rows"), axis=0, tiled=True),
        lax.all_gather(outer_weight, ("seq", "rows"), axis=0, tiled=True),
        lax.all_gather(adapter_down, ("seq", "rows"), axis=0, tiled=True),
        lax.all_gather(adapter_up, ("seq", "rows"), axis=0, tiled=True),
        lax.all_gather(norm_gains, ("seq", "rows"), axis=1, tiled=True),
        lax.all_gather(prefixes, ("seq", "rows"), axis=2, tiled=True),
    )


def fetch_again(
    self_project,
    self_output,
    cross_query,
    cross_memory,
    cross_output,
    inner_weight,
    outer_weight,
    adapter_down,
    adapter_up,
    norm_gains,
    prefixes,
):
    return (
        lax.all_gather(self_project, ("seq", "rows"), axis=0, tiled=True),
        lax.all_gather(self_output, ("seq", "rows"), axis=0, tiled=True),
        lax.all_gather(cross_query, ("seq", "rows"), axis=0, tiled=True),
        lax.all_gather(cross_memory, ("seq", "rows"), axis=0, tiled=True),
        lax.all_gather(cross_output, ("seq", "rows"), axis=0, tiled=True),
        lax.all_gather(inner_weight, ("seq", "rows"), axis=0, tiled=True),
        lax.all_gather(outer_weight, ("seq", "rows"), axis=0, tiled=True),
        lax.all_gather(adapter_down, ("seq", "rows"), axis=0, tiled=True),
        lax.all_gather(adapter_up, ("seq", "rows"), axis=0, tiled=True),
        lax.all_gather(norm_gains, ("seq", "rows"), axis=1, tiled=True),
        lax.all_gather(prefixes, ("seq", "rows"), axis=2, tiled=True),
    )


def forward_row(tokens, memory_rows, query_docs, token_docs, memory_docs, query_first, weights):
    (
        self_project,
        self_output,
        cross_query,
        cross_memory,
        cross_output,
        inner_weight,
        outer_weight,
        adapter_down,
        adapter_up,
        norm_gains,
        prefixes,
    ) = weights
    gains = norm_gains.astype(jnp.float32)
    projected = jnp.dot(tokens, self_project, preferred_element_type=jnp.float32).astype(
        jnp.bfloat16
    )
    queries = heads_of(projected[:, :D])
    local_pairs = projected[:, D:]
    start_self = prefix_terms(queries, prefixes[0], prefixes[1])
    totals, summed = fold_keys(
        start_self,
        lax.all_gather(local_pairs, "seq", axis=0, tiled=True),
        queries,
        query_docs,
        token_docs,
        query_first,
        True,
    )
    attended = (summed / totals.T[:, :, None]).reshape(-1, D)
    first_resid = tokens.astype(jnp.float32) + jnp.dot(
        attended.astype(jnp.bfloat16), self_output, preferred_element_type=jnp.float32
    )
    first_norm = norm_rows(first_resid, gains[0])
    first_low = first_norm.astype(jnp.bfloat16)
    cross_queries = heads_of(
        jnp.dot(first_low, cross_query, preferred_element_type=jnp.float32).astype(jnp.bfloat16)
    )
    memory_pairs = jnp.dot(memory_rows, cross_memory, preferred_element_type=jnp.float32).astype(
        jnp.bfloat16
    )
    start_cross = prefix_terms(cross_queries, prefixes[2], prefixes[3])
    cross_totals, cross_summed = fold_keys(
        start_cross,
        lax.all_gather(memory_pairs, "seq", axis=0, tiled=True),
        cross_queries,
        query_docs,
        memory_docs,
        query_first,
        False,
    )
    crossed = (cross_summed / cross_totals.T[:, :, None]).reshape(-1, D)
    second_resid = first_norm + jnp.dot(
        crossed.astype(jnp.bfloat16), cross_output, preferred_element_type=jnp.float32
    )
    second_norm = norm_rows(second_resid, gains[1])
    second_low = second_norm.astype(jnp.bfloat16)
    hidden_pre = jnp.dot(second_low, inner_weight, preferred_element_type=jnp.float32)
    hidden_act = jax.nn.gelu(hidden_pre, approximate=False).astype(jnp.bfloat16)
    adapter_pre = jnp.dot(second_low, adapter_down, preferred_element_type=jnp.float32)
    adapter_act = jax.nn.gelu(adapter_pre, approximate=False).astype(jnp.bfloat16)
    third_resid = (
        second_norm
        + jnp.dot(hidden_act, outer_weight, preferred_element_type=jnp.float32)
        + 4.0 * jnp.dot(adapter_act, adapter_up, preferred_element_type=jnp.float32)
    )
    layer_out = norm_rows(third_resid, gains[2]).astype(jnp.bfloat16)
    saved = (
        queries,
        local_pairs,
        totals,
        attended,
        first_resid,
        cross_queries,
        memory_pairs,
        cross_totals,
        crossed,
        second_resid,
        second_low,
        hidden_pre,
        adapter_pre,
        adapter_act,
        third_resid,
    )
    return (layer_out, saved)


def backward_row(cotangent, saved, weights, query_docs, token_docs, memory_docs, query_first):
    (
        self_project,
        self_output,
        cross_query,
        cross_memory,
        cross_output,
        inner_weight,
        outer_weight,
        adapter_down,
        adapter_up,
        norm_gains,
        prefixes,
    ) = weights
    (
        queries,
        local_pairs,
        totals,
        attended,
        first_resid,
        cross_queries,
        memory_pairs,
        cross_totals,
        crossed,
        second_resid,
        second_low,
        hidden_pre,
        adapter_pre,
        adapter_act,
        third_resid,
    ) = saved
    gains = norm_gains.astype(jnp.float32)
    third_grad = norm_back(third_resid, gains[2], cotangent.astype(jnp.float32))
    feed_low = third_grad.astype(jnp.bfloat16)
    adapter_low = (4.0 * third_grad).astype(jnp.bfloat16)
    hidden_grad = gelu_back(hidden_pre, dot_right(feed_low, outer_weight)).astype(jnp.bfloat16)
    up_grad = dot_left(adapter_act, adapter_low)
    adapter_grad = gelu_back(adapter_pre, dot_right(adapter_low, adapter_up)).astype(jnp.bfloat16)
    down_grad = dot_left(second_low, adapter_grad)
    second_grad = (
        third_grad + dot_right(hidden_grad, inner_weight) + dot_right(adapter_grad, adapter_down)
    )
    second_resid_grad = norm_back(second_resid, gains[1], second_grad)
    self_all, memory_all = (
        lax.all_gather(local_pairs, "seq", axis=0, tiled=True),
        lax.all_gather(memory_pairs, "seq", axis=0, tiled=True),
    )
    cross_out_grad = dot_right(second_resid_grad.astype(jnp.bfloat16), cross_output)
    (
        cross_query_low,
        memory_terms,
        cross_key_prefix,
        cross_value_prefix,
        cross_summed_grad,
        cross_dot,
    ) = attend_back(
        cross_queries,
        memory_all,
        prefixes[2],
        prefixes[3],
        cross_out_grad,
        crossed,
        cross_totals,
        query_docs,
        memory_docs,
        query_first,
        False,
    )
    first_grad = second_resid_grad + dot_right(cross_query_low, cross_query)
    first_resid_grad = norm_back(first_resid, gains[0], first_grad)
    self_out_grad = dot_right(first_resid_grad.astype(jnp.bfloat16), self_output)
    query_low, self_terms, self_key_prefix, self_value_prefix, self_summed_grad, self_dot = (
        attend_back(
            queries,
            self_all,
            prefixes[0],
            prefixes[1],
            self_out_grad,
            attended,
            totals,
            query_docs,
            token_docs,
            query_first,
            True,
        )
    )
    self_sums, memory_sums = (
        lax.psum_scatter(
            self_terms.astype(jnp.bfloat16), "seq", scatter_dimension=0, tiled=True
        ).astype(jnp.float32),
        lax.psum_scatter(
            memory_terms.astype(jnp.bfloat16), "seq", scatter_dimension=0, tiled=True
        ).astype(jnp.float32),
    )
    project_grad = jnp.concatenate([query_low, self_sums.astype(jnp.bfloat16)], axis=1)
    input_grad = first_resid_grad + dot_right(project_grad, self_project)
    memory_grad = dot_right(memory_sums.astype(jnp.bfloat16), cross_memory)
    prefix_grad = jnp.stack(
        [self_key_prefix, self_value_prefix, cross_key_prefix, cross_value_prefix]
    )
    return (input_grad, memory_grad, (down_grad, up_grad, prefix_grad))


def per_device(
    inputs,
    memory,
    out_grad,
    token_docs,
    memory_docs,
    self_project,
    self_output,
    cross_query,
    cross_memory,
    cross_output,
    inner_weight,
    outer_weight,
    adapter_down,
    adapter_up,
    norm_gains,
    prefixes,
):
    docs_full, memory_full = (
        lax.all_gather(token_docs, "seq", axis=1, tiled=True),
        lax.all_gather(memory_docs, "seq", axis=1, tiled=True),
    )
    query_first = lax.axis_index("seq") * inputs.shape[1]
    outputs = []
    input_grads = []
    memory_grads = []
    adjusted_grads = None
    for row_index in range(inputs.shape[0]):
        weights = fetch_all(
            self_project,
            self_output,
            cross_query,
            cross_memory,
            cross_output,
            inner_weight,
            outer_weight,
            adapter_down,
            adapter_up,
            norm_gains,
            prefixes,
        )
        layer_out, saved = forward_row(
            inputs[row_index],
            memory[row_index],
            token_docs[row_index],
            docs_full[row_index],
            memory_full[row_index],
            query_first,
            weights,
        )
        weights_back = fetch_again(
            self_project,
            self_output,
            cross_query,
            cross_memory,
            cross_output,
            inner_weight,
            outer_weight,
            adapter_down,
            adapter_up,
            norm_gains,
            prefixes,
        )
        input_grad, memory_grad, row_grads = backward_row(
            out_grad[row_index],
            saved,
            weights_back,
            token_docs[row_index],
            docs_full[row_index],
            memory_full[row_index],
            query_first,
        )
        shares = (
            lax.psum_scatter(row_grads[0], ("seq", "rows"), scatter_dimension=0, tiled=True),
            lax.psum_scatter(row_grads[1], ("seq", "rows"), scatter_dimension=0, tiled=True),
            lax.psum_scatter(row_grads[2], ("seq", "rows"), scatter_dimension=2, tiled=True),
        )
        if adjusted_grads is None:
            adjusted_grads = shares
        else:
            adjusted_grads = tuple(
                (former + latter for former, latter in zip(adjusted_grads, shares))
            )
        outputs.append(layer_out)
        input_grads.append(input_grad)
        memory_grads.append(memory_grad)
    return (
        jnp.stack(outputs),
        jnp.stack(input_grads),
        jnp.stack(memory_grads),
        adjusted_grads[2],
        adjusted_grads[0],
        adjusted_grads[1],
    )


MESH_ID = pl.DeviceIdType.MESH
F32 = jnp.float32
BF16 = jnp.bfloat16
VMEM_BYTES = 60 * 1024 * 1024
PAIRS = HEADS // 2
LANES = 2 * HEAD_DIM
Q_AT, K_AT, V_AT, SELF_OUT_AT, CROSS_Q_AT, MEM_K_AT, MEM_V_AT, CROSS_OUT_AT = range(0, 256, 32)
INNER_AT, OUTER_AT, MIXED_AT = 256, 384, 512
ALL_ROWS = 544
SMALL_ROWS = 144
PIECE_ROWS = 16
GAP = 6
LEAD = 4
SENDS = 3
Z_LAST = ()
WAIT_TICKS = 4
STEP_TICKS = 1


def whole(space=pltpu.VMEM):
    return pl.BlockSpec(memory_space=space)


def params(collective_id=None):
    if collective_id is None:
        return pltpu.CompilerParams(vmem_limit_bytes=VMEM_BYTES)
    return pltpu.CompilerParams(
        vmem_limit_bytes=VMEM_BYTES, collective_id=collective_id, has_side_effects=True
    )


def remote(src, dst, send_sem, recv_sem, device):
    return pltpu.make_async_remote_copy(
        src_ref=src, dst_ref=dst, send_sem=send_sem, recv_sem=recv_sem,
        device_id=device, device_id_type=MESH_ID,
    )


def greet(peers):
    barrier = pltpu.get_barrier_semaphore()
    for peer in peers:
        pl.semaphore_signal(barrier, inc=1, device_id=peer, device_id_type=MESH_ID)
    pl.semaphore_wait(barrier, len(peers))


def dot_nn(left, right):
    return lax.dot_general(left, right, (((1,), (0,)), ((), ())), preferred_element_type=F32)


class Place:
    def __init__(self):
        self.seq, self.x = lax.axis_index("seq"), lax.axis_index("rows")
        self.z, self.y, self.core = self.seq // 4, (self.seq // 2) % 2, self.seq % 2
        self.pair, self.row = self.seq // 2, self.seq % 2

    def device(self, z, y, core, x):
        return ((z * 2 + y) * 2 + core, x)

    def along_z(self, step):
        return self.device((self.z + step) % 4, self.y, self.core, self.x)

    def along_y(self):
        return self.device(self.z, 1 - self.y, self.core, self.x)

    def along_x(self):
        return self.device(self.z, self.y, self.core, 1 - self.x)

    def other_core(self):
        return self.device(self.z, self.y, 1 - self.core, self.x)

    def diagonal(self):
        return self.device(self.z, self.y, 1 - self.core, 1 - self.x)

    def others(self):
        return [((self.seq + step) % 16, self.x) for step in range(1, 16)]


class Gather:
    def __init__(self, place, full, local_sem, sems, gap):
        self.place, self.full, self.local_sem, self.sems, self.gap = place, full, local_sem, sems, gap
        self.stages = []
        self.waiting = []
        self.cut = 1
        self.tick_at = 0

    def copies(self, level, source, target, device, slot):
        k = len(self.stages)
        return remote(source, target, self.sems[2 * level].at[k, slot], self.sems[2 * level + 1].at[k, slot], device)

    def add(self, source, first, count, piece=PIECE_ROWS):
        for from_row in range(0, count, piece):
            self.add_piece(source.at[pl.ds(from_row, piece)], first + from_row, piece)
        return len(self.stages) - 1

    def add_piece(self, source, first, count):
        at, full = self.place, self.full
        z, y, core, x = at.z, at.y, at.core, at.x
        rows = pl.ds(first, count)
        mine = full.at[z, y, core, x, rows]
        k = len(self.stages)
        if k in Z_LAST:
            plane = full.at[z, :, core, :, rows]
            first_way, then_way = (at.along_x(), at.along_y()) if k % 2 else (at.along_y(), at.along_x())
            line = full.at[z, y, core, :, rows] if k % 2 else full.at[z, :, core, x, rows]
            self.stages.append((
                pltpu.make_async_copy(source, mine, self.local_sem.at[k]),
                [self.copies(0, source, mine, first_way, 0)],
                [self.copies(1, line, line, then_way, 0)],
                [self.copies(2, plane, plane, at.along_z(d + 1), d) for d in range(3)],
                [self.copies(3, full.at[:, :, core, :, rows], full.at[:, :, core, :, rows], at.other_core(), 0)],
            ))
            return
        cut = self.cut
        near, far = pl.ds(0, cut), pl.ds(cut, 4 - cut)
        near1, far1 = full.at[near, y, core, x, rows], full.at[far, y, core, x, rows]
        near2, far2 = full.at[near, y, core, :, rows], full.at[far, :, core, x, rows]
        half = full.at[:, :, core, :, rows]
        self.stages.append((
            pltpu.make_async_copy(source, mine, self.local_sem.at[len(self.stages)]),
            [self.copies(0, source, mine, at.along_z(d + 1), d) for d in range(3)],
            [self.copies(1, near1, near1, at.along_x(), 0), self.copies(1, far1, far1, at.along_y(), 1)],
            [self.copies(2, near2, near2, at.along_y(), 0), self.copies(2, far2, far2, at.along_x(), 1)],
            [self.copies(3, half, half, at.other_core(), 0)],
        ))

    def add_memory_row(self, source, full):
        at = self.place
        mine, column, half = full.at[at.z, at.y, at.core], full.at[:, at.y, at.core], full.at[:, :, at.core]
        self.stages.append((
            pltpu.make_async_copy(source, mine, self.local_sem.at[len(self.stages)]),
            [self.copies(0, source, mine, at.along_z(d + 1), d) for d in range(3)],
            [self.copies(1, column, column, at.along_y(), 1)],
            [],
            [self.copies(3, half, half, at.other_core(), 0)],
        ))

    def start(self):
        for stage in self.stages:
            stage[0].start()

    def tick(self, count=1):
        for _ in range(count):
            for level in range(5):
                k = self.tick_at - self.after(level)
                if not 0 <= k < len(self.stages):
                    continue
                if level == 1:
                    self.stages[k][0].wait()
                if level > 0:
                    for copy in self.stages[k][level]:
                        copy.wait_recv()
                if level < 4:
                    for copy in self.stages[k][level + 1]:
                        copy.start()
            self.tick_at += 1
            for _ in range(SENDS):
                if self.waiting:
                    self.waiting.pop(0).start()

    def after(self, level):
        return 0 if level == 0 else LEAD + (level - 1) * self.gap

    def until(self, k):
        while self.tick_at <= k + self.after(4):
            self.tick()

    def finish(self):
        self.until(len(self.stages) - 1)
        for _, *levels in self.stages:
            for level in levels:
                for copy in level:
                    copy.wait_send()


def head_masks():
    lane = lax.broadcasted_iota(jnp.int32, (1, LANES), 1)
    first = (lane < HEAD_DIM).astype(F32).astype(BF16)
    return first, (1.0 - first.astype(F32)).astype(BF16)


def stack_heads(block):
    first, second = head_masks()
    return jnp.concatenate([block * first, block * second], axis=0)


def merge_heads(stacked):
    half = stacked.shape[0] // 2
    lane = lax.broadcasted_iota(jnp.int32, (half, LANES), 1)
    return jnp.where(lane < HEAD_DIM, stacked[:half], stacked[half:])


def rows_in_lanes(values):
    lane = lax.broadcasted_iota(jnp.int32, (8, LANES), 1)
    row = lax.broadcasted_iota(jnp.int32, (8, LANES), 0)
    picks = (lane // HEAD_DIM == row).astype(F32)
    return lax.dot_general(
        picks, values, (((1,), (1,)), ((), ())),
        precision=lax.Precision.HIGHEST, preferred_element_type=F32,
    )


def first_kernel(
    tokens, memory, small, docs,
    project, self_out, cross_q, cross_mem, cross_out, inner, outer, mixed,
    full, memory_full, memory_pairs_far, docs_column_far, arrived_far, attended_far, inverse_far,
    first_resid_far, cross_queries_far, crossed_far, cross_inverse_far,
    small_full, docs_all, docs_row, second_resid, second_norm,
    memory_pairs, docs_column, arrived, attended, inverse, first_resid, cross_queries, crossed, cross_inverse,
    gathered, first_norm, weights, staged, quad, memory_held, result_staged, sums, parts,
    local_sem, send0, recv0, send1, recv1, send2, recv2, send3, recv3,
    fetch_sem, own_sem, quad_send, quad_recv, small_send, small_recv, docs_send, docs_recv,
    head_send, head_recv, out_send, out_recv, leave_sem,
):
    leaving = []

    def leave(*arrays):
        for held, target in arrays:
            leaving.append(pltpu.make_async_copy(held, target, leave_sem.at[len(leaving)]))
            leaving[-1].start()

    place = Place()
    seq, x, pair, row = place.seq, place.x, place.pair, place.row
    others = place.others()
    quad_peers = [place.other_core(), place.along_x(), place.diagonal()]
    greet(others + quad_peers[1:])

    engine = Gather(place, full, local_sem, (send0, recv0, send1, recv1, send2, recv2, send3, recv3), GAP)
    project_done = [
        engine.add(project.at[:, pl.ds(part * D, D)], at, 32) for part, at in enumerate((Q_AT, K_AT, V_AT))
    ]
    for part, at in enumerate((MEM_K_AT, MEM_V_AT)):
        for half in range(2):
            held = pl.ds(16 * half, 16)
            engine.add_memory_row(memory.at[part, held], memory_full.at[:, :, :, part, held])
            memory_done = engine.add(cross_mem.at[held, pl.ds(part * D, D)], at + 16 * half, 16)
    out_done = engine.add(self_out, SELF_OUT_AT, 32)
    query_done = engine.add(cross_q, CROSS_Q_AT, 32)
    cross_done = engine.add(cross_out, CROSS_OUT_AT, 32)
    engine.cut = 2
    for part in range(4):
        engine.add(inner.at[:, pl.ds(part * D, D)], INNER_AT + 32 * part, 32)
    for part in range(4):
        engine.add(outer.at[pl.ds(32 * part, 32)], OUTER_AT + 32 * part, 32)
    engine.add(mixed, MIXED_AT, 32)
    engine.start()
    engine.tick()

    mine = place.core * 2 + x
    quad_copies = [
        remote(small, quad.at[mine], quad_send.at[k], quad_recv.at[k], quad_peers[k]) for k in range(3)
    ]
    own_small = pltpu.make_async_copy(small, quad.at[mine], own_sem.at[0])
    docs_copies = [
        remote(docs, docs_all.at[seq], docs_send.at[k], docs_recv.at[k], others[k]) for k in range(15)
    ]
    own_docs = pltpu.make_async_copy(docs, docs_all.at[seq], own_sem.at[1])
    own_small.start()
    own_docs.start()
    for copy in quad_copies + docs_copies:
        copy.start()
    rows = tokens[...].reshape(2 * S_DEV, D)
    fetches = []
    for part in range(3):
        engine.until(project_done[part])
        fetches.append(pltpu.make_async_copy(full_rows(full, 32 * part), weights.at[part], fetch_sem.at[part]))
        fetches[part].start()
    for part in range(3):
        fetches[part].wait()
        result = dot_nn(rows, weights[part].reshape(D, D)).astype(BF16)
        for at_row in range(2):
            for at_pair in range(PAIRS):
                staged[at_pair, at_row, part] = result[
                    at_row * S_DEV:(at_row + 1) * S_DEV, at_pair * LANES:(at_pair + 1) * LANES
                ]
        engine.tick()
    head_copies = []
    for k in range(15):
        to = (seq + k + 1) % 16
        head_copies.append(
            remote(staged.at[to // 2, to % 2], arrived.at[seq], head_send.at[k], head_recv.at[k], others[k])
        )
    own_heads = pltpu.make_async_copy(staged.at[pair, row], arrived.at[seq], own_sem.at[2])
    own_heads.start()
    engine.waiting = list(head_copies)
    engine.tick(2)
    own_small.wait()
    for copy in quad_copies:
        copy.wait()
    small_full[pair] = (quad[0] + quad[1]) + (quad[2] + quad[3])
    small_copies = []
    for k in range(1, 8):
        to = (((pair + k) % 8) * 2 + place.core, x)
        small_copies.append(
            remote(small_full.at[pair], small_full.at[pair], small_send.at[k], small_recv.at[k], to)
        )
        small_copies[-1].start()
    own_docs.wait()
    for copy in docs_copies:
        copy.wait()

    def spread_docs(at, carry):
        tile = docs_all[at]
        line = jnp.where(row == 0, tile[0:1], tile[1:2])
        docs_row[:, pl.ds(pl.multiple_of(at * S_DEV, S_DEV), S_DEV)] = jnp.broadcast_to(line, (8, S_DEV))
        docs_column[pl.ds(at * S_DEV, S_DEV)] = jnp.transpose(jnp.broadcast_to(line, (S_DEV, LANES)))
        return carry

    lax.fori_loop(0, 16, spread_docs, 0)

    engine.until(memory_done)
    fetch_memory = pltpu.make_async_copy(memory_full, memory_held, own_sem.at[3])
    fetch_memory.start()
    fetches = [
        pltpu.make_async_copy(full_rows(full, at), weights.at[part], fetch_sem.at[part])
        for part, at in enumerate((MEM_K_AT, MEM_V_AT))
    ]
    for fetch in fetches:
        fetch.start()
    fetch_memory.wait()
    for part in range(2):
        fetches[part].wait()

        def project_memory(at, carry):
            held = memory_held[at].reshape(4 * 2 * M_DEV, D)
            result = dot_nn(held, weights[part].reshape(D, D)).astype(BF16)
            memory_pairs[pl.ds(4 * at, 4), :, :, pl.ds(part * D, D)] = result.reshape(4, 2, M_DEV, D)
            return carry

        lax.fori_loop(0, 4, project_memory, 0)
    engine.tick(max(WAIT_TICKS, -(-len(engine.waiting) // SENDS)))
    own_heads.wait()
    for copy in head_copies:
        copy.wait()

    leave((memory_pairs, memory_pairs_far), (docs_column, docs_column_far), (arrived, arrived_far))

    block = 2 * S_DEV
    columns = pl.ds(pl.multiple_of(pair * LANES, LANES), LANES)
    target = gathered.at[row, :, columns]
    away = (
        lax.broadcasted_iota(jnp.int32, (block, block), 1)
        - lax.broadcasted_iota(jnp.int32, (block, block), 0)
    )
    prefix_lane = lax.broadcasted_iota(jnp.int32, (2 * block, 32), 1)
    prefix_keys, prefix_values = small_full[pair, 0:32], small_full[pair, 32:64]

    for step in range(8):
        at = (step + pair) % 8
        queries = stack_heads(arrived[pl.ds(2 * at, 2), 0].reshape(block, LANES))
        query_docs = docs_column[pl.ds(at * block, block)]
        scores = dot_right(queries, prefix_keys) * score_scale
        e = jnp.where(prefix_lane < PREFIX, jnp.exp(scores), 0.0)
        sums[...] = jnp.concatenate([e, jnp.zeros((2 * block, LANES - 32), F32)], axis=1)
        parts[...] = dot_nn(e.astype(BF16), prefix_values)

        def one_tile(key_at, carry):
            keys = arrived[pl.ds(2 * key_at, 2), 1].reshape(block, LANES)
            values = arrived[pl.ds(2 * key_at, 2), 2].reshape(block, LANES)
            key_docs = docs_row[0:1, pl.ds(pl.multiple_of(key_at * block, block), block)]
            same = jnp.concatenate([query_docs, query_docs], axis=1) == key_docs
            allowed = same & (away <= (at - key_at) * block)
            scores = dot_right(queries, keys) * score_scale
            e = jnp.where(allowed[None], jnp.exp(scores).reshape(2, block, block), 0.0)
            e = e.reshape(2 * block, block)
            sums[...] += e[:, :LANES] + e[:, LANES:]
            parts[...] += dot_nn(e.astype(BF16), values)
            return carry

        lax.fori_loop(0, at + 1, one_tile, 0)
        totals = 1.0 / jnp.sum(sums[...], axis=1, keepdims=True)
        result = merge_heads(parts[...] * totals)
        here = pl.ds(at * block, block)
        attended[here] = result
        inverse[here] = merge_heads(jnp.broadcast_to(totals, (2 * block, LANES)))
        result_staged[pl.ds(2 * at, 2)] = result.astype(BF16).reshape(2, S_DEV, LANES)
        for half in range(2):
            to = 2 * at + half

            @pl.when(to != seq)
            def _():
                remote(result_staged.at[to], target, out_send.at[to], out_recv.at[seq], (to, x)).start()

            @pl.when(to == seq)
            def _():
                pltpu.make_async_copy(result_staged.at[to], target, own_sem.at[4]).start()

        engine.tick(step % 4 // 3)

    leave((attended, attended_far), (inverse, inverse_far))

    for copy in small_copies:
        copy.wait()
    engine.until(cross_done)
    fetches = [
        pltpu.make_async_copy(full_rows(full, at), weights.at[part], fetch_sem.at[part])
        for part, at in enumerate((SELF_OUT_AT, CROSS_Q_AT, CROSS_OUT_AT))
    ]
    for fetch in fetches:
        fetch.start()
    gains = [
        jnp.concatenate(
            [small_full[at_pair, 128:144].astype(F32)[part:part + 1] for at_pair in range(PAIRS)], axis=1
        )
        for part in range(2)
    ]
    pltpu.make_async_copy(result_staged.at[seq], target, own_sem.at[4]).wait()
    for other, _ in others:
        remote(result_staged.at[other], target, out_send.at[other], out_recv.at[other], (other, x)).wait()
    fetches[0].wait()
    resid = tokens[...].reshape(2 * S_DEV, D).astype(F32) + dot_nn(
        gathered[...].reshape(2 * S_DEV, D), weights[0].reshape(D, D)
    )
    first_resid[...] = resid
    normed = norm_rows(resid, gains[0])
    first_norm[...] = normed
    engine.tick(STEP_TICKS)
    fetches[1].wait()
    cross_queries[...] = dot_nn(normed.astype(BF16), weights[1].reshape(D, D)).astype(BF16).reshape(2, S_DEV, D)
    engine.tick(STEP_TICKS)
    memory_len = 16 * M_DEV
    cross_prefix_lane = lax.broadcasted_iota(jnp.int32, (2 * S_DEV, 32), 1)
    for at_row in range(2):
        own = jnp.transpose(jnp.broadcast_to(docs[at_row:at_row + 1], (LANES, S_DEV)))
        own = jnp.concatenate([own] * (memory_len // LANES), axis=1)
        lines = [
            sum(docs_all[4 * at + k, 2 + at_row:3 + at_row] for k in range(4)) for at in range(4)
        ]
        allowed = own == jnp.concatenate(lines, axis=1)

        def one_pair(at_pair, carry):
            first = pl.multiple_of(at_pair * LANES, LANES)
            columns, value_columns = pl.ds(first, LANES), pl.ds(pl.multiple_of(first + D, LANES), LANES)
            stacked = stack_heads(cross_queries[at_row, :, columns])
            keys = memory_pairs[:, at_row, :, columns].reshape(memory_len, LANES)
            values = memory_pairs[:, at_row, :, value_columns].reshape(memory_len, LANES)
            scores = dot_right(stacked, small_full[at_pair, 64:96]) * score_scale
            prefix_e = jnp.where(cross_prefix_lane < PREFIX, jnp.exp(scores), 0.0)
            scores = dot_right(stacked, keys) * score_scale
            e = jnp.where(allowed[None], jnp.exp(scores).reshape(2, S_DEV, memory_len), 0.0)
            e = e.reshape(2 * S_DEV, memory_len)
            totals = jnp.sum(e, axis=1, keepdims=True) + jnp.sum(prefix_e, axis=1, keepdims=True)
            totals = 1.0 / totals
            summed = dot_nn(e.astype(BF16), values) + dot_nn(prefix_e.astype(BF16), small_full[at_pair, 96:128])
            crossed[at_row, :, columns] = merge_heads(summed * totals)
            cross_inverse[at_row, :, columns] = merge_heads(jnp.broadcast_to(totals, (2 * S_DEV, LANES)))
            return carry

        lax.fori_loop(0, PAIRS // 2, one_pair, 0)
        engine.tick(STEP_TICKS)
        lax.fori_loop(PAIRS // 2, PAIRS, one_pair, 0)
        engine.tick(STEP_TICKS)
    leave(
        (first_resid, first_resid_far), (cross_queries, cross_queries_far),
        (crossed, crossed_far), (cross_inverse, cross_inverse_far),
    )
    fetches[2].wait()
    resid = first_norm[...] + dot_nn(
        crossed[...].reshape(2 * S_DEV, D).astype(BF16), weights[2].reshape(D, D)
    )
    second_resid[...] = resid
    second_norm[...] = norm_rows(resid, gains[1])
    for copy in leaving:
        copy.wait()
    engine.finish()


def full_rows(full, first):
    return full.at[:, :, :, :, pl.ds(first, 32)]


def first_call(tokens, memory, small, docs, *weights):
    length = 16 * S_DEV
    chunks = 16 * 32 // PIECE_ROWS + 32 // PIECE_ROWS + 4
    dma = pltpu.SemaphoreType.DMA
    shape = jax.ShapeDtypeStruct
    outs = pl.pallas_call(
        first_kernel,
        out_shape=(
            shape((4, 2, 2, 2, ALL_ROWS, D), BF16),
            shape((4, 2, 2, 2, M_DEV, D), BF16),
            shape((16, 2, M_DEV, 2 * D), BF16),
            shape((length, LANES), F32),
            shape((16, 3, S_DEV, LANES), BF16),
            shape((length, LANES), F32),
            shape((length, LANES), F32),
            shape((2 * S_DEV, D), F32),
            shape((2, S_DEV, D), BF16),
            shape((2, S_DEV, D), F32),
            shape((2, S_DEV, D), F32),
            shape((8, SMALL_ROWS, LANES), BF16),
            shape((16, 8, LANES), F32),
            shape((8, length), F32),
            shape((2 * S_DEV, D), F32),
            shape((2 * S_DEV, D), F32),
        ),
        in_specs=[whole(), whole(pl.ANY), whole(), whole()] + [whole(pl.ANY)] * 8,
        out_specs=(whole(pl.ANY),) * 11 + (whole(),) * 5,
        scratch_shapes=[
            pltpu.VMEM((16, 2, M_DEV, 2 * D), BF16),
            pltpu.VMEM((length, LANES), F32),
            pltpu.VMEM((16, 3, S_DEV, LANES), BF16),
            pltpu.VMEM((length, LANES), F32),
            pltpu.VMEM((length, LANES), F32),
            pltpu.VMEM((2 * S_DEV, D), F32),
            pltpu.VMEM((2, S_DEV, D), BF16),
            pltpu.VMEM((2, S_DEV, D), F32),
            pltpu.VMEM((2, S_DEV, D), F32),
            pltpu.VMEM((2, S_DEV, D), BF16),
            pltpu.VMEM((2 * S_DEV, D), F32),
            pltpu.VMEM((3, 4, 2, 2, 2, 32, D), BF16),
            pltpu.VMEM((PAIRS, 2, 3, S_DEV, LANES), BF16),
            pltpu.VMEM((4, SMALL_ROWS, LANES), BF16),
            pltpu.VMEM((4, 2, 2, 2, M_DEV, D), BF16),
            pltpu.VMEM((16, S_DEV, LANES), BF16),
            pltpu.VMEM((4 * S_DEV, LANES), F32),
            pltpu.VMEM((4 * S_DEV, LANES), F32),
            dma((chunks,)),
            dma((chunks, 3)), dma((chunks, 3)), dma((chunks, 2)), dma((chunks, 2)),
            dma((chunks, 3)), dma((chunks, 3)), dma((chunks, 1)), dma((chunks, 1)),
            dma((3,)), dma((5,)), dma((3,)), dma((3,)), dma((8,)), dma((8,)), dma((15,)), dma((15,)),
            dma((15,)), dma((15,)), dma((16,)), dma((16,)), dma((9,)),
        ],
        compiler_params=params(0),
        name="first",
    )(tokens, memory, small, docs, *weights)
    return (outs[0].reshape(32, ALL_ROWS, D),) + tuple(outs[2:])


def second_kernel(
    second_grad, second_resid, small_full, docs, docs_all, docs_row, crossed, cross_inverse, cross_queries,
    full, memory_pairs_far, first_resid_far, arrived_far, attended_far, inverse_far, docs_column_far, small_grads,
    input_grad, memory_grad, down_grad, up_grad, prefix_sum,
    weights, memory_pairs, first_resid, arrived, attended, inverse, docs_column,
    pull, cross_grad, cross_query_grad, key_terms, value_terms, cross_prefix,
    small_core, small_mine, small_x, small_pair, small_y, small_line, small_all,
    memory_part, memory_core, memory_mine, memory_y, memory_line, memory_all,
    prefix_y, prefix_line, prefix_all, prefix_mine, prefix_quad,
    heads_out, grads, grad_low, delta, query_grads, key_grads, value_grads, staged, gathered,
    fetch_sem, own_sem, near_send, near_recv, line_send, line_recv, small_send, small_recv, memory_send, memory_recv,
    prefix_send, prefix_recv, quad_send, quad_recv,
    in_send, in_recv, out_send, out_recv, query_send, query_recv,
):
    place = Place()
    seq, x, pair, row, core = place.seq, place.x, place.pair, place.row, place.core
    z, y = place.z, place.y
    others = place.others()
    tokens = 2 * S_DEV
    memory_len = 16 * M_DEV
    block = 2 * S_DEV

    fetches = {}

    def fetch(name, source, target):
        fetches[name] = pltpu.make_async_copy(source, target, fetch_sem.at[len(fetches)])
        fetches[name].start()

    firsts = (CROSS_OUT_AT, CROSS_Q_AT, SELF_OUT_AT, MEM_K_AT, MEM_V_AT, Q_AT, K_AT, V_AT)

    def fetch_weight(at):
        fetch(at, full.at[:, pl.ds(at, 32)], weights.at[firsts.index(at)])

    def weight(at):
        return weights[firsts.index(at)].reshape(D, D)

    fetch_weight(CROSS_OUT_AT)
    fetch("pairs", memory_pairs_far, memory_pairs)
    fetch_weight(CROSS_Q_AT)
    fetch("resid", first_resid_far, first_resid)
    fetch_weight(SELF_OUT_AT)
    fetch_weight(MEM_K_AT)
    fetch_weight(MEM_V_AT)
    fetch("arrived", arrived_far, arrived)
    fetch("attended", attended_far, attended)
    fetch("inverse", inverse_far, inverse)
    fetch("docs", docs_column_far, docs_column)
    for at in (K_AT, V_AT, Q_AT):
        fetch_weight(at)
    greet(others + [place.along_x(), place.diagonal()])

    small_first = remote(
        small_grads.at[:, :, 1 - core], small_core, near_send.at[0], near_recv.at[0], place.other_core()
    )
    small_own = pltpu.make_async_copy(small_grads.at[:, :, core], small_mine, own_sem.at[0])
    small_second = remote(small_mine.at[:, :, 1 - x], small_x, near_send.at[1], near_recv.at[1], place.along_x())

    def along_y(k, source, target):
        return remote(source.at[:, 1 - y], target, line_send.at[k], line_recv.at[k], place.along_y())

    def along_z(source, target, sends, recvs):
        return [
            remote(source.at[(z + k) % 4], target.at[z], sends.at[k], recvs.at[k], place.along_z(k))
            for k in range(1, 4)
        ]

    small_third = along_y(0, small_pair, small_y)
    small_fourth = along_z(small_line, small_all, small_send, small_recv)
    memory_first = remote(
        memory_part.at[:, :, 1 - core], memory_core, near_send.at[2], near_recv.at[2], place.other_core()
    )
    memory_second = along_y(1, memory_mine, memory_y)
    memory_third = along_z(memory_line, memory_all, memory_send, memory_recv)
    prefix_first = along_y(2, cross_prefix, prefix_y)
    prefix_second = along_z(prefix_line, prefix_all, prefix_send, prefix_recv)
    small_first.start()
    small_own.start()

    gains = [
        jnp.concatenate(
            [small_full[at_pair, 128:144].astype(F32)[part:part + 1] for at_pair in range(PAIRS)], axis=1
        )
        for part in range(2)
    ]
    pulled = norm_back_rows(second_resid[...], gains[1], second_grad[...])
    pull[...] = pulled
    fetches[CROSS_OUT_AT].wait()
    cross_grad[...] = dot_right(pulled.astype(BF16), weight(CROSS_OUT_AT)).reshape(2, S_DEV, D)
    fetches["pairs"].wait()

    cross_pad = lax.broadcasted_iota(jnp.int32, (64, S_DEV), 0) % 32
    for at_row in range(2):
        lines = [sum(docs_all[4 * at + k, 2 + at_row:3 + at_row] for k in range(4)) for at in range(4)]
        key_docs = jnp.concatenate(
            [jnp.transpose(jnp.broadcast_to(line, (S_DEV, LANES))) for line in lines], axis=0
        )
        allowed = key_docs == docs[at_row:at_row + 1]

        def one_pair(at_pair, carry):
            first = pl.multiple_of(at_pair * LANES, LANES)
            columns, value_columns = pl.ds(first, LANES), pl.ds(pl.multiple_of(first + D, LANES), LANES)
            heads = cross_queries[at_row, :, columns]
            grad = cross_grad[at_row, :, columns] * cross_inverse[at_row, :, columns]
            low = grad.astype(BF16)
            lines = rows_in_lanes(grad * crossed[at_row, :, columns])

            def head_rows(count):
                return jnp.concatenate(
                    [jnp.broadcast_to(lines[0:1], (count, S_DEV)), jnp.broadcast_to(lines[1:2], (count, S_DEV))],
                    axis=0,
                )

            prefix_key_stack = stack_heads(small_full[at_pair, 64:96])
            prefix_value_stack = stack_heads(small_full[at_pair, 96:128])
            e = jnp.exp(dot_right(prefix_key_stack, heads) * score_scale)
            e = jnp.where(cross_pad < PREFIX, e, 0.0)
            slopes = (e * (dot_right(prefix_value_stack, low) - head_rows(32))).astype(BF16)
            from_prefix = dot_left(slopes, prefix_key_stack)
            key_grad = merge_heads(dot_nn(slopes, heads)) * score_scale
            value_grad = merge_heads(dot_nn(e.astype(BF16), low))
            held = cross_prefix.at[at_pair // 2, at_pair % 2]
            if at_row == 0:
                held[0] = key_grad
                held[1] = value_grad
            else:
                held[0] += key_grad
                held[1] += value_grad
            key_stack = stack_heads(memory_pairs[:, at_row, :, columns].reshape(memory_len, LANES))
            value_stack = stack_heads(memory_pairs[:, at_row, :, value_columns].reshape(memory_len, LANES))
            e = jnp.exp(dot_right(key_stack, heads) * score_scale).reshape(2, memory_len, S_DEV)
            e = jnp.where(allowed[None], e, 0.0).reshape(2 * memory_len, S_DEV)
            slopes = (e * (dot_right(value_stack, low) - head_rows(memory_len))).astype(BF16)
            terms = merge_heads(dot_nn(slopes, heads)) * score_scale
            key_terms[:, at_row, :, columns] = terms.astype(BF16).reshape(16, M_DEV, LANES)
            terms = merge_heads(dot_nn(e.astype(BF16), low))
            value_terms[:, at_row, :, columns] = terms.astype(BF16).reshape(16, M_DEV, LANES)
            query_grad = (from_prefix + dot_left(slopes, key_stack)) * score_scale
            cross_query_grad[at_row, :, columns] = query_grad.astype(BF16)
            return carry

        lax.fori_loop(0, PAIRS, one_pair, 0)
        if at_row == 0:
            small_own.wait()
            small_first.wait_recv()
            small_mine[...] = small_mine[...] + small_core[...]
            small_second.start()
    prefix_first.start()

    fetches[CROSS_Q_AT].wait()
    fetches["resid"].wait()
    first_grad = pull[...] + dot_right(cross_query_grad[...].reshape(tokens, D), weight(CROSS_Q_AT))
    resid_grad = norm_back_rows(first_resid[...], gains[0], first_grad)
    pull[...] = resid_grad
    fetches[SELF_OUT_AT].wait()
    out_grad = dot_right(resid_grad.astype(BF16), weight(SELF_OUT_AT)).astype(BF16)
    for at_pair in range(PAIRS):
        for at_row in range(2):
            heads_out[at_pair, at_row] = out_grad[
                at_row * S_DEV:(at_row + 1) * S_DEV, at_pair * LANES:(at_pair + 1) * LANES
            ]
    arrivals = []
    for k in range(15):
        to = (seq + k + 1) % 16
        arrivals.append(remote(heads_out.at[to // 2, to % 2], grads.at[seq], in_send.at[k], in_recv.at[k], others[k]))
        arrivals[-1].start()
    own_heads = pltpu.make_async_copy(heads_out.at[pair, row], grads.at[seq], own_sem.at[1])
    own_heads.start()

    fetches[MEM_K_AT].wait()
    fetches[MEM_V_AT].wait()

    def memory_block(at, carry):
        there = pl.ds(4 * at, 4)
        terms = dot_right(key_terms[there].reshape(8 * M_DEV, D), weight(MEM_K_AT))
        terms += dot_right(value_terms[there].reshape(8 * M_DEV, D), weight(MEM_V_AT))
        memory_part[at] = terms.astype(BF16).reshape(2, 2, 2 * M_DEV, D)
        return carry

    lax.fori_loop(0, 4, memory_block, 0)
    memory_first.start()
    small_second.wait()
    small_pair[...] = small_mine[:, :, x] + small_x[...]
    small_third.start()
    memory_first.wait()
    memory_mine[...] = memory_part[:, :, core] + memory_core[...]
    memory_second.start()
    for name in ("arrived", "attended", "inverse", "docs"):
        fetches[name].wait()
    own_heads.wait()
    for copy in arrivals:
        copy.wait()

    pad_row = lax.broadcasted_iota(jnp.int32, (64, block), 0) % 32
    prefix_key_stack = stack_heads(small_full[pair, 0:32])
    prefix_value_stack = stack_heads(small_full[pair, 32:64])

    def head_rows(at, count):
        there = delta[:, pl.ds(pl.multiple_of(at * block, block), block)]
        return jnp.concatenate(
            [jnp.broadcast_to(there[0:1], (count, block)), jnp.broadcast_to(there[1:2], (count, block))],
            axis=0,
        )

    prefix_mine[...] = jnp.zeros(prefix_mine.shape, F32)

    def prepare(at, carry):
        here = pl.ds(at * block, block)
        grad = grads[pl.ds(2 * at, 2)].reshape(block, LANES).astype(F32) * inverse[here]
        low = grad.astype(BF16)
        grad_low[here] = low
        delta[:, pl.ds(pl.multiple_of(at * block, block), block)] = rows_in_lanes(grad * attended[here])
        queries = arrived[pl.ds(2 * at, 2), 0].reshape(block, LANES)
        e = jnp.exp(dot_right(prefix_key_stack, queries) * score_scale)
        e = jnp.where(pad_row < PREFIX, e, 0.0)
        slopes = (e * (dot_right(prefix_value_stack, low) - head_rows(at, 32))).astype(BF16)
        prefix_mine[0] += merge_heads(dot_nn(slopes, queries)) * score_scale
        prefix_mine[1] += merge_heads(dot_nn(e.astype(BF16), low))
        query_grads[here] = dot_left(slopes, prefix_key_stack)
        return carry

    lax.fori_loop(0, 8, prepare, 0)
    prefix_first.wait()
    prefix_line[...] = cross_prefix[:, y] + prefix_y[...]
    for copy in prefix_second:
        copy.start()
    prefix_all[z] = prefix_line[z]
    small_third.wait()
    small_line[...] = small_pair[:, y] + small_y[...]
    for copy in small_fourth:
        copy.start()
    small_all[z] = small_line[z]

    away = (
        lax.broadcasted_iota(jnp.int32, (block, block), 0)
        - lax.broadcasted_iota(jnp.int32, (block, block), 1)
    )

    def send_block(part, count, at, send, recv):
        for half in range(2):
            to = 2 * at + half
            source = staged.at[to, pl.ds(part, count)]
            mine = gathered.at[pair, row, pl.ds(part, count)]

            @pl.when(to != seq)
            def _():
                remote(source, mine, send.at[to], recv.at[seq], (to, x)).start()

            @pl.when(to == seq)
            def _():
                pltpu.make_async_copy(source, mine, own_sem.at[2 + part]).start()

    def one_block(step, carry):
        key_at = (step + pair) % 8
        keys = stack_heads(arrived[pl.ds(2 * key_at, 2), 1].reshape(block, LANES))
        values = stack_heads(arrived[pl.ds(2 * key_at, 2), 2].reshape(block, LANES))
        key_docs = docs_column[pl.ds(key_at * block, block)]
        key_docs = jnp.concatenate([key_docs, key_docs], axis=1)
        key_grads[...] = jnp.zeros(key_grads.shape, F32)
        value_grads[...] = jnp.zeros(value_grads.shape, F32)

        def one_tile(at, carry):
            here = pl.ds(at * block, block)
            queries = arrived[pl.ds(2 * at, 2), 0].reshape(block, LANES)
            low = grad_low[here]
            query_docs = docs_row[0:1, pl.ds(pl.multiple_of(at * block, block), block)]
            allowed = (key_docs == query_docs) & (away <= (at - key_at) * block)
            e = jnp.exp(dot_right(keys, queries) * score_scale).reshape(2, block, block)
            e = jnp.where(allowed[None], e, 0.0).reshape(2 * block, block)
            slopes = (e * (dot_right(values, low) - head_rows(at, block))).astype(BF16)
            key_grads[...] += dot_nn(slopes, queries)
            value_grads[...] += dot_nn(e.astype(BF16), low)
            query_grads[here] += dot_left(slopes, keys)
            return carry

        lax.fori_loop(key_at, 8, one_tile, 0)
        there = pl.ds(2 * key_at, 2)
        staged[there, 1] = (merge_heads(key_grads[...]) * score_scale).astype(BF16).reshape(2, S_DEV, LANES)
        staged[there, 2] = merge_heads(value_grads[...]).astype(BF16).reshape(2, S_DEV, LANES)
        send_block(1, 2, key_at, out_send, out_recv)
        return carry

    lax.fori_loop(0, 2, one_block, 0)
    memory_second.wait()
    memory_line[...] = memory_mine[:, y] + memory_y[...]
    for copy in memory_third:
        copy.start()
    memory_all[z] = memory_line[z]
    lax.fori_loop(2, 8, one_block, 0)

    def last_block(step, carry):
        at = (step + pair) % 8
        result = (query_grads[pl.ds(at * block, block)] * score_scale).astype(BF16)
        staged[pl.ds(2 * at, 2), 0] = result.reshape(2, S_DEV, LANES)
        send_block(0, 1, at, query_send, query_recv)
        return carry

    lax.fori_loop(0, 8, last_block, 0)
    small_first.wait_send()
    for copy in prefix_second:
        copy.wait()
    for part in range(2):
        prefix_mine[2 + part] = sum(prefix_all[k, part] for k in range(4))
    prefix_quad[core * 2 + x] = prefix_mine[...]
    quad_copies = [
        remote(prefix_mine, prefix_quad.at[core * 2 + x], quad_send.at[k], quad_recv.at[k], peer)
        for k, peer in enumerate((place.other_core(), place.along_x(), place.diagonal()))
    ]
    for copy in quad_copies:
        copy.start()
    for copy in small_fourth:
        copy.wait()
    total = small_all[0].astype(F32)
    for k in range(1, 4):
        total += small_all[k].astype(F32)
    down_grad[...] = total[:, :ADAPTER]
    up_grad[:, :ADAPTER] = total[:16, ADAPTER:]
    up_grad[:, ADAPTER:] = total[16:, ADAPTER:]
    for copy in memory_third:
        copy.wait()
    total = memory_all[0].astype(F32)
    for k in range(1, 4):
        total += memory_all[k].astype(F32)
    memory_grad[...] = total
    for copy in quad_copies:
        copy.wait()
    prefix_sum[...] = (prefix_quad[0] + prefix_quad[1]) + (prefix_quad[2] + prefix_quad[3])

    pltpu.make_async_copy(staged.at[seq, pl.ds(1, 2)], gathered.at[pair, row, pl.ds(1, 2)], own_sem.at[3]).wait()
    for other, _ in others:
        remote(
            staged.at[other, pl.ds(1, 2)], gathered.at[other // 2, other % 2, pl.ds(1, 2)],
            out_send.at[other], out_recv.at[other], (other, x),
        ).wait()

    def part_grad(part, at):
        fetches[at].wait()
        joined = jnp.concatenate([gathered[k, :, part].reshape(tokens, LANES) for k in range(PAIRS)], axis=1)
        return dot_right(joined, weight(at))

    input_grad[...] = pull[...] + part_grad(1, K_AT) + part_grad(2, V_AT)
    pltpu.make_async_copy(staged.at[seq, pl.ds(0, 1)], gathered.at[pair, row, pl.ds(0, 1)], own_sem.at[2]).wait()
    for other, _ in others:
        remote(
            staged.at[other, pl.ds(0, 1)], gathered.at[other // 2, other % 2, pl.ds(0, 1)],
            query_send.at[other], query_recv.at[other], (other, x),
        ).wait()
    input_grad[...] += part_grad(0, Q_AT)


def second_call(*operands):
    length = 16 * S_DEV
    tokens = 2 * S_DEV
    dma = pltpu.SemaphoreType.DMA
    shape = jax.ShapeDtypeStruct
    return pl.pallas_call(
        second_kernel,
        out_shape=(
            shape((tokens, D), F32),
            shape((2 * M_DEV, D), F32),
            shape((32, ADAPTER), F32),
            shape((16, D), F32),
            shape((4, 32, LANES), F32),
        ),
        in_specs=[whole()] * 9 + [whole(pl.ANY)] * 8,
        out_specs=(whole(),) * 5,
        scratch_shapes=[
            pltpu.VMEM((8, 32, 32, D), BF16),
            pltpu.VMEM((16, 2, M_DEV, 2 * D), BF16),
            pltpu.VMEM((tokens, D), F32),
            pltpu.VMEM((16, 3, S_DEV, LANES), BF16),
            pltpu.VMEM((length, LANES), F32),
            pltpu.VMEM((length, LANES), F32),
            pltpu.VMEM((length, LANES), F32),
            pltpu.VMEM((tokens, D), F32),
            pltpu.VMEM((2, S_DEV, D), F32),
            pltpu.VMEM((2, S_DEV, D), BF16),
            pltpu.VMEM((16, 2, M_DEV, D), BF16),
            pltpu.VMEM((16, 2, M_DEV, D), BF16),
            pltpu.VMEM((4, 2, 2, 32, LANES), F32),
            pltpu.VMEM((4, 2, 2, 32, D), BF16),
            pltpu.VMEM((4, 2, 2, 32, D), BF16),
            pltpu.VMEM((4, 2, 32, D), BF16),
            pltpu.VMEM((4, 2, 32, D), BF16),
            pltpu.VMEM((4, 32, D), BF16),
            pltpu.VMEM((4, 32, D), BF16),
            pltpu.VMEM((4, 32, D), BF16),
            pltpu.VMEM((4, 2, 2, 2 * M_DEV, D), BF16),
            pltpu.VMEM((4, 2, 2 * M_DEV, D), BF16),
            pltpu.VMEM((4, 2, 2 * M_DEV, D), BF16),
            pltpu.VMEM((4, 2 * M_DEV, D), BF16),
            pltpu.VMEM((4, 2 * M_DEV, D), BF16),
            pltpu.VMEM((4, 2 * M_DEV, D), BF16),
            pltpu.VMEM((4, 2, 32, LANES), F32),
            pltpu.VMEM((4, 2, 32, LANES), F32),
            pltpu.VMEM((4, 2, 32, LANES), F32),
            pltpu.VMEM((4, 32, LANES), F32),
            pltpu.VMEM((4, 4, 32, LANES), F32),
            pltpu.VMEM((PAIRS, 2, S_DEV, LANES), BF16),
            pltpu.VMEM((16, S_DEV, LANES), BF16),
            pltpu.VMEM((length, LANES), BF16),
            pltpu.VMEM((8, length), F32),
            pltpu.VMEM((length, LANES), F32),
            pltpu.VMEM((4 * S_DEV, LANES), F32),
            pltpu.VMEM((4 * S_DEV, LANES), F32),
            pltpu.VMEM((16, 3, S_DEV, LANES), BF16),
            pltpu.VMEM((PAIRS, 2, 3, S_DEV, LANES), BF16),
            dma((14,)), dma((4,)), dma((3,)), dma((3,)), dma((3,)), dma((3,)), dma((4,)), dma((4,)), dma((4,)), dma((4,)),
            dma((4,)), dma((4,)), dma((3,)), dma((3,)),
            dma((15,)), dma((15,)), dma((16,)), dma((16,)), dma((16,)), dma((16,)),
        ],
        compiler_params=params(1),
        name="second",
    )(*operands)


def gelu_parts(pre):
    upper = 0.5 * (1.0 + lax.erf(pre * (0.5 ** 0.5)))
    return upper


def gelu_slope(pre):
    return gelu_parts(pre) + pre * jnp.exp(-0.5 * pre * pre) * (1.0 / math.sqrt(2.0 * math.pi))


def norm_back_rows(resid, gain, upstream):
    middle = jnp.mean(resid, axis=-1, keepdims=True)
    centred = resid - middle
    scale = lax.rsqrt(jnp.mean(centred * centred, axis=-1, keepdims=True) + 1e-05)
    unit = centred * scale
    pulled = upstream * gain
    return scale * (
        pulled - jnp.mean(pulled, axis=-1, keepdims=True) - unit * jnp.mean(pulled * unit, axis=-1, keepdims=True)
    )


def feed_kernel(
    normed, cotangent, gain, inner, outer, mixed,
    layer_out, second_grad, small_grads,
    low, pre, adapter_pre, total, feed_low,
):
    step = pl.program_id(0)
    down = mixed[:, :, :ADAPTER].reshape(D, ADAPTER)
    up_left = mixed[:, :16, ADAPTER:].reshape(ADAPTER, ADAPTER)
    up_right = mixed[:, 16:, ADAPTER:].reshape(ADAPTER, ADAPTER)
    half = ADAPTER

    @pl.when(step == 0)
    def _():
        low[...] = normed[...].astype(BF16)
        adapter_pre[...] = dot_nn(low[...], down)
        act = adapter_pre[...]
        act = (act * gelu_parts(act)).astype(BF16)
        total[:, :half] = normed[:, :half] + 4.0 * dot_nn(act, up_left)
        total[:, half:] = normed[:, half:] + 4.0 * dot_nn(act, up_right)

    @pl.when(step < 4)
    def _():
        hidden = dot_nn(low[...], inner[...].reshape(D, D))
        pre[jnp.minimum(step, 3)] = hidden
        act = (hidden * gelu_parts(hidden)).astype(BF16)
        total[...] += dot_nn(act, outer[...].reshape(D, D))

    @pl.when(step == 3)
    def _():
        resid = total[...]
        layer_out[...] = norm_rows(resid, gain[...]).astype(BF16)
        third_grad = norm_back_rows(resid, gain[...], cotangent[...].astype(F32))
        feed_low[...] = third_grad.astype(BF16)
        adapter_low = (4.0 * third_grad).astype(BF16)
        act = adapter_pre[...]
        upper = gelu_parts(act)
        slope = gelu_slope(act)
        act = (act * upper).astype(BF16)
        grad = dot_right(adapter_low[:, :half], up_left) + dot_right(adapter_low[:, half:], up_right)
        grad = (slope * grad).astype(BF16)
        second_grad[...] = third_grad + dot_right(grad, down)
        small_grads[:, :, :half] = dot_left(low[...], grad).astype(BF16).reshape(32, 32, half)
        small_grads[:, :16, half:] = dot_left(act, adapter_low[:, :half]).astype(BF16).reshape(32, 16, half)
        small_grads[:, 16:, half:] = dot_left(act, adapter_low[:, half:]).astype(BF16).reshape(32, 16, half)

    @pl.when(step >= 4)
    def _():
        hidden = pre[jnp.clip(7 - step, 0, 3)]
        grad = dot_right(feed_low[...], outer[...].reshape(D, D))
        grad = (gelu_slope(hidden) * grad).astype(BF16)
        second_grad[...] += dot_right(grad, inner[...].reshape(D, D))


def feed_forward_backward(normed, cotangent, gain, weights):
    tokens = normed.shape[0]
    at = lambda step: jnp.minimum(step, 7 - step)
    still = lambda step: (0, 0)
    rows = pl.BlockSpec((tokens, D), still)
    return pl.pallas_call(
        feed_kernel,
        grid=(8,),
        out_shape=(
            jax.ShapeDtypeStruct((tokens, D), BF16),
            jax.ShapeDtypeStruct((tokens, D), F32),
            jax.ShapeDtypeStruct((32, 32, D), BF16),
        ),
        in_specs=[
            rows, rows, pl.BlockSpec((1, D), still),
            pl.BlockSpec((32, 32, D), lambda step: (0, INNER_AT // 32 + at(step), 0)),
            pl.BlockSpec((8, 128, D), lambda step: (at(step), OUTER_AT // 128, 0)),
            pl.BlockSpec((32, 32, D), lambda step: (0, MIXED_AT // 32, 0)),
        ],
        out_specs=(rows, rows, pl.BlockSpec((32, 32, D), lambda step: (0, 0, 0))),
        scratch_shapes=[
            pltpu.VMEM((tokens, D), BF16),
            pltpu.VMEM((4, tokens, D), F32),
            pltpu.VMEM((tokens, ADAPTER), F32),
            pltpu.VMEM((tokens, D), F32),
            pltpu.VMEM((tokens, D), BF16),
        ],
        compiler_params=params(),
        name="feed",
    )(normed, cotangent, gain, weights, weights, weights)


def fast_device(
    inputs, memory, out_grad, token_docs, memory_docs, self_project, self_output, cross_query,
    cross_memory, cross_output, inner_weight, outer_weight, adapter_down, adapter_up, norm_gains, prefixes,
):
    seq, x = lax.axis_index("seq"), lax.axis_index("rows")
    tokens = 2 * S_DEV
    mixed = jnp.concatenate(
        [adapter_down, jnp.concatenate([adapter_up[:, :ADAPTER], adapter_up[:, ADAPTER:]], axis=0)], axis=1
    )
    lane_group = lax.broadcasted_iota(jnp.int32, (1, LANES), 1) // 32
    small = jnp.concatenate([
        jnp.pad(prefixes, ((0, 0), (0, 2), (0, 0))).reshape(128, 32), jnp.pad(norm_gains, ((0, 13), (0, 0)))
    ])
    small = jnp.where(lane_group == (seq % 2) * 2 + x, jnp.tile(small, (1, 4)), jnp.zeros((), BF16))
    memory_line = jnp.where(lane_group == seq % 4, jnp.tile(memory_docs, (1, 4)), 0)
    docs = jnp.concatenate([token_docs, memory_line, jnp.zeros((4, LANES), jnp.int32)]).astype(F32)
    (
        full, memory_pairs, docs_column, arrived, pair_attended, pair_inverse,
        first_resid, cross_queries, crossed, cross_inverse, small_full, docs_all, docs_row, second_resid, second_norm,
    ) = first_call(
        inputs, memory.reshape(2, M_DEV, D), small, docs,
        self_project, self_output, cross_query, cross_memory, cross_output, inner_weight, outer_weight, mixed,
    )

    third_gain = small_full[:, 130].reshape(1, D).astype(F32)
    layer_out, second_grad, small_grads = feed_forward_backward(
        second_norm, out_grad.reshape(tokens, D), third_gain, full
    )
    input_grad, memory_grad, down_grad, up_grad, prefix_sum = second_call(
        second_grad, second_resid, small_full, docs, docs_all, docs_row, crossed, cross_inverse, cross_queries,
        full, memory_pairs, first_resid, arrived, pair_attended, pair_inverse, docs_column,
        small_grads.reshape(4, 2, 2, 2, 32, D),
    )
    prefix_grad = lax.dynamic_slice_in_dim(prefix_sum[:, :PREFIX], 32 * ((seq % 2) * 2 + x), 32, 2)
    return (
        layer_out.reshape(2, S_DEV, D),
        input_grad.reshape(2, S_DEV, D),
        memory_grad.reshape(2, M_DEV, D),
        prefix_grad,
        down_grad,
        up_grad,
    )


def solution(mesh):
    placed = (
        P("rows", "seq", None),
        P("rows", "seq", None),
        P("rows", "seq", None),
        P("rows", "seq"),
        P("rows", "seq"),
        P(("seq", "rows"), None),
        P(("seq", "rows"), None),
        P(("seq", "rows"), None),
        P(("seq", "rows"), None),
        P(("seq", "rows"), None),
        P(("seq", "rows"), None),
        P(("seq", "rows"), None),
        P(("seq", "rows"), None),
        P(("seq", "rows"), None),
        P(None, ("seq", "rows")),
        P(None, None, ("seq", "rows")),
    )
    small_slice = mesh.shape["seq"] == 16 and mesh.shape["rows"] == 2
    return jax.shard_map(
        fast_device if small_slice else per_device,
        mesh=mesh,
        in_specs=placed,
        out_specs=(
            P("rows", "seq", None),
            P("rows", "seq", None),
            P("rows", "seq", None),
            P(None, None, ("seq", "rows")),
            P(("seq", "rows"), None),
            P(("seq", "rows"), None),
        ),
        check_vma=False,
    )
```
